32 devices in a mesh: seq: 16 (over z, y, core), tensor: 2 (over x).
Axes of the slice: x: 2, y: 2, z: 4, core: 2. Of those that a mesh axis runs over, the one named last changes fastest.
Arguments:
- latents: bfloat16 [2, 4096, 1536], P(None, 'seq'), may hold values from -6 to 6
- context: bfloat16 [2, 512, 768], replicated, may hold values from -6 to 6
- lengths: int32 [2, 4], replicated, may hold values from 512 to 1536, as said below
- text_len: int32 [2, 4], replicated, may hold values from 1 to 128, as said below
- timesteps: int32 [2, 4], replicated, may hold values from 0 to 999
- self_qkv: bfloat16 [3, 1536, 1536], P(None, 'seq', 'tensor'), may hold values from -0.15625 to 0.15625
- self_out: bfloat16 [1536, 1536], P('tensor', 'seq'), may hold values from -0.625 to 0.625
- cross_query: bfloat16 [1536, 1536], P('seq', 'tensor'), may hold values from -0.15625 to 0.15625
- cross_kv: bfloat16 [2, 768, 1536], P(None, 'seq', 'tensor'), may hold values from -0.21875 to 0.21875
- cross_out: bfloat16 [1536, 1536], P('tensor', 'seq'), may hold values from -0.4375 to 0.4375
- ffn_in: bfloat16 [2, 1536, 6144], P(None, 'seq', 'tensor'), may hold values from -0.15625 to 0.15625
- ffn_out: bfloat16 [6144, 1536], P('tensor', 'seq'), may hold values from -0.15625 to 0.15625
- mod_weight: bfloat16 [256, 6, 1536], P('seq'), may hold values from -0.1875 to 0.1875
- mod_bias: bfloat16 [6, 1536], P(None, 'seq'), may hold values from -1.5 to 1.5
- out_grad: bfloat16 [2, 4096, 1536], P(None, 'seq'), may hold values from -6 to 6
Outputs:
- block_out: bfloat16 [2, 4096, 1536], P(None, 'seq')
- latent_grad: float32 [2, 4096, 1536], P(None, 'seq')
- grad_self_qkv: float32 [3, 1536, 1536], P(None, 'seq', 'tensor')
- grad_self_out: float32 [1536, 1536], P('tensor', 'seq')
- grad_cross_query: float32 [1536, 1536], P('seq', 'tensor')
- grad_cross_kv: float32 [2, 768, 1536], P(None, 'seq', 'tensor')
- grad_cross_out: float32 [1536, 1536], P('tensor', 'seq')
- grad_ffn_in: float32 [2, 1536, 6144], P(None, 'seq', 'tensor')
- grad_ffn_out: float32 [6144, 1536], P('tensor', 'seq')
- grad_mod_weight: float32 [256, 6, 1536], P('seq')
- grad_mod_bias: float32 [6, 1536], P(None, 'seq')
The draws below stay inside these ranges and needn't reach their ends.
Inputs may be any that keep to these rules, and one draw needn't show every extreme that they name: Within each micro-batch the lengths sum to 4096; in every micro-batch some item has exactly 1536 frames and some exactly 512. `text_len`: in every micro-batch some item uses all 128 slots and some item one slot.
All inputs are finite; a program needn't handle non-finite values.
Results may differ from the reference program's by a relative error of at most 0.023.
Values may be sent and summed in bfloat16 or wider, within the bound.
A program may use at most 384 MiB of HBM per device.

```python
import math
import jax
import jax.numpy as jnp
from jax import lax

D = 1536
HD = 64
FF = 6144
C = 768
TXT = 128
TEMB = 256
HALF = 128
MEANLEN = 1024
LEN_LO = 512
FR_DEV = 256
MB = 2
FRAMES = 4096
ITEMS = 4


def draw_lengths(key, part):
    key = jax.random.fold_in(key, 11)
    reach = MEANLEN - LEN_LO
    pair_count = ITEMS // 2
    offsets = jax.random.randint(jax.random.fold_in(key, 1), (MB, pair_count), 0, reach + 1)
    column = jnp.arange(pair_count)[None, :]
    offsets = jnp.where(column == 0, reach, offsets)
    paired = jnp.concatenate([MEANLEN + offsets, MEANLEN - offsets], axis=1)
    order_keys = jax.random.split(jax.random.fold_in(key, 2), MB)

    def shuffled(order_key):
        return jax.random.permutation(order_key, ITEMS)
    order = jax.vmap(shuffled)(order_keys)
    return jnp.take_along_axis(paired, order, axis=1).astype(jnp.int32)


def draw_text_len(key, part):
    key = jax.random.fold_in(key, 23)
    drawn = jax.random.randint(jax.random.fold_in(key, 1), (MB, ITEMS), 1, TXT + 1)
    chosen = jax.random.randint(jax.random.fold_in(key, 2), (MB, 1), 0, ITEMS)
    column = jnp.arange(ITEMS)[None, :]
    longest = jnp.where(column == chosen, TXT, drawn)
    return jnp.where(column == (chosen + 1) % ITEMS, 1, longest).astype(jnp.int32)


def place_ends(values, rng, least, high):
    spot = [jax.random.randint(jax.random.fold_in(rng, axis), (), 0, length) for axis, length in enumerate(values.shape)]
    widest = values.shape.index(max(values.shape))
    neighbour = spot[:widest] + [(spot[widest] + 1) % values.shape[widest]] + spot[widest + 1:]
    return values.at[tuple(spot)].set(least).at[tuple(neighbour)].set(high)


def block_scale(rng, extent, shards, low, top_value):
    gain = 1.0
    for dim, shards_of in shards:
        steps = jax.random.uniform(jax.random.fold_in(jax.random.fold_in(rng, 6), dim), (shards_of,), jnp.float32, low / len(shards), top_value / len(shards))
        gain = gain * jnp.repeat(jnp.exp(steps), extent[dim] // shards_of).reshape((-1,) + (1,) * (len(extent) - 1 - dim))
    return gain


def centred(stream_key, shape, width, most, shards=(), held_as=jnp.bfloat16):
    values = width * jax.random.normal(stream_key, shape, jnp.float32)
    if shards:
        values = values * block_scale(stream_key, shape, shards, -0.22, 0.18)
    return jnp.clip(values, -most, most).astype(held_as)


def setup_inputs(seed: int = 0) -> dict:
    arg_keys = jax.random.split(jax.random.key(seed), 16)
    return {
        "latents": centred(arg_keys[0], (MB, FRAMES, D), 1.0, 6.0, ((1, 16),)),
        "context": centred(arg_keys[1], (MB, ITEMS * TXT, C), 1.0, 6.0),
        "lengths": draw_lengths(jax.random.fold_in(arg_keys[15], 71), 0),
        "text_len": draw_text_len(jax.random.fold_in(arg_keys[15], 71), 0),
        "timesteps": place_ends(jax.random.randint(arg_keys[4], (MB, ITEMS), 0, 1000), jax.random.fold_in(arg_keys[4], 1), 0, 999).astype(jnp.int32),
        "self_qkv": centred(arg_keys[5], (3, D, D), D ** -0.5, 0.15625, ((1, 16), (2, 2))),
        "self_out": centred(arg_keys[6], (D, D), (D // 16) ** -0.5, 0.625, ((0, 2), (1, 16))),
        "cross_query": centred(arg_keys[7], (D, D), D ** -0.5, 0.15625, ((0, 16), (1, 2))),
        "cross_kv": centred(arg_keys[8], (2, C, D), C ** -0.5, 0.21875, ((1, 16), (2, 2))),
        "cross_out": centred(arg_keys[9], (D, D), (D // 8) ** -0.5, 0.4375, ((0, 2), (1, 16))),
        "ffn_in": centred(arg_keys[10], (2, D, FF), D ** -0.5, 0.15625, ((1, 16), (2, 2))),
        "ffn_out": centred(arg_keys[11], (FF, D), (FF // 4) ** -0.5, 0.15625, ((0, 2), (1, 16))),
        "mod_weight": centred(arg_keys[12], (TEMB, 6, D), (TEMB * 4) ** -0.5, 0.1875, ((0, 16),)),
        "mod_bias": centred(arg_keys[13], (6, D), 0.3, 1.5, ((1, 16),)),
        "out_grad": centred(arg_keys[14], (MB, FRAMES, D), 1.0, 6.0, ((1, 16),)),
    }


@jax.custom_vjp
def low(v):
    return lax.optimization_barrier(v.astype(jnp.bfloat16)).astype(jnp.float32)

@jax.custom_vjp
def low_back(v):
    return v

def low_keep(v):
    return (low(v), None)

def low_pass(kept, grad):
    return (grad,)

def back_keep(v):
    return (v, None)

def back_low(kept, grad):
    return (low(grad),)
low.defvjp(low_keep, low_pass)
low_back.defvjp(back_keep, back_low)
norm_eps = 1e-05
highest = lax.Precision.HIGHEST

def modulated_norm(hidden, offset, factor):
    center = hidden - lax.optimization_barrier(jnp.mean(hidden, axis=-1, keepdims=True))
    spread = lax.optimization_barrier(jnp.mean(center * center, axis=-1, keepdims=True))
    return center * lax.rsqrt(spread + norm_eps) * (1.0 + factor) + offset

def rotary(values, places):
    quarter = HD // 4
    ladder = jnp.exp(-math.log(10000.0) * jnp.arange(quarter, dtype=jnp.float32) / quarter)
    angles = places.astype(jnp.float32)[:, None] * ladder[None, :]
    cosine = jnp.cos(angles)[:, None, :]
    sine_part = jnp.sin(angles)[:, None, :]
    first_half = values[..., :quarter]
    second_half = values[..., quarter:2 * quarter]
    return jnp.concatenate([first_half * cosine - second_half * sine_part, second_half * cosine + first_half * sine_part, values[..., 2 * quarter:]], axis=-1)

def time_features(steps_row):
    half_width = TEMB // 2
    ladder = jnp.exp(-math.log(10000.0) * jnp.arange(half_width, dtype=jnp.float32) / half_width)
    angles = steps_row.astype(jnp.float32)[:, None] * ladder[None, :]
    return jnp.concatenate([jnp.cos(angles), jnp.sin(angles)], axis=-1)

def item_table(item_ends, places):
    return lax.optimization_barrier(jnp.sum((item_ends[None, :] <= places[:, None]).astype(jnp.int32), axis=1)).astype(jnp.int32)

def attend_ref(query_rows, key_rows, value_rows, allowed, factor):
    scores = low_back(jnp.einsum('qhd,khd->hqk', query_rows, key_rows, precision=highest) * factor)
    scores = jnp.where(allowed[None], scores, -1e+30)
    weights = low(jax.nn.softmax(scores, axis=-1))
    return jnp.einsum('hqk,khd->qhd', weights, value_rows, precision=highest)

def one_batch(latent, context_rows, lengths_row, text_row, steps_row, qkv_weight, self_weight, query_weight, pair_weight, cross_weight, inner_weight, outer_weight, mod_full, bias_full):
    frame_count = latent.shape[0]
    model_width = latent.shape[1]
    item_count = lengths_row.shape[0]
    head_count = model_width // HD
    block_rows = FR_DEV
    factor = HD ** (-0.5)
    places = jnp.arange(frame_count, dtype=jnp.int32)
    item_ends = jnp.cumsum(lengths_row).astype(jnp.int32)
    item_starts = (item_ends - lengths_row).astype(jnp.int32)
    item_ids = item_table(item_ends, places)
    catalog = jnp.arange(item_count, dtype=jnp.int32)
    choose = item_ids[:, None] == catalog[None, :]
    offsets_in = (places - lax.optimization_barrier(jnp.sum(choose.astype(jnp.int32) * item_starts[None, :], axis=1))).astype(jnp.int32)
    modulation = jnp.dot(time_features(steps_row), mod_full.reshape(mod_full.shape[0], -1), precision=highest) + bias_full.reshape(1, -1)
    framewise = jnp.dot(choose.astype(jnp.float32), modulation, precision=highest).reshape(frame_count, 6, model_width)
    normed_one = low(modulated_norm(latent, framewise[:, 0], framewise[:, 1]))
    projected = low_back(jnp.einsum('nd,tde->tne', normed_one, qkv_weight, precision=highest))
    queries = low(rotary(projected[0].reshape(frame_count, head_count, HD), offsets_in))
    key_rows = low(rotary(projected[1].reshape(frame_count, head_count, HD), offsets_in))
    value_rows = low(projected[2].reshape(frame_count, head_count, HD))
    padded_keys = jnp.pad(key_rows, ((HALF, HALF), (0, 0), (0, 0)))
    padded_values = jnp.pad(value_rows, ((HALF, HALF), (0, 0), (0, 0)))
    outer_places = jnp.arange(frame_count + 2 * HALF, dtype=jnp.int32) - HALF
    outer_ids = item_table(item_ends, outer_places)
    outer_inside = (outer_places >= 0) & (outer_places < frame_count)

    def self_block(block_index):
        first_row = (block_index * block_rows).astype(jnp.int32)
        query_rows = lax.dynamic_slice_in_dim(queries, first_row, block_rows, 0)
        near_keys = lax.dynamic_slice_in_dim(padded_keys, first_row, block_rows + 2 * HALF, 0)
        near_values = lax.dynamic_slice_in_dim(padded_values, first_row, block_rows + 2 * HALF, 0)
        own_places = lax.dynamic_slice_in_dim(places, first_row, block_rows, 0)
        own_ids = lax.dynamic_slice_in_dim(item_ids, first_row, block_rows, 0)
        near_places = lax.dynamic_slice_in_dim(outer_places, first_row, block_rows + 2 * HALF, 0)
        near_ids = lax.dynamic_slice_in_dim(outer_ids, first_row, block_rows + 2 * HALF, 0)
        near_inside = lax.dynamic_slice_in_dim(outer_inside, first_row, block_rows + 2 * HALF, 0)
        allowed = (own_ids[:, None] == near_ids[None, :]) & near_inside[None, :] & (jnp.abs(own_places[:, None] - near_places[None, :]) <= HALF)
        return attend_ref(query_rows, near_keys, near_values, allowed, factor)
    blocks = jnp.arange(frame_count // block_rows, dtype=jnp.int32)
    mixed_one = lax.map(jax.checkpoint(self_block), blocks).reshape(frame_count, model_width)
    mixed_one = low(low_back(mixed_one))
    hidden_one = latent + low_back(jnp.dot(mixed_one, self_weight, precision=highest))
    normed_two = low(modulated_norm(hidden_one, framewise[:, 2], framewise[:, 3]))
    cross_queries = low(low_back(jnp.dot(normed_two, query_weight, precision=highest))).reshape(frame_count, head_count, HD)

    def cross_block(block_index):
        first_row = (block_index * block_rows).astype(jnp.int32)
        query_rows = lax.dynamic_slice_in_dim(cross_queries, first_row, block_rows, 0)
        own_ids = lax.dynamic_slice_in_dim(item_ids, first_row, block_rows, 0)
        base_item = jnp.minimum(own_ids[0], item_count - 2).astype(jnp.int32)
        near_context = lax.dynamic_slice_in_dim(context_rows, (base_item * TXT).astype(jnp.int32), 2 * TXT, 0)
        near_pairs = low(low_back(jnp.einsum('rc,tce->tre', near_context, pair_weight, precision=highest)))
        near_keys = near_pairs[0].reshape(2 * TXT, head_count, HD)
        near_values = near_pairs[1].reshape(2 * TXT, head_count, HD)
        text_slots = jnp.arange(2 * TXT, dtype=jnp.int32)
        key_items = base_item + text_slots // TXT
        key_lengths = lax.optimization_barrier(jnp.sum((key_items[:, None] == catalog[None, :]).astype(jnp.int32) * text_row[None, :], axis=1)).astype(jnp.int32)
        allowed = (own_ids[:, None] == key_items[None, :]) & (text_slots % TXT < key_lengths)[None, :]
        return attend_ref(query_rows, near_keys, near_values, allowed, factor)
    mixed_two = lax.map(jax.checkpoint(cross_block), blocks).reshape(frame_count, model_width)
    mixed_two = low(low_back(mixed_two))
    hidden_two = hidden_one + low_back(jnp.dot(mixed_two, cross_weight, precision=highest))
    normed_three = low(modulated_norm(hidden_two, framewise[:, 4], framewise[:, 5]))
    gate_up = low_back(jnp.einsum('nd,tdf->tnf', normed_three, inner_weight, precision=highest))
    activated = low(jax.nn.silu(gate_up[0]) * gate_up[1])
    return hidden_two + low_back(jnp.dot(activated, outer_weight, precision=highest))

def reference(latents, context, lengths, text_len, timesteps, self_qkv, self_out, cross_query, cross_kv, cross_out, ffn_in, ffn_out, mod_weight, mod_bias, out_grad):
    text_rows = context.astype(jnp.float32)

    def forward(latent_all, qkv_weight, self_weight, query_weight, pair_weight, cross_weight, inner_weight, outer_weight, mod_full, bias_full):
        outputs = []
        for micro_index in range(latent_all.shape[0]):
            outputs.append(one_batch(latent_all[micro_index], text_rows[micro_index], lengths[micro_index], text_len[micro_index], timesteps[micro_index], qkv_weight, self_weight, query_weight, pair_weight, cross_weight, inner_weight, outer_weight, mod_full, bias_full))
        return jnp.stack(outputs)
    result, pullback = jax.vjp(forward, latents.astype(jnp.float32), self_qkv.astype(jnp.float32), self_out.astype(jnp.float32), cross_query.astype(jnp.float32), cross_kv.astype(jnp.float32), cross_out.astype(jnp.float32), ffn_in.astype(jnp.float32), ffn_out.astype(jnp.float32), mod_weight.astype(jnp.float32), mod_bias.astype(jnp.float32))
    grads = pullback(out_grad.astype(jnp.float32))
    return (result.astype(jnp.bfloat16), grads[0], grads[1], grads[2], grads[3], grads[4], grads[5], grads[6], grads[7], grads[8], grads[9])
```

```python
import math

import jax
import jax.numpy as jnp
from jax import lax
from jax.sharding import PartitionSpec as P

HD = 64
TXT = 128
TEMB = 256
HALF = 128


norm_eps = 1e-05
highest = lax.Precision.HIGHEST
f32 = jnp.float32
bf16 = jnp.bfloat16


def dot(a, b, dims):
    return lax.dot_general(a, b, ((dims[0], dims[1]), ((), ())), preferred_element_type=f32)


def nn(a, b):
    return dot(a, b, ((1,), (0,)))


def nt(a, b):
    return dot(a, b, ((1,), (1,)))


def tn(a, b):
    return dot(a, b, ((0,), (0,)))


def halves(count):
    stride = 1
    strides = []
    while stride < count:
        strides.append(stride)
        stride *= 2
    return strides


def flip(block, stride):
    count = lax.axis_size("seq")
    return lax.ppermute(block, "seq", [(i, i ^ stride) for i in range(count)])


def pair_sum(part):
    count = lax.axis_size("tensor")
    other = lax.ppermute(part, "tensor", [(i, (i + 1) % count) for i in range(count)])
    return part.astype(f32) + other.astype(f32)


def seq_sum(part):
    for stride in halves(lax.axis_size("seq")):
        part = part + flip(part, stride)
    return part


def scatter_sum(grad):
    count = lax.axis_size("seq")
    me = lax.axis_index("seq")
    width = grad.shape[1]
    rows = grad.shape[0] // count
    cur = grad.reshape(count, rows, width)
    for stride in halves(count):
        digit = (me // stride) % 2
        pairs = cur.reshape(cur.shape[0] // 2, 2, rows, width)
        kept = lax.dynamic_index_in_dim(pairs, digit, 1, keepdims=False)
        sent = lax.dynamic_index_in_dim(pairs, 1 - digit, 1, keepdims=False)
        got = flip(sent, stride)
        cur = kept.astype(f32) + got.astype(f32)
        if cur.shape[0] > 1:
            cur = cur.astype(bf16)
    return cur[0]


def rotary_tables(places):
    quarter = HD // 4
    ladder = jnp.exp(-math.log(10000.0) * jnp.arange(quarter, dtype=f32) / quarter)
    angles = places.astype(f32)[:, None] * ladder[None, :]
    return jnp.cos(angles), jnp.sin(angles)


def rotate(values, cosine, sine, sign):
    rows, width = values.shape
    quarter = HD // 4
    heads = values.reshape(rows, width // HD, HD)
    cosine = cosine[:, None, :]
    sine = sign * sine[:, None, :]
    first = heads[..., :quarter]
    second = heads[..., quarter : 2 * quarter]
    return jnp.concatenate(
        [
            first * cosine - second * sine,
            second * cosine + first * sine,
            heads[..., 2 * quarter :],
        ],
        axis=-1,
    ).reshape(rows, width)


def time_features(steps_row):
    half_width = TEMB // 2
    ladder = jnp.exp(-math.log(10000.0) * jnp.arange(half_width, dtype=f32) / half_width)
    angles = steps_row.astype(f32)[:, None] * ladder[None, :]
    return jnp.concatenate([jnp.cos(angles), jnp.sin(angles)], axis=-1)


def normalize(hidden):
    center = hidden - jnp.mean(hidden, axis=-1, keepdims=True)
    spread = jnp.mean(center * center, axis=-1, keepdims=True)
    scale = lax.rsqrt(spread + norm_eps)
    return center * scale, scale


def masked_scores(query_rows, key_rows, allowed, factor):
    scores = (
        jnp.einsum("mqhd,mkhd->mhqk", query_rows, key_rows, preferred_element_type=f32) * factor
    )
    return jnp.where(allowed[:, None], scores, -1e30)


def attend(query_rows, key_rows, value_rows, allowed, factor):
    scores = masked_scores(query_rows, key_rows, allowed, factor)
    row_peak = jnp.max(scores, axis=-1, keepdims=True)
    log_total = row_peak + jnp.log(jnp.sum(jnp.exp(scores - row_peak), axis=-1, keepdims=True))
    weights = jnp.exp(scores - log_total).astype(bf16)
    mixed = jnp.einsum("mhqk,mkhd->mqhd", weights, value_rows, preferred_element_type=f32)
    return (mixed, log_total)


def attend_back(query_rows, key_rows, value_rows, allowed, factor, log_total, mixed_grad):
    scores = masked_scores(query_rows, key_rows, allowed, factor)
    chances = jnp.exp(scores - log_total)
    weights = chances.astype(bf16)
    chance_grad = jnp.einsum("mqhd,mkhd->mhqk", mixed_grad, value_rows, preferred_element_type=f32)
    value_grad = jnp.einsum("mhqk,mqhd->mkhd", weights, mixed_grad, preferred_element_type=f32)
    score_grad = (
        chances * (chance_grad - jnp.sum(chances * chance_grad, axis=-1, keepdims=True))
    ).astype(bf16)
    query_grad = (
        jnp.einsum("mhqk,mkhd->mqhd", score_grad, key_rows, preferred_element_type=f32) * factor
    )
    key_grad = (
        jnp.einsum("mhqk,mqhd->mkhd", score_grad, query_rows, preferred_element_type=f32) * factor
    )
    return (query_grad, key_grad, value_grad)


def on_device(
    latents,
    context,
    lengths,
    text_len,
    timesteps,
    self_qkv,
    self_out,
    cross_query,
    cross_kv,
    cross_out,
    ffn_in,
    ffn_out,
    mod_weight,
    mod_bias,
    out_grad,
):
    micro, block_rows, model_width = latents.shape
    seq_count = lax.axis_size("seq")
    me = lax.axis_index("seq")
    frame_count = block_rows * seq_count
    item_count = lengths.shape[1]
    local = self_qkv.shape[2]
    hidden = ffn_in.shape[2]
    heads = local // HD
    rows = micro * block_rows
    text_width = context.shape[2]
    factor = HD ** (-0.5)

    attn_share = jnp.concatenate(
        [
            self_qkv[0],
            self_qkv[1],
            self_qkv[2],
            self_out.T,
            cross_query,
            cross_out.T,
            jnp.concatenate([cross_kv[0], cross_kv[1]], axis=0),
        ],
        axis=1,
    )
    ffn_share = jnp.concatenate([ffn_out.T, ffn_in[0], ffn_in[1]], axis=1)
    attn_all = lax.all_gather(attn_share, "seq", axis=0, tiled=True)
    ffn_all = lax.all_gather(ffn_share, "seq", axis=0, tiled=True)
    qkv_w = attn_all[:, : 3 * local]
    self_wt = attn_all[:, 3 * local : 4 * local]
    query_w = attn_all[:, 4 * local : 5 * local]
    cross_wt = attn_all[:, 5 * local : 6 * local]
    pair_w = attn_all[:, 6 * local :].reshape(seq_count, 2, text_width // seq_count, local)
    key_w = pair_w[:, 0].reshape(text_width, local)
    value_w = pair_w[:, 1].reshape(text_width, local)
    outer_wt = ffn_all[:, :hidden]
    inner_w = ffn_all[:, hidden:]
    gate_w = inner_w[:, :hidden]
    up_w = inner_w[:, hidden:]

    features = time_features(timesteps.reshape(-1))
    own_features = lax.dynamic_slice_in_dim(
        features, me * mod_weight.shape[0], mod_weight.shape[0], 1
    )
    bias_share = mod_bias.shape[1]
    bias_wide = lax.dynamic_update_slice_in_dim(
        jnp.zeros((6, model_width), f32), mod_bias.astype(f32), me * bias_share, 1
    )
    mod_part = jnp.dot(
        own_features, mod_weight.astype(f32).reshape(mod_weight.shape[0], -1), precision=highest
    ) + bias_wide.reshape(1, -1)
    modulation = seq_sum(mod_part).reshape(micro, item_count, 6, model_width)

    first_frame = me * block_rows
    own_places = first_frame + jnp.arange(block_rows, dtype=jnp.int32)
    near_places = first_frame - HALF + jnp.arange(block_rows + 2 * HALF, dtype=jnp.int32)
    near_inside = (near_places >= 0) & (near_places < frame_count)
    item_ends = jnp.cumsum(lengths, axis=1)
    item_starts = item_ends - lengths
    own_ids = jnp.sum(
        (item_ends[:, None, :] <= own_places[None, :, None]).astype(jnp.int32), axis=2
    )
    near_ids = jnp.sum(
        (item_ends[:, None, :] <= near_places[None, :, None]).astype(jnp.int32), axis=2
    )
    base_item = jnp.minimum(own_ids[:, 0], item_count - 2)
    catalog = jnp.arange(item_count, dtype=jnp.int32)
    choose = own_ids[:, :, None] == catalog[None, None, :]
    offsets_in = own_places[None, :] - jnp.sum(
        choose.astype(jnp.int32) * item_starts[:, None, :], axis=2
    )
    later = (own_ids != base_item[:, None])[:, :, None]
    two = jax.vmap(lambda table, start: lax.dynamic_slice_in_dim(table, start, 2, 0))(
        modulation, base_item
    )

    def framewise(index):
        chosen = jnp.where(later, two[:, 1, index][:, None, :], two[:, 0, index][:, None, :])
        return chosen.reshape(rows, model_width)

    cosine, sine = rotary_tables(offsets_in.reshape(-1))
    self_allowed = (
        (own_ids[:, :, None] == near_ids[:, None, :])
        & near_inside[None, None, :]
        & (jnp.abs(own_places[:, None] - near_places[None, :]) <= HALF)[None]
    )
    text_slots = jnp.arange(2 * TXT, dtype=jnp.int32)
    key_items = base_item[:, None] + (text_slots // TXT)[None, :]
    key_lengths = jnp.sum(
        (key_items[:, :, None] == catalog[None, None, :]).astype(jnp.int32) * text_len[:, None, :],
        axis=2,
    )
    cross_allowed = (own_ids[:, :, None] == key_items[:, None, :]) & (
        (text_slots % TXT)[None, :] < key_lengths
    )[:, None, :]

    def by_heads(flat, count):
        return flat.reshape(micro, count, heads, HD)

    latent = latents.astype(f32).reshape(rows, model_width)
    cotangent = out_grad.reshape(rows, model_width)
    xhat_one, inv_one = normalize(latent)
    normed_one = (xhat_one * (1.0 + framewise(1)) + framewise(0)).astype(bf16)
    projected = nn(normed_one, qkv_w)
    query_one = rotate(projected[:, :local], cosine, sine, 1.0).astype(bf16)
    key_one = rotate(projected[:, local : 2 * local], cosine, sine, 1.0).astype(bf16)
    value_one = projected[:, 2 * local :].astype(bf16)
    key_value = jnp.stack([key_one, value_one]).reshape(2, micro, block_rows, local)
    ahead = [(i, i + 1) for i in range(seq_count - 1)]
    behind = [(i + 1, i) for i in range(seq_count - 1)]
    low_rows = lax.ppermute(key_value[:, :, block_rows - HALF :], "seq", ahead)
    high_rows = lax.ppermute(key_value[:, :, :HALF], "seq", behind)
    near_pairs = jnp.concatenate([low_rows, key_value, high_rows], axis=2)
    near_keys = by_heads(near_pairs[0], block_rows + 2 * HALF)
    near_values = by_heads(near_pairs[1], block_rows + 2 * HALF)
    query_heads = by_heads(query_one, block_rows)
    mixed_one, total_one = attend(query_heads, near_keys, near_values, self_allowed, factor)
    mixed_one = mixed_one.reshape(rows, local).astype(bf16)
    hidden_one = latent + pair_sum(nt(mixed_one, self_wt).astype(bf16))

    xhat_two, inv_two = normalize(hidden_one)
    normed_two = (xhat_two * (1.0 + framewise(3)) + framewise(2)).astype(bf16)
    query_two = nn(normed_two, query_w).astype(bf16)
    near_context = jax.vmap(
        lambda table, start: lax.dynamic_slice_in_dim(table, start * TXT, 2 * TXT, 0)
    )(context, base_item).reshape(micro * 2 * TXT, text_width)
    text_keys = by_heads(nn(near_context, key_w).astype(bf16), 2 * TXT)
    text_values = by_heads(nn(near_context, value_w).astype(bf16), 2 * TXT)
    query_two_heads = by_heads(query_two, block_rows)
    mixed_two, total_two = attend(query_two_heads, text_keys, text_values, cross_allowed, factor)
    mixed_two = mixed_two.reshape(rows, local).astype(bf16)
    hidden_two = hidden_one + pair_sum(nt(mixed_two, cross_wt).astype(bf16))

    xhat_three, inv_three = normalize(hidden_two)
    normed_three = (xhat_three * (1.0 + framewise(5)) + framewise(4)).astype(bf16)
    gate = nn(normed_three, gate_w)
    up = nn(normed_three, up_w)
    chance = jax.nn.sigmoid(gate)
    swish = gate * chance
    activated = (swish * up).astype(bf16)
    block_out = (hidden_two + pair_sum(nt(activated, outer_wt).astype(bf16))).astype(bf16)

    activated_grad = nn(cotangent, outer_wt)
    gate_grad = (activated_grad * up * (chance * (1.0 + gate * (1.0 - chance)))).astype(bf16)
    up_grad = (activated_grad * swish).astype(bf16)
    outer_total = scatter_sum(tn(cotangent, activated).astype(bf16))
    gate_total = scatter_sum(tn(normed_three, gate_grad).astype(bf16))
    up_total = scatter_sum(tn(normed_three, up_grad).astype(bf16))
    normed_three_grad = pair_sum((nt(gate_grad, gate_w) + nt(up_grad, up_w)).astype(bf16))

    def norm_back(normed_grad, xhat, inv, scale_row):
        inner = normed_grad * (1.0 + scale_row)
        mean_inner = jnp.mean(inner, axis=-1, keepdims=True)
        mean_cross = jnp.mean(inner * xhat, axis=-1, keepdims=True)
        back = inv * (inner - mean_inner - xhat * mean_cross)
        cube = normed_grad.reshape(micro, block_rows, model_width)
        scaled = (normed_grad * xhat).reshape(micro, block_rows, model_width)

        def by_item(values):
            high_part = jnp.sum(jnp.where(later, values, 0.0), axis=1)
            low_part = jnp.sum(jnp.where(later, 0.0, values), axis=1)
            return jnp.stack([low_part, high_part], axis=1)

        return back, by_item(cube), by_item(scaled)

    back_three, shift_three, scale_three = norm_back(
        normed_three_grad, xhat_three, inv_three, framewise(5)
    )
    hidden_two_grad = cotangent.astype(f32) + back_three
    two_low = hidden_two_grad.astype(bf16)
    mixed_two_grad = by_heads(nn(two_low, cross_wt).astype(bf16), block_rows)
    query_two_grad, text_key_grad, text_value_grad = attend_back(
        query_two_heads, text_keys, text_values, cross_allowed, factor, total_two, mixed_two_grad
    )
    query_two_low = query_two_grad.reshape(rows, local).astype(bf16)
    text_key_low = text_key_grad.reshape(micro * 2 * TXT, local).astype(bf16)
    text_value_low = text_value_grad.reshape(micro * 2 * TXT, local).astype(bf16)
    normed_two_grad = pair_sum(nt(query_two_low, query_w).astype(bf16))
    share = text_width // seq_count
    pair_grad = jnp.concatenate(
        [
            tn(near_context, text_key_low).reshape(seq_count, share, local),
            tn(near_context, text_value_low).reshape(seq_count, share, local),
        ],
        axis=1,
    ).reshape(2 * text_width, local)
    cross_total = scatter_sum(
        jnp.concatenate(
            [tn(two_low, mixed_two), tn(normed_two, query_two_low), pair_grad], axis=1
        ).astype(bf16)
    )
    back_two, shift_two, scale_two = norm_back(normed_two_grad, xhat_two, inv_two, framewise(3))
    hidden_one_grad = hidden_two_grad + back_two
    one_low = hidden_one_grad.astype(bf16)
    mixed_one_grad = by_heads(nn(one_low, self_wt).astype(bf16), block_rows)
    query_one_grad, near_key_grad, near_value_grad = attend_back(
        query_heads, near_keys, near_values, self_allowed, factor, total_one, mixed_one_grad
    )
    near_grads = jnp.stack([near_key_grad, near_value_grad]).reshape(
        2, micro, block_rows + 2 * HALF, local
    )
    to_behind = lax.ppermute(near_grads[:, :, :HALF].astype(bf16), "seq", behind)
    to_ahead = lax.ppermute(near_grads[:, :, block_rows + HALF :].astype(bf16), "seq", ahead)
    pair_grads = near_grads[:, :, HALF : HALF + block_rows]
    pair_grads = pair_grads + jnp.pad(
        to_ahead.astype(f32), ((0, 0), (0, 0), (0, block_rows - HALF), (0, 0))
    )
    pair_grads = pair_grads + jnp.pad(
        to_behind.astype(f32), ((0, 0), (0, 0), (block_rows - HALF, 0), (0, 0))
    )
    projected_grad = jnp.concatenate(
        [
            rotate(query_one_grad.reshape(rows, local), cosine, sine, -1.0),
            rotate(pair_grads[0].reshape(rows, local), cosine, sine, -1.0),
            pair_grads[1].reshape(rows, local),
        ],
        axis=1,
    ).astype(bf16)
    normed_one_grad = pair_sum(nt(projected_grad, qkv_w).astype(bf16))
    self_total = scatter_sum(
        jnp.concatenate(
            [tn(normed_one, projected_grad).astype(bf16), tn(one_low, mixed_one).astype(bf16)],
            axis=1,
        )
    )
    back_one, shift_one, scale_one = norm_back(normed_one_grad, xhat_one, inv_one, framewise(1))
    latent_grad = hidden_one_grad + back_one

    pieces = jnp.stack(
        [shift_one, scale_one, shift_two, scale_two, shift_three, scale_three], axis=2
    )
    spots = (base_item[:, None] + jnp.arange(2)[None, :])[:, :, None] == catalog[None, None, :]
    item_grad = jnp.sum(
        jnp.where(spots[:, :, :, None, None], pieces[:, :, None], 0.0), axis=1
    ).reshape(micro * item_count, 6 * model_width)
    item_total = seq_sum(item_grad)
    mod_grad = jnp.dot(own_features.T, item_total, precision=highest).reshape(mod_weight.shape)
    bias_grad = lax.dynamic_slice_in_dim(
        jnp.sum(item_total, axis=0).reshape(6, model_width), me * bias_share, bias_share, 1
    )

    grad_qkv = jnp.stack([self_total[:, i * local : (i + 1) * local] for i in range(3)])
    grad_self_out = self_total[:, 3 * local :].T
    grad_cross_out = cross_total[:, :local].T
    grad_cross_query = cross_total[:, local : 2 * local]
    grad_cross_kv = cross_total[:, 2 * local :].reshape(2, share, local)
    return (
        block_out.reshape(latents.shape),
        latent_grad.reshape(latents.shape),
        grad_qkv,
        grad_self_out,
        grad_cross_query,
        grad_cross_kv,
        grad_cross_out,
        jnp.stack([gate_total, up_total]),
        outer_total.T,
        mod_grad,
        bias_grad,
    )


def solution(mesh):
    return jax.shard_map(
        on_device,
        mesh=mesh,
        in_specs=(
            P(None, "seq", None),
            P(),
            P(),
            P(),
            P(),
            P(None, "seq", "tensor"),
            P("tensor", "seq"),
            P("seq", "tensor"),
            P(None, "seq", "tensor"),
            P("tensor", "seq"),
            P(None, "seq", "tensor"),
            P("tensor", "seq"),
            P("seq", None, None),
            P(None, "seq"),
            P(None, "seq", None),
        ),
        out_specs=(
            P(None, "seq", None),
            P(None, "seq", None),
            P(None, "seq", "tensor"),
            P("tensor", "seq"),
            P("seq", "tensor"),
            P(None, "seq", "tensor"),
            P("tensor", "seq"),
            P(None, "seq", "tensor"),
            P("tensor", "seq"),
            P("seq", None, None),
            P(None, "seq"),
        ),
        check_vma=False,
    )
```

```python
import functools
import math

import jax
import jax.numpy as jnp
from jax import lax
from jax.experimental import pallas as pl
from jax.experimental.pallas import tpu as pltpu
from jax.sharding import PartitionSpec as P

HD = 64
TXT = 128
TEMB = 256
HALF = 128


norm_eps = 1e-05
highest = lax.Precision.HIGHEST
f32 = jnp.float32
bf16 = jnp.bfloat16


def dot(a, b, dims):
    return lax.dot_general(a, b, ((dims[0], dims[1]), ((), ())), preferred_element_type=f32)


def nn(a, b):
    return dot(a, b, ((1,), (0,)))


def nt(a, b):
    return dot(a, b, ((1,), (1,)))


def tn(a, b):
    return dot(a, b, ((0,), (0,)))


def halves(count):
    stride = 1
    strides = []
    while stride < count:
        strides.append(stride)
        stride *= 2
    return strides


def flip(block, stride):
    count = lax.axis_size("seq")
    return lax.ppermute(block, "seq", [(i, i ^ stride) for i in range(count)])


def pair_sum(part):
    count = lax.axis_size("tensor")
    other = lax.ppermute(part, "tensor", [(i, (i + 1) % count) for i in range(count)])
    return part.astype(f32) + other.astype(f32)


def seq_sum(part):
    for stride in halves(lax.axis_size("seq")):
        part = part + flip(part, stride)
    return part


def kernel_params(grid_rank, mib):
    return pltpu.CompilerParams(
        dimension_semantics=("arbitrary",) * grid_rank, vmem_limit_bytes=mib * 1024 * 1024
    )


SLOTS = 5


def scatter_kernel(*refs, widths, step):
    sources = refs[: len(widths)]
    out_ref = refs[len(widths)]
    (own, got0, got1, got2, got3, staged, own_sem, out_sem, send_sem, recv_sem) = refs[
        len(widths) + 1 :
    ]
    me = lax.axis_index("seq")
    core, y, z_lo, z_hi = [(me // stride) % 2 for stride in (1, 2, 4, 8)]
    partners = [
        me + stride * (1 - 2 * digit)
        for stride, digit in zip((1, 2, 4, 8), (core, y, z_lo, z_hi))
    ]
    barrier = pltpu.get_barrier_semaphore()
    for partner in partners:
        pl.semaphore_signal(
            barrier, inc=1, device_id={"seq": partner}, device_id_type=pl.DeviceIdType.MESH
        )
    pl.semaphore_wait(barrier, len(partners))
    count = sum(widths) // step

    def exchange(stage, source, target, slot):
        return pltpu.make_async_remote_copy(
            src_ref=source,
            dst_ref=target,
            send_sem=send_sem.at[stage, slot],
            recv_sem=recv_sem.at[stage, slot],
            device_id={"seq": partners[stage]},
            device_id_type=pl.DeviceIdType.MESH,
        )

    def over_core(source, column, slot):
        return exchange(
            0, source.at[:, :, :, 1 - core, :, pl.ds(column, step)], got0.at[slot], slot
        )

    def load(source, column, slot):
        return pltpu.make_async_copy(
            source.at[:, :, :, core, :, pl.ds(column, step)], own.at[slot], own_sem.at[slot]
        )

    def over_y(slot):
        return exchange(1, own.at[slot, :, :, 1 - y], got1.at[slot], slot)

    def over_z_lo(slot):
        return exchange(2, own.at[slot, :, 1 - z_lo, y], got2.at[slot], slot)

    def over_z_hi(slot):
        return exchange(3, own.at[slot, 1 - z_hi, z_lo, y], got3.at[slot], slot)

    def store(item, slot):
        return pltpu.make_async_copy(
            staged.at[slot],
            out_ref.at[:, pl.ds(pl.multiple_of(item * step, step), step)],
            out_sem.at[slot],
        )

    def added(left, right):
        return left.astype(f32) + right.astype(f32)

    def tick(t, carry):
        @pl.when(t < count)
        def _():
            slot = t % SLOTS

            @pl.when(t >= SLOTS)
            def _():
                over_y(slot).wait_send()
                over_z_lo(slot).wait_send()
                over_z_hi(slot).wait_send()

            first = 0
            for source, width in zip(sources, widths):
                pieces = width // step

                @pl.when((t >= first) & (t < first + pieces))
                def _(source=source, first=first):
                    column = pl.multiple_of((t - first) * step, step)
                    over_core(source, column, slot).start()
                    load(source, column, slot).start()

                first += pieces

        @pl.when((t >= 1) & (t - 1 < count))
        def _():
            slot = (t - 1) % SLOTS
            load(sources[0], 0, slot).wait()
            over_core(sources[0], 0, slot).wait()
            for i in range(2):
                for j in range(2):
                    for k in range(2):
                        own[slot, i, j, k] = added(own[slot, i, j, k], got0[slot, i, j, k]).astype(
                            bf16
                        )
            over_y(slot).start()

        @pl.when((t >= 2) & (t - 2 < count))
        def _():
            slot = (t - 2) % SLOTS
            over_y(slot).wait_recv()
            for i in range(2):
                for j in range(2):
                    own[slot, i, j, y] = added(own[slot, i, j, y], got1[slot, i, j]).astype(bf16)
            over_z_lo(slot).start()

        @pl.when((t >= 3) & (t - 3 < count))
        def _():
            slot = (t - 3) % SLOTS
            over_z_lo(slot).wait_recv()
            for i in range(2):
                own[slot, i, z_lo, y] = added(own[slot, i, z_lo, y], got2[slot, i]).astype(bf16)
            over_z_hi(slot).start()

        @pl.when((t >= 4) & (t - 4 < count))
        def _():
            slot = (t - 4) % SLOTS
            over_z_hi(slot).wait_recv()

            @pl.when(t - 4 >= SLOTS)
            def _():
                store(0, slot).wait()

            staged[slot] = added(own[slot, z_hi, z_lo, y], got3[slot])
            store(t - 4, slot).start()

        return carry

    lax.fori_loop(0, count + 4, tick, 0)
    for back in range(min(SLOTS, count)):
        slot = (count - 1 - back) % SLOTS
        store(0, slot).wait()
        over_y(slot).wait_send()
        over_z_lo(slot).wait_send()
        over_z_hi(slot).wait_send()


def scatter_sums(grads, step=256):
    count = lax.axis_size("seq")
    rows = grads[0].shape[0] // count
    widths = tuple(grad.shape[1] for grad in grads)
    if count != 16 or rows % 16 or any(width % step for width in widths):
        return [
            lax.psum_scatter(grad.astype(f32), "seq", scatter_dimension=0, tiled=True)
            for grad in grads
        ]
    any_space = pl.BlockSpec(memory_space=pl.ANY)
    total = pl.pallas_call(
        functools.partial(scatter_kernel, widths=widths, step=step),
        out_shape=jax.ShapeDtypeStruct((rows, sum(widths)), f32),
        in_specs=[any_space] * len(grads),
        out_specs=any_space,
        scratch_shapes=[
            pltpu.VMEM((SLOTS, 2, 2, 2, rows, step), bf16),
            pltpu.VMEM((SLOTS, 2, 2, 2, rows, step), bf16),
            pltpu.VMEM((SLOTS, 2, 2, rows, step), bf16),
            pltpu.VMEM((SLOTS, 2, rows, step), bf16),
            pltpu.VMEM((SLOTS, rows, step), bf16),
            pltpu.VMEM((SLOTS, rows, step), f32),
            pltpu.SemaphoreType.DMA((SLOTS,)),
            pltpu.SemaphoreType.DMA((SLOTS,)),
            pltpu.SemaphoreType.DMA((4, SLOTS)),
            pltpu.SemaphoreType.DMA((4, SLOTS)),
        ],
        compiler_params=pltpu.CompilerParams(
            collective_id=0, has_side_effects=True, vmem_limit_bytes=40 * 1024 * 1024
        ),
        cost_estimate=pl.CostEstimate(
            flops=0, bytes_accessed=8 * count * rows * sum(widths), transcendentals=0
        ),
        name="scatter_sums",
    )(*[grad.reshape(2, 2, 2, 2, rows, grad.shape[1]) for grad in grads])
    firsts = [sum(widths[:i]) for i in range(len(widths))]
    return [total[:, first : first + width] for first, width in zip(firsts, widths)]


def early_sum(grad):
    return lax.psum_scatter(grad, "seq", scatter_dimension=0, tiled=True).astype(f32)


def rotary_tables(places):
    quarter = HD // 4
    ladder = jnp.exp(-math.log(10000.0) * jnp.arange(quarter, dtype=f32) / quarter)
    angles = places.astype(f32)[:, None] * ladder[None, :]
    cosine = jnp.cos(angles)
    sine = jnp.sin(angles)
    one = jnp.ones_like(cosine)
    zero = jnp.zeros_like(cosine)
    own = jnp.concatenate([cosine, cosine, one, one] * 2, axis=1)
    below = jnp.concatenate([zero, sine, zero, zero] * 2, axis=1)
    above = jnp.concatenate([-sine, zero, zero, zero] * 2, axis=1)
    return jnp.stack([own, below, above])


def turn(values, own, below, above):
    quarter = HD // 4
    return (
        values * own
        + pltpu.roll(values, quarter, 1) * below
        + pltpu.roll(values, 2 * HD - quarter, 1) * above
    )


def project_kernel(normed_ref, weight_ref, table_ref, out_ref, *, turned):
    j = pl.program_id(0)
    product = nn(normed_ref[...], weight_ref[...])

    @pl.when(j < turned)
    def _():
        for part in range(product.shape[1] // 128):
            lanes = slice(part * 128, (part + 1) * 128)
            out_ref[:, lanes] = turn(
                product[:, lanes], table_ref[0], table_ref[1], table_ref[2]
            ).astype(bf16)

    @pl.when(j >= turned)
    def _():
        out_ref[...] = product.astype(bf16)


def project(normed, weights, table, local, step=256):
    rows, width = normed.shape
    return pl.pallas_call(
        functools.partial(project_kernel, turned=2 * local // step),
        grid=(3 * local // step,),
        in_specs=[
            pl.BlockSpec((rows, width), lambda j: (0, 0)),
            pl.BlockSpec((width, step), lambda j: (0, j)),
            pl.BlockSpec((3, rows, 128), lambda j: (0, 0, 0)),
        ],
        out_specs=pl.BlockSpec((rows, step), lambda j: (0, j)),
        out_shape=jax.ShapeDtypeStruct((rows, 3 * local), bf16),
        compiler_params=kernel_params(1, 32),
        cost_estimate=pl.CostEstimate(
            flops=2 * rows * width * 3 * local,
            bytes_accessed=2 * (rows * width + 3 * local * (width + rows)),
            transcendentals=0,
        ),
        name="qkv_projection",
    )(normed, weights, table)


def head_lanes(shape):
    return lax.broadcasted_iota(jnp.int32, shape, 1) < HD


def one_head(values, first, which):
    return jnp.where(first if which == 0 else ~first, values, jnp.zeros_like(values))


def soft_rows(scores):
    peak = jnp.max(scores, axis=-1, keepdims=True)
    raised = jnp.exp(scores - peak)
    total = jnp.sum(raised, axis=-1, keepdims=True)
    return raised * (1.0 / total), peak + jnp.log(total)


def attend_rows(query, keys, values, bias):
    first = head_lanes(query.shape)
    out = None
    logs = []
    for which in range(2):
        scores = nt(one_head(query, first, which), keys) * (HD**-0.5) + bias
        weights, log_total = soft_rows(scores)
        mixed = nn(weights.astype(bf16), values)
        out = mixed if which == 0 else jnp.where(first, out, mixed)
        logs.append(log_total)
    return out, logs


def attend_rows_back(query, keys, values, bias, logs, grad):
    first = head_lanes(query.shape)
    query_grad = key_grad = value_grad = None
    for which in range(2):
        own_query = one_head(query, first, which)
        own_grad = one_head(grad, first, which)
        scores = nt(own_query, keys) * (HD**-0.5) + bias
        chances = jnp.exp(scores - logs[which])
        chance_grad = nt(own_grad, values)
        score_grad = (
            chances * (chance_grad - jnp.sum(chances * chance_grad, axis=-1, keepdims=True))
        ).astype(bf16)
        to_query = nn(score_grad, keys) * (HD**-0.5)
        to_key = tn(score_grad, own_query) * (HD**-0.5)
        to_value = tn(chances.astype(bf16), own_grad)
        if which == 0:
            query_grad, key_grad, value_grad = to_query, to_key, to_value
        else:
            query_grad = jnp.where(first, query_grad, to_query)
            key_grad = key_grad + to_key
            value_grad = value_grad + to_value
    return query_grad, key_grad, value_grad


def put_logs(log_ref, rows, logs, pair):
    lane = lax.broadcasted_iota(jnp.int32, (logs[0].shape[0], 128), 1)
    kept = log_ref[rows, :]
    kept = jnp.where(lane == 2 * pair, logs[0], kept)
    log_ref[rows, :] = jnp.where(lane == 2 * pair + 1, logs[1], kept)


def get_logs(log_ref, rows, pair):
    kept = log_ref[rows, :]
    lane = lax.broadcasted_iota(jnp.int32, kept.shape, 1)
    return [
        jnp.sum(jnp.where(lane == 2 * pair + which, kept, 0.0), axis=1, keepdims=True)
        for which in range(2)
    ]


def near(low_ref, own_ref, high_ref):
    return jnp.concatenate([low_ref[...], own_ref[...], high_ref[...]], axis=0)


def self_kernel(q_ref, k_ref, v_ref, kl_ref, vl_ref, kh_ref, vh_ref, bias_ref, out_ref, log_ref):
    pair = pl.program_id(1)
    keys = near(kl_ref, k_ref, kh_ref)
    values = near(vl_ref, v_ref, vh_ref)
    for part in range(q_ref.shape[0] // HALF):
        rows = slice(part * HALF, (part + 1) * HALF)
        span = slice(part * HALF, (part + 3) * HALF)
        out, logs = attend_rows(q_ref[rows, :], keys[span], values[span], bias_ref[rows, :])
        out_ref[rows, :] = out.astype(bf16)
        put_logs(log_ref, rows, logs, pair)


def self_specs(block_rows, pairs):
    own = lambda first: pl.BlockSpec((block_rows, 128), lambda m, h: (m, first + h))
    edge = lambda first: pl.BlockSpec((None, HALF, 128), lambda m, h: (m, 0, first + h))
    return [
        own(0),
        own(pairs),
        own(2 * pairs),
        edge(0),
        edge(pairs),
        edge(0),
        edge(pairs),
        pl.BlockSpec((block_rows, 3 * HALF), lambda m, h: (m, 0)),
    ]


def self_attention(qkv, low_rows, high_rows, bias, micro, block_rows):
    rows, width = qkv.shape
    pairs = width // 3 // 128
    return pl.pallas_call(
        self_kernel,
        grid=(micro, pairs),
        in_specs=self_specs(block_rows, pairs),
        out_specs=[
            pl.BlockSpec((block_rows, 128), lambda m, h: (m, h)),
            pl.BlockSpec((block_rows, 128), lambda m, h: (m, 0)),
        ],
        out_shape=[
            jax.ShapeDtypeStruct((rows, width // 3), bf16),
            jax.ShapeDtypeStruct((rows, 128), f32),
        ],
        compiler_params=kernel_params(2, 32),
        cost_estimate=pl.CostEstimate(
            flops=4 * rows * 3 * HALF * 128 * 2 * pairs,
            bytes_accessed=10 * rows * width,
            transcendentals=rows * 3 * HALF * 2 * pairs,
        ),
        name="self_attention",
    )(qkv, qkv, qkv, low_rows, low_rows, high_rows, high_rows, bias)


def self_back_kernel(
    q_ref, k_ref, v_ref, kl_ref, vl_ref, kh_ref, vh_ref, bias_ref, grad_ref, log_ref,
    own_ref, to_low_ref, to_high_ref,
):
    pair = pl.program_id(1)
    keys = near(kl_ref, k_ref, kh_ref)
    values = near(vl_ref, v_ref, vh_ref)
    parts = q_ref.shape[0] // HALF
    pieces = [[None] * (parts + 2), [None] * (parts + 2)]
    for part in range(parts):
        rows = slice(part * HALF, (part + 1) * HALF)
        span = slice(part * HALF, (part + 3) * HALF)
        query_grad, key_grad, value_grad = attend_rows_back(
            q_ref[rows, :],
            keys[span],
            values[span],
            bias_ref[rows, :],
            get_logs(log_ref, rows, pair),
            grad_ref[rows, :],
        )
        own_ref[0, rows, :] = query_grad
        for kind, near_grad in enumerate((key_grad, value_grad)):
            for third in range(3):
                piece = near_grad[third * HALF : (third + 1) * HALF]
                held = pieces[kind][part + third]
                pieces[kind][part + third] = piece if held is None else held + piece
    for kind in range(2):
        to_low_ref[kind] = pieces[kind][0].astype(bf16)
        for part in range(parts):
            own_ref[1 + kind, part * HALF : (part + 1) * HALF, :] = pieces[kind][part + 1]
        to_high_ref[kind] = pieces[kind][parts + 1].astype(bf16)


def self_attention_back(qkv, low_rows, high_rows, bias, grad, logs, micro, block_rows):
    rows, width = qkv.shape
    local = width // 3
    pairs = local // 128
    edge = pl.BlockSpec((2, None, HALF, 128), lambda m, h: (0, m, 0, h))
    return pl.pallas_call(
        self_back_kernel,
        grid=(micro, pairs),
        in_specs=self_specs(block_rows, pairs)
        + [
            pl.BlockSpec((block_rows, 128), lambda m, h: (m, h)),
            pl.BlockSpec((block_rows, 128), lambda m, h: (m, 0)),
        ],
        out_specs=[
            pl.BlockSpec((3, block_rows, 128), lambda m, h: (0, m, h)),
            edge,
            edge,
        ],
        out_shape=[
            jax.ShapeDtypeStruct((3, rows, local), f32),
            jax.ShapeDtypeStruct((2, micro, HALF, local), bf16),
            jax.ShapeDtypeStruct((2, micro, HALF, local), bf16),
        ],
        compiler_params=kernel_params(2, 32),
        cost_estimate=pl.CostEstimate(
            flops=10 * rows * 3 * HALF * 128 * 2 * pairs,
            bytes_accessed=20 * rows * width,
            transcendentals=rows * 3 * HALF * 2 * pairs,
        ),
        name="self_attention_back",
    )(qkv, qkv, qkv, low_rows, low_rows, high_rows, high_rows, bias, grad, logs)


def cross_kernel(q_ref, k_ref, v_ref, bias_ref, out_ref, log_ref):
    pair = pl.program_id(1)
    for part in range(q_ref.shape[0] // HALF):
        rows = slice(part * HALF, (part + 1) * HALF)
        out, logs = attend_rows(q_ref[rows, :], k_ref[...], v_ref[...], bias_ref[rows, :])
        out_ref[rows, :] = out.astype(bf16)
        put_logs(log_ref, rows, logs, pair)


def cross_specs(block_rows, pairs):
    return [
        pl.BlockSpec((block_rows, 128), lambda m, h: (m, h)),
        pl.BlockSpec((2 * TXT, 128), lambda m, h: (m, h)),
        pl.BlockSpec((2 * TXT, 128), lambda m, h: (m, h)),
        pl.BlockSpec((block_rows, 2 * TXT), lambda m, h: (m, 0)),
    ]


def cross_attention(query, keys, values, bias, micro, block_rows):
    rows, local = query.shape
    pairs = local // 128
    return pl.pallas_call(
        cross_kernel,
        grid=(micro, pairs),
        in_specs=cross_specs(block_rows, pairs),
        out_specs=[
            pl.BlockSpec((block_rows, 128), lambda m, h: (m, h)),
            pl.BlockSpec((block_rows, 128), lambda m, h: (m, 0)),
        ],
        out_shape=[
            jax.ShapeDtypeStruct((rows, local), bf16),
            jax.ShapeDtypeStruct((rows, 128), f32),
        ],
        compiler_params=kernel_params(2, 32),
        cost_estimate=pl.CostEstimate(
            flops=4 * rows * 2 * TXT * 128 * 2 * pairs,
            bytes_accessed=8 * rows * local,
            transcendentals=rows * 2 * TXT * 2 * pairs,
        ),
        name="cross_attention",
    )(query, keys, values, bias)


def cross_back_kernel(q_ref, k_ref, v_ref, bias_ref, grad_ref, log_ref, dq_ref, dk_ref, dv_ref):
    pair = pl.program_id(1)
    key_total = value_total = None
    for part in range(q_ref.shape[0] // HALF):
        rows = slice(part * HALF, (part + 1) * HALF)
        query_grad, key_grad, value_grad = attend_rows_back(
            q_ref[rows, :],
            k_ref[...],
            v_ref[...],
            bias_ref[rows, :],
            get_logs(log_ref, rows, pair),
            grad_ref[rows, :],
        )
        dq_ref[rows, :] = query_grad.astype(bf16)
        key_total = key_grad if part == 0 else key_total + key_grad
        value_total = value_grad if part == 0 else value_total + value_grad
    dk_ref[...] = key_total.astype(bf16)
    dv_ref[...] = value_total.astype(bf16)


def cross_attention_back(query, keys, values, bias, grad, logs, micro, block_rows):
    rows, local = query.shape
    pairs = local // 128
    text = pl.BlockSpec((2 * TXT, 128), lambda m, h: (m, h))
    return pl.pallas_call(
        cross_back_kernel,
        grid=(micro, pairs),
        in_specs=cross_specs(block_rows, pairs)
        + [
            pl.BlockSpec((block_rows, 128), lambda m, h: (m, h)),
            pl.BlockSpec((block_rows, 128), lambda m, h: (m, 0)),
        ],
        out_specs=[pl.BlockSpec((block_rows, 128), lambda m, h: (m, h)), text, text],
        out_shape=[
            jax.ShapeDtypeStruct((rows, local), bf16),
            jax.ShapeDtypeStruct(keys.shape, bf16),
            jax.ShapeDtypeStruct(keys.shape, bf16),
        ],
        compiler_params=kernel_params(2, 32),
        cost_estimate=pl.CostEstimate(
            flops=10 * rows * 2 * TXT * 128 * 2 * pairs,
            bytes_accessed=16 * rows * local,
            transcendentals=rows * 2 * TXT * 2 * pairs,
        ),
        name="cross_attention_back",
    )(query, keys, values, bias, grad, logs)


def ffn_kernel(
    normed_ref, normed_t_ref, cot_ref, cot_t_ref, outer_ref, gate_ref, up_ref,
    g_early_ref, g_up_ref, out_ref, back_ref, out_acc, back_acc,
):
    j = pl.program_id(0)
    gate = nn(normed_ref[...], gate_ref[...])
    up = nn(normed_ref[...], up_ref[...])
    grad = nn(cot_ref[...], outer_ref[...])
    chance = 1.0 / (1.0 + jnp.exp(-gate))
    swish = gate * chance
    active = (swish * up).astype(bf16)
    gate_grad = (grad * up * (chance * (1.0 + gate * (1.0 - chance)))).astype(bf16)
    up_grad = (grad * swish).astype(bf16)
    step = active.shape[1]
    g_early_ref[:, :step] = nn(cot_t_ref[...], active).astype(bf16)
    g_early_ref[:, step:] = nn(normed_t_ref[...], gate_grad).astype(bf16)
    g_up_ref[...] = nn(normed_t_ref[...], up_grad).astype(bf16)
    out_part = nt(active, outer_ref[...])
    back_part = nt(gate_grad, gate_ref[...]) + nt(up_grad, up_ref[...])

    @pl.when(j == 0)
    def _():
        out_acc[...] = out_part
        back_acc[...] = back_part

    @pl.when(j > 0)
    def _():
        out_acc[...] += out_part
        back_acc[...] += back_part

    @pl.when(j == pl.num_programs(0) - 1)
    def _():
        out_ref[...] = out_acc[...].astype(bf16)
        back_ref[...] = back_acc[...].astype(bf16)


FFN_STEP = 256


def feed_forward(normed, cotangent, weights, hidden, step=FFN_STEP):
    rows, width = normed.shape
    steps = hidden // step
    whole = lambda shape: pl.BlockSpec(shape, lambda j: (0, 0))
    column = lambda first: pl.BlockSpec((width, step), lambda j: (0, first + j))
    return pl.pallas_call(
        ffn_kernel,
        grid=(steps,),
        in_specs=[
            whole((rows, width)),
            whole((width, rows)),
            whole((rows, width)),
            whole((width, rows)),
            column(0),
            column(steps),
            column(2 * steps),
        ],
        out_specs=[
            pl.BlockSpec((width, 2 * step), lambda j: (0, j)),
            column(0),
            whole((rows, width)),
            whole((rows, width)),
        ],
        out_shape=[
            jax.ShapeDtypeStruct((width, 2 * hidden), bf16),
            jax.ShapeDtypeStruct((width, hidden), bf16),
            jax.ShapeDtypeStruct((rows, width), bf16),
            jax.ShapeDtypeStruct((rows, width), bf16),
        ],
        scratch_shapes=[pltpu.VMEM((rows, width), f32)] * 2,
        compiler_params=kernel_params(1, 56),
        cost_estimate=pl.CostEstimate(
            flops=18 * rows * width * hidden,
            bytes_accessed=12 * width * hidden,
            transcendentals=rows * hidden,
        ),
        name="feed_forward",
    )(normed, normed.T, cotangent, cotangent.T, weights, weights, weights)


def qkv_back_kernel(
    own_ref, after_ref, before_ref, normed_t_ref, weight_ref, table_ref,
    grad_ref, back_ref, acc, *, kind_steps, micro, block_rows,
):
    j = pl.program_id(0)
    kind = j // kind_steps
    edges = (kind > 0).astype(f32)
    turned = kind < 2
    own_factor = jnp.where(turned, table_ref[0], 1.0)
    below_factor = jnp.where(turned, -table_ref[1], 0.0)
    above_factor = jnp.where(turned, -table_ref[2], 0.0)
    total = []
    for m in range(micro):
        first = m * block_rows
        total.append(own_ref[first : first + HALF] + edges * after_ref[m].astype(f32))
        if block_rows > 2 * HALF:
            total.append(own_ref[first + HALF : first + block_rows - HALF])
        total.append(
            own_ref[first + block_rows - HALF : first + block_rows]
            + edges * before_ref[m].astype(f32)
        )
    total = jnp.concatenate(total, axis=0)
    grad = jnp.concatenate(
        [
            turn(total[:, i : i + 128], own_factor, below_factor, above_factor)
            for i in range(0, total.shape[1], 128)
        ],
        axis=1,
    ).astype(bf16)
    grad_ref[...] = nn(normed_t_ref[...], grad).astype(bf16)
    part = nt(grad, weight_ref[...])

    @pl.when(j == 0)
    def _():
        acc[...] = part

    @pl.when(j > 0)
    def _():
        acc[...] += part

    @pl.when(j == pl.num_programs(0) - 1)
    def _():
        back_ref[...] = acc[...].astype(bf16)


def qkv_back(own, after, before, normed, weights, table, micro, block_rows, step=256):
    _, rows, local = own.shape
    width = normed.shape[1]
    kind_steps = local // step
    edge = pl.BlockSpec(
        (None, micro, HALF, step),
        lambda j: (jnp.maximum(j // kind_steps - 1, 0), 0, 0, j % kind_steps),
    )
    return pl.pallas_call(
        functools.partial(
            qkv_back_kernel, kind_steps=kind_steps, micro=micro, block_rows=block_rows
        ),
        grid=(3 * kind_steps,),
        in_specs=[
            pl.BlockSpec((None, rows, step), lambda j: (j // kind_steps, 0, j % kind_steps)),
            edge,
            edge,
            pl.BlockSpec((width, rows), lambda j: (0, 0)),
            pl.BlockSpec((width, step), lambda j: (0, j)),
            pl.BlockSpec((3, rows, 128), lambda j: (0, 0, 0)),
        ],
        out_specs=[
            pl.BlockSpec((width, step), lambda j: (0, j)),
            pl.BlockSpec((rows, width), lambda j: (0, 0)),
        ],
        out_shape=[
            jax.ShapeDtypeStruct((width, 3 * local), bf16),
            jax.ShapeDtypeStruct((rows, width), bf16),
        ],
        scratch_shapes=[pltpu.VMEM((rows, width), f32)],
        compiler_params=kernel_params(1, 40),
        cost_estimate=pl.CostEstimate(
            flops=12 * rows * width * local,
            bytes_accessed=12 * width * local + 12 * rows * local,
            transcendentals=0,
        ),
        name="qkv_back",
    )(own, after, before, normed.T, weights, table)


def time_features(steps_row):
    half_width = TEMB // 2
    ladder = jnp.exp(-math.log(10000.0) * jnp.arange(half_width, dtype=f32) / half_width)
    angles = steps_row.astype(f32)[:, None] * ladder[None, :]
    return jnp.concatenate([jnp.cos(angles), jnp.sin(angles)], axis=-1)


def normalize(hidden):
    center = hidden - jnp.mean(hidden, axis=-1, keepdims=True)
    spread = jnp.mean(center * center, axis=-1, keepdims=True)
    scale = lax.rsqrt(spread + norm_eps)
    return center * scale, scale


def on_device(
    latents,
    context,
    lengths,
    text_len,
    timesteps,
    self_qkv,
    self_out,
    cross_query,
    cross_kv,
    cross_out,
    ffn_in,
    ffn_out,
    mod_weight,
    mod_bias,
    out_grad,
):
    micro, block_rows, model_width = latents.shape
    seq_count = lax.axis_size("seq")
    me = lax.axis_index("seq")
    frame_count = block_rows * seq_count
    item_count = lengths.shape[1]
    local = self_qkv.shape[2]
    hidden = ffn_in.shape[2]
    rows = micro * block_rows
    text_width = context.shape[2]

    attn_share = jnp.concatenate(
        [
            self_qkv[0],
            self_qkv[1],
            self_qkv[2],
            self_out.T,
            cross_query,
            cross_out.T,
            jnp.concatenate([cross_kv[0], cross_kv[1]], axis=0),
        ],
        axis=1,
    )
    ffn_share = jnp.concatenate([ffn_out.T, ffn_in[0], ffn_in[1]], axis=1)
    attn_all = lax.all_gather(attn_share, "seq", axis=0, tiled=True)
    ffn_all = lax.all_gather(ffn_share, "seq", axis=0, tiled=True)
    self_wt = attn_all[:, 3 * local : 4 * local]
    query_w = attn_all[:, 4 * local : 5 * local]
    cross_wt = attn_all[:, 5 * local : 6 * local]
    pair_w = attn_all[:, 6 * local :].reshape(seq_count, 2, text_width // seq_count, local)
    key_w = pair_w[:, 0].reshape(text_width, local)
    value_w = pair_w[:, 1].reshape(text_width, local)

    features = time_features(timesteps.reshape(-1))
    own_features = lax.dynamic_slice_in_dim(
        features, me * mod_weight.shape[0], mod_weight.shape[0], 1
    )
    bias_share = mod_bias.shape[1]
    bias_wide = lax.dynamic_update_slice_in_dim(
        jnp.zeros((6, model_width), f32), mod_bias.astype(f32), me * bias_share, 1
    )
    mod_part = jnp.dot(
        own_features, mod_weight.astype(f32).reshape(mod_weight.shape[0], -1), precision=highest
    ) + bias_wide.reshape(1, -1)
    modulation = seq_sum(mod_part).reshape(micro, item_count, 6, model_width)

    first_frame = me * block_rows
    own_places = first_frame + jnp.arange(block_rows, dtype=jnp.int32)
    near_places = first_frame - HALF + jnp.arange(block_rows + 2 * HALF, dtype=jnp.int32)
    near_inside = (near_places >= 0) & (near_places < frame_count)
    item_ends = jnp.cumsum(lengths, axis=1)
    item_starts = item_ends - lengths
    own_ids = jnp.sum(
        (item_ends[:, None, :] <= own_places[None, :, None]).astype(jnp.int32), axis=2
    )
    near_ids = jnp.sum(
        (item_ends[:, None, :] <= near_places[None, :, None]).astype(jnp.int32), axis=2
    )
    base_item = jnp.minimum(own_ids[:, 0], item_count - 2)
    catalog = jnp.arange(item_count, dtype=jnp.int32)
    choose = own_ids[:, :, None] == catalog[None, None, :]
    offsets_in = own_places[None, :] - jnp.sum(
        choose.astype(jnp.int32) * item_starts[:, None, :], axis=2
    )
    later = (own_ids != base_item[:, None])[:, :, None]
    two = jax.vmap(lambda table, start: lax.dynamic_slice_in_dim(table, start, 2, 0))(
        modulation, base_item
    )

    def framewise(index):
        chosen = jnp.where(later, two[:, 1, index][:, None, :], two[:, 0, index][:, None, :])
        return chosen.reshape(rows, model_width)

    table = rotary_tables(offsets_in.reshape(-1))
    windows = jnp.stack(
        [
            near_ids[:, part * HALF : (part + 3) * HALF]
            for part in range(block_rows // HALF)
        ],
        axis=1,
    )
    inside = jnp.stack(
        [near_inside[part * HALF : (part + 3) * HALF] for part in range(block_rows // HALF)]
    )
    row_in = jnp.arange(HALF, dtype=jnp.int32)
    key_in = jnp.arange(3 * HALF, dtype=jnp.int32) - HALF
    self_allowed = (
        (own_ids.reshape(micro, -1, HALF, 1) == windows[:, :, None, :])
        & inside[None, :, None, :]
        & (jnp.abs(row_in[:, None] - key_in[None, :]) <= HALF)[None, None]
    )
    self_bias = jnp.where(self_allowed, 0.0, -1e30).astype(f32).reshape(rows, 3 * HALF)
    text_slots = jnp.arange(2 * TXT, dtype=jnp.int32)
    key_items = base_item[:, None] + (text_slots // TXT)[None, :]
    key_lengths = jnp.sum(
        (key_items[:, :, None] == catalog[None, None, :]).astype(jnp.int32) * text_len[:, None, :],
        axis=2,
    )
    cross_allowed = (own_ids[:, :, None] == key_items[:, None, :]) & (
        (text_slots % TXT)[None, :] < key_lengths
    )[:, None, :]
    cross_bias = jnp.where(cross_allowed, 0.0, -1e30).astype(f32).reshape(rows, 2 * TXT)

    latent = latents.astype(f32).reshape(rows, model_width)
    cotangent = out_grad.reshape(rows, model_width)
    xhat_one, inv_one = normalize(latent)
    normed_one = (xhat_one * (1.0 + framewise(1)) + framewise(0)).astype(bf16)
    qkv = project(normed_one, attn_all, table, local)
    edges = qkv[:, local:].reshape(micro, block_rows, 2 * local)
    ahead = [(i, i + 1) for i in range(seq_count - 1)]
    behind = [(i + 1, i) for i in range(seq_count - 1)]
    low_rows = lax.ppermute(edges[:, block_rows - HALF :], "seq", ahead)
    high_rows = lax.ppermute(edges[:, :HALF], "seq", behind)
    mixed_one, logs_one = self_attention(qkv, low_rows, high_rows, self_bias, micro, block_rows)
    hidden_one = latent + pair_sum(nt(mixed_one, self_wt).astype(bf16))

    xhat_two, inv_two = normalize(hidden_one)
    normed_two = (xhat_two * (1.0 + framewise(3)) + framewise(2)).astype(bf16)
    query_two = nn(normed_two, query_w).astype(bf16)
    near_context = jax.vmap(
        lambda table, start: lax.dynamic_slice_in_dim(table, start * TXT, 2 * TXT, 0)
    )(context, base_item).reshape(micro * 2 * TXT, text_width)
    text_keys = nn(near_context, key_w).astype(bf16)
    text_values = nn(near_context, value_w).astype(bf16)
    mixed_two, logs_two = cross_attention(
        query_two, text_keys, text_values, cross_bias, micro, block_rows
    )
    hidden_two = hidden_one + pair_sum(nt(mixed_two, cross_wt).astype(bf16))

    xhat_three, inv_three = normalize(hidden_two)
    normed_three = (xhat_three * (1.0 + framewise(5)) + framewise(4)).astype(bf16)
    g_early, g_up, out_part, back_part = feed_forward(normed_three, cotangent, ffn_all, hidden)

    normed_three_grad = pair_sum(back_part)
    early = early_sum(g_early).reshape(-1, hidden // FFN_STEP, 2, FFN_STEP)
    outer_total = early[:, :, 0].reshape(-1, hidden)
    gate_total = early[:, :, 1].reshape(-1, hidden)
    block_out = (hidden_two + pair_sum(out_part)).astype(bf16)

    def norm_back(normed_grad, xhat, inv, scale_row):
        inner = normed_grad * (1.0 + scale_row)
        mean_inner = jnp.mean(inner, axis=-1, keepdims=True)
        mean_cross = jnp.mean(inner * xhat, axis=-1, keepdims=True)
        back = inv * (inner - mean_inner - xhat * mean_cross)
        cube = normed_grad.reshape(micro, block_rows, model_width)
        scaled = (normed_grad * xhat).reshape(micro, block_rows, model_width)

        def by_item(values):
            high_part = jnp.sum(jnp.where(later, values, 0.0), axis=1)
            low_part = jnp.sum(jnp.where(later, 0.0, values), axis=1)
            return jnp.stack([low_part, high_part], axis=1)

        return back, by_item(cube), by_item(scaled)

    back_three, shift_three, scale_three = norm_back(
        normed_three_grad, xhat_three, inv_three, framewise(5)
    )
    hidden_two_grad = cotangent.astype(f32) + back_three
    two_low = hidden_two_grad.astype(bf16)
    mixed_two_grad = nn(two_low, cross_wt).astype(bf16)
    query_two_low, text_key_low, text_value_low = cross_attention_back(
        query_two, text_keys, text_values, cross_bias, mixed_two_grad, logs_two, micro, block_rows
    )
    normed_two_grad = pair_sum(nt(query_two_low, query_w).astype(bf16))
    share = text_width // seq_count
    pair_grad = jnp.concatenate(
        [
            tn(near_context, text_key_low).reshape(seq_count, share, local),
            tn(near_context, text_value_low).reshape(seq_count, share, local),
        ],
        axis=1,
    ).reshape(2 * text_width, local)
    g_cross_out = tn(two_low, mixed_two).astype(bf16)
    g_cross_query = tn(normed_two, query_two_low).astype(bf16)
    back_two, shift_two, scale_two = norm_back(normed_two_grad, xhat_two, inv_two, framewise(3))
    hidden_one_grad = hidden_two_grad + back_two
    one_low = hidden_one_grad.astype(bf16)
    mixed_one_grad = nn(one_low, self_wt).astype(bf16)
    own_grads, to_low, to_high = self_attention_back(
        qkv, low_rows, high_rows, self_bias, mixed_one_grad, logs_one, micro, block_rows
    )
    from_high = lax.ppermute(to_low, "seq", behind)
    from_low = lax.ppermute(to_high, "seq", ahead)
    g_qkv, normed_one_part = qkv_back(
        own_grads, from_low, from_high, normed_one, attn_all, table, micro, block_rows
    )
    normed_one_grad = pair_sum(normed_one_part)
    g_self_out = tn(one_low, mixed_one).astype(bf16)
    (
        up_total,
        grad_cross_out,
        grad_cross_query,
        grad_cross_kv,
        grad_self_out,
        qkv_total,
    ) = scatter_sums([g_up, g_cross_out, g_cross_query, pair_grad.astype(bf16), g_self_out, g_qkv])
    back_one, shift_one, scale_one = norm_back(normed_one_grad, xhat_one, inv_one, framewise(1))
    latent_grad = hidden_one_grad + back_one

    pieces = jnp.stack(
        [shift_one, scale_one, shift_two, scale_two, shift_three, scale_three], axis=2
    )
    spots = (base_item[:, None] + jnp.arange(2)[None, :])[:, :, None] == catalog[None, None, :]
    item_grad = jnp.sum(
        jnp.where(spots[:, :, :, None, None], pieces[:, :, None], 0.0), axis=1
    ).reshape(micro * item_count, 6 * model_width)
    item_total = seq_sum(item_grad)
    mod_grad = jnp.dot(own_features.T, item_total, precision=highest).reshape(mod_weight.shape)
    bias_grad = lax.dynamic_slice_in_dim(
        jnp.sum(item_total, axis=0).reshape(6, model_width), me * bias_share, bias_share, 1
    )

    grad_qkv = jnp.stack([qkv_total[:, i * local : (i + 1) * local] for i in range(3)])
    return (
        block_out.reshape(latents.shape),
        latent_grad.reshape(latents.shape),
        grad_qkv,
        grad_self_out.T,
        grad_cross_query,
        grad_cross_kv.reshape(2, share, local),
        grad_cross_out.T,
        jnp.stack([gate_total, up_total]),
        outer_total.T,
        mod_grad,
        bias_grad,
    )


def solution(mesh):
    return jax.shard_map(
        on_device,
        mesh=mesh,
        in_specs=(
            P(None, "seq", None),
            P(),
            P(),
            P(),
            P(),
            P(None, "seq", "tensor"),
            P("tensor", "seq"),
            P("seq", "tensor"),
            P(None, "seq", "tensor"),
            P("tensor", "seq"),
            P(None, "seq", "tensor"),
            P("tensor", "seq"),
            P("seq", None, None),
            P(None, "seq"),
            P(None, "seq", None),
        ),
        out_specs=(
            P(None, "seq", None),
            P(None, "seq", None),
            P(None, "seq", "tensor"),
            P("tensor", "seq"),
            P("seq", "tensor"),
            P(None, "seq", "tensor"),
            P("tensor", "seq"),
            P(None, "seq", "tensor"),
            P("tensor", "seq"),
            P("seq", None, None),
            P(None, "seq"),
        ),
        check_vma=False,
    )
```

```python
import functools
import math

import jax
import jax.numpy as jnp
import numpy as np
from jax import lax
from jax.experimental import pallas as pl
from jax.experimental.pallas import tpu as pltpu
from jax.sharding import PartitionSpec as P

HD = 64
TXT = 128
TEMB = 256
HALF = 128


norm_eps = 1e-05
highest = lax.Precision.HIGHEST
f32 = jnp.float32
bf16 = jnp.bfloat16


def dot(a, b, dims):
    return lax.dot_general(a, b, ((dims[0], dims[1]), ((), ())), preferred_element_type=f32)


def nn(a, b):
    return dot(a, b, ((1,), (0,)))


def nt(a, b):
    return dot(a, b, ((1,), (1,)))


def tn(a, b):
    return dot(a, b, ((0,), (0,)))


def halves(count):
    stride = 1
    strides = []
    while stride < count:
        strides.append(stride)
        stride *= 2
    return strides


def flip(block, stride):
    count = lax.axis_size("seq")
    return lax.ppermute(block, "seq", [(i, i ^ stride) for i in range(count)])


def swap(part):
    count = lax.axis_size("tensor")
    return lax.ppermute(part, "tensor", [(i, (i + 1) % count) for i in range(count)])


def seq_sum(part):
    for stride in halves(lax.axis_size("seq")):
        part = part + flip(part, stride)
    return part


def kernel_params(grid_rank, mib):
    return pltpu.CompilerParams(
        dimension_semantics=("arbitrary",) * grid_rank, vmem_limit_bytes=mib * 1024 * 1024
    )


STRIDES = (1, 2, 4, 8)


def seq_digits(me):
    return [(me // stride) % 2 for stride in STRIDES]


def greet(me, digits, others=()):
    partners = [me + stride * (1 - 2 * digit) for stride, digit in zip(STRIDES, digits)]
    barrier = pltpu.get_barrier_semaphore()

    def tell(target):
        pl.semaphore_signal(
            barrier, inc=1, device_id={"seq": target}, device_id_type=pl.DeviceIdType.MESH
        )

    expected = len(partners)
    for partner in partners:
        tell(partner)
    for there, target in others:
        pl.when(there)(functools.partial(tell, target))
        expected = expected + there.astype(jnp.int32)
    pl.semaphore_wait(barrier, expected)
    return partners


def send_to(partner, source, target, send_sem, recv_sem):
    return pltpu.make_async_remote_copy(
        src_ref=source,
        dst_ref=target,
        send_sem=send_sem,
        recv_sem=recv_sem,
        device_id={"seq": partner},
        device_id_type=pl.DeviceIdType.MESH,
    )


def small_sum(partners, part_ref, held, got, total_ref, send_sem, recv_sem):
    def exchange(k):
        return send_to(partners[k], held.at[k], got.at[k], send_sem.at[k], recv_sem.at[k])

    def step(k):
        if k == 0:
            held[0] = part_ref[...]
        else:
            exchange(k - 1).wait()
            summed = held[k - 1] + got[k - 1]
            if k == len(STRIDES):
                total_ref[...] = summed
            else:
                held[k] = summed
        if k < len(STRIDES):
            exchange(k).start()

    return step


def small_scratch(shape):
    return [
        pltpu.VMEM((len(STRIDES),) + shape, f32),
        pltpu.VMEM((len(STRIDES),) + shape, f32),
        pltpu.SemaphoreType.DMA((len(STRIDES),)),
        pltpu.SemaphoreType.DMA((len(STRIDES),)),
    ]


def lane_ladder():
    quarter = HD // 4
    return np.exp(-math.log(10000.0) * (np.arange(128) % quarter) / quarter).astype(np.float32)


def prepare(first, frame_count, lengths, text_len, block_rows):
    items = len(lengths)
    ends = [lengths[0]]
    for length in lengths[1:]:
        ends.append(ends[-1] + length)

    def item_of(place):
        return sum((end <= place).astype(jnp.int32) for end in ends)

    def pick(ids, values):
        return sum(jnp.where(ids == k, value, 0) for k, value in enumerate(values))

    near_rows = block_rows + 2 * HALF
    place = first - HALF + lax.broadcasted_iota(jnp.int32, (near_rows, 1), 0)
    ids = item_of(place)
    offset = place - pick(ids, [end - length for end, length in zip(ends, lengths)])
    base = jnp.minimum(item_of(first), items - 2)
    own_ids = ids[HALF : HALF + block_rows]
    self_bias = []
    for part in range(block_rows // HALF):
        row = lax.broadcasted_iota(jnp.int32, (HALF, 1), 0)
        key = lax.broadcasted_iota(jnp.int32, (1, 3 * HALF), 1) - HALF
        key_place = first + part * HALF + key
        inside = (key_place >= 0) & (key_place < frame_count)
        key_ids = jnp.where(inside, item_of(key_place), -1)
        near_enough = jnp.abs(row - key) <= HALF
        same = own_ids[part * HALF : (part + 1) * HALF] == key_ids
        self_bias.append(jnp.where(near_enough & same, 0.0, -1e30))
    slot = lax.broadcasted_iota(jnp.int32, (1, 2 * TXT), 1)
    key_item = jnp.where(slot < TXT, base, base + 1)
    used = jnp.where(slot < TXT, slot, slot - TXT) < pick(key_item, text_len)
    key_item = jnp.where(used, key_item, -1)
    cross_bias = jnp.where(own_ids == key_item, 0.0, -1e30)
    later = (ids != base).astype(f32)
    return base, offset, later, self_bias, cross_bias


def lane_tables(offset, ladder):
    quarter = HD // 4
    angles = offset.astype(f32) * ladder
    lane = lax.broadcasted_iota(jnp.int32, angles.shape, 1) % HD
    cosine = jnp.cos(angles)
    sine = jnp.sin(angles)
    return (
        jnp.where(lane < 2 * quarter, cosine, 1.0),
        jnp.where((lane >= quarter) & (lane < 2 * quarter), sine, 0.0),
        jnp.where(lane < quarter, -sine, 0.0),
    )


def gather_kernel(
    share_ref, part_ref, latent_ref, lengths_ref, text_ref, ladder_ref,
    out_ref, near_normed_ref, normed_t_ref, two_ref, later_ref, table_ref, self_ref, cross_ref,
    near_ref, total_ref, held, got, small_send, small_recv, copy_sem, send_sem, recv_sem,
    near_sem, halo_send, halo_recv, *, pieces, step, y_first, seq_count,
):
    micro, block_rows, width = latent_ref.shape
    items = lengths_ref.shape[1]
    near_rows = block_rows + 2 * HALF
    me = lax.axis_index("seq")
    digits = seq_digits(me)
    core, y, z_lo, z_hi = digits
    first = me * block_rows
    has_low = me > 0
    has_high = me < seq_count - 1
    partners = greet(me, digits, ((has_low, me - 1), (has_high, me + 1)))
    small = small_sum(partners, part_ref, held, got, total_ref, small_send, small_recv)

    def to_low():
        return send_to(
            me - 1,
            latent_ref.at[:, :HALF],
            near_ref.at[:, near_rows - HALF :],
            halo_send.at[0],
            halo_recv.at[0],
        )

    def to_high():
        return send_to(
            me + 1,
            latent_ref.at[:, block_rows - HALF :],
            near_ref.at[:, :HALF],
            halo_send.at[1],
            halo_recv.at[1],
        )

    def load_own():
        return pltpu.make_async_copy(
            latent_ref, near_ref.at[:, HALF : near_rows - HALF], near_sem
        )

    def piece(p):
        return pl.ds(p * step, step)

    def exchange(p, stage):
        cols = piece(p)
        if p in y_first:
            axis = (1, 3, 2, 0)[stage]
            spots = ((z_hi, z_lo, y, core), (z_hi, z_lo, None, core), (None, z_lo, None, core), None)
        else:
            axis = (3, 2, 1, 0)[stage]
            spots = ((z_hi, z_lo, y, core), (None, z_lo, y, core), (None, None, y, core), None)
        spot = spots[stage] or (None, None, None, core)
        index = tuple(slice(None) if digit is None else digit for digit in spot)
        block = out_ref.at[index + (slice(None), cols)]
        source = share_ref.at[:, cols] if stage == 0 else block
        return send_to(partners[axis], source, block, send_sem.at[stage, p], recv_sem.at[stage, p])

    def own(p):
        return pltpu.make_async_copy(
            share_ref.at[:, piece(p)],
            out_ref.at[z_hi, z_lo, y, core, :, piece(p)],
            copy_sem.at[p],
        )

    def masks(m):
        base, offset, later, self_bias, cross_bias = prepare(
            first,
            seq_count * block_rows,
            [lengths_ref[m, k] for k in range(items)],
            [text_ref[m, k] for k in range(items)],
            block_rows,
        )
        rows = slice(m * block_rows, (m + 1) * block_rows)
        later_ref[rows, :] = later[HALF : HALF + block_rows]
        for part, bias in enumerate(self_bias):
            start = m * block_rows + part * HALF
            self_ref[start : start + HALF, :] = bias
        cross_ref[rows, :] = cross_bias
        state[m] = base, offset, later

    def tables(m, start):
        offset = state[m][1][start : start + HALF]
        target = m * near_rows + start
        for index, values in enumerate(lane_tables(offset, ladder_ref[...])):
            table_ref[index, target : target + HALF, :] = values

    def modulation(m, base):
        for which in range(2):
            two_ref[m, which : which + 1] = sum(
                jnp.where(base + which == k, total_ref[m * items + k : m * items + k + 1], 0.0)
                for k in range(items)
            )

    def norm(m, start):
        shift = [two_ref[m, which : which + 1, :width] for which in range(2)]
        factor = [two_ref[m, which : which + 1, width : 2 * width] for which in range(2)]
        tile = near_ref[m, start : start + HALF].astype(f32)
        chosen = state[m][2][start : start + HALF] > 0.5
        xhat, _ = spread_rows(tile)
        normed = (
            xhat * (1.0 + jnp.where(chosen, factor[1], factor[0]))
            + jnp.where(chosen, shift[1], shift[0])
        ).astype(bf16)
        target = m * near_rows + start
        near_normed_ref[target : target + HALF, :] = normed
        if HALF <= start < HALF + block_rows:
            target = m * block_rows + start - HALF
            normed_t_ref[:, target : target + HALF] = normed.T

    beside = {}
    state = {}
    gap = 4

    def add(t, work):
        beside.setdefault(t, []).append(work)

    def finish_near():
        load_own().wait()
        pl.when(has_low)(lambda: to_high().wait_recv())
        pl.when(has_high)(lambda: to_low().wait_recv())

    tick = 1
    for m in range(micro):
        add(tick, functools.partial(masks, m))
        for start in range(0, near_rows, HALF):
            tick += 1
            add(tick, functools.partial(tables, m, start))
        tick += 1
    for k in range(1, len(STRIDES) + 1):
        add(gap * k, functools.partial(small, k))
    tick = gap * len(STRIDES)
    add(tick, finish_near)
    for m in range(micro):
        tick += 1
        add(tick, lambda m=m: modulation(m, state[m][0]))
        for start in range(0, near_rows, HALF):
            add(tick, functools.partial(norm, m, start))
            tick += 1
    last_tick = tick

    small(0)
    load_own().start()
    pl.when(has_low)(lambda: to_low().start())
    pl.when(has_high)(lambda: to_high().start())

    @pl.when(jnp.logical_not(has_low))
    def _():
        near_ref[:, :HALF] = jnp.zeros((micro, HALF, width), near_ref.dtype)

    @pl.when(jnp.logical_not(has_high))
    def _():
        near_ref[:, near_rows - HALF :] = jnp.zeros((micro, HALF, width), near_ref.dtype)

    lags = (0, 3, 6, 10, 12)
    for t in range(max(pieces + lags[-1], last_tick + 1)):
        if t < pieces:
            exchange(t, 0).start()
            own(t).start()
        for stage in (1, 2, 3):
            p = t - lags[stage]
            if 0 <= p < pieces:
                if stage == 1:
                    own(p).wait()
                exchange(p, stage - 1).wait_recv()
                exchange(p, stage).start()
        if 0 <= t - lags[4] < pieces:
            exchange(t - lags[4], 3).wait_recv()
        for work in beside.get(t, ()):
            work()
    for p in range(pieces):
        for stage in range(4):
            exchange(p, stage).wait_send()
    pl.when(has_low)(lambda: to_low().wait_send())
    pl.when(has_high)(lambda: to_high().wait_send())


def gather_and_prepare(share, part, latents, lengths, text_len, step=256):
    count = lax.axis_size("seq")
    me = lax.axis_index("seq")
    rows, width = share.shape
    micro, block_rows, model_width = latents.shape
    items = lengths.shape[1]
    near_rows = block_rows + 2 * HALF
    own_rows = micro * block_rows
    ladder = jnp.asarray(lane_ladder()).reshape(1, 128)
    if count != 16 or rows % 16 or width % step:
        ahead = [(i, i + 1) for i in range(count - 1)]
        behind = [(i + 1, i) for i in range(count - 1)]
        low_rows = lax.ppermute(latents[:, block_rows - HALF :], "seq", ahead)
        high_rows = lax.ppermute(latents[:, :HALF], "seq", behind)
        near_latent = jnp.concatenate([low_rows, latents, high_rows], axis=1)
        total = seq_sum(part).reshape(micro, items, 6 * model_width)
        parts = []
        for m in range(micro):
            base, offset, later, self_bias, cross_bias = prepare(
                me * block_rows,
                count * block_rows,
                [lengths[m, k] for k in range(items)],
                [text_len[m, k] for k in range(items)],
                block_rows,
            )
            two = lax.dynamic_slice_in_dim(total[m], base, 2, 0)
            xhat, _ = spread_rows(near_latent[m].astype(f32))
            shift, factor = [
                jnp.where(later > 0.5, two[1], two[0])[:, i * model_width : (i + 1) * model_width]
                for i in range(2)
            ]
            normed = (xhat * (1.0 + factor) + shift).astype(bf16)
            parts.append(
                (
                    normed,
                    normed[HALF : HALF + block_rows].T,
                    two[None],
                    later[HALF : HALF + block_rows],
                    jnp.stack(lane_tables(offset, ladder)),
                    jnp.concatenate(self_bias, axis=0),
                    cross_bias,
                )
            )
        axes = (0, 1, 0, 0, 1, 0, 0)
        joined = [jnp.concatenate(group, axis=axis) for group, axis in zip(zip(*parts), axes)]
        return [lax.all_gather(share, "seq", axis=0, tiled=True)] + joined
    pieces = width // step
    any_space = pl.BlockSpec(memory_space=pl.ANY)
    vmem = pl.BlockSpec(memory_space=pltpu.VMEM)
    smem = pl.BlockSpec(memory_space=pltpu.SMEM)
    outs = pl.pallas_call(
        functools.partial(
            gather_kernel,
            pieces=pieces,
            step=step,
            y_first=tuple(range(pieces // 6, pieces, pieces // 3)),
            seq_count=count,
        ),
        out_shape=[
            jax.ShapeDtypeStruct((2, 2, 2, 2, rows, width), share.dtype),
            jax.ShapeDtypeStruct((micro * near_rows, model_width), bf16),
            jax.ShapeDtypeStruct((model_width, own_rows), bf16),
            jax.ShapeDtypeStruct((micro, 2, 6 * model_width), f32),
            jax.ShapeDtypeStruct((own_rows, 1), f32),
            jax.ShapeDtypeStruct((3, micro * near_rows, 128), f32),
            jax.ShapeDtypeStruct((own_rows, 3 * HALF), f32),
            jax.ShapeDtypeStruct((own_rows, 2 * TXT), f32),
        ],
        in_specs=[any_space, vmem, any_space, smem, smem, vmem],
        out_specs=[any_space] + [vmem] * 7,
        scratch_shapes=[
            pltpu.VMEM((micro, near_rows, model_width), bf16),
            pltpu.VMEM(part.shape, f32),
        ]
        + small_scratch(part.shape)
        + [
            pltpu.SemaphoreType.DMA((pieces,)),
            pltpu.SemaphoreType.DMA((4, pieces)),
            pltpu.SemaphoreType.DMA((4, pieces)),
            pltpu.SemaphoreType.DMA,
            pltpu.SemaphoreType.DMA((2,)),
            pltpu.SemaphoreType.DMA((2,)),
        ],
        compiler_params=pltpu.CompilerParams(
            collective_id=1, has_side_effects=True, vmem_limit_bytes=48 * 1024 * 1024
        ),
        cost_estimate=pl.CostEstimate(
            flops=0, bytes_accessed=20 * count * rows * width, transcendentals=0
        ),
        name="gather_and_prepare",
    )(share, part, latents, lengths, text_len, ladder)
    return [outs[0].reshape(count * rows, width)] + list(outs[1:])


SLOTS = 5


def when(condition):
    if isinstance(condition, bool):
        return (lambda work: work()) if condition else (lambda work: None)
    return pl.when(condition)


class Pieces:
    def __init__(self, refs, out_ref, partners, digits, step):
        (
            self.own, self.got0, self.got1, self.got2, self.got3, self.staged,
            self.out_sem, self.send_sem, self.recv_sem,
        ) = refs
        self.out_ref = out_ref
        self.partners = partners
        self.digits = digits
        self.step = step

    @staticmethod
    def scratch(rows, step):
        return [
            pltpu.VMEM((SLOTS, 2, 2, 2, rows, step), bf16),
            pltpu.VMEM((SLOTS, 2, 2, 2, rows, step), bf16),
            pltpu.VMEM((SLOTS, 2, 2, rows, step), bf16),
            pltpu.VMEM((SLOTS, 2, rows, step), bf16),
            pltpu.VMEM((SLOTS, rows, step), bf16),
            pltpu.VMEM((SLOTS, rows, step), f32),
            pltpu.SemaphoreType.DMA((SLOTS,)),
            pltpu.SemaphoreType.DMA((4, SLOTS)),
            pltpu.SemaphoreType.DMA((4, SLOTS)),
        ]

    def exchange(self, stage, source, target, slot):
        return send_to(
            self.partners[stage],
            source,
            target,
            self.send_sem.at[stage, slot],
            self.recv_sem.at[stage, slot],
        )

    def over_core(self, source, slot):
        return self.exchange(0, source, self.got0.at[slot], slot)

    def over_y(self, slot):
        y = self.digits[1]
        return self.exchange(1, self.own.at[slot, :, :, 1 - y], self.got1.at[slot], slot)

    def over_z_lo(self, slot):
        _, y, z_lo, _ = self.digits
        return self.exchange(2, self.own.at[slot, :, 1 - z_lo, y], self.got2.at[slot], slot)

    def over_z_hi(self, slot):
        _, y, z_lo, z_hi = self.digits
        return self.exchange(3, self.own.at[slot, 1 - z_hi, z_lo, y], self.got3.at[slot], slot)

    def store(self, item, slot):
        columns = pl.ds(pl.multiple_of(item * self.step, self.step), self.step)
        return pltpu.make_async_copy(
            self.staged.at[slot], self.out_ref.at[:, columns], self.out_sem.at[slot]
        )

    def wait_sent(self, slot):
        self.over_y(slot).wait_send()
        self.over_z_lo(slot).wait_send()
        self.over_z_hi(slot).wait_send()

    def add_core(self, slot, left):
        for i in range(2):
            for j in range(2):
                for k in range(2):
                    total = left(i, j, k).astype(f32) + self.got0[slot, i, j, k].astype(f32)
                    self.own[slot, i, j, k] = total.astype(bf16)
        self.over_y(slot).start()

    def later_steps(self, t, count):
        own = self.own
        _, y, z_lo, z_hi = self.digits

        @when((t >= 2) & (t - 2 < count))
        def _():
            slot = (t - 2) % SLOTS
            self.over_y(slot).wait_recv()
            for i in range(2):
                for j in range(2):
                    total = own[slot, i, j, y].astype(f32) + self.got1[slot, i, j].astype(f32)
                    own[slot, i, j, y] = total.astype(bf16)
            self.over_z_lo(slot).start()

        @when((t >= 3) & (t - 3 < count))
        def _():
            slot = (t - 3) % SLOTS
            self.over_z_lo(slot).wait_recv()
            for i in range(2):
                total = own[slot, i, z_lo, y].astype(f32) + self.got2[slot, i].astype(f32)
                own[slot, i, z_lo, y] = total.astype(bf16)
            self.over_z_hi(slot).start()

        @when((t >= 4) & (t - 4 < count))
        def _():
            slot = (t - 4) % SLOTS
            self.over_z_hi(slot).wait_recv()
            when(t - 4 >= SLOTS)(lambda: self.store(0, slot).wait())
            self.staged[slot] = own[slot, z_hi, z_lo, y].astype(f32) + self.got3[slot].astype(f32)
            self.store(t - 4, slot).start()

    def finish(self, count):
        for back in range(min(SLOTS, count)):
            slot = (count - 1 - back) % SLOTS
            self.store(0, slot).wait()
            self.wait_sent(slot)


PIECE_REFS = 9


def scatter_kernel(*refs, widths, step, with_small):
    refs = list(refs)
    sources = [refs.pop(0) for _ in widths]
    if with_small:
        part_ref = refs.pop(0)
    out_ref = refs.pop(0)
    if with_small:
        total_ref = refs.pop(0)
    own_sem = refs.pop(0)
    me = lax.axis_index("seq")
    digits = seq_digits(me)
    core = digits[0]
    partners = greet(me, digits)
    pieces = Pieces(refs[:PIECE_REFS], out_ref, partners, digits, step)
    if with_small:
        small = small_sum(partners, part_ref, refs[-4], refs[-3], total_ref, refs[-2], refs[-1])
        small(0)
    count = sum(widths) // step

    def over_core(source, column, slot):
        return pieces.over_core(source.at[:, :, :, 1 - core, :, pl.ds(column, step)], slot)

    def load(source, column, slot):
        return pltpu.make_async_copy(
            source.at[:, :, :, core, :, pl.ds(column, step)],
            pieces.own.at[slot],
            own_sem.at[slot],
        )

    def tick(t, carry):
        @pl.when(t < count)
        def _():
            slot = t % SLOTS
            pl.when(t >= SLOTS)(lambda: pieces.wait_sent(slot))
            first = 0
            for source, width in zip(sources, widths):

                @pl.when((t >= first) & (t < first + width // step))
                def _(source=source, first=first):
                    column = pl.multiple_of((t - first) * step, step)
                    over_core(source, column, slot).start()
                    load(source, column, slot).start()

                first += width // step

        @pl.when((t >= 1) & (t - 1 < count))
        def _():
            slot = (t - 1) % SLOTS
            load(sources[0], 0, slot).wait()
            over_core(sources[0], 0, slot).wait()
            pieces.add_core(slot, lambda i, j, k: pieces.own[slot, i, j, k])

        pieces.later_steps(t, count)
        if with_small:
            for k in range(1, len(STRIDES) + 1):
                pl.when(t == 3 * k)(functools.partial(small, k))
        return carry

    lax.fori_loop(0, count + 4, tick, 0)
    pieces.finish(count)


def scatter_sums(grads, which, part=None, step=256):
    count = lax.axis_size("seq")
    rows = grads[0].shape[0] // count
    widths = tuple(grad.shape[1] for grad in grads)
    if count != 16 or rows % 16 or any(width % step for width in widths):
        sums = [
            lax.psum_scatter(grad.astype(f32), "seq", scatter_dimension=0, tiled=True)
            for grad in grads
        ]
        return sums if part is None else sums + [seq_sum(part)]
    any_space = pl.BlockSpec(memory_space=pl.ANY)
    vmem = pl.BlockSpec(memory_space=pltpu.VMEM)
    scratch = [pltpu.SemaphoreType.DMA((SLOTS,))] + Pieces.scratch(rows, step)
    out_shape = [jax.ShapeDtypeStruct((rows, sum(widths)), f32)]
    extra = []
    if part is not None:
        scratch += small_scratch(part.shape)
        out_shape.append(jax.ShapeDtypeStruct(part.shape, f32))
        extra = [vmem]
    outs = pl.pallas_call(
        functools.partial(
            scatter_kernel, widths=widths, step=step, with_small=part is not None
        ),
        out_shape=out_shape,
        in_specs=[any_space] * len(grads) + extra,
        out_specs=[any_space] + extra,
        scratch_shapes=scratch,
        compiler_params=pltpu.CompilerParams(
            collective_id=which, has_side_effects=True, vmem_limit_bytes=40 * 1024 * 1024
        ),
        cost_estimate=pl.CostEstimate(
            flops=0, bytes_accessed=8 * count * rows * sum(widths), transcendentals=0
        ),
        name="scatter_sums",
    )(
        *[grad.reshape(2, 2, 2, 2, rows, grad.shape[1]) for grad in grads],
        *([] if part is None else [part]),
    )
    firsts = [sum(widths[:i]) for i in range(len(widths))]
    return [outs[0][:, first : first + width] for first, width in zip(firsts, widths)] + list(
        outs[1:]
    )


def early_sum(grad):
    return lax.psum_scatter(grad, "seq", scatter_dimension=0, tiled=True).astype(f32)


def turn(values, own, below, above):
    quarter = HD // 4
    return (
        values * own
        + pltpu.roll(values, quarter, 1) * below
        + pltpu.roll(values, 2 * HD - quarter, 1) * above
    )


def project_kernel(normed_ref, weight_ref, table_ref, out_ref, *, turned):
    j = pl.program_id(0)
    product = nn(normed_ref[...], weight_ref[...])

    @pl.when(j < turned)
    def _():
        for part in range(product.shape[1] // 128):
            lanes = slice(part * 128, (part + 1) * 128)
            out_ref[:, lanes] = turn(
                product[:, lanes], table_ref[0], table_ref[1], table_ref[2]
            ).astype(bf16)

    @pl.when(j >= turned)
    def _():
        out_ref[...] = product.astype(bf16)


def project(normed, weights, table, local, step=256):
    rows, width = normed.shape
    return pl.pallas_call(
        functools.partial(project_kernel, turned=2 * local // step),
        grid=(3 * local // step,),
        in_specs=[
            pl.BlockSpec((rows, width), lambda j: (0, 0)),
            pl.BlockSpec((width, step), lambda j: (0, j)),
            pl.BlockSpec((3, rows, 128), lambda j: (0, 0, 0)),
        ],
        out_specs=pl.BlockSpec((rows, step), lambda j: (0, j)),
        out_shape=jax.ShapeDtypeStruct((rows, 3 * local), bf16),
        compiler_params=kernel_params(1, 32),
        cost_estimate=pl.CostEstimate(
            flops=2 * rows * width * 3 * local,
            bytes_accessed=2 * (rows * width + 3 * local * (width + rows)),
            transcendentals=0,
        ),
        name="qkv_projection",
    )(normed, weights, table)


def head_lanes(shape):
    return lax.broadcasted_iota(jnp.int32, shape, 1) < HD


def one_head(values, first, which):
    return jnp.where(first if which == 0 else ~first, values, jnp.zeros_like(values))


def soft_rows(scores):
    peak = jnp.max(scores, axis=-1, keepdims=True)
    raised = jnp.exp(scores - peak)
    total = jnp.sum(raised, axis=-1, keepdims=True)
    return raised * (1.0 / total), peak + jnp.log(total)


def attend_rows(query, keys, values, bias):
    first = head_lanes(query.shape)
    out = None
    logs = []
    for which in range(2):
        scores = nt(one_head(query, first, which), keys) * (HD**-0.5) + bias
        weights, log_total = soft_rows(scores)
        mixed = nn(weights.astype(bf16), values)
        out = mixed if which == 0 else jnp.where(first, out, mixed)
        logs.append(log_total)
    return out, logs


def attend_rows_back(query, keys, values, bias, logs, grad):
    first = head_lanes(query.shape)
    query_grad = key_grad = value_grad = None
    for which in range(2):
        own_query = one_head(query, first, which)
        own_grad = one_head(grad, first, which)
        scores = nt(own_query, keys) * (HD**-0.5) + bias
        chances = jnp.exp(scores - logs[which])
        chance_grad = nt(own_grad, values)
        score_grad = (
            chances * (chance_grad - jnp.sum(chances * chance_grad, axis=-1, keepdims=True))
        ).astype(bf16)
        to_query = nn(score_grad, keys) * (HD**-0.5)
        to_key = tn(score_grad, own_query) * (HD**-0.5)
        to_value = tn(chances.astype(bf16), own_grad)
        if which == 0:
            query_grad, key_grad, value_grad = to_query, to_key, to_value
        else:
            query_grad = jnp.where(first, query_grad, to_query)
            key_grad = key_grad + to_key
            value_grad = value_grad + to_value
    return query_grad, key_grad, value_grad


def put_logs(log_ref, rows, logs, pair):
    lane = lax.broadcasted_iota(jnp.int32, (logs[0].shape[0], 128), 1)
    kept = log_ref[rows, :]
    kept = jnp.where(lane == 2 * pair, logs[0], kept)
    log_ref[rows, :] = jnp.where(lane == 2 * pair + 1, logs[1], kept)


def get_logs(log_ref, rows, pair):
    kept = log_ref[rows, :]
    lane = lax.broadcasted_iota(jnp.int32, kept.shape, 1)
    return [
        jnp.sum(jnp.where(lane == 2 * pair + which, kept, 0.0), axis=1, keepdims=True)
        for which in range(2)
    ]


def spread_rows(hidden):
    center = hidden - jnp.mean(hidden, axis=-1, keepdims=True)
    spread = jnp.mean(center * center, axis=-1, keepdims=True)
    scale = lax.rsqrt(spread + norm_eps)
    return center * scale, scale


def item_row(two_ref, later_ref, index):
    width = two_ref.shape[2] // 6
    lanes = slice(index * width, (index + 1) * width)
    return jnp.where(later_ref[...] > 0.5, two_ref[0, 1:2, lanes], two_ref[0, 0:1, lanes])


def norm_kernel(*refs, index, with_weight):
    refs = list(refs)
    base_ref, own_ref, got_ref, two_ref, later_ref = refs[:5]
    weight_ref = refs[5] if with_weight else None
    outs = refs[5 + with_weight :]
    hidden = (
        base_ref[...].astype(f32) + own_ref[...].astype(f32) + got_ref[...].astype(f32)
    )
    xhat, _ = spread_rows(hidden)
    normed = (
        xhat * (1.0 + item_row(two_ref, later_ref, index + 1)) + item_row(two_ref, later_ref, index)
    ).astype(bf16)
    outs[0][...] = hidden
    outs[1][...] = normed
    outs[2][...] = normed.T
    if with_weight:
        outs[3][...] = nn(normed, weight_ref[...]).astype(bf16)


def norm_forward(base, own, got, two, later, index, micro, weights=None, column=0, out_width=0):
    rows, width = base.shape
    tile = rows // micro
    row_tile = pl.BlockSpec((tile, width), lambda i: (i, 0))
    in_specs = [
        row_tile,
        row_tile,
        row_tile,
        pl.BlockSpec((1, 2, 6 * width), lambda i: (i, 0, 0)),
        pl.BlockSpec((tile, 1), lambda i: (i, 0)),
    ]
    out_specs = [row_tile, row_tile, pl.BlockSpec((width, tile), lambda i: (0, i))]
    out_shape = [
        jax.ShapeDtypeStruct((rows, width), f32),
        jax.ShapeDtypeStruct((rows, width), bf16),
        jax.ShapeDtypeStruct((width, rows), bf16),
    ]
    args = [base, own, got, two, later]
    if weights is not None:
        in_specs.append(pl.BlockSpec((width, out_width), lambda i: (0, column)))
        out_specs.append(pl.BlockSpec((tile, out_width), lambda i: (i, 0)))
        out_shape.append(jax.ShapeDtypeStruct((rows, out_width), bf16))
        args.append(weights)
    return pl.pallas_call(
        functools.partial(norm_kernel, index=index, with_weight=weights is not None),
        grid=(micro,),
        in_specs=in_specs,
        out_specs=out_specs,
        out_shape=out_shape,
        compiler_params=kernel_params(1, 40),
        cost_estimate=pl.CostEstimate(
            flops=2 * rows * width * out_width, bytes_accessed=16 * rows * width, transcendentals=0
        ),
        name="norm_forward",
    )(*args)


def norm_back_kernel(*refs, index, with_weight):
    refs = list(refs)
    up_ref, own_ref, got_ref, hidden_ref, two_ref, later_ref = refs[:6]
    weight_ref = refs[6] if with_weight else None
    outs = refs[6 + with_weight :]
    xhat, scale = spread_rows(hidden_ref[...].astype(f32))
    grad = own_ref[...].astype(f32) + got_ref[...].astype(f32)
    inner = grad * (1.0 + item_row(two_ref, later_ref, index + 1))
    mean_inner = jnp.mean(inner, axis=-1, keepdims=True)
    mean_cross = jnp.mean(inner * xhat, axis=-1, keepdims=True)
    total = up_ref[...].astype(f32) + scale * (inner - mean_inner - xhat * mean_cross)
    outs[0][...] = total
    later = later_ref[...] > 0.5
    scaled = grad * xhat
    for item in range(2):
        chosen = later if item else ~later
        outs[1][0, item, 0:1] = jnp.sum(jnp.where(chosen, grad, 0.0), axis=0, keepdims=True)
        outs[1][0, item, 1:2] = jnp.sum(jnp.where(chosen, scaled, 0.0), axis=0, keepdims=True)
    if with_weight:
        rounded = total.astype(bf16)
        outs[2][...] = rounded.T
        outs[3][...] = nn(rounded, weight_ref[...]).astype(bf16)


def norm_back(up, own, got, hidden, two, later, index, micro, weights=None, column=0, out_width=0):
    rows, width = hidden.shape
    tile = rows // micro
    row_tile = pl.BlockSpec((tile, width), lambda i: (i, 0))
    in_specs = [
        row_tile,
        row_tile,
        row_tile,
        row_tile,
        pl.BlockSpec((1, 2, 6 * width), lambda i: (i, 0, 0)),
        pl.BlockSpec((tile, 1), lambda i: (i, 0)),
    ]
    out_specs = [row_tile, pl.BlockSpec((1, 2, 2, width), lambda i: (i, 0, 0, 0))]
    out_shape = [
        jax.ShapeDtypeStruct((rows, width), f32),
        jax.ShapeDtypeStruct((micro, 2, 2, width), f32),
    ]
    args = [up, own, got, hidden, two, later]
    if weights is not None:
        in_specs.append(pl.BlockSpec((width, out_width), lambda i: (0, column)))
        out_specs += [
            pl.BlockSpec((width, tile), lambda i: (0, i)),
            pl.BlockSpec((tile, out_width), lambda i: (i, 0)),
        ]
        out_shape += [
            jax.ShapeDtypeStruct((width, rows), bf16),
            jax.ShapeDtypeStruct((rows, out_width), bf16),
        ]
        args.append(weights)
    return pl.pallas_call(
        functools.partial(norm_back_kernel, index=index, with_weight=weights is not None),
        grid=(micro,),
        in_specs=in_specs,
        out_specs=out_specs,
        out_shape=out_shape,
        compiler_params=kernel_params(1, 48),
        cost_estimate=pl.CostEstimate(
            flops=2 * rows * width * out_width, bytes_accessed=20 * rows * width, transcendentals=0
        ),
        name="norm_back",
    )(*args)


def add_product(acc_ref, out_ref, product):
    pair = pl.program_id(1)

    @pl.when(pair == 0)
    def _():
        acc_ref[...] = product

    @pl.when(pair > 0)
    def _():
        acc_ref[...] += product

    @pl.when(pair == pl.num_programs(1) - 1)
    def _():
        out_ref[...] = acc_ref[...].astype(bf16)


def self_kernel(q_ref, k_ref, v_ref, bias_ref, weight_ref, out_ref, log_ref, sum_ref, acc_ref):
    pair = pl.program_id(1)
    block_rows = out_ref.shape[0]
    for part in range(block_rows // HALF):
        rows = slice(part * HALF, (part + 1) * HALF)
        span = slice(part * HALF, (part + 3) * HALF)
        out, logs = attend_rows(
            q_ref[(part + 1) * HALF : (part + 2) * HALF, :],
            k_ref[span, :],
            v_ref[span, :],
            bias_ref[rows, :],
        )
        out_ref[rows, :] = out.astype(bf16)
        put_logs(log_ref, rows, logs, pair)
    add_product(acc_ref, sum_ref, nt(out_ref[...], weight_ref[...]))


def self_specs(block_rows, pairs):
    near = lambda first: pl.BlockSpec((block_rows + 2 * HALF, 128), lambda m, h: (m, first + h))
    return [
        near(0),
        near(pairs),
        near(2 * pairs),
        pl.BlockSpec((block_rows, 3 * HALF), lambda m, h: (m, 0)),
    ]


def self_attention(qkv, bias, weights, column, micro, block_rows):
    rows = micro * block_rows
    local = qkv.shape[1] // 3
    width = weights.shape[0]
    pairs = local // 128
    return pl.pallas_call(
        self_kernel,
        grid=(micro, pairs),
        in_specs=self_specs(block_rows, pairs)
        + [pl.BlockSpec((width, 128), lambda m, h: (0, column + h))],
        out_specs=[
            pl.BlockSpec((block_rows, 128), lambda m, h: (m, h)),
            pl.BlockSpec((block_rows, 128), lambda m, h: (m, 0)),
            pl.BlockSpec((block_rows, width), lambda m, h: (m, 0)),
        ],
        out_shape=[
            jax.ShapeDtypeStruct((rows, local), bf16),
            jax.ShapeDtypeStruct((rows, 128), f32),
            jax.ShapeDtypeStruct((rows, width), bf16),
        ],
        scratch_shapes=[pltpu.VMEM((block_rows, width), f32)],
        compiler_params=kernel_params(2, 32),
        cost_estimate=pl.CostEstimate(
            flops=rows * 2 * local * (width + 12 * HALF),
            bytes_accessed=20 * rows * local,
            transcendentals=rows * 3 * HALF * 2 * pairs,
        ),
        name="self_attention",
    )(qkv, qkv, qkv, bias, weights)


def self_back_kernel(
    q_ref, k_ref, v_ref, bias_ref, grad_ref, log_ref, own_ref, to_low_ref, to_high_ref
):
    pair = pl.program_id(1)
    parts = grad_ref.shape[0] // HALF
    pieces = [[None] * (parts + 2), [None] * (parts + 2)]
    for part in range(parts):
        rows = slice(part * HALF, (part + 1) * HALF)
        span = slice(part * HALF, (part + 3) * HALF)
        query_grad, key_grad, value_grad = attend_rows_back(
            q_ref[(part + 1) * HALF : (part + 2) * HALF, :],
            k_ref[span, :],
            v_ref[span, :],
            bias_ref[rows, :],
            get_logs(log_ref, rows, pair),
            grad_ref[rows, :],
        )
        own_ref[0, rows, :] = query_grad
        for kind, near_grad in enumerate((key_grad, value_grad)):
            for third in range(3):
                piece = near_grad[third * HALF : (third + 1) * HALF]
                held = pieces[kind][part + third]
                pieces[kind][part + third] = piece if held is None else held + piece
    for kind in range(2):
        to_low_ref[kind] = pieces[kind][0].astype(bf16)
        for part in range(parts):
            own_ref[1 + kind, part * HALF : (part + 1) * HALF, :] = pieces[kind][part + 1]
        to_high_ref[kind] = pieces[kind][parts + 1].astype(bf16)


def self_attention_back(qkv, bias, grad, logs, micro, block_rows):
    rows, local = grad.shape
    pairs = local // 128
    edge = pl.BlockSpec((2, None, HALF, 128), lambda m, h: (0, m, 0, h))
    return pl.pallas_call(
        self_back_kernel,
        grid=(micro, pairs),
        in_specs=self_specs(block_rows, pairs)
        + [
            pl.BlockSpec((block_rows, 128), lambda m, h: (m, h)),
            pl.BlockSpec((block_rows, 128), lambda m, h: (m, 0)),
        ],
        out_specs=[
            pl.BlockSpec((3, block_rows, 128), lambda m, h: (0, m, h)),
            edge,
            edge,
        ],
        out_shape=[
            jax.ShapeDtypeStruct((3, rows, local), f32),
            jax.ShapeDtypeStruct((2, micro, HALF, local), bf16),
            jax.ShapeDtypeStruct((2, micro, HALF, local), bf16),
        ],
        compiler_params=kernel_params(2, 32),
        cost_estimate=pl.CostEstimate(
            flops=20 * rows * 3 * HALF * local,
            bytes_accessed=40 * rows * local,
            transcendentals=rows * 3 * HALF * 2 * pairs,
        ),
        name="self_attention_back",
    )(qkv, qkv, qkv, bias, grad, logs)


def cross_kernel(q_ref, k_ref, v_ref, bias_ref, weight_ref, out_ref, log_ref, sum_ref, acc_ref):
    pair = pl.program_id(1)
    for part in range(q_ref.shape[0] // HALF):
        rows = slice(part * HALF, (part + 1) * HALF)
        out, logs = attend_rows(q_ref[rows, :], k_ref[...], v_ref[...], bias_ref[rows, :])
        out_ref[rows, :] = out.astype(bf16)
        put_logs(log_ref, rows, logs, pair)
    add_product(acc_ref, sum_ref, nt(out_ref[...], weight_ref[...]))


def cross_specs(block_rows, pairs):
    return [
        pl.BlockSpec((block_rows, 128), lambda m, h: (m, h)),
        pl.BlockSpec((2 * TXT, 128), lambda m, h: (m, h)),
        pl.BlockSpec((2 * TXT, 128), lambda m, h: (m, h)),
        pl.BlockSpec((block_rows, 2 * TXT), lambda m, h: (m, 0)),
    ]


def cross_attention(query, keys, values, bias, weights, column, micro, block_rows):
    rows, local = query.shape
    width = weights.shape[0]
    pairs = local // 128
    return pl.pallas_call(
        cross_kernel,
        grid=(micro, pairs),
        in_specs=cross_specs(block_rows, pairs)
        + [pl.BlockSpec((width, 128), lambda m, h: (0, column + h))],
        out_specs=[
            pl.BlockSpec((block_rows, 128), lambda m, h: (m, h)),
            pl.BlockSpec((block_rows, 128), lambda m, h: (m, 0)),
            pl.BlockSpec((block_rows, width), lambda m, h: (m, 0)),
        ],
        out_shape=[
            jax.ShapeDtypeStruct((rows, local), bf16),
            jax.ShapeDtypeStruct((rows, 128), f32),
            jax.ShapeDtypeStruct((rows, width), bf16),
        ],
        scratch_shapes=[pltpu.VMEM((block_rows, width), f32)],
        compiler_params=kernel_params(2, 32),
        cost_estimate=pl.CostEstimate(
            flops=rows * 2 * local * (width + 8 * TXT),
            bytes_accessed=16 * rows * local,
            transcendentals=rows * 2 * TXT * 2 * pairs,
        ),
        name="cross_attention",
    )(query, keys, values, bias, weights)


def cross_back_kernel(
    q_ref, k_ref, v_ref, bias_ref, grad_ref, log_ref, weight_ref,
    dq_ref, dk_ref, dv_ref, sum_ref, acc_ref,
):
    pair = pl.program_id(1)
    key_total = value_total = None
    for part in range(q_ref.shape[0] // HALF):
        rows = slice(part * HALF, (part + 1) * HALF)
        query_grad, key_grad, value_grad = attend_rows_back(
            q_ref[rows, :],
            k_ref[...],
            v_ref[...],
            bias_ref[rows, :],
            get_logs(log_ref, rows, pair),
            grad_ref[rows, :],
        )
        dq_ref[rows, :] = query_grad.astype(bf16)
        key_total = key_grad if part == 0 else key_total + key_grad
        value_total = value_grad if part == 0 else value_total + value_grad
    dk_ref[...] = key_total.astype(bf16)
    dv_ref[...] = value_total.astype(bf16)
    add_product(acc_ref, sum_ref, nt(dq_ref[...], weight_ref[...]))


def cross_attention_back(
    query, keys, values, bias, grad, logs, weights, column, micro, block_rows
):
    rows, local = query.shape
    width = weights.shape[0]
    pairs = local // 128
    text = pl.BlockSpec((2 * TXT, 128), lambda m, h: (m, h))
    return pl.pallas_call(
        cross_back_kernel,
        grid=(micro, pairs),
        in_specs=cross_specs(block_rows, pairs)
        + [
            pl.BlockSpec((block_rows, 128), lambda m, h: (m, h)),
            pl.BlockSpec((block_rows, 128), lambda m, h: (m, 0)),
            pl.BlockSpec((width, 128), lambda m, h: (0, column + h)),
        ],
        out_specs=[
            pl.BlockSpec((block_rows, 128), lambda m, h: (m, h)),
            text,
            text,
            pl.BlockSpec((block_rows, width), lambda m, h: (m, 0)),
        ],
        out_shape=[
            jax.ShapeDtypeStruct((rows, local), bf16),
            jax.ShapeDtypeStruct(keys.shape, bf16),
            jax.ShapeDtypeStruct(keys.shape, bf16),
            jax.ShapeDtypeStruct((rows, width), bf16),
        ],
        scratch_shapes=[pltpu.VMEM((block_rows, width), f32)],
        compiler_params=kernel_params(2, 32),
        cost_estimate=pl.CostEstimate(
            flops=rows * 2 * local * (width + 20 * TXT),
            bytes_accessed=30 * rows * local,
            transcendentals=rows * 2 * TXT * 2 * pairs,
        ),
        name="cross_attention_back",
    )(query, keys, values, bias, grad, logs, weights)


def ffn_kernel(*refs, summed):
    (
        normed_ref, normed_t_ref, cot_ref, cot_t_ref, outer_ref, gate_ref, up_ref,
        g_early_ref, g_up_ref, out_ref, back_ref, out_acc, back_acc,
    ) = refs[:13]
    j = pl.program_id(0)
    step = gate_ref.shape[1]
    if summed:
        full = refs[13]
        me = lax.axis_index("seq")
        digits = seq_digits(me)
        core = digits[0]
        partners = [me + stride * (1 - 2 * digit) for stride, digit in zip(STRIDES, digits)]
        pl.when(j == 0)(lambda: [greet(me, digits), None][1])
        pieces = Pieces(refs[14:], g_up_ref, partners, digits, step)
        count = summed

        def over_core(slot):
            return pieces.over_core(full.at[slot, :, :, :, 1 - core], slot)

        def tick(t):
            @when((t >= 1) & (t - 1 < count))
            def _():
                slot = (t - 1) % SLOTS
                when(t - 1 >= SLOTS)(lambda: pieces.wait_sent(slot))
                over_core(slot).wait()
                pieces.add_core(slot, lambda a, b, c: full[slot, a, b, c, core])

            pieces.later_steps(t, count)

    gate = nn(normed_ref[...], gate_ref[...])
    up = nn(normed_ref[...], up_ref[...])
    grad = nn(cot_ref[...], outer_ref[...])
    if summed:
        tick(j)
    chance = 1.0 / (1.0 + jnp.exp(-gate))
    swish = gate * chance
    active = (swish * up).astype(bf16)
    gate_grad = (grad * up * (chance * (1.0 + gate * (1.0 - chance)))).astype(bf16)
    up_grad = (grad * swish).astype(bf16)
    g_up = nn(normed_t_ref[...], up_grad).astype(bf16)
    if summed:
        slot = j % SLOTS
        full[slot] = g_up.reshape(full.shape[1:])
        over_core(slot).start()
    else:
        g_up_ref[...] = g_up
    g_early_ref[:, :step] = nn(cot_t_ref[...], active).astype(bf16)
    g_early_ref[:, step:] = nn(normed_t_ref[...], gate_grad).astype(bf16)
    out_part = nt(active, outer_ref[...])
    back_part = nt(gate_grad, gate_ref[...]) + nt(up_grad, up_ref[...])

    @pl.when(j == 0)
    def _():
        out_acc[...] = out_part
        back_acc[...] = back_part

    @pl.when(j > 0)
    def _():
        out_acc[...] += out_part
        back_acc[...] += back_part

    @pl.when(j == pl.num_programs(0) - 1)
    def _():
        out_ref[...] = out_acc[...].astype(bf16)
        back_ref[...] = back_acc[...].astype(bf16)
        if summed:
            for t in range(count, count + 4):
                tick(t)
            pieces.finish(count)


FFN_STEP = 256


def feed_forward(normed, normed_t, cotangent, weights, hidden, step=FFN_STEP):
    rows, width = normed.shape
    steps = hidden // step
    seq_count = lax.axis_size("seq")
    share = width // seq_count
    summed = steps if seq_count == 16 and share % 16 == 0 else 0
    whole = lambda shape: pl.BlockSpec(shape, lambda j: (0, 0))
    column = lambda first: pl.BlockSpec((width, step), lambda j: (0, first + j))
    scratch = [pltpu.VMEM((rows, width), f32)] * 2
    if summed:
        scratch += [pltpu.VMEM((SLOTS, 2, 2, 2, 2, share, step), bf16)]
        scratch += Pieces.scratch(share, step)
        up_spec = pl.BlockSpec(memory_space=pl.ANY)
        up_shape = jax.ShapeDtypeStruct((share, hidden), f32)
        params = pltpu.CompilerParams(
            dimension_semantics=("arbitrary",),
            collective_id=3,
            has_side_effects=True,
            vmem_limit_bytes=58 * 1024 * 1024,
        )
    else:
        up_spec = column(0)
        up_shape = jax.ShapeDtypeStruct((width, hidden), bf16)
        params = kernel_params(1, 56)
    outs = pl.pallas_call(
        functools.partial(ffn_kernel, summed=summed),
        grid=(steps,),
        in_specs=[
            whole((rows, width)),
            whole((width, rows)),
            whole((rows, width)),
            whole((width, rows)),
            column(0),
            column(steps),
            column(2 * steps),
        ],
        out_specs=[
            pl.BlockSpec((width, 2 * step), lambda j: (0, j)),
            up_spec,
            whole((rows, width)),
            whole((rows, width)),
        ],
        out_shape=[
            jax.ShapeDtypeStruct((width, 2 * hidden), bf16),
            up_shape,
            jax.ShapeDtypeStruct((rows, width), bf16),
            jax.ShapeDtypeStruct((rows, width), bf16),
        ],
        scratch_shapes=scratch,
        compiler_params=params,
        cost_estimate=pl.CostEstimate(
            flops=18 * rows * width * hidden,
            bytes_accessed=12 * width * hidden,
            transcendentals=rows * hidden,
        ),
        name="feed_forward",
    )(normed, normed_t, cotangent, cotangent.T, weights, weights, weights)
    if summed:
        return outs
    up_total = lax.psum_scatter(outs[1].astype(f32), "seq", scatter_dimension=0, tiled=True)
    return outs[0], up_total, outs[2], outs[3]


def qkv_back_kernel(
    own_ref, after_ref, before_ref, normed_t_ref, weight_ref, table_ref,
    grad_ref, back_ref, acc, *, kind_steps, micro, block_rows,
):
    j = pl.program_id(0)
    kind = j // kind_steps
    edges = (kind > 0).astype(f32)
    turned = kind < 2
    near_rows = block_rows + 2 * HALF

    def own_table(index):
        return jnp.concatenate(
            [
                table_ref[index, m * near_rows + HALF : (m + 1) * near_rows - HALF]
                for m in range(micro)
            ],
            axis=0,
        )

    own_factor = jnp.where(turned, own_table(0), 1.0)
    below_factor = jnp.where(turned, -own_table(1), 0.0)
    above_factor = jnp.where(turned, -own_table(2), 0.0)
    total = []
    for m in range(micro):
        first = m * block_rows
        total.append(own_ref[first : first + HALF] + edges * after_ref[m].astype(f32))
        if block_rows > 2 * HALF:
            total.append(own_ref[first + HALF : first + block_rows - HALF])
        total.append(
            own_ref[first + block_rows - HALF : first + block_rows]
            + edges * before_ref[m].astype(f32)
        )
    total = jnp.concatenate(total, axis=0)
    grad = jnp.concatenate(
        [
            turn(total[:, i : i + 128], own_factor, below_factor, above_factor)
            for i in range(0, total.shape[1], 128)
        ],
        axis=1,
    ).astype(bf16)
    grad_ref[...] = nn(normed_t_ref[...], grad).astype(bf16)
    part = nt(grad, weight_ref[...])

    @pl.when(j == 0)
    def _():
        acc[...] = part

    @pl.when(j > 0)
    def _():
        acc[...] += part

    @pl.when(j == pl.num_programs(0) - 1)
    def _():
        back_ref[...] = acc[...].astype(bf16)


def qkv_back(own, after, before, normed_t, weights, table, micro, block_rows, step=256):
    _, rows, local = own.shape
    width = normed_t.shape[0]
    kind_steps = local // step
    edge = pl.BlockSpec(
        (None, micro, HALF, step),
        lambda j: (jnp.maximum(j // kind_steps - 1, 0), 0, 0, j % kind_steps),
    )
    return pl.pallas_call(
        functools.partial(
            qkv_back_kernel, kind_steps=kind_steps, micro=micro, block_rows=block_rows
        ),
        grid=(3 * kind_steps,),
        in_specs=[
            pl.BlockSpec((None, rows, step), lambda j: (j // kind_steps, 0, j % kind_steps)),
            edge,
            edge,
            pl.BlockSpec((width, rows), lambda j: (0, 0)),
            pl.BlockSpec((width, step), lambda j: (0, j)),
            pl.BlockSpec(table.shape, lambda j: (0, 0, 0)),
        ],
        out_specs=[
            pl.BlockSpec((width, step), lambda j: (0, j)),
            pl.BlockSpec((rows, width), lambda j: (0, 0)),
        ],
        out_shape=[
            jax.ShapeDtypeStruct((width, 3 * local), bf16),
            jax.ShapeDtypeStruct((rows, width), bf16),
        ],
        scratch_shapes=[pltpu.VMEM((rows, width), f32)],
        compiler_params=kernel_params(1, 40),
        cost_estimate=pl.CostEstimate(
            flops=12 * rows * width * local,
            bytes_accessed=12 * width * local + 12 * rows * local,
            transcendentals=0,
        ),
        name="qkv_back",
    )(own, after, before, normed_t, weights, table)


def time_features(steps_row):
    half_width = TEMB // 2
    ladder = jnp.exp(-math.log(10000.0) * jnp.arange(half_width, dtype=f32) / half_width)
    angles = steps_row.astype(f32)[:, None] * ladder[None, :]
    return jnp.concatenate([jnp.cos(angles), jnp.sin(angles)], axis=-1)


def on_device(
    latents,
    context,
    lengths,
    text_len,
    timesteps,
    self_qkv,
    self_out,
    cross_query,
    cross_kv,
    cross_out,
    ffn_in,
    ffn_out,
    mod_weight,
    mod_bias,
    out_grad,
):
    micro, block_rows, model_width = latents.shape
    seq_count = lax.axis_size("seq")
    me = lax.axis_index("seq")
    frame_count = block_rows * seq_count
    item_count = lengths.shape[1]
    local = self_qkv.shape[2]
    hidden = ffn_in.shape[2]
    rows = micro * block_rows
    text_width = context.shape[2]

    attn_share = jnp.concatenate(
        [
            self_qkv[0],
            self_qkv[1],
            self_qkv[2],
            self_out.T,
            cross_query,
            cross_out.T,
            jnp.concatenate([cross_kv[0], cross_kv[1]], axis=0),
        ],
        axis=1,
    )
    ffn_share = jnp.concatenate([ffn_out.T, ffn_in[0], ffn_in[1]], axis=1)
    features = time_features(timesteps.reshape(-1))
    own_features = lax.dynamic_slice_in_dim(
        features, me * mod_weight.shape[0], mod_weight.shape[0], 1
    )
    bias_share = mod_bias.shape[1]
    bias_wide = lax.dynamic_update_slice_in_dim(
        jnp.zeros((6, model_width), f32), mod_bias.astype(f32), me * bias_share, 1
    )
    mod_part = jnp.dot(
        own_features, mod_weight.astype(f32).reshape(mod_weight.shape[0], -1), precision=highest
    ) + bias_wide.reshape(1, -1)
    (
        attn_all,
        normed_near,
        normed_one_t,
        two,
        later,
        near_table,
        self_bias,
        cross_bias,
    ) = gather_and_prepare(attn_share, mod_part, latents, lengths, text_len)
    ffn_share, attn_all = lax.optimization_barrier((ffn_share, attn_all))
    ffn_all = lax.all_gather(ffn_share, "seq", axis=0, tiled=True)
    pair_w = attn_all[:, 6 * local :].reshape(seq_count, 2, text_width // seq_count, local)
    key_w = pair_w[:, 0].reshape(text_width, local)
    value_w = pair_w[:, 1].reshape(text_width, local)

    first_frame = me * block_rows
    first_item = jnp.sum((jnp.cumsum(lengths, axis=1) <= first_frame).astype(jnp.int32), axis=1)
    base_item = jnp.minimum(first_item, item_count - 2)
    catalog = jnp.arange(item_count, dtype=jnp.int32)

    ahead = [(i, i + 1) for i in range(seq_count - 1)]
    behind = [(i + 1, i) for i in range(seq_count - 1)]
    latent = latents.reshape(rows, model_width)
    cotangent = out_grad.reshape(rows, model_width)
    near_context = jnp.concatenate(
        [
            lax.dynamic_slice_in_dim(context[m], base_item[m] * TXT, 2 * TXT, 0)
            for m in range(micro)
        ]
    )
    column = local // 128

    qkv = project(normed_near, attn_all, near_table, local)
    mixed_one, logs_one, part_one = self_attention(
        qkv, self_bias, attn_all, 3 * column, micro, block_rows
    )
    got_one = swap(part_one)
    text_keys = nn(near_context, key_w).astype(bf16)
    text_values = nn(near_context, value_w).astype(bf16)
    hidden_one, _, normed_two_t, query_two = norm_forward(
        latent, part_one, got_one, two, later, 2, micro, attn_all, 4, local
    )
    mixed_two, logs_two, part_two = cross_attention(
        query_two, text_keys, text_values, cross_bias, attn_all, 5 * column, micro, block_rows
    )
    got_two = swap(part_two)
    hidden_two, normed_three, normed_three_t = norm_forward(
        hidden_one, part_two, got_two, two, later, 4, micro
    )
    g_early, up_total, out_part, back_three = feed_forward(
        normed_three, normed_three_t, cotangent, ffn_all, hidden
    )

    got_three = swap(back_three)
    early = early_sum(g_early).reshape(-1, hidden // FFN_STEP, 2, FFN_STEP)
    outer_total = early[:, :, 0].reshape(-1, hidden)
    gate_total = early[:, :, 1].reshape(-1, hidden)
    hidden_two_grad, pieces_three, two_low_t, mixed_two_grad = norm_back(
        cotangent, back_three, got_three, hidden_two, two, later, 4, micro, attn_all, 5, local
    )
    out_part, hidden_two_grad = lax.optimization_barrier((out_part, hidden_two_grad))
    out_got = swap(out_part)
    query_two_low, text_key_low, text_value_low, back_two = cross_attention_back(
        query_two, text_keys, text_values, cross_bias, mixed_two_grad, logs_two,
        attn_all, 4 * column, micro, block_rows,
    )
    got_back_two = swap(back_two)
    share = text_width // seq_count
    pair_grad = jnp.concatenate(
        [
            tn(near_context, text_key_low).astype(bf16).reshape(seq_count, share, local),
            tn(near_context, text_value_low).astype(bf16).reshape(seq_count, share, local),
        ],
        axis=1,
    ).reshape(2 * text_width, local)
    g_cross_out = nn(two_low_t, mixed_two).astype(bf16)
    g_cross_query = nn(normed_two_t, query_two_low).astype(bf16)
    hidden_one_grad, pieces_two, one_low_t, mixed_one_grad = norm_back(
        hidden_two_grad, back_two, got_back_two, hidden_one, two, later, 2, micro,
        attn_all, 3, local,
    )
    own_grads, to_low, to_high = self_attention_back(
        qkv, self_bias, mixed_one_grad, logs_one, micro, block_rows
    )
    from_high = lax.ppermute(to_low, "seq", behind)
    from_low = lax.ppermute(to_high, "seq", ahead)
    g_self_out = nn(one_low_t, mixed_one).astype(bf16)
    g_qkv, back_one = qkv_back(
        own_grads, from_low, from_high, normed_one_t, attn_all, near_table, micro, block_rows
    )
    got_back_one = swap(back_one)
    grad_cross_out, grad_cross_query, grad_cross_kv, grad_self_out = scatter_sums(
        [g_cross_out, g_cross_query, pair_grad, g_self_out], 0
    )
    block_out = (hidden_two + (out_part.astype(f32) + out_got.astype(f32))).astype(bf16)
    got_back_one, grad_self_out = lax.optimization_barrier((got_back_one, grad_self_out))
    latent_grad, pieces_one = norm_back(
        hidden_one_grad, back_one, got_back_one, latent, two, later, 0, micro
    )

    pieces = jnp.concatenate([pieces_one, pieces_two, pieces_three], axis=2)
    spots = (base_item[:, None] + jnp.arange(2)[None, :])[:, :, None] == catalog[None, None, :]
    item_grad = jnp.concatenate(
        [
            jnp.sum(
                jnp.where(spots[m][:, :, None, None], pieces[m][:, None], 0.0), axis=0
            )
            for m in range(micro)
        ]
    ).reshape(micro * item_count, 6 * model_width)
    qkv_total, item_total = scatter_sums([g_qkv], 2, item_grad)
    mod_grad = jnp.dot(own_features.T, item_total, precision=highest).reshape(mod_weight.shape)
    bias_grad = lax.dynamic_slice_in_dim(
        jnp.sum(item_total, axis=0).reshape(6, model_width), me * bias_share, bias_share, 1
    )

    grad_qkv = jnp.stack([qkv_total[:, i * local : (i + 1) * local] for i in range(3)])
    return (
        block_out.reshape(latents.shape),
        latent_grad.reshape(latents.shape),
        grad_qkv,
        grad_self_out.T,
        grad_cross_query,
        grad_cross_kv.reshape(2, share, local),
        grad_cross_out.T,
        jnp.stack([gate_total, up_total]),
        outer_total.T,
        mod_grad,
        bias_grad,
    )


def solution(mesh):
    return jax.shard_map(
        on_device,
        mesh=mesh,
        in_specs=(
            P(None, "seq", None),
            P(),
            P(),
            P(),
            P(),
            P(None, "seq", "tensor"),
            P("tensor", "seq"),
            P("seq", "tensor"),
            P(None, "seq", "tensor"),
            P("tensor", "seq"),
            P(None, "seq", "tensor"),
            P("tensor", "seq"),
            P("seq", None, None),
            P(None, "seq"),
            P(None, "seq", None),
        ),
        out_specs=(
            P(None, "seq", None),
            P(None, "seq", None),
            P(None, "seq", "tensor"),
            P("tensor", "seq"),
            P("seq", "tensor"),
            P(None, "seq", "tensor"),
            P("tensor", "seq"),
            P(None, "seq", "tensor"),
            P("tensor", "seq"),
            P("seq", None, None),
            P(None, "seq"),
        ),
        check_vma=False,
    )
```

```python
import functools
import math

import jax
import jax.numpy as jnp
import numpy as np
from jax import lax
from jax.experimental import pallas as pl
from jax.experimental.pallas import tpu as pltpu
from jax.sharding import PartitionSpec as P

HD = 64
TXT = 128
TEMB = 256
HALF = 128


norm_eps = 1e-05
highest = lax.Precision.HIGHEST
f32 = jnp.float32
bf16 = jnp.bfloat16


def dot(a, b, dims):
    return lax.dot_general(a, b, ((dims[0], dims[1]), ((), ())), preferred_element_type=f32)


def nn(a, b):
    return dot(a, b, ((1,), (0,)))


def nt(a, b):
    return dot(a, b, ((1,), (1,)))


def tn(a, b):
    return dot(a, b, ((0,), (0,)))


def halves(count):
    stride = 1
    strides = []
    while stride < count:
        strides.append(stride)
        stride *= 2
    return strides


def flip(block, stride):
    count = lax.axis_size("seq")
    return lax.ppermute(block, "seq", [(i, i ^ stride) for i in range(count)])


def swap(part):
    count = lax.axis_size("tensor")
    return lax.ppermute(part, "tensor", [(i, (i + 1) % count) for i in range(count)])


def seq_sum(part):
    for stride in halves(lax.axis_size("seq")):
        part = part + flip(part, stride)
    return part


def kernel_params(grid_rank, mib):
    return pltpu.CompilerParams(
        dimension_semantics=("arbitrary",) * grid_rank, vmem_limit_bytes=mib * 1024 * 1024
    )


STRIDES = (1, 2, 4, 8)


def seq_digits(me):
    return [(me // stride) % 2 for stride in STRIDES]


def greet(me, digits, others=(), mine=None):
    partners = [me + stride * (1 - 2 * digit) for stride, digit in zip(STRIDES, digits)]
    barrier = pltpu.get_barrier_semaphore()

    def tell(**target):
        pl.semaphore_signal(barrier, inc=1, device_id=target, device_id_type=pl.DeviceIdType.MESH)

    expected = len(partners)
    for partner in partners:
        tell(seq=partner)
    if mine is not None:
        tell(tensor=1 - mine)
        expected += 1
    for there, target in others:
        pl.when(there)(functools.partial(tell, seq=target))
        expected = expected + there.astype(jnp.int32)
    pl.semaphore_wait(barrier, expected)
    return partners


def send_to(partner, source, target, send_sem, recv_sem):
    return pltpu.make_async_remote_copy(
        src_ref=source,
        dst_ref=target,
        send_sem=send_sem,
        recv_sem=recv_sem,
        device_id={"seq": partner},
        device_id_type=pl.DeviceIdType.MESH,
    )


def greet_all(me, mine, digits, others=()):
    return greet(me, digits, others, mine)


def to_tensor(mine, source, target, send_sem, recv_sem):
    return pltpu.make_async_remote_copy(
        src_ref=source,
        dst_ref=target,
        send_sem=send_sem,
        recv_sem=recv_sem,
        device_id={"tensor": 1 - mine},
        device_id_type=pl.DeviceIdType.MESH,
    )


SMALL_STEPS = 6


def small_sum(partners, mine, core, fill, prep, held, got, total, finish, send_sem, recv_sem):
    own = 2 * mine + core
    half = pl.ds(2 * mine, 2)

    def exchange(k):
        sems = send_sem.at[k], recv_sem.at[k]
        if k == 0:
            return send_to(partners[0], prep.at[2 * mine + 1 - core], got.at[0], *sems)
        if k < 4:
            return send_to(partners[k], held.at[k], got.at[k], *sems)
        if k == 4:
            return send_to(partners[0], total.at[own], total.at[own], *sems)
        return to_tensor(mine, total.at[half], total.at[half], *sems)

    def step(k):
        if k == 0:
            fill(prep)
        else:
            exchange(k - 1).wait()
        if k == 1:
            held[1] = prep[own] + got[0]
        elif 1 < k < 4:
            held[k] = held[k - 1] + got[k - 1]
        elif k == 4:
            total[own] = held[3] + got[3]
        elif k == SMALL_STEPS:
            finish(total)
        if k < SMALL_STEPS:
            exchange(k).start()

    return step


def small_scratch(shape):
    quarter = (4, shape[0], shape[1] // 4)
    return [pltpu.VMEM(quarter, f32)] * 4 + [pltpu.SemaphoreType.DMA((SMALL_STEPS,))] * 2


def lane_ladder():
    quarter = HD // 4
    return np.exp(-math.log(10000.0) * (np.arange(128) % quarter) / quarter).astype(np.float32)


def prepare(first, frame_count, lengths, text_len, block_rows):
    items = len(lengths)
    ends = [lengths[0]]
    for length in lengths[1:]:
        ends.append(ends[-1] + length)

    def item_of(place):
        return sum((end <= place).astype(jnp.int32) for end in ends)

    def pick(ids, values):
        return sum(jnp.where(ids == k, value, 0) for k, value in enumerate(values))

    near_rows = block_rows + 2 * HALF
    place = first - HALF + lax.broadcasted_iota(jnp.int32, (near_rows, 1), 0)
    ids = item_of(place)
    offset = place - pick(ids, [end - length for end, length in zip(ends, lengths)])
    base = jnp.minimum(item_of(first), items - 2)
    own_ids = ids[HALF : HALF + block_rows]
    self_bias = []
    for part in range(block_rows // HALF):
        row = lax.broadcasted_iota(jnp.int32, (HALF, 1), 0)
        key = lax.broadcasted_iota(jnp.int32, (1, 3 * HALF), 1) - HALF
        key_place = first + part * HALF + key
        inside = (key_place >= 0) & (key_place < frame_count)
        key_ids = jnp.where(inside, item_of(key_place), -1)
        near_enough = jnp.abs(row - key) <= HALF
        same = own_ids[part * HALF : (part + 1) * HALF] == key_ids
        self_bias.append(jnp.where(near_enough & same, 0.0, -1e30))
    slot = lax.broadcasted_iota(jnp.int32, (1, 2 * TXT), 1)
    key_item = jnp.where(slot < TXT, base, base + 1)
    used = jnp.where(slot < TXT, slot, slot - TXT) < pick(key_item, text_len)
    key_item = jnp.where(used, key_item, -1)
    cross_bias = jnp.where(own_ids == key_item, 0.0, -1e30)
    later = (ids != base).astype(f32)
    return base, offset, later, self_bias, cross_bias


def lane_tables(offset, ladder):
    quarter = HD // 4
    angles = offset.astype(f32) * ladder
    lane = lax.broadcasted_iota(jnp.int32, angles.shape, 1) % HD
    cosine = jnp.cos(angles)
    sine = jnp.sin(angles)
    return (
        jnp.where(lane < 2 * quarter, cosine, 1.0),
        jnp.where((lane >= quarter) & (lane < 2 * quarter), sine, 0.0),
        jnp.where(lane < quarter, -sine, 0.0),
    )


def gather_kernel(
    share_ref, part_ref, latent_ref, lengths_ref, text_ref, ladder_ref,
    out_ref, near_normed_ref, normed_t_ref, two_ref, later_ref, table_ref, self_ref, cross_ref,
    near_ref, prep, held, got, total_ref, small_send, small_recv, copy_sem, send_sem, recv_sem,
    near_sem, halo_send, halo_recv, *, pieces, step, y_first, seq_count,
):
    micro, block_rows, width = latent_ref.shape
    items = lengths_ref.shape[1]
    near_rows = block_rows + 2 * HALF
    me = lax.axis_index("seq")
    digits = seq_digits(me)
    core, y, z_lo, z_hi = digits
    first = me * block_rows
    has_low = me > 0
    has_high = me < seq_count - 1
    mine = lax.axis_index("tensor")
    partners = greet_all(me, mine, digits, ((has_low, me - 1), (has_high, me + 1)))

    def fill(target):
        span = target.shape[2]
        for index in range(4):
            target[index] = part_ref[:, index * span : (index + 1) * span]

    small = small_sum(
        partners, mine, core, fill, prep, held, got, total_ref, lambda total: None,
        small_send, small_recv,
    )

    def to_low():
        return send_to(
            me - 1,
            latent_ref.at[:, :HALF],
            near_ref.at[:, near_rows - HALF :],
            halo_send.at[0],
            halo_recv.at[0],
        )

    def to_high():
        return send_to(
            me + 1,
            latent_ref.at[:, block_rows - HALF :],
            near_ref.at[:, :HALF],
            halo_send.at[1],
            halo_recv.at[1],
        )

    def load_own():
        return pltpu.make_async_copy(
            latent_ref, near_ref.at[:, HALF : near_rows - HALF], near_sem
        )

    def piece(p):
        return pl.ds(p * step, step)

    def exchange(p, stage):
        cols = piece(p)
        if p in y_first:
            axis = (1, 3, 2, 0)[stage]
            spots = ((z_hi, z_lo, y, core), (z_hi, z_lo, None, core), (None, z_lo, None, core), None)
        else:
            axis = (3, 2, 1, 0)[stage]
            spots = ((z_hi, z_lo, y, core), (None, z_lo, y, core), (None, None, y, core), None)
        spot = spots[stage] or (None, None, None, core)
        index = tuple(slice(None) if digit is None else digit for digit in spot)
        block = out_ref.at[index + (slice(None), cols)]
        source = share_ref.at[:, cols] if stage == 0 else block
        return send_to(partners[axis], source, block, send_sem.at[stage, p], recv_sem.at[stage, p])

    def own(p):
        return pltpu.make_async_copy(
            share_ref.at[:, piece(p)],
            out_ref.at[z_hi, z_lo, y, core, :, piece(p)],
            copy_sem.at[p],
        )

    def masks(m):
        base, offset, later, self_bias, cross_bias = prepare(
            first,
            seq_count * block_rows,
            [lengths_ref[m, k] for k in range(items)],
            [text_ref[m, k] for k in range(items)],
            block_rows,
        )
        rows = slice(m * block_rows, (m + 1) * block_rows)
        later_ref[rows, :] = later[HALF : HALF + block_rows]
        for part, bias in enumerate(self_bias):
            start = m * block_rows + part * HALF
            self_ref[start : start + HALF, :] = bias
        cross_ref[rows, :] = cross_bias
        state[m] = base, offset, later

    def tables(m, start):
        offset = state[m][1][start : start + HALF]
        target = m * near_rows + start
        for index, values in enumerate(lane_tables(offset, ladder_ref[...])):
            table_ref[index, target : target + HALF, :] = values

    def modulation(m, base):
        span = total_ref.shape[2]
        for which in range(2):
            for index in range(4):
                two_ref[m, which : which + 1, index * span : (index + 1) * span] = sum(
                    jnp.where(
                        base + which == k,
                        total_ref[index, m * items + k : m * items + k + 1],
                        0.0,
                    )
                    for k in range(items)
                )

    def norm(m, start):
        shift = [two_ref[m, which : which + 1, :width] for which in range(2)]
        factor = [two_ref[m, which : which + 1, width : 2 * width] for which in range(2)]
        tile = near_ref[m, start : start + HALF].astype(f32)
        chosen = state[m][2][start : start + HALF] > 0.5
        xhat, _ = spread_rows(tile)
        normed = (
            xhat * (1.0 + jnp.where(chosen, factor[1], factor[0]))
            + jnp.where(chosen, shift[1], shift[0])
        ).astype(bf16)
        target = m * near_rows + start
        near_normed_ref[target : target + HALF, :] = normed
        if HALF <= start < HALF + block_rows:
            target = m * block_rows + start - HALF
            normed_t_ref[:, target : target + HALF] = normed.T

    beside = {}
    state = {}
    gap = 3

    def add(t, work):
        beside.setdefault(t, []).append(work)

    def finish_near():
        load_own().wait()
        pl.when(has_low)(lambda: to_high().wait_recv())
        pl.when(has_high)(lambda: to_low().wait_recv())

    tick = 1
    for m in range(micro):
        add(tick, functools.partial(masks, m))
        for start in range(0, near_rows, HALF):
            tick += 1
            add(tick, functools.partial(tables, m, start))
        tick += 1
    for k in range(1, SMALL_STEPS + 1):
        add(gap * k, functools.partial(small, k))
    tick = gap * SMALL_STEPS
    add(tick, finish_near)
    for m in range(micro):
        tick += 1
        add(tick, lambda m=m: modulation(m, state[m][0]))
        for start in range(0, near_rows, HALF):
            add(tick, functools.partial(norm, m, start))
            tick += 1
    last_tick = tick

    small(0)
    load_own().start()
    pl.when(has_low)(lambda: to_low().start())
    pl.when(has_high)(lambda: to_high().start())

    @pl.when(jnp.logical_not(has_low))
    def _():
        near_ref[:, :HALF] = jnp.zeros((micro, HALF, width), near_ref.dtype)

    @pl.when(jnp.logical_not(has_high))
    def _():
        near_ref[:, near_rows - HALF :] = jnp.zeros((micro, HALF, width), near_ref.dtype)

    lags = (0, 3, 6, 10, 12)
    for t in range(max(pieces + lags[-1], last_tick + 1)):
        if t < pieces:
            exchange(t, 0).start()
            own(t).start()
        for stage in (1, 2, 3):
            p = t - lags[stage]
            if 0 <= p < pieces:
                if stage == 1:
                    own(p).wait()
                exchange(p, stage - 1).wait_recv()
                exchange(p, stage).start()
        if 0 <= t - lags[4] < pieces:
            exchange(t - lags[4], 3).wait_recv()
        for work in beside.get(t, ()):
            work()
    for p in range(pieces):
        for stage in range(4):
            exchange(p, stage).wait_send()
    pl.when(has_low)(lambda: to_low().wait_send())
    pl.when(has_high)(lambda: to_high().wait_send())


def gather_and_prepare(share, part, latents, lengths, text_len, step=256):
    count = lax.axis_size("seq")
    me = lax.axis_index("seq")
    rows, width = share.shape
    micro, block_rows, model_width = latents.shape
    items = lengths.shape[1]
    near_rows = block_rows + 2 * HALF
    own_rows = micro * block_rows
    ladder = jnp.asarray(lane_ladder()).reshape(1, 128)
    if count != 16 or rows % 16 or width % step or lax.axis_size("tensor") != 2:
        ahead = [(i, i + 1) for i in range(count - 1)]
        behind = [(i + 1, i) for i in range(count - 1)]
        low_rows = lax.ppermute(latents[:, block_rows - HALF :], "seq", ahead)
        high_rows = lax.ppermute(latents[:, :HALF], "seq", behind)
        near_latent = jnp.concatenate([low_rows, latents, high_rows], axis=1)
        total = seq_sum(part).reshape(micro, items, 6 * model_width)
        parts = []
        for m in range(micro):
            base, offset, later, self_bias, cross_bias = prepare(
                me * block_rows,
                count * block_rows,
                [lengths[m, k] for k in range(items)],
                [text_len[m, k] for k in range(items)],
                block_rows,
            )
            two = lax.dynamic_slice_in_dim(total[m], base, 2, 0)
            xhat, _ = spread_rows(near_latent[m].astype(f32))
            shift, factor = [
                jnp.where(later > 0.5, two[1], two[0])[:, i * model_width : (i + 1) * model_width]
                for i in range(2)
            ]
            normed = (xhat * (1.0 + factor) + shift).astype(bf16)
            parts.append(
                (
                    normed,
                    normed[HALF : HALF + block_rows].T,
                    two[None],
                    later[HALF : HALF + block_rows],
                    jnp.stack(lane_tables(offset, ladder)),
                    jnp.concatenate(self_bias, axis=0),
                    cross_bias,
                )
            )
        axes = (0, 1, 0, 0, 1, 0, 0)
        joined = [jnp.concatenate(group, axis=axis) for group, axis in zip(zip(*parts), axes)]
        return [lax.all_gather(share, "seq", axis=0, tiled=True)] + joined
    pieces = width // step
    any_space = pl.BlockSpec(memory_space=pl.ANY)
    vmem = pl.BlockSpec(memory_space=pltpu.VMEM)
    smem = pl.BlockSpec(memory_space=pltpu.SMEM)
    outs = pl.pallas_call(
        functools.partial(
            gather_kernel,
            pieces=pieces,
            step=step,
            y_first=tuple(range(pieces // 6, pieces, pieces // 3)),
            seq_count=count,
        ),
        out_shape=[
            jax.ShapeDtypeStruct((2, 2, 2, 2, rows, width), share.dtype),
            jax.ShapeDtypeStruct((micro * near_rows, model_width), bf16),
            jax.ShapeDtypeStruct((model_width, own_rows), bf16),
            jax.ShapeDtypeStruct((micro, 2, 6 * model_width), f32),
            jax.ShapeDtypeStruct((own_rows, 1), f32),
            jax.ShapeDtypeStruct((3, micro * near_rows, 128), f32),
            jax.ShapeDtypeStruct((own_rows, 3 * HALF), f32),
            jax.ShapeDtypeStruct((own_rows, 2 * TXT), f32),
        ],
        in_specs=[any_space, vmem, any_space, smem, smem, vmem],
        out_specs=[any_space] + [vmem] * 7,
        scratch_shapes=[
            pltpu.VMEM((micro, near_rows, model_width), bf16),
        ]
        + small_scratch(part.shape)
        + [
            pltpu.SemaphoreType.DMA((pieces,)),
            pltpu.SemaphoreType.DMA((4, pieces)),
            pltpu.SemaphoreType.DMA((4, pieces)),
            pltpu.SemaphoreType.DMA,
            pltpu.SemaphoreType.DMA((2,)),
            pltpu.SemaphoreType.DMA((2,)),
        ],
        compiler_params=pltpu.CompilerParams(
            collective_id=1, has_side_effects=True, vmem_limit_bytes=48 * 1024 * 1024
        ),
        cost_estimate=pl.CostEstimate(
            flops=0, bytes_accessed=20 * count * rows * width, transcendentals=0
        ),
        name="gather_and_prepare",
    )(share, part, latents, lengths, text_len, ladder)
    return [outs[0].reshape(count * rows, width)] + list(outs[1:])


SLOTS = 6


def when(condition):
    if isinstance(condition, bool):
        return (lambda work: work()) if condition else (lambda work: None)
    return pl.when(condition)


class Pieces:
    def __init__(self, refs, out_ref, partners, digits, step, lag=2):
        (
            self.own, self.got0, self.got1, self.got2, self.got3, self.staged,
            self.out_sem, self.send_sem, self.recv_sem,
        ) = refs
        self.out_ref = out_ref
        self.partners = partners
        self.digits = digits
        self.step = step
        self.lag = lag

    @staticmethod
    def scratch(rows, step):
        return [
            pltpu.VMEM((SLOTS, 2, 2, 2, rows, step), bf16),
            pltpu.VMEM((SLOTS, 2, 2, 2, rows, step), bf16),
            pltpu.VMEM((SLOTS, 2, 2, rows, step), bf16),
            pltpu.VMEM((SLOTS, 2, rows, step), bf16),
            pltpu.VMEM((SLOTS, rows, step), bf16),
            pltpu.VMEM((SLOTS, rows, step), f32),
            pltpu.SemaphoreType.DMA((SLOTS,)),
            pltpu.SemaphoreType.DMA((4, SLOTS)),
            pltpu.SemaphoreType.DMA((4, SLOTS)),
        ]

    def exchange(self, stage, source, target, slot):
        return send_to(
            self.partners[stage],
            source,
            target,
            self.send_sem.at[stage, slot],
            self.recv_sem.at[stage, slot],
        )

    def over_core(self, source, slot):
        return self.exchange(0, source, self.got0.at[slot], slot)

    PATHS = ((2, 1, 0),)

    def spot(self, path, stage, other):
        axes = (self.digits[3], self.digits[2], self.digits[1])
        index = [slice(None)] * 3
        for axis in path[: stage - 1]:
            index[axis] = axes[axis]
        axis = path[stage - 1]
        index[axis] = 1 - axes[axis] if other else axes[axis]
        return tuple(index)

    def hop(self, path, stage, slot):
        partner = (3, 2, 1)[path[stage - 1]]
        target = (self.got1, self.got2, self.got3)[stage - 1].at[slot]
        source = self.own.at[(slot,) + self.spot(path, stage, True)]
        return send_to(
            self.partners[partner],
            source,
            target,
            self.send_sem.at[stage, slot],
            self.recv_sem.at[stage, slot],
        )

    def by_path(self, item, work):
        work(self.PATHS[0])

    def add_hop(self, path, stage, slot):
        got = (self.got1, self.got2, self.got3)[stage - 1]
        index = self.spot(path, stage, False)
        free = [k for k in range(3) if isinstance(index[k], slice)]
        for count in range(2 ** len(free)):
            bits = [(count >> k) & 1 for k in range(len(free))]
            full = list(index)
            for k, bit in zip(free, bits):
                full[k] = bit
            at = (slot,) + tuple(full)
            total = self.own[at].astype(f32) + got[(slot,) + tuple(bits)].astype(f32)
            if stage < 3:
                self.own[at] = total.astype(bf16)
            else:
                self.staged[slot] = total

    def store(self, item, slot):
        columns = pl.ds(pl.multiple_of(item * self.step, self.step), self.step)
        return pltpu.make_async_copy(
            self.staged.at[slot], self.out_ref.at[:, columns], self.out_sem.at[slot]
        )

    def wait_sent(self, slot):
        for stage in (1, 2, 3):
            self.hop(self.PATHS[0], stage, slot).wait_send()

    def add_core(self, item, slot, left):
        for i in range(2):
            for j in range(2):
                for k in range(2):
                    total = left(i, j, k).astype(f32) + self.got0[slot, i, j, k].astype(f32)
                    self.own[slot, i, j, k] = total.astype(bf16)
        self.by_path(item, lambda path: self.hop(path, 1, slot).start())

    def later_steps(self, t, count):
        lag = self.lag

        @when((t >= lag) & (t - lag < count))
        def _():
            item = t - lag
            slot = item % SLOTS
            self.hop(self.PATHS[0], 1, slot).wait_recv()

            def work(path):
                self.add_hop(path, 1, slot)
                self.hop(path, 2, slot).start()

            self.by_path(item, work)

        @when((t >= lag + 1) & (t - lag - 1 < count))
        def _():
            item = t - lag - 1
            slot = item % SLOTS
            self.hop(self.PATHS[0], 2, slot).wait_recv()

            def work(path):
                self.add_hop(path, 2, slot)
                self.hop(path, 3, slot).start()

            self.by_path(item, work)

        @when((t >= lag + 2) & (t - lag - 2 < count))
        def _():
            item = t - lag - 2
            slot = item % SLOTS
            self.hop(self.PATHS[0], 3, slot).wait_recv()
            when(item >= SLOTS)(lambda: self.store(0, slot).wait())
            self.by_path(item, lambda path: self.add_hop(path, 3, slot))
            self.store(item, slot).start()

    def run(self, sources, spans, own_sem, beside=(), last=0):
        core = self.digits[0]
        step = self.step
        count = sum(width for _, width in spans) // step

        def over_core(source, column, slot):
            return self.over_core(source.at[:, :, :, 1 - core, :, pl.ds(column, step)], slot)

        def load(source, column, slot):
            return pltpu.make_async_copy(
                source.at[:, :, :, core, :, pl.ds(column, step)],
                self.own.at[slot],
                own_sem.at[slot],
            )

        def tick(t, carry):
            @pl.when(t < count)
            def _():
                slot = t % SLOTS
                pl.when(t >= SLOTS)(lambda: self.wait_sent(slot))
                done = 0
                for source, (column, width) in zip(sources, spans):

                    @pl.when((t >= done) & (t < done + width // step))
                    def _(source=source, done=done, column=column):
                        spot = pl.multiple_of(column + (t - done) * step, step)
                        over_core(source, spot, slot).start()
                        load(source, spot, slot).start()

                    done += width // step

            @pl.when((t >= 1) & (t - 1 < count))
            def _():
                slot = (t - 1) % SLOTS
                load(sources[0], 0, slot).wait()
                over_core(sources[0], 0, slot).wait()
                self.add_core(t - 1, slot, lambda i, j, k: self.own[slot, i, j, k])

            self.later_steps(t, count)
            for begin, end, work in beside:
                pl.when((t >= begin) & (t < end))(functools.partial(work, t))
            return carry

        lax.fori_loop(0, max(count + self.lag + 2, last + 1), tick, 0)
        self.finish(count)

    def finish(self, count):
        for back in range(min(SLOTS, count)):
            slot = (count - 1 - back) % SLOTS
            self.store(0, slot).wait()
            self.wait_sent(slot)


PIECE_REFS = 9


def norm_back_tile(grad, upstream, hidden, shift_rows, factor):
    xhat, scale = spread_rows(hidden)
    inner = grad * (1.0 + factor)
    mean_inner = jnp.mean(inner, axis=-1, keepdims=True)
    mean_cross = jnp.mean(inner * xhat, axis=-1, keepdims=True)
    total = upstream + scale * (inner - mean_inner - xhat * mean_cross)
    scaled = grad * xhat
    sums = [
        [
            jnp.sum(jnp.where(chosen, values, 0.0), axis=0, keepdims=True)
            for values in (grad, scaled)
        ]
        for chosen in shift_rows
    ]
    return total, sums


def finish_kernel(*refs, spans, step, micro):
    refs = list(refs)
    sources = [refs.pop(0) for _ in spans]
    (
        own_ref, from_low_ref, from_high_ref, normed_t_ref, weight_ref, table_ref,
        up_ref, latent_ref, two_ref, later_ref, sums_ref, lengths_ref, feature_ref, other_ref,
        out_ref, grad_ref, mod_ref, bias_ref, got_other_ref,
        own_sem, back_ref, got_back, qkv_w_ref, weight_sem, g_qkv_ref, first_sums,
        back_send, back_recv, other_sem,
    ) = refs[:29]
    pieces_refs = refs[29 : 29 + PIECE_REFS]
    prep, held, got, small_total, small_send, small_recv = refs[29 + PIECE_REFS :]
    me = lax.axis_index("seq")
    mine = lax.axis_index("tensor")
    digits = seq_digits(me)
    core = digits[0]
    rows, width = latent_ref.shape
    local = own_ref.shape[2]
    block_rows = rows // micro
    near_rows = block_rows + 2 * HALF
    items = lengths_ref.shape[1]
    load = pltpu.make_async_copy(weight_ref.at[:, : 3 * local], qkv_w_ref, weight_sem)
    load.start()
    partners = greet_all(me, mine, digits)
    pieces = Pieces(pieces_refs, out_ref, partners, digits, step)

    def over_tensor(m):
        span = pl.ds(m * block_rows, block_rows)
        return to_tensor(
            mine, back_ref.at[span], got_back.at[span], back_send.at[m], back_recv.at[m]
        )

    def own_table(index):
        return jnp.concatenate(
            [
                table_ref[index, m * near_rows + HALF : (m + 1) * near_rows - HALF]
                for m in range(micro)
            ],
            axis=0,
        )

    def project_back(kind, column):
        lanes = pl.ds(pl.multiple_of(column, step), step)
        total = own_ref[kind, :, lanes]
        if kind:
            blocks = []
            for m in range(micro):
                first = m * block_rows
                blocks.append(
                    total[first : first + HALF] + from_low_ref[m, kind - 1, :, lanes].astype(f32)
                )
                if block_rows > 2 * HALF:
                    blocks.append(total[first + HALF : first + block_rows - HALF])
                blocks.append(
                    total[first + block_rows - HALF : first + block_rows]
                    + from_high_ref[m, kind - 1, :, lanes].astype(f32)
                )
            total = jnp.concatenate(blocks, axis=0)
        if kind < 2:
            tables = own_table(0), -own_table(1), -own_table(2)
            total = jnp.concatenate(
                [turn(total[:, i : i + 128], *tables) for i in range(0, step, 128)], axis=1
            )
        grad = total.astype(bf16)
        lanes = pl.ds(pl.multiple_of(kind * local + column, step), step)
        g_qkv_ref[:, :, :, :, :, lanes] = (
            nn(normed_t_ref[...], grad).astype(bf16).reshape(g_qkv_ref.shape[:5] + (step,))
        )
        grad_ref[...] += nt(grad, qkv_w_ref[:, lanes])

    def send_back():
        back_ref[...] = grad_ref[...].astype(bf16)
        for m in range(micro):
            over_tensor(m).start()

    def norm_one(m):
        over_tensor(m).wait_recv()

        def emit(span, start, total):
            grad_ref[span, :] = total

        norm_back_unit(
            m, 0, block_rows,
            lambda span: back_ref[span, :].astype(f32) + got_back[span, :].astype(f32),
            up_ref, latent_ref, two_ref, later_ref, first_sums, emit,
        )

    def fill(target):
        span = target.shape[2]
        size = 128 * math.gcd(span // 128, width // 128)
        for m in range(micro):
            ends = [lengths_ref[m, 0]]
            for k in range(1, items):
                ends.append(ends[-1] + lengths_ref[m, k])
            first_item = sum((end <= me * block_rows).astype(jnp.int32) for end in ends)
            base = jnp.minimum(first_item, items - 2)
            for k in range(items):
                row = slice(m * items + k, m * items + k + 1)
                for first in range(0, 6 * width, size):
                    ref, at = (
                        (first_sums, first) if first < 2 * width else (sums_ref, first - 2 * width)
                    )
                    target[first // span, row, first % span : first % span + size] = sum(
                        jnp.where(
                            base + item == k, ref[m, item : item + 1, at : at + size], 0.0
                        )
                        for item in range(2)
                    )

    def modulation_grads(total):
        span = total.shape[2]
        for index in range(4):
            lanes = slice(index * span, (index + 1) * span)
            bias_ref[:, lanes] = jnp.sum(total[index], axis=0, keepdims=True)
            mod_ref[:, lanes] = sum(
                feature_ref[:, i : i + 1] * total[index, i : i + 1] for i in range(micro * items)
            )

    small = small_sum(
        partners, mine, core, fill, prep, held, got, small_total, modulation_grads,
        small_send, small_recv,
    )
    work = []
    spot = 0
    columns = local // step
    work.append((0, 1, lambda t: load.wait()))
    for kind in range(3):
        work.append(
            (spot, spot + columns, lambda t, k=kind, s=spot: project_back(k, (t - s) * step))
        )
        spot += columns
    work.append((spot - 1, spot, lambda t: send_back()))
    spot += 3
    for m in range(micro):
        work.append((spot, spot + 1, lambda t, m=m: norm_one(m)))
        spot += 4 if m < micro - 1 else 1
    for k in range(SMALL_STEPS + 1):
        work.append((spot, spot + 1, lambda t, k=k: small(k)))
        spot += 2 if k < 3 else 1
    grad_ref[...] = jnp.zeros_like(grad_ref)
    over_other = to_tensor(
        mine, other_ref.at[pl.ds(0, block_rows)], got_other_ref, other_sem.at[0], other_sem.at[1]
    )
    over_other.start()
    pieces.run(sources + [g_qkv_ref], spans + ((0, 3 * local),), own_sem, work, spot)
    for m in range(micro):
        over_tensor(m).wait_send()
    over_other.wait()


def finish_stage(
    own, from_low, from_high, normed_t, weights, table, upstream, latent, two, later, sums,
    lengths, features, other, sources, spans, micro, which=0, step=256,
):
    seq_count = lax.axis_size("seq")
    rows, width = latent.shape
    items = lengths.shape[1]
    local = own.shape[2]
    share = width // seq_count
    own_features = features.T
    any_space = pl.BlockSpec(memory_space=pl.ANY)
    vmem = pl.BlockSpec(memory_space=pltpu.VMEM)
    smem = pl.BlockSpec(memory_space=pltpu.SMEM)
    return pl.pallas_call(
        functools.partial(finish_kernel, spans=spans, step=step, micro=micro),
        out_shape=[
            jax.ShapeDtypeStruct((share, sum(span for _, span in spans) + 3 * local), f32),
            jax.ShapeDtypeStruct((rows, width), f32),
            jax.ShapeDtypeStruct((own_features.shape[0], 6 * width), f32),
            jax.ShapeDtypeStruct((1, 6 * width), f32),
            jax.ShapeDtypeStruct((rows // micro, width), bf16),
        ],
        in_specs=[any_space] * len(sources)
        + [vmem] * 4
        + [any_space]
        + [vmem] * 6
        + [smem, vmem, any_space],
        out_specs=[any_space, vmem, vmem, vmem, any_space],
        scratch_shapes=[
            pltpu.SemaphoreType.DMA((SLOTS,)),
            pltpu.VMEM((rows, width), bf16),
            pltpu.VMEM((rows, width), bf16),
            pltpu.VMEM((width, 3 * local), bf16),
            pltpu.SemaphoreType.DMA,
            pltpu.VMEM((2, 2, 2, 2, share, 3 * local), bf16),
            pltpu.VMEM((micro, 2, 2 * width), f32),
            pltpu.SemaphoreType.DMA((micro,)),
            pltpu.SemaphoreType.DMA((micro,)),
            pltpu.SemaphoreType.DMA((2,)),
        ]
        + Pieces.scratch(share, step)
        + small_scratch((micro * items, 6 * width)),
        compiler_params=pltpu.CompilerParams(
            collective_id=which, has_side_effects=True, vmem_limit_bytes=60 * 1024 * 1024
        ),
        cost_estimate=pl.CostEstimate(
            flops=12 * rows * width * local, bytes_accessed=40 * rows * width, transcendentals=0
        ),
        name="finish_stage",
    )(
        *[source.reshape(2, 2, 2, 2, share, source.shape[1]) for source in sources],
        own, from_low, from_high, normed_t, weights, table,
        upstream, latent, two, later, sums, lengths, own_features, other,
    )


def finish_apart(grads, back, upstream, latent, two, later, sums, lengths, features, other):
    rows, width = latent.shape
    micro, items = lengths.shape
    totals = [early_sum(grad) for grad in grads]
    latent_grad, first_sums = norm_back(upstream, back, swap(back), latent, two, later, 0, micro)
    pieces = jnp.concatenate([first_sums.reshape(micro, 2, 2 * width), sums], axis=2)
    first_item = jnp.sum(
        (jnp.cumsum(lengths, axis=1) <= lax.axis_index("seq") * (rows // micro)).astype(jnp.int32),
        axis=1,
    )
    base = jnp.minimum(first_item, items - 2)
    spots = (base[:, None] + jnp.arange(2))[:, :, None] == jnp.arange(items)
    item_grad = jnp.sum(jnp.where(spots[..., None], pieces[:, :, None], 0.0), axis=1)
    total = seq_sum(item_grad.reshape(micro * items, 6 * width))
    mod_grad = jnp.dot(features.T, total, precision=highest)
    return totals, latent_grad, mod_grad, jnp.sum(total, axis=0, keepdims=True), swap(other)


def early_sum(grad):
    return lax.psum_scatter(grad, "seq", scatter_dimension=0, tiled=True).astype(f32)


def turn(values, own, below, above):
    quarter = HD // 4
    return (
        values * own
        + pltpu.roll(values, quarter, 1) * below
        + pltpu.roll(values, 2 * HD - quarter, 1) * above
    )


def project_kernel(normed_ref, weight_ref, table_ref, out_ref, *, turned):
    j = pl.program_id(0)
    product = nn(normed_ref[...], weight_ref[...])

    @pl.when(j < turned)
    def _():
        for part in range(product.shape[1] // 128):
            lanes = slice(part * 128, (part + 1) * 128)
            out_ref[:, lanes] = turn(
                product[:, lanes], table_ref[0], table_ref[1], table_ref[2]
            ).astype(bf16)

    @pl.when(j >= turned)
    def _():
        out_ref[...] = product.astype(bf16)


def project(normed, weights, table, local, step=256):
    rows, width = normed.shape
    return pl.pallas_call(
        functools.partial(project_kernel, turned=2 * local // step),
        grid=(3 * local // step,),
        in_specs=[
            pl.BlockSpec((rows, width), lambda j: (0, 0)),
            pl.BlockSpec((width, step), lambda j: (0, j)),
            pl.BlockSpec((3, rows, 128), lambda j: (0, 0, 0)),
        ],
        out_specs=pl.BlockSpec((rows, step), lambda j: (0, j)),
        out_shape=jax.ShapeDtypeStruct((rows, 3 * local), bf16),
        compiler_params=kernel_params(1, 32),
        cost_estimate=pl.CostEstimate(
            flops=2 * rows * width * 3 * local,
            bytes_accessed=2 * (rows * width + 3 * local * (width + rows)),
            transcendentals=0,
        ),
        name="qkv_projection",
    )(normed, weights, table)


def head_lanes(shape):
    return lax.broadcasted_iota(jnp.int32, shape, 1) < HD


def one_head(values, first, which):
    return jnp.where(first if which == 0 else ~first, values, jnp.zeros_like(values))


def soft_rows(scores):
    peak = jnp.max(scores, axis=-1, keepdims=True)
    raised = jnp.exp(scores - peak)
    total = jnp.sum(raised, axis=-1, keepdims=True)
    return raised * (1.0 / total), peak + jnp.log(total)


def attend_rows(query, keys, values, bias):
    first = head_lanes(query.shape)
    out = None
    logs = []
    for which in range(2):
        scores = nt(one_head(query, first, which), keys) * (HD**-0.5) + bias
        weights, log_total = soft_rows(scores)
        mixed = nn(weights.astype(bf16), values)
        out = mixed if which == 0 else jnp.where(first, out, mixed)
        logs.append(log_total)
    return out, logs


def attend_rows_back(query, keys, values, bias, logs, grad):
    first = head_lanes(query.shape)
    query_grad = key_grad = value_grad = None
    for which in range(2):
        own_query = one_head(query, first, which)
        own_grad = one_head(grad, first, which)
        scores = nt(own_query, keys) * (HD**-0.5) + bias
        chances = jnp.exp(scores - logs[which])
        chance_grad = nt(own_grad, values)
        score_grad = (
            chances * (chance_grad - jnp.sum(chances * chance_grad, axis=-1, keepdims=True))
        ).astype(bf16)
        to_query = nn(score_grad, keys) * (HD**-0.5)
        to_key = tn(score_grad, own_query) * (HD**-0.5)
        to_value = tn(chances.astype(bf16), own_grad)
        if which == 0:
            query_grad, key_grad, value_grad = to_query, to_key, to_value
        else:
            query_grad = jnp.where(first, query_grad, to_query)
            key_grad = key_grad + to_key
            value_grad = value_grad + to_value
    return query_grad, key_grad, value_grad


def put_logs(log_ref, rows, logs, pair):
    lane = lax.broadcasted_iota(jnp.int32, (logs[0].shape[0], 128), 1)
    kept = log_ref[rows, :]
    kept = jnp.where(lane == 2 * pair, logs[0], kept)
    log_ref[rows, :] = jnp.where(lane == 2 * pair + 1, logs[1], kept)


def get_logs(log_ref, rows, pair):
    kept = log_ref[rows, :]
    lane = lax.broadcasted_iota(jnp.int32, kept.shape, 1)
    return [
        jnp.sum(jnp.where(lane == 2 * pair + which, kept, 0.0), axis=1, keepdims=True)
        for which in range(2)
    ]


def spread_rows(hidden):
    center = hidden - jnp.mean(hidden, axis=-1, keepdims=True)
    spread = jnp.mean(center * center, axis=-1, keepdims=True)
    scale = lax.rsqrt(spread + norm_eps)
    return center * scale, scale


def item_row(two_ref, later_ref, index):
    width = two_ref.shape[2] // 6
    lanes = slice(index * width, (index + 1) * width)
    return jnp.where(later_ref[...] > 0.5, two_ref[0, 1:2, lanes], two_ref[0, 0:1, lanes])


def norm_kernel(*refs, index, with_weight):
    refs = list(refs)
    base_ref, own_ref, got_ref, two_ref, later_ref = refs[:5]
    weight_ref = refs[5] if with_weight else None
    outs = refs[5 + with_weight :]
    hidden = (
        base_ref[...].astype(f32) + own_ref[...].astype(f32) + got_ref[...].astype(f32)
    )
    xhat, _ = spread_rows(hidden)
    normed = (
        xhat * (1.0 + item_row(two_ref, later_ref, index + 1)) + item_row(two_ref, later_ref, index)
    ).astype(bf16)
    outs[0][...] = hidden
    outs[1][...] = normed
    outs[2][...] = normed.T
    if with_weight:
        outs[3][...] = nn(normed, weight_ref[...]).astype(bf16)


def norm_forward(base, own, got, two, later, index, micro, weights=None, column=0, out_width=0):
    rows, width = base.shape
    tile = rows // micro
    row_tile = pl.BlockSpec((tile, width), lambda i: (i, 0))
    in_specs = [
        row_tile,
        row_tile,
        row_tile,
        pl.BlockSpec((1, 2, 6 * width), lambda i: (i, 0, 0)),
        pl.BlockSpec((tile, 1), lambda i: (i, 0)),
    ]
    out_specs = [row_tile, row_tile, pl.BlockSpec((width, tile), lambda i: (0, i))]
    out_shape = [
        jax.ShapeDtypeStruct((rows, width), f32),
        jax.ShapeDtypeStruct((rows, width), bf16),
        jax.ShapeDtypeStruct((width, rows), bf16),
    ]
    args = [base, own, got, two, later]
    if weights is not None:
        in_specs.append(pl.BlockSpec((width, out_width), lambda i: (0, column)))
        out_specs.append(pl.BlockSpec((tile, out_width), lambda i: (i, 0)))
        out_shape.append(jax.ShapeDtypeStruct((rows, out_width), bf16))
        args.append(weights)
    return pl.pallas_call(
        functools.partial(norm_kernel, index=index, with_weight=weights is not None),
        grid=(micro,),
        in_specs=in_specs,
        out_specs=out_specs,
        out_shape=out_shape,
        compiler_params=kernel_params(1, 40),
        cost_estimate=pl.CostEstimate(
            flops=2 * rows * width * out_width, bytes_accessed=16 * rows * width, transcendentals=0
        ),
        name="norm_forward",
    )(*args)


def norm_back_kernel(*refs, index, with_weight):
    refs = list(refs)
    up_ref, own_ref, got_ref, hidden_ref, two_ref, later_ref = refs[:6]
    weight_ref = refs[6] if with_weight else None
    outs = refs[6 + with_weight :]
    xhat, scale = spread_rows(hidden_ref[...].astype(f32))
    grad = own_ref[...].astype(f32) + got_ref[...].astype(f32)
    inner = grad * (1.0 + item_row(two_ref, later_ref, index + 1))
    mean_inner = jnp.mean(inner, axis=-1, keepdims=True)
    mean_cross = jnp.mean(inner * xhat, axis=-1, keepdims=True)
    total = up_ref[...].astype(f32) + scale * (inner - mean_inner - xhat * mean_cross)
    outs[0][...] = total
    later = later_ref[...] > 0.5
    scaled = grad * xhat
    for item in range(2):
        chosen = later if item else ~later
        outs[1][0, item, 0:1] = jnp.sum(jnp.where(chosen, grad, 0.0), axis=0, keepdims=True)
        outs[1][0, item, 1:2] = jnp.sum(jnp.where(chosen, scaled, 0.0), axis=0, keepdims=True)
    if with_weight:
        rounded = total.astype(bf16)
        outs[2][...] = rounded.T
        outs[3][...] = nn(rounded, weight_ref[...]).astype(bf16)


def norm_back(up, own, got, hidden, two, later, index, micro, weights=None, column=0, out_width=0):
    rows, width = hidden.shape
    tile = rows // micro
    row_tile = pl.BlockSpec((tile, width), lambda i: (i, 0))
    in_specs = [
        row_tile,
        row_tile,
        row_tile,
        row_tile,
        pl.BlockSpec((1, 2, 6 * width), lambda i: (i, 0, 0)),
        pl.BlockSpec((tile, 1), lambda i: (i, 0)),
    ]
    out_specs = [row_tile, pl.BlockSpec((1, 2, 2, width), lambda i: (i, 0, 0, 0))]
    out_shape = [
        jax.ShapeDtypeStruct((rows, width), f32),
        jax.ShapeDtypeStruct((micro, 2, 2, width), f32),
    ]
    args = [up, own, got, hidden, two, later]
    if weights is not None:
        in_specs.append(pl.BlockSpec((width, out_width), lambda i: (0, column)))
        out_specs += [
            pl.BlockSpec((width, tile), lambda i: (0, i)),
            pl.BlockSpec((tile, out_width), lambda i: (i, 0)),
        ]
        out_shape += [
            jax.ShapeDtypeStruct((width, rows), bf16),
            jax.ShapeDtypeStruct((rows, out_width), bf16),
        ]
        args.append(weights)
    return pl.pallas_call(
        functools.partial(norm_back_kernel, index=index, with_weight=weights is not None),
        grid=(micro,),
        in_specs=in_specs,
        out_specs=out_specs,
        out_shape=out_shape,
        compiler_params=kernel_params(1, 48),
        cost_estimate=pl.CostEstimate(
            flops=2 * rows * width * out_width, bytes_accessed=20 * rows * width, transcendentals=0
        ),
        name="norm_back",
    )(*args)


def add_product(acc_ref, out_ref, product):
    pair = pl.program_id(1)

    @pl.when(pair == 0)
    def _():
        acc_ref[...] = product

    @pl.when(pair > 0)
    def _():
        acc_ref[...] += product

    @pl.when(pair == pl.num_programs(1) - 1)
    def _():
        out_ref[...] = acc_ref[...].astype(bf16)


def self_kernel(q_ref, k_ref, v_ref, bias_ref, weight_ref, out_ref, log_ref, sum_ref, acc_ref):
    pair = pl.program_id(1)
    block_rows = out_ref.shape[0]
    for part in range(block_rows // HALF):
        rows = slice(part * HALF, (part + 1) * HALF)
        span = slice(part * HALF, (part + 3) * HALF)
        out, logs = attend_rows(
            q_ref[(part + 1) * HALF : (part + 2) * HALF, :],
            k_ref[span, :],
            v_ref[span, :],
            bias_ref[rows, :],
        )
        out_ref[rows, :] = out.astype(bf16)
        put_logs(log_ref, rows, logs, pair)
    add_product(acc_ref, sum_ref, nt(out_ref[...], weight_ref[...]))


def self_specs(block_rows, pairs):
    near = lambda first: pl.BlockSpec((block_rows + 2 * HALF, 128), lambda m, h: (m, first + h))
    return [
        near(0),
        near(pairs),
        near(2 * pairs),
        pl.BlockSpec((block_rows, 3 * HALF), lambda m, h: (m, 0)),
    ]


def self_attention(qkv, bias, weights, column, micro, block_rows):
    rows = micro * block_rows
    local = qkv.shape[1] // 3
    width = weights.shape[0]
    pairs = local // 128
    return pl.pallas_call(
        self_kernel,
        grid=(micro, pairs),
        in_specs=self_specs(block_rows, pairs)
        + [pl.BlockSpec((width, 128), lambda m, h: (0, column + h))],
        out_specs=[
            pl.BlockSpec((block_rows, 128), lambda m, h: (m, h)),
            pl.BlockSpec((block_rows, 128), lambda m, h: (m, 0)),
            pl.BlockSpec((block_rows, width), lambda m, h: (m, 0)),
        ],
        out_shape=[
            jax.ShapeDtypeStruct((rows, local), bf16),
            jax.ShapeDtypeStruct((rows, 128), f32),
            jax.ShapeDtypeStruct((rows, width), bf16),
        ],
        scratch_shapes=[pltpu.VMEM((block_rows, width), f32)],
        compiler_params=kernel_params(2, 32),
        cost_estimate=pl.CostEstimate(
            flops=rows * 2 * local * (width + 12 * HALF),
            bytes_accessed=20 * rows * local,
            transcendentals=rows * 3 * HALF * 2 * pairs,
        ),
        name="self_attention",
    )(qkv, qkv, qkv, bias, weights)


def self_back_kernel(
    q_ref, k_ref, v_ref, bias_ref, grad_ref, log_ref, own_ref, to_low_ref, to_high_ref
):
    pair = pl.program_id(1)
    parts = grad_ref.shape[0] // HALF
    pieces = [[None] * (parts + 2), [None] * (parts + 2)]
    for part in range(parts):
        rows = slice(part * HALF, (part + 1) * HALF)
        span = slice(part * HALF, (part + 3) * HALF)
        query_grad, key_grad, value_grad = attend_rows_back(
            q_ref[(part + 1) * HALF : (part + 2) * HALF, :],
            k_ref[span, :],
            v_ref[span, :],
            bias_ref[rows, :],
            get_logs(log_ref, rows, pair),
            grad_ref[rows, :],
        )
        own_ref[0, rows, :] = query_grad
        for kind, near_grad in enumerate((key_grad, value_grad)):
            for third in range(3):
                piece = near_grad[third * HALF : (third + 1) * HALF]
                held = pieces[kind][part + third]
                pieces[kind][part + third] = piece if held is None else held + piece
    for kind in range(2):
        to_low_ref[kind] = pieces[kind][0].astype(bf16)
        for part in range(parts):
            own_ref[1 + kind, part * HALF : (part + 1) * HALF, :] = pieces[kind][part + 1]
        to_high_ref[kind] = pieces[kind][parts + 1].astype(bf16)


def self_attention_back(qkv, bias, grad, logs, micro, block_rows):
    rows, local = grad.shape
    pairs = local // 128
    edge = pl.BlockSpec((2, None, HALF, 128), lambda m, h: (0, m, 0, h))
    return pl.pallas_call(
        self_back_kernel,
        grid=(micro, pairs),
        in_specs=self_specs(block_rows, pairs)
        + [
            pl.BlockSpec((block_rows, 128), lambda m, h: (m, h)),
            pl.BlockSpec((block_rows, 128), lambda m, h: (m, 0)),
        ],
        out_specs=[
            pl.BlockSpec((3, block_rows, 128), lambda m, h: (0, m, h)),
            edge,
            edge,
        ],
        out_shape=[
            jax.ShapeDtypeStruct((3, rows, local), f32),
            jax.ShapeDtypeStruct((2, micro, HALF, local), bf16),
            jax.ShapeDtypeStruct((2, micro, HALF, local), bf16),
        ],
        compiler_params=kernel_params(2, 32),
        cost_estimate=pl.CostEstimate(
            flops=20 * rows * 3 * HALF * local,
            bytes_accessed=40 * rows * local,
            transcendentals=rows * 3 * HALF * 2 * pairs,
        ),
        name="self_attention_back",
    )(qkv, qkv, qkv, bias, grad, logs)


def cross_kernel(q_ref, k_ref, v_ref, bias_ref, weight_ref, out_ref, log_ref, sum_ref, acc_ref):
    pair = pl.program_id(1)
    for part in range(q_ref.shape[0] // HALF):
        rows = slice(part * HALF, (part + 1) * HALF)
        out, logs = attend_rows(q_ref[rows, :], k_ref[...], v_ref[...], bias_ref[rows, :])
        out_ref[rows, :] = out.astype(bf16)
        put_logs(log_ref, rows, logs, pair)
    add_product(acc_ref, sum_ref, nt(out_ref[...], weight_ref[...]))


def cross_specs(block_rows, pairs):
    return [
        pl.BlockSpec((block_rows, 128), lambda m, h: (m, h)),
        pl.BlockSpec((2 * TXT, 128), lambda m, h: (m, h)),
        pl.BlockSpec((2 * TXT, 128), lambda m, h: (m, h)),
        pl.BlockSpec((block_rows, 2 * TXT), lambda m, h: (m, 0)),
    ]


def cross_attention(query, keys, values, bias, weights, column, micro, block_rows):
    rows, local = query.shape
    width = weights.shape[0]
    pairs = local // 128
    return pl.pallas_call(
        cross_kernel,
        grid=(micro, pairs),
        in_specs=cross_specs(block_rows, pairs)
        + [pl.BlockSpec((width, 128), lambda m, h: (0, column + h))],
        out_specs=[
            pl.BlockSpec((block_rows, 128), lambda m, h: (m, h)),
            pl.BlockSpec((block_rows, 128), lambda m, h: (m, 0)),
            pl.BlockSpec((block_rows, width), lambda m, h: (m, 0)),
        ],
        out_shape=[
            jax.ShapeDtypeStruct((rows, local), bf16),
            jax.ShapeDtypeStruct((rows, 128), f32),
            jax.ShapeDtypeStruct((rows, width), bf16),
        ],
        scratch_shapes=[pltpu.VMEM((block_rows, width), f32)],
        compiler_params=kernel_params(2, 32),
        cost_estimate=pl.CostEstimate(
            flops=rows * 2 * local * (width + 8 * TXT),
            bytes_accessed=16 * rows * local,
            transcendentals=rows * 2 * TXT * 2 * pairs,
        ),
        name="cross_attention",
    )(query, keys, values, bias, weights)


def cross_back_kernel(
    q_ref, k_ref, v_ref, bias_ref, grad_ref, log_ref, weight_ref,
    dq_ref, dk_ref, dv_ref, sum_ref, acc_ref,
):
    pair = pl.program_id(1)
    key_total = value_total = None
    for part in range(q_ref.shape[0] // HALF):
        rows = slice(part * HALF, (part + 1) * HALF)
        query_grad, key_grad, value_grad = attend_rows_back(
            q_ref[rows, :],
            k_ref[...],
            v_ref[...],
            bias_ref[rows, :],
            get_logs(log_ref, rows, pair),
            grad_ref[rows, :],
        )
        dq_ref[rows, :] = query_grad.astype(bf16)
        key_total = key_grad if part == 0 else key_total + key_grad
        value_total = value_grad if part == 0 else value_total + value_grad
    dk_ref[...] = key_total.astype(bf16)
    dv_ref[...] = value_total.astype(bf16)
    add_product(acc_ref, sum_ref, nt(dq_ref[...], weight_ref[...]))


def cross_attention_back(
    query, keys, values, bias, grad, logs, weights, column, micro, block_rows
):
    rows, local = query.shape
    width = weights.shape[0]
    pairs = local // 128
    text = pl.BlockSpec((2 * TXT, 128), lambda m, h: (m, h))
    return pl.pallas_call(
        cross_back_kernel,
        grid=(micro, pairs),
        in_specs=cross_specs(block_rows, pairs)
        + [
            pl.BlockSpec((block_rows, 128), lambda m, h: (m, h)),
            pl.BlockSpec((block_rows, 128), lambda m, h: (m, 0)),
            pl.BlockSpec((width, 128), lambda m, h: (0, column + h)),
        ],
        out_specs=[
            pl.BlockSpec((block_rows, 128), lambda m, h: (m, h)),
            text,
            text,
            pl.BlockSpec((block_rows, width), lambda m, h: (m, 0)),
        ],
        out_shape=[
            jax.ShapeDtypeStruct((rows, local), bf16),
            jax.ShapeDtypeStruct(keys.shape, bf16),
            jax.ShapeDtypeStruct(keys.shape, bf16),
            jax.ShapeDtypeStruct((rows, width), bf16),
        ],
        scratch_shapes=[pltpu.VMEM((block_rows, width), f32)],
        compiler_params=kernel_params(2, 32),
        cost_estimate=pl.CostEstimate(
            flops=rows * 2 * local * (width + 20 * TXT),
            bytes_accessed=30 * rows * local,
            transcendentals=rows * 2 * TXT * 2 * pairs,
        ),
        name="cross_attention_back",
    )(query, keys, values, bias, grad, logs, weights)


def ffn_kernel(*refs, summed):
    (
        normed_ref, normed_t_ref, cot_ref, cot_t_ref, outer_ref, gate_ref, up_ref,
        g_outer_ref, g_gate_ref, g_up_ref, out_ref, back_ref, *refs,
    ) = refs
    j = pl.program_id(0)
    step = gate_ref.shape[1]
    if summed:
        sum_ref, out_acc, back_acc, full = refs[:4]
        me = lax.axis_index("seq")
        digits = seq_digits(me)
        core = digits[0]
        partners = [me + stride * (1 - 2 * digit) for stride, digit in zip(STRIDES, digits)]
        pl.when(j == 0)(lambda: [greet(me, digits), None][1])
        pieces = Pieces(refs[4:], sum_ref, partners, digits, step, lag=2)
        count = summed

        def over_core(slot):
            return pieces.over_core(full.at[slot, :, :, :, 1 - core], slot)

        def tick(t):
            @when((t >= 1) & (t - 1 < count))
            def _():
                slot = (t - 1) % SLOTS
                when(t - 1 >= SLOTS)(lambda: pieces.wait_sent(slot))
                over_core(slot).wait()
                pieces.add_core(t - 1, slot, lambda a, b, c: full[slot, a, b, c, core])

            pieces.later_steps(t, count)

    else:
        out_acc, back_acc = refs
    if summed:
        tick(j)
    gate = nn(normed_ref[...], gate_ref[...])
    up = nn(normed_ref[...], up_ref[...])
    grad = nn(cot_ref[...], outer_ref[...])
    chance = 1.0 / (1.0 + jnp.exp(-gate))
    swish = gate * chance
    active = (swish * up).astype(bf16)
    gate_grad = (grad * up * (chance * (1.0 + gate * (1.0 - chance)))).astype(bf16)
    up_grad = (grad * swish).astype(bf16)
    g_up = nn(normed_t_ref[...], up_grad).astype(bf16)
    if summed:

        @pl.when(j < count)
        def _():
            slot = j % SLOTS
            full[slot] = g_up.reshape(full.shape[1:])
            over_core(slot).start()

        @pl.when(j >= count)
        def _():
            g_up_ref[...] = g_up
    else:
        g_up_ref[...] = g_up
    g_gate_ref[...] = nn(normed_t_ref[...], gate_grad).astype(bf16)
    g_outer_ref[...] = nn(cot_t_ref[...], active).astype(bf16)
    out_part = nt(active, outer_ref[...])
    back_part = nt(gate_grad, gate_ref[...]) + nt(up_grad, up_ref[...])

    @pl.when(j == 0)
    def _():
        out_acc[...] = out_part
        back_acc[...] = back_part

    @pl.when(j > 0)
    def _():
        out_acc[...] += out_part
        back_acc[...] += back_part

    @pl.when(j == pl.num_programs(0) - 1)
    def _():
        out_ref[...] = out_acc[...].astype(bf16)
        back_ref[...] = back_acc[...].astype(bf16)
        if summed:
            for t in range(pl.num_programs(0), count + 4):
                tick(t)
            pieces.finish(count)


FFN_STEP = 256
SUMMED_STEPS = 9


def feed_forward(normed, normed_t, cotangent, weights, hidden, step=FFN_STEP):
    rows, width = normed.shape
    steps = hidden // step
    seq_count = lax.axis_size("seq")
    share = width // seq_count
    summed = SUMMED_STEPS if seq_count == 16 and share % 16 == 0 else 0
    assert not summed or summed < steps <= 2 * summed
    whole = lambda shape: pl.BlockSpec(shape, lambda j: (0, 0))
    held = lambda shape: pl.BlockSpec(shape, lambda j: (0, 0), pipeline_mode=pl.Buffered(1))
    column = lambda first: pl.BlockSpec((width, step), lambda j: (0, first + j))
    scratch = [pltpu.VMEM((rows, width), f32)] * 2
    out_specs = [
        column(0),
        column(0),
        column(0),
        whole((rows, width)),
        whole((rows, width)),
    ]
    out_shape = [
        jax.ShapeDtypeStruct((width, hidden), bf16),
        jax.ShapeDtypeStruct((width, hidden), bf16),
        jax.ShapeDtypeStruct((width, hidden - summed * step), bf16),
        jax.ShapeDtypeStruct((rows, width), bf16),
        jax.ShapeDtypeStruct((rows, width), bf16),
    ]
    params = kernel_params(1, 56)
    if summed:
        scratch += [pltpu.VMEM((SLOTS, 2, 2, 2, 2, share, step), bf16)]
        scratch += Pieces.scratch(share, step)
        out_specs[2] = pl.BlockSpec((width, step), lambda j: (0, j // summed * (j - summed)))
        out_specs.append(pl.BlockSpec(memory_space=pl.ANY))
        out_shape.append(jax.ShapeDtypeStruct((share, summed * step), f32))
        params = pltpu.CompilerParams(
            dimension_semantics=("arbitrary",),
            collective_id=3,
            has_side_effects=True,
            vmem_limit_bytes=60 * 1024 * 1024,
        )
    outs = pl.pallas_call(
        functools.partial(ffn_kernel, summed=summed),
        grid=(steps,),
        in_specs=[
            held((rows, width)),
            held((width, rows)),
            held((rows, width)),
            held((width, rows)),
            column(0),
            column(steps),
            column(2 * steps),
        ],
        out_specs=out_specs,
        out_shape=out_shape,
        scratch_shapes=scratch,
        compiler_params=params,
        cost_estimate=pl.CostEstimate(
            flops=18 * rows * width * hidden,
            bytes_accessed=12 * width * hidden,
            transcendentals=rows * hidden,
        ),
        name="feed_forward",
    )(normed, normed_t, cotangent, cotangent.T, weights, weights, weights)
    return outs


def qkv_back_kernel(
    own_ref, after_ref, before_ref, normed_t_ref, weight_ref, table_ref,
    grad_ref, back_ref, acc, *, kind_steps, micro, block_rows,
):
    j = pl.program_id(0)
    kind = j // kind_steps
    edges = (kind > 0).astype(f32)
    turned = kind < 2
    near_rows = block_rows + 2 * HALF

    def own_table(index):
        return jnp.concatenate(
            [
                table_ref[index, m * near_rows + HALF : (m + 1) * near_rows - HALF]
                for m in range(micro)
            ],
            axis=0,
        )

    own_factor = jnp.where(turned, own_table(0), 1.0)
    below_factor = jnp.where(turned, -own_table(1), 0.0)
    above_factor = jnp.where(turned, -own_table(2), 0.0)
    total = []
    for m in range(micro):
        first = m * block_rows
        total.append(own_ref[first : first + HALF] + edges * after_ref[m].astype(f32))
        if block_rows > 2 * HALF:
            total.append(own_ref[first + HALF : first + block_rows - HALF])
        total.append(
            own_ref[first + block_rows - HALF : first + block_rows]
            + edges * before_ref[m].astype(f32)
        )
    total = jnp.concatenate(total, axis=0)
    grad = jnp.concatenate(
        [
            turn(total[:, i : i + 128], own_factor, below_factor, above_factor)
            for i in range(0, total.shape[1], 128)
        ],
        axis=1,
    ).astype(bf16)
    grad_ref[...] = nn(normed_t_ref[...], grad).astype(bf16)
    part = nt(grad, weight_ref[...])

    @pl.when(j == 0)
    def _():
        acc[...] = part

    @pl.when(j > 0)
    def _():
        acc[...] += part

    @pl.when(j == pl.num_programs(0) - 1)
    def _():
        back_ref[...] = acc[...].astype(bf16)


def qkv_back(own, after, before, normed_t, weights, table, micro, block_rows, step=256):
    _, rows, local = own.shape
    width = normed_t.shape[0]
    kind_steps = local // step
    edge = pl.BlockSpec(
        (None, micro, HALF, step),
        lambda j: (jnp.maximum(j // kind_steps - 1, 0), 0, 0, j % kind_steps),
    )
    return pl.pallas_call(
        functools.partial(
            qkv_back_kernel, kind_steps=kind_steps, micro=micro, block_rows=block_rows
        ),
        grid=(3 * kind_steps,),
        in_specs=[
            pl.BlockSpec((None, rows, step), lambda j: (j // kind_steps, 0, j % kind_steps)),
            edge,
            edge,
            pl.BlockSpec((width, rows), lambda j: (0, 0)),
            pl.BlockSpec((width, step), lambda j: (0, j)),
            pl.BlockSpec(table.shape, lambda j: (0, 0, 0)),
        ],
        out_specs=[
            pl.BlockSpec((width, step), lambda j: (0, j)),
            pl.BlockSpec((rows, width), lambda j: (0, 0)),
        ],
        out_shape=[
            jax.ShapeDtypeStruct((width, 3 * local), bf16),
            jax.ShapeDtypeStruct((rows, width), bf16),
        ],
        scratch_shapes=[pltpu.VMEM((rows, width), f32)],
        compiler_params=kernel_params(1, 40),
        cost_estimate=pl.CostEstimate(
            flops=12 * rows * width * local,
            bytes_accessed=12 * width * local + 12 * rows * local,
            transcendentals=0,
        ),
        name="qkv_back",
    )(own, after, before, normed_t, weights, table)


def time_features(steps_row):
    half_width = TEMB // 2
    ladder = jnp.exp(-math.log(10000.0) * jnp.arange(half_width, dtype=f32) / half_width)
    angles = steps_row.astype(f32)[:, None] * ladder[None, :]
    return jnp.concatenate([jnp.cos(angles), jnp.sin(angles)], axis=-1)


def norm_back_unit(m, index, block_rows, grad_of, up_ref, hidden_ref, two_ref, later_ref, sums_ref, emit):
    width = hidden_ref.shape[1]
    for start in range(0, block_rows, HALF):
        span = slice(m * block_rows + start, m * block_rows + start + HALF)
        later = later_ref[span, :] > 0.5
        lanes = slice((index + 1) * width, (index + 2) * width)
        factor = jnp.where(later, two_ref[m, 1:2, lanes], two_ref[m, 0:1, lanes])
        total, sums = norm_back_tile(
            grad_of(span),
            up_ref[span, :].astype(f32),
            hidden_ref[span, :].astype(f32),
            (~later, later),
            factor,
        )
        for item in range(2):
            for kind in range(2):
                at = slice(kind * width, (kind + 1) * width)
                before = sums_ref[m, item : item + 1, at] if start else 0.0
                sums_ref[m, item : item + 1, at] = sums[item][kind] + before
        emit(span, start, total)


def cross_stage_kernel(
    back_ref, up_ref, hidden_ref, two_ref, later_ref, weight_ref, q_ref, k_ref, v_ref, bias_ref,
    log_ref, *refs, spans, step, micro, ready,
):
    sources, refs = refs[: len(spans)], refs[len(spans) :]
    (
        grad_ref, sums_ref, low_t_ref, dq_ref, dk_ref, dv_ref, next_ref, got_next_ref, out_ref,
        own_sem, got_ref, mixed_ref, acc_ref, out_w_ref, query_w_ref, weight_sem,
        swap_send, swap_recv, next_send, next_recv,
    ) = refs[:20]
    refs = refs[20:]
    me = lax.axis_index("seq")
    mine = lax.axis_index("tensor")
    digits = seq_digits(me)
    partners = greet_all(me, mine, digits)
    rows = back_ref.shape[0]
    block_rows = rows // micro
    pairs = q_ref.shape[1] // 128
    text = k_ref.shape[0] // micro

    def over_tensor(m):
        span = pl.ds(m * block_rows, block_rows)
        return to_tensor(
            mine, back_ref.at[span], got_ref.at[span], swap_send.at[m], swap_recv.at[m]
        )

    def over_next(m):
        span = pl.ds(m * block_rows, block_rows)
        return to_tensor(
            mine, next_ref.at[span], got_next_ref.at[span], next_send.at[m], next_recv.at[m]
        )

    def norm_unit(m):
        over_tensor(m).wait_recv()
        if m == 0:
            for load in loads:
                load.wait()

        def emit(span, start, total):
            grad_ref[span, :] = total
            rounded = total.astype(bf16)
            low_t_ref[:, span] = rounded.T
            mixed_ref[start : start + HALF, :] = nn(rounded, out_w_ref[...]).astype(bf16)

        norm_back_unit(
            m, 4, block_rows,
            lambda span: back_ref[span, :].astype(f32) + got_ref[span, :].astype(f32),
            up_ref, hidden_ref, two_ref, later_ref, sums_ref, emit,
        )

    def pair_unit(m, pair):
        lanes = pl.ds(pl.multiple_of(pair * 128, 128), 128)
        keys = slice(m * text, (m + 1) * text)
        key_total = value_total = None
        for start in range(0, block_rows, HALF):
            span = slice(m * block_rows + start, m * block_rows + start + HALF)
            query_grad, key_grad, value_grad = attend_rows_back(
                q_ref[span, lanes],
                k_ref[keys, lanes],
                v_ref[keys, lanes],
                bias_ref[span, :],
                get_logs(log_ref, span, pair),
                mixed_ref[start : start + HALF, lanes],
            )
            dq_ref[span, lanes] = query_grad.astype(bf16)
            key_total = key_grad if start == 0 else key_total + key_grad
            value_total = value_grad if start == 0 else value_total + value_grad
        dk_ref[keys, lanes] = key_total.astype(bf16)
        dv_ref[keys, lanes] = value_total.astype(bf16)
        own = slice(m * block_rows, (m + 1) * block_rows)
        product = nt(dq_ref[own, lanes], query_w_ref[:, lanes])
        acc_ref[...] = product + jnp.where(pair == 0, 0.0, acc_ref[...])

    def close(m):
        own = slice(m * block_rows, (m + 1) * block_rows)
        next_ref[own, :] = acc_ref[...].astype(bf16)
        if m < micro - 1:
            over_next(m).start()

    local = q_ref.shape[1]
    loads = [
        pltpu.make_async_copy(
            weight_ref.at[:, k * local : (k + 1) * local], target, weight_sem.at[i]
        )
        for i, (k, target) in enumerate(((5, out_w_ref), (4, query_w_ref)))
    ]
    for load in loads:
        load.start()
    acc_ref[...] = jnp.zeros_like(acc_ref)
    pieces = Pieces(refs, out_ref, partners, digits, step)
    work = []
    spot = 0
    for m in range(micro):
        spot = max(spot, ready * (m + 1))
        work.append((spot, spot + 1, lambda t, m=m: norm_unit(m)))
        spot += 1
        begin = spot

        def pair_units(t, m=m, begin=begin):
            for k in range(2):
                pair_unit(m, 2 * (t - begin) + k)

        work.append((begin, begin + pairs // 2, pair_units))
        spot += pairs // 2
        work.append((spot - 1, spot, lambda t, m=m: close(m)))
    for m in range(micro):
        over_tensor(m).start()
    pieces.run(sources, spans, own_sem, work, spot)
    for m in range(micro):
        over_tensor(m).wait_send()
        if m < micro - 1:
            over_next(m).wait()


def cross_stage(
    back, up, hidden, two, later, query, keys, values, bias, logs, weights, local, sources,
    spans, micro, which=2, step=256,
):
    seq_count = lax.axis_size("seq")
    rows, width = hidden.shape
    share = width // seq_count
    block_rows = rows // micro
    any_space = pl.BlockSpec(memory_space=pl.ANY)
    vmem = pl.BlockSpec(memory_space=pltpu.VMEM)
    return pl.pallas_call(
        functools.partial(
            cross_stage_kernel, spans=spans, step=step, micro=micro, ready=4
        ),
        out_shape=[
            jax.ShapeDtypeStruct((rows, width), f32),
            jax.ShapeDtypeStruct((micro, 2, 2 * width), f32),
            jax.ShapeDtypeStruct((width, rows), bf16),
            jax.ShapeDtypeStruct((rows, local), bf16),
            jax.ShapeDtypeStruct(keys.shape, bf16),
            jax.ShapeDtypeStruct(keys.shape, bf16),
            jax.ShapeDtypeStruct((rows, width), bf16),
            jax.ShapeDtypeStruct((rows - block_rows, width), bf16),
            jax.ShapeDtypeStruct((share, sum(span for _, span in spans)), f32),
        ],
        in_specs=[vmem] * 5 + [any_space] + [vmem] * 5 + [any_space] * len(spans),
        out_specs=[vmem] * 7 + [any_space] * 2,
        scratch_shapes=[
            pltpu.SemaphoreType.DMA((SLOTS,)),
            pltpu.VMEM((rows, width), bf16),
            pltpu.VMEM((block_rows, local), bf16),
            pltpu.VMEM((block_rows, width), f32),
            pltpu.VMEM((width, local), bf16),
            pltpu.VMEM((width, local), bf16),
            pltpu.SemaphoreType.DMA((2,)),
        ]
        + [pltpu.SemaphoreType.DMA((micro,))] * 4
        + Pieces.scratch(share, step),
        compiler_params=pltpu.CompilerParams(
            collective_id=which, has_side_effects=True, vmem_limit_bytes=56 * 1024 * 1024
        ),
        cost_estimate=pl.CostEstimate(
            flops=8 * rows * width * local, bytes_accessed=40 * rows * width, transcendentals=0
        ),
        name="cross_stage",
    )(
        back, up, hidden, two, later, weights, query, keys, values, bias, logs,
        *[source.reshape(2, 2, 2, 2, share, source.shape[1]) for source in sources],
    )


def self_stage_kernel(
    back_ref, got_early_ref, up_ref, hidden_ref, two_ref, later_ref, weight_ref, qkv_ref, bias_ref,
    log_ref, other_ref, *refs,
    spans, step, micro, ready, seq_count,
):
    sources, refs = refs[: len(spans)], refs[len(spans) :]
    (
        grad_ref, sums_ref, low_t_ref, own_ref, from_low_ref, from_high_ref, got_other_ref, out_ref,
        own_sem, got_ref, mixed_ref, to_low_ref, to_high_ref, out_w_ref, weight_sem, swap_sem,
        halo_send, halo_recv,
    ) = refs[:18]
    refs = refs[18:]
    me = lax.axis_index("seq")
    mine = lax.axis_index("tensor")
    digits = seq_digits(me)
    has_low = me > 0
    has_high = me < seq_count - 1
    partners = greet_all(me, mine, digits, ((has_low, me - 1), (has_high, me + 1)))
    rows = back_ref.shape[0]
    block_rows = rows // micro
    near_rows = block_rows + 2 * HALF
    local = qkv_ref.shape[1] // 3
    pairs = local // 128
    last = micro - 1

    def over_tensor():
        return to_tensor(
            mine,
            back_ref.at[pl.ds(last * block_rows, block_rows)],
            got_ref,
            swap_sem.at[0],
            swap_sem.at[1],
        )

    def over_other():
        span = pl.ds(block_rows, rows - block_rows)
        return to_tensor(
            mine, other_ref.at[span], got_other_ref, swap_sem.at[2], swap_sem.at[3]
        )

    def to_low(m):
        return send_to(
            me - 1, to_low_ref.at[m], from_high_ref.at[m], halo_send.at[0, m], halo_recv.at[0, m]
        )

    def to_high(m):
        return send_to(
            me + 1, to_high_ref.at[m], from_low_ref.at[m], halo_send.at[1, m], halo_recv.at[1, m]
        )

    load = pltpu.make_async_copy(
        weight_ref.at[:, 3 * local : 4 * local], out_w_ref, weight_sem
    )
    load.start()

    def norm_unit(m):
        if m == 0:
            load.wait()
        if m == last:
            over_tensor().wait_recv()

        def grad_of(span):
            if m == last:
                other = got_ref[span.start - last * block_rows : span.stop - last * block_rows, :]
            else:
                other = got_early_ref[span, :]
            return back_ref[span, :].astype(f32) + other.astype(f32)

        def emit(span, start, total):
            grad_ref[span, :] = total
            rounded = total.astype(bf16)
            low_t_ref[:, span] = rounded.T
            mixed_ref[start : start + HALF, :] = nn(rounded, out_w_ref[...]).astype(bf16)

        norm_back_unit(
            m, 2, block_rows, grad_of, up_ref, hidden_ref, two_ref, later_ref, sums_ref, emit
        )

    def pair_unit(m, pair):
        def lanes(kind):
            return pl.ds(pl.multiple_of(kind * local + pair * 128, 128), 128)

        parts = block_rows // HALF
        held = [[None] * (parts + 2), [None] * (parts + 2)]
        at = lanes(0)
        for part in range(parts):
            span = slice(m * block_rows + part * HALF, m * block_rows + (part + 1) * HALF)
            own_rows = slice(m * near_rows + (part + 1) * HALF, m * near_rows + (part + 2) * HALF)
            near = slice(m * near_rows + part * HALF, m * near_rows + (part + 3) * HALF)
            query_grad, key_grad, value_grad = attend_rows_back(
                qkv_ref[own_rows, at],
                qkv_ref[near, lanes(1)],
                qkv_ref[near, lanes(2)],
                bias_ref[span, :],
                get_logs(log_ref, span, pair),
                mixed_ref[part * HALF : (part + 1) * HALF, at],
            )
            own_ref[0, span, at] = query_grad
            for kind, near_grad in enumerate((key_grad, value_grad)):
                for third in range(3):
                    piece = near_grad[third * HALF : (third + 1) * HALF]
                    before = held[kind][part + third]
                    held[kind][part + third] = piece if before is None else before + piece
        for kind in range(2):
            to_low_ref[m, kind, :, at] = held[kind][0].astype(bf16)
            for part in range(parts):
                span = slice(m * block_rows + part * HALF, m * block_rows + (part + 1) * HALF)
                own_ref[1 + kind, span, at] = held[kind][part + 1]
            to_high_ref[m, kind, :, at] = held[kind][parts + 1].astype(bf16)

    def close(m):
        pl.when(has_low)(lambda: to_low(m).start())
        pl.when(has_high)(lambda: to_high(m).start())

    pieces = Pieces(refs, out_ref, partners, digits, step)
    work = []
    spot = 1
    for m in range(micro):
        if m == last:
            spot = max(spot, ready)
        work.append((spot, spot + 1, lambda t, m=m: norm_unit(m)))
        spot += 1
        begin = spot

        def pair_units(t, m=m, begin=begin):
            for k in range(2):
                pair_unit(m, 2 * (t - begin) + k)

        work.append((begin, begin + pairs // 2, pair_units))
        spot += pairs // 2
        work.append((spot - 1, spot, lambda t, m=m: close(m)))
    over_tensor().start()
    over_other().start()

    @pl.when(jnp.logical_not(has_low))
    def _():
        from_low_ref[...] = jnp.zeros_like(from_low_ref)

    @pl.when(jnp.logical_not(has_high))
    def _():
        from_high_ref[...] = jnp.zeros_like(from_high_ref)

    pieces.run(sources, spans, own_sem, work, spot)
    over_tensor().wait_send()
    over_other().wait()
    for m in range(micro):

        @pl.when(has_low)
        def _(m=m):
            to_low(m).wait_send()
            to_high(m).wait_recv()

        @pl.when(has_high)
        def _(m=m):
            to_high(m).wait_send()
            to_low(m).wait_recv()


def self_stage(
    back, got_early, up, hidden, two, later, qkv, bias, logs, weights, local, other, sources,
    spans, micro, which=4, step=256,
):
    seq_count = lax.axis_size("seq")
    rows, width = hidden.shape
    share = width // seq_count
    block_rows = rows // micro
    any_space = pl.BlockSpec(memory_space=pl.ANY)
    vmem = pl.BlockSpec(memory_space=pltpu.VMEM)
    edge = (micro, 2, HALF, local)
    return pl.pallas_call(
        functools.partial(
            self_stage_kernel, spans=spans, step=step, micro=micro, ready=4, seq_count=seq_count
        ),
        out_shape=[
            jax.ShapeDtypeStruct((rows, width), f32),
            jax.ShapeDtypeStruct((micro, 2, 2 * width), f32),
            jax.ShapeDtypeStruct((width, rows), bf16),
            jax.ShapeDtypeStruct((3, rows, local), f32),
            jax.ShapeDtypeStruct(edge, bf16),
            jax.ShapeDtypeStruct(edge, bf16),
            jax.ShapeDtypeStruct((rows - block_rows, width), bf16),
            jax.ShapeDtypeStruct((share, sum(span for _, span in spans)), f32),
        ],
        in_specs=[vmem] * 6 + [any_space] + [vmem] * 3 + [any_space] * (1 + len(spans)),
        out_specs=[vmem] * 6 + [any_space] * 2,
        scratch_shapes=[
            pltpu.SemaphoreType.DMA((SLOTS,)),
            pltpu.VMEM((block_rows, width), bf16),
            pltpu.VMEM((block_rows, local), bf16),
            pltpu.VMEM(edge, bf16),
            pltpu.VMEM(edge, bf16),
            pltpu.VMEM((width, local), bf16),
            pltpu.SemaphoreType.DMA,
            pltpu.SemaphoreType.DMA((4,)),
            pltpu.SemaphoreType.DMA((2, micro)),
            pltpu.SemaphoreType.DMA((2, micro)),
        ]
        + Pieces.scratch(share, step),
        compiler_params=pltpu.CompilerParams(
            collective_id=which, has_side_effects=True, vmem_limit_bytes=58 * 1024 * 1024
        ),
        cost_estimate=pl.CostEstimate(
            flops=8 * rows * width * local, bytes_accessed=40 * rows * width, transcendentals=0
        ),
        name="self_stage",
    )(
        back, got_early, up, hidden, two, later, weights, qkv, bias, logs, other,
        *[source.reshape(2, 2, 2, 2, share, source.shape[1]) for source in sources],
    )


EARLY_COLUMNS = 1792


def on_device(
    latents,
    context,
    lengths,
    text_len,
    timesteps,
    self_qkv,
    self_out,
    cross_query,
    cross_kv,
    cross_out,
    ffn_in,
    ffn_out,
    mod_weight,
    mod_bias,
    out_grad,
):
    micro, block_rows, model_width = latents.shape
    seq_count = lax.axis_size("seq")
    me = lax.axis_index("seq")
    frame_count = block_rows * seq_count
    item_count = lengths.shape[1]
    local = self_qkv.shape[2]
    hidden = ffn_in.shape[2]
    rows = micro * block_rows
    text_width = context.shape[2]

    attn_share = jnp.concatenate(
        [
            self_qkv[0],
            self_qkv[1],
            self_qkv[2],
            self_out.T,
            cross_query,
            cross_out.T,
            jnp.concatenate([cross_kv[0], cross_kv[1]], axis=0),
        ],
        axis=1,
    )
    ffn_share = jnp.concatenate([ffn_out.T, ffn_in[0], ffn_in[1]], axis=1)
    features = time_features(timesteps.reshape(-1))
    own_features = lax.dynamic_slice_in_dim(
        features, me * mod_weight.shape[0], mod_weight.shape[0], 1
    )
    bias_share = mod_bias.shape[1]
    bias_wide = lax.dynamic_update_slice_in_dim(
        jnp.zeros((6, model_width), f32), mod_bias.astype(f32), me * bias_share, 1
    )
    mod_part = jnp.dot(
        own_features, mod_weight.astype(f32).reshape(mod_weight.shape[0], -1), precision=highest
    ) + bias_wide.reshape(1, -1)
    (
        attn_all,
        normed_near,
        normed_one_t,
        two,
        later,
        near_table,
        self_bias,
        cross_bias,
    ) = gather_and_prepare(attn_share, mod_part, latents, lengths, text_len)
    ffn_share, attn_all = lax.optimization_barrier((ffn_share, attn_all))
    ffn_all = lax.all_gather(ffn_share, "seq", axis=0, tiled=True)
    pair_w = attn_all[:, 6 * local :].reshape(seq_count, 2, text_width // seq_count, local)
    key_w = pair_w[:, 0].reshape(text_width, local)
    value_w = pair_w[:, 1].reshape(text_width, local)

    first_frame = me * block_rows
    first_item = jnp.sum((jnp.cumsum(lengths, axis=1) <= first_frame).astype(jnp.int32), axis=1)
    base_item = jnp.minimum(first_item, item_count - 2)
    catalog = jnp.arange(item_count, dtype=jnp.int32)

    ahead = [(i, i + 1) for i in range(seq_count - 1)]
    behind = [(i + 1, i) for i in range(seq_count - 1)]
    latent = latents.reshape(rows, model_width)
    cotangent = out_grad.reshape(rows, model_width)
    near_context = jnp.concatenate(
        [
            lax.dynamic_slice_in_dim(context[m], base_item[m] * TXT, 2 * TXT, 0)
            for m in range(micro)
        ]
    )
    column = local // 128

    qkv = project(normed_near, attn_all, near_table, local)
    mixed_one, logs_one, part_one = self_attention(
        qkv, self_bias, attn_all, 3 * column, micro, block_rows
    )
    got_one = swap(part_one)
    text_keys = nn(near_context, key_w).astype(bf16)
    text_values = nn(near_context, value_w).astype(bf16)
    hidden_one, _, normed_two_t, query_two = norm_forward(
        latent, part_one, got_one, two, later, 2, micro, attn_all, 4, local
    )
    mixed_two, logs_two, part_two = cross_attention(
        query_two, text_keys, text_values, cross_bias, attn_all, 5 * column, micro, block_rows
    )
    got_two = swap(part_two)
    hidden_two, normed_three, normed_three_t = norm_forward(
        hidden_one, part_two, got_two, two, later, 4, micro
    )
    g_outer, g_gate, g_up, out_part, back_three, *up_early = feed_forward(
        normed_three, normed_three_t, cotangent, ffn_all, hidden
    )
    outer_total = early_sum(g_outer)

    share = text_width // seq_count
    fused = (
        seq_count == 16 and lax.axis_size("tensor") == 2 and (model_width // seq_count) % 16 == 0
    )

    def cross_grads(two_low_t, query_two_low, text_key_low, text_value_low):
        pair_grad = jnp.concatenate(
            [
                tn(near_context, text_key_low).astype(bf16).reshape(seq_count, share, local),
                tn(near_context, text_value_low).astype(bf16).reshape(seq_count, share, local),
            ],
            axis=1,
        ).reshape(2 * text_width, local)
        return [
            nn(two_low_t, mixed_two).astype(bf16),
            nn(normed_two_t, query_two_low).astype(bf16),
            pair_grad,
        ]

    if fused:
        (
            hidden_two_grad, sums_three, two_low_t, query_two_low, text_key_low, text_value_low,
            back_two, got_early, totals_a,
        ) = cross_stage(
            back_three, cotangent, hidden_two, two, later, query_two, text_keys, text_values,
            cross_bias, logs_two, attn_all, local, [g_gate], ((0, EARLY_COLUMNS),), micro,
        )
        (
            hidden_one_grad, sums_two, one_low_t, own_grads, from_low, from_high, got_last,
            totals_b,
        ) = self_stage(
            back_two, got_early, hidden_two_grad, hidden_one, two, later, qkv, self_bias, logs_one,
            attn_all, local, out_part, [g_gate], ((EARLY_COLUMNS, hidden - EARLY_COLUMNS),), micro,
        )
        crossed = cross_grads(two_low_t, query_two_low, text_key_low, text_value_low)
        g_self_out = nn(one_low_t, mixed_one).astype(bf16)
        sums = jnp.concatenate([sums_two, sums_three], axis=2)
        late = g_up.shape[1]
        spans = ((0, late),) + ((0, local),) * 4
        sources = [g_up] + crossed + [g_self_out]
        totals_c, latent_grad, mod_grad, bias_sum, got_first = finish_stage(
            own_grads, from_low, from_high, normed_one_t, attn_all, near_table, hidden_one_grad,
            latent, two, later, sums, lengths, own_features, out_part,
            sources, spans, micro,
        )
        totals = [totals_c[:, late + k * local : late + (k + 1) * local] for k in range(4)]
        grad_cross_out, grad_cross_query, grad_cross_kv, grad_self_out = totals
        qkv_total = totals_c[:, late + 4 * local :]
        gate_total = jnp.concatenate([totals_a, totals_b], axis=1)
        up_total = jnp.concatenate([up_early[0], totals_c[:, :late]], axis=1)
        out_got = jnp.concatenate([got_first, got_last], axis=0)
    else:
        got_three = swap(back_three)
        gate_total = early_sum(g_gate)
        up_total = early_sum(g_up)
        hidden_two_grad, sums_three, two_low_t, mixed_two_grad = norm_back(
            cotangent, back_three, got_three, hidden_two, two, later, 4, micro, attn_all, 5, local
        )
        query_two_low, text_key_low, text_value_low, back_two = cross_attention_back(
            query_two, text_keys, text_values, cross_bias, mixed_two_grad, logs_two,
            attn_all, 4 * column, micro, block_rows,
        )
        got_back_two = swap(back_two)
        hidden_one_grad, sums_two, one_low_t, mixed_one_grad = norm_back(
            hidden_two_grad, back_two, got_back_two, hidden_one, two, later, 2, micro,
            attn_all, 3, local,
        )
        own_grads, to_low, to_high = self_attention_back(
            qkv, self_bias, mixed_one_grad, logs_one, micro, block_rows
        )
        from_high = lax.ppermute(to_low, "seq", behind)
        from_low = lax.ppermute(to_high, "seq", ahead)
        g_self_out = nn(one_low_t, mixed_one).astype(bf16)
        g_qkv, back_one = qkv_back(
            own_grads, from_low, from_high, normed_one_t, attn_all, near_table, micro, block_rows
        )
        crossed = cross_grads(two_low_t, query_two_low, text_key_low, text_value_low)
        sums = jnp.concatenate(
            [piece.reshape(micro, 2, 2 * model_width) for piece in (sums_two, sums_three)], axis=2
        )
        totals, latent_grad, mod_grad, bias_sum, out_got = finish_apart(
            crossed + [g_self_out, g_qkv], back_one, hidden_one_grad, latent, two, later, sums,
            lengths, own_features, out_part,
        )
        grad_cross_out, grad_cross_query, grad_cross_kv, grad_self_out, qkv_total = totals
    block_out = (hidden_two + (out_part.astype(f32) + out_got.astype(f32))).astype(bf16)
    mod_grad = mod_grad.reshape(mod_weight.shape)
    bias_grad = lax.dynamic_slice_in_dim(
        bias_sum.reshape(6, model_width), me * bias_share, bias_share, 1
    )

    grad_qkv = jnp.stack([qkv_total[:, i * local : (i + 1) * local] for i in range(3)])
    return (
        block_out.reshape(latents.shape),
        latent_grad.reshape(latents.shape),
        grad_qkv,
        grad_self_out.T,
        grad_cross_query,
        grad_cross_kv.reshape(2, share, local),
        grad_cross_out.T,
        jnp.stack([gate_total, up_total]),
        outer_total.T,
        mod_grad,
        bias_grad,
    )


def solution(mesh):
    return jax.shard_map(
        on_device,
        mesh=mesh,
        in_specs=(
            P(None, "seq", None),
            P(),
            P(),
            P(),
            P(),
            P(None, "seq", "tensor"),
            P("tensor", "seq"),
            P("seq", "tensor"),
            P(None, "seq", "tensor"),
            P("tensor", "seq"),
            P(None, "seq", "tensor"),
            P("tensor", "seq"),
            P("seq", None, None),
            P(None, "seq"),
            P(None, "seq", None),
        ),
        out_specs=(
            P(None, "seq", None),
            P(None, "seq", None),
            P(None, "seq", "tensor"),
            P("tensor", "seq"),
            P("seq", "tensor"),
            P(None, "seq", "tensor"),
            P("tensor", "seq"),
            P(None, "seq", "tensor"),
            P("tensor", "seq"),
            P("seq", None, None),
            P(None, "seq"),
        ),
        check_vma=False,
    )
```

```python
import functools
import math

import jax
import jax.numpy as jnp
import numpy as np
from jax import lax
from jax.experimental import pallas as pl
from jax.experimental.pallas import tpu as pltpu
from jax.sharding import PartitionSpec as P

HD = 64
TXT = 128
TEMB = 256
HALF = 128


norm_eps = 1e-05
highest = lax.Precision.HIGHEST
f32 = jnp.float32
bf16 = jnp.bfloat16


def dot(a, b, dims):
    return lax.dot_general(a, b, ((dims[0], dims[1]), ((), ())), preferred_element_type=f32)


def nn(a, b):
    return dot(a, b, ((1,), (0,)))


def nt(a, b):
    return dot(a, b, ((1,), (1,)))


def tn(a, b):
    return dot(a, b, ((0,), (0,)))


def halves(count):
    stride = 1
    strides = []
    while stride < count:
        strides.append(stride)
        stride *= 2
    return strides


def flip(block, stride):
    count = lax.axis_size("seq")
    return lax.ppermute(block, "seq", [(i, i ^ stride) for i in range(count)])


def swap(part):
    count = lax.axis_size("tensor")
    return lax.ppermute(part, "tensor", [(i, (i + 1) % count) for i in range(count)])


def seq_sum(part):
    for stride in halves(lax.axis_size("seq")):
        part = part + flip(part, stride)
    return part


def kernel_params(grid_rank, mib):
    return pltpu.CompilerParams(
        dimension_semantics=("arbitrary",) * grid_rank, vmem_limit_bytes=mib * 1024 * 1024
    )


STRIDES = (1, 2, 4, 8)


def seq_digits(me):
    return [(me // stride) % 2 for stride in STRIDES]


def greet(me, digits, others=(), mine=None):
    partners = [me + stride * (1 - 2 * digit) for stride, digit in zip(STRIDES, digits)]
    barrier = pltpu.get_barrier_semaphore()

    def tell(**target):
        pl.semaphore_signal(barrier, inc=1, device_id=target, device_id_type=pl.DeviceIdType.MESH)

    expected = len(partners)
    for partner in partners:
        tell(seq=partner)
    if mine is not None:
        tell(tensor=1 - mine)
        expected += 1
    for there, target in others:
        pl.when(there)(functools.partial(tell, seq=target))
        expected = expected + there.astype(jnp.int32)
    pl.semaphore_wait(barrier, expected)
    return partners


def send_to(partner, source, target, send_sem, recv_sem):
    return pltpu.make_async_remote_copy(
        src_ref=source,
        dst_ref=target,
        send_sem=send_sem,
        recv_sem=recv_sem,
        device_id={"seq": partner},
        device_id_type=pl.DeviceIdType.MESH,
    )


def greet_all(me, mine, digits, others=()):
    return greet(me, digits, others, mine)


def to_tensor(mine, source, target, send_sem, recv_sem):
    return pltpu.make_async_remote_copy(
        src_ref=source,
        dst_ref=target,
        send_sem=send_sem,
        recv_sem=recv_sem,
        device_id={"tensor": 1 - mine},
        device_id_type=pl.DeviceIdType.MESH,
    )


SMALL_STEPS = 6


def small_sum(partners, mine, core, fill, prep, held, got, total, finish, send_sem, recv_sem):
    own = 2 * mine + core
    half = pl.ds(2 * mine, 2)

    def exchange(k):
        sems = send_sem.at[k], recv_sem.at[k]
        if k == 0:
            return send_to(partners[0], prep.at[2 * mine + 1 - core], got.at[0], *sems)
        if k < 4:
            return send_to(partners[k], held.at[k], got.at[k], *sems)
        if k == 4:
            return send_to(partners[0], total.at[own], total.at[own], *sems)
        return to_tensor(mine, total.at[half], total.at[half], *sems)

    def step(k):
        if k == 0:
            fill(prep)
        else:
            exchange(k - 1).wait()
        if k == 1:
            held[1] = prep[own] + got[0]
        elif 1 < k < 4:
            held[k] = held[k - 1] + got[k - 1]
        elif k == 4:
            total[own] = held[3] + got[3]
        elif k == SMALL_STEPS:
            finish(total)
        if k < SMALL_STEPS:
            exchange(k).start()

    return step


def small_scratch(shape):
    quarter = (4, shape[0], shape[1] // 4)
    return [pltpu.VMEM(quarter, f32)] * 4 + [pltpu.SemaphoreType.DMA((SMALL_STEPS,))] * 2


def lane_ladder():
    quarter = HD // 4
    return np.exp(-math.log(10000.0) * (np.arange(128) % quarter) / quarter).astype(np.float32)


def prepare(first, frame_count, lengths, text_len, block_rows):
    items = len(lengths)
    ends = [lengths[0]]
    for length in lengths[1:]:
        ends.append(ends[-1] + length)

    def item_of(place):
        return sum((end <= place).astype(jnp.int32) for end in ends)

    def pick(ids, values):
        return sum(jnp.where(ids == k, value, 0) for k, value in enumerate(values))

    near_rows = block_rows + 2 * HALF
    place = first - HALF + lax.broadcasted_iota(jnp.int32, (near_rows, 1), 0)
    ids = item_of(place)
    offset = place - pick(ids, [end - length for end, length in zip(ends, lengths)])
    base = jnp.minimum(item_of(first), items - 2)
    own_ids = ids[HALF : HALF + block_rows]
    self_bias = []
    for part in range(block_rows // HALF):
        row = lax.broadcasted_iota(jnp.int32, (HALF, 1), 0)
        key = lax.broadcasted_iota(jnp.int32, (1, 3 * HALF), 1) - HALF
        key_place = first + part * HALF + key
        inside = (key_place >= 0) & (key_place < frame_count)
        key_ids = jnp.where(inside, item_of(key_place), -1)
        near_enough = jnp.abs(row - key) <= HALF
        same = own_ids[part * HALF : (part + 1) * HALF] == key_ids
        self_bias.append(jnp.where(near_enough & same, 0.0, -1e30))
    slot = lax.broadcasted_iota(jnp.int32, (1, 2 * TXT), 1)
    key_item = jnp.where(slot < TXT, base, base + 1)
    used = jnp.where(slot < TXT, slot, slot - TXT) < pick(key_item, text_len)
    key_item = jnp.where(used, key_item, -1)
    cross_bias = jnp.where(own_ids == key_item, 0.0, -1e30)
    later = (ids != base).astype(f32)
    return base, offset, later, self_bias, cross_bias


def lane_tables(offset, ladder):
    quarter = HD // 4
    angles = offset.astype(f32) * ladder
    lane = lax.broadcasted_iota(jnp.int32, angles.shape, 1) % HD
    cosine = jnp.cos(angles)
    sine = jnp.sin(angles)
    return (
        jnp.where(lane < 2 * quarter, cosine, 1.0),
        jnp.where((lane >= quarter) & (lane < 2 * quarter), sine, 0.0),
        jnp.where(lane < quarter, -sine, 0.0),
    )


def gather_kernel(
    share_ref, part_ref, latent_ref, lengths_ref, text_ref, ladder_ref,
    out_ref, near_normed_ref, normed_t_ref, two_ref, later_ref, table_ref, self_ref, cross_ref,
    near_ref, prep, held, got, total_ref, small_send, small_recv, copy_sem, send_sem, recv_sem,
    near_sem, halo_send, halo_recv, *, pieces, step, y_first, seq_count,
):
    micro, block_rows, width = latent_ref.shape
    items = lengths_ref.shape[1]
    near_rows = block_rows + 2 * HALF
    me = lax.axis_index("seq")
    digits = seq_digits(me)
    core, y, z_lo, z_hi = digits
    first = me * block_rows
    has_low = me > 0
    has_high = me < seq_count - 1
    mine = lax.axis_index("tensor")
    partners = greet_all(me, mine, digits, ((has_low, me - 1), (has_high, me + 1)))

    def fill(target):
        span = target.shape[2]
        for index in range(4):
            target[index] = part_ref[:, index * span : (index + 1) * span]

    small = small_sum(
        partners, mine, core, fill, prep, held, got, total_ref, lambda total: None,
        small_send, small_recv,
    )

    def to_low():
        return send_to(
            me - 1,
            latent_ref.at[:, :HALF],
            near_ref.at[:, near_rows - HALF :],
            halo_send.at[0],
            halo_recv.at[0],
        )

    def to_high():
        return send_to(
            me + 1,
            latent_ref.at[:, block_rows - HALF :],
            near_ref.at[:, :HALF],
            halo_send.at[1],
            halo_recv.at[1],
        )

    def load_own():
        return pltpu.make_async_copy(
            latent_ref, near_ref.at[:, HALF : near_rows - HALF], near_sem
        )

    def piece(p):
        return pl.ds(p * step, step)

    def exchange(p, stage):
        cols = piece(p)
        if p in y_first:
            axis = (1, 3, 2, 0)[stage]
            spots = ((z_hi, z_lo, y, core), (z_hi, z_lo, None, core), (None, z_lo, None, core), None)
        else:
            axis = (3, 2, 1, 0)[stage]
            spots = ((z_hi, z_lo, y, core), (None, z_lo, y, core), (None, None, y, core), None)
        spot = spots[stage] or (None, None, None, core)
        index = tuple(slice(None) if digit is None else digit for digit in spot)
        block = out_ref.at[index + (slice(None), cols)]
        source = share_ref.at[:, cols] if stage == 0 else block
        return send_to(partners[axis], source, block, send_sem.at[stage, p], recv_sem.at[stage, p])

    def own(p):
        return pltpu.make_async_copy(
            share_ref.at[:, piece(p)],
            out_ref.at[z_hi, z_lo, y, core, :, piece(p)],
            copy_sem.at[p],
        )

    def masks(m):
        base, offset, later, self_bias, cross_bias = prepare(
            first,
            seq_count * block_rows,
            [lengths_ref[m, k] for k in range(items)],
            [text_ref[m, k] for k in range(items)],
            block_rows,
        )
        rows = slice(m * block_rows, (m + 1) * block_rows)
        later_ref[rows, :] = later[HALF : HALF + block_rows]
        for part, bias in enumerate(self_bias):
            start = m * block_rows + part * HALF
            self_ref[start : start + HALF, :] = bias
        cross_ref[rows, :] = cross_bias
        state[m] = base, offset, later

    def tables(m, start):
        offset = state[m][1][start : start + HALF]
        target = m * near_rows + start
        for index, values in enumerate(lane_tables(offset, ladder_ref[...])):
            table_ref[index, target : target + HALF, :] = values

    def modulation(m, base):
        span = total_ref.shape[2]
        for which in range(2):
            for index in range(4):
                two_ref[m, which : which + 1, index * span : (index + 1) * span] = sum(
                    jnp.where(
                        base + which == k,
                        total_ref[index, m * items + k : m * items + k + 1],
                        0.0,
                    )
                    for k in range(items)
                )

    def norm(m, start):
        shift = [two_ref[m, which : which + 1, :width] for which in range(2)]
        factor = [two_ref[m, which : which + 1, width : 2 * width] for which in range(2)]
        tile = near_ref[m, start : start + HALF].astype(f32)
        chosen = state[m][2][start : start + HALF] > 0.5
        xhat, _ = spread_rows(tile)
        normed = (
            xhat * (1.0 + jnp.where(chosen, factor[1], factor[0]))
            + jnp.where(chosen, shift[1], shift[0])
        ).astype(bf16)
        target = m * near_rows + start
        near_normed_ref[target : target + HALF, :] = normed
        if HALF <= start < HALF + block_rows:
            target = m * block_rows + start - HALF
            normed_t_ref[:, target : target + HALF] = normed.T

    beside = {}
    state = {}
    gap = 3

    def add(t, work):
        beside.setdefault(t, []).append(work)

    def finish_near():
        load_own().wait()
        pl.when(has_low)(lambda: to_high().wait_recv())
        pl.when(has_high)(lambda: to_low().wait_recv())

    tick = 1
    for m in range(micro):
        add(tick, functools.partial(masks, m))
        for start in range(0, near_rows, HALF):
            tick += 1
            add(tick, functools.partial(tables, m, start))
        tick += 1
    for k in range(1, SMALL_STEPS + 1):
        add(gap * k, functools.partial(small, k))
    tick = gap * SMALL_STEPS
    add(tick, finish_near)
    for m in range(micro):
        tick += 1
        add(tick, lambda m=m: modulation(m, state[m][0]))
        for start in range(0, near_rows, HALF):
            add(tick, functools.partial(norm, m, start))
            tick += 1
    last_tick = tick

    small(0)
    load_own().start()
    pl.when(has_low)(lambda: to_low().start())
    pl.when(has_high)(lambda: to_high().start())

    @pl.when(jnp.logical_not(has_low))
    def _():
        near_ref[:, :HALF] = jnp.zeros((micro, HALF, width), near_ref.dtype)

    @pl.when(jnp.logical_not(has_high))
    def _():
        near_ref[:, near_rows - HALF :] = jnp.zeros((micro, HALF, width), near_ref.dtype)

    lags = (0, 3, 6, 10, 12)
    for t in range(max(pieces + lags[-1], last_tick + 1)):
        if t < pieces:
            exchange(t, 0).start()
            own(t).start()
        for stage in (1, 2, 3):
            p = t - lags[stage]
            if 0 <= p < pieces:
                if stage == 1:
                    own(p).wait()
                exchange(p, stage - 1).wait_recv()
                exchange(p, stage).start()
        if 0 <= t - lags[4] < pieces:
            exchange(t - lags[4], 3).wait_recv()
        for work in beside.get(t, ()):
            work()
    for p in range(pieces):
        for stage in range(4):
            exchange(p, stage).wait_send()
    pl.when(has_low)(lambda: to_low().wait_send())
    pl.when(has_high)(lambda: to_high().wait_send())


def gather_and_prepare(share, part, latents, lengths, text_len, step=256):
    count = lax.axis_size("seq")
    me = lax.axis_index("seq")
    rows, width = share.shape
    micro, block_rows, model_width = latents.shape
    items = lengths.shape[1]
    near_rows = block_rows + 2 * HALF
    own_rows = micro * block_rows
    ladder = jnp.asarray(lane_ladder()).reshape(1, 128)
    if count != 16 or rows % 16 or width % step or lax.axis_size("tensor") != 2:
        ahead = [(i, i + 1) for i in range(count - 1)]
        behind = [(i + 1, i) for i in range(count - 1)]
        low_rows = lax.ppermute(latents[:, block_rows - HALF :], "seq", ahead)
        high_rows = lax.ppermute(latents[:, :HALF], "seq", behind)
        near_latent = jnp.concatenate([low_rows, latents, high_rows], axis=1)
        total = seq_sum(part).reshape(micro, items, 6 * model_width)
        parts = []
        for m in range(micro):
            base, offset, later, self_bias, cross_bias = prepare(
                me * block_rows,
                count * block_rows,
                [lengths[m, k] for k in range(items)],
                [text_len[m, k] for k in range(items)],
                block_rows,
            )
            two = lax.dynamic_slice_in_dim(total[m], base, 2, 0)
            xhat, _ = spread_rows(near_latent[m].astype(f32))
            shift, factor = [
                jnp.where(later > 0.5, two[1], two[0])[:, i * model_width : (i + 1) * model_width]
                for i in range(2)
            ]
            normed = (xhat * (1.0 + factor) + shift).astype(bf16)
            parts.append(
                (
                    normed,
                    normed[HALF : HALF + block_rows].T,
                    two[None],
                    later[HALF : HALF + block_rows],
                    jnp.stack(lane_tables(offset, ladder)),
                    jnp.concatenate(self_bias, axis=0),
                    cross_bias,
                )
            )
        axes = (0, 1, 0, 0, 1, 0, 0)
        joined = [jnp.concatenate(group, axis=axis) for group, axis in zip(zip(*parts), axes)]
        return [lax.all_gather(share, "seq", axis=0, tiled=True)] + joined
    pieces = width // step
    any_space = pl.BlockSpec(memory_space=pl.ANY)
    vmem = pl.BlockSpec(memory_space=pltpu.VMEM)
    smem = pl.BlockSpec(memory_space=pltpu.SMEM)
    outs = pl.pallas_call(
        functools.partial(
            gather_kernel,
            pieces=pieces,
            step=step,
            y_first=tuple(range(pieces // 6, pieces, pieces // 3)),
            seq_count=count,
        ),
        out_shape=[
            jax.ShapeDtypeStruct((2, 2, 2, 2, rows, width), share.dtype),
            jax.ShapeDtypeStruct((micro * near_rows, model_width), bf16),
            jax.ShapeDtypeStruct((model_width, own_rows), bf16),
            jax.ShapeDtypeStruct((micro, 2, 6 * model_width), f32),
            jax.ShapeDtypeStruct((own_rows, 1), f32),
            jax.ShapeDtypeStruct((3, micro * near_rows, 128), f32),
            jax.ShapeDtypeStruct((own_rows, 3 * HALF), f32),
            jax.ShapeDtypeStruct((own_rows, 2 * TXT), f32),
        ],
        in_specs=[any_space, vmem, any_space, smem, smem, vmem],
        out_specs=[any_space] + [vmem] * 7,
        scratch_shapes=[
            pltpu.VMEM((micro, near_rows, model_width), bf16),
        ]
        + small_scratch(part.shape)
        + [
            pltpu.SemaphoreType.DMA((pieces,)),
            pltpu.SemaphoreType.DMA((4, pieces)),
            pltpu.SemaphoreType.DMA((4, pieces)),
            pltpu.SemaphoreType.DMA,
            pltpu.SemaphoreType.DMA((2,)),
            pltpu.SemaphoreType.DMA((2,)),
        ],
        compiler_params=pltpu.CompilerParams(
            collective_id=1, has_side_effects=True, vmem_limit_bytes=48 * 1024 * 1024
        ),
        cost_estimate=pl.CostEstimate(
            flops=0, bytes_accessed=20 * count * rows * width, transcendentals=0
        ),
        name="gather_and_prepare",
    )(share, part, latents, lengths, text_len, ladder)
    return [outs[0].reshape(count * rows, width)] + list(outs[1:])


SLOTS = 6


def when(condition):
    if isinstance(condition, bool):
        return (lambda work: work()) if condition else (lambda work: None)
    return pl.when(condition)


class Pieces:
    def __init__(self, refs, out_ref, partners, digits, step, lag=3):
        (
            self.own, self.got0, self.got1, self.got2, self.got3, self.staged,
            self.out_sem, self.send_sem, self.recv_sem,
        ) = refs
        self.out_ref = out_ref
        self.partners = partners
        self.digits = digits
        self.step = step
        self.lag = lag

    @staticmethod
    def scratch(rows, step):
        return [
            pltpu.VMEM((SLOTS, 2, 2, 2, rows, step), bf16),
            pltpu.VMEM((SLOTS, 2, 2, 2, rows, step), bf16),
            pltpu.VMEM((SLOTS, 2, 2, rows, step), bf16),
            pltpu.VMEM((SLOTS, 2, rows, step), bf16),
            pltpu.VMEM((SLOTS, rows, step), bf16),
            pltpu.VMEM((SLOTS, rows, step), f32),
            pltpu.SemaphoreType.DMA((SLOTS,)),
            pltpu.SemaphoreType.DMA((4, SLOTS)),
            pltpu.SemaphoreType.DMA((4, SLOTS)),
        ]

    def exchange(self, stage, source, target, slot):
        return send_to(
            self.partners[stage],
            source,
            target,
            self.send_sem.at[stage, slot],
            self.recv_sem.at[stage, slot],
        )

    def over_core(self, source, slot):
        return self.exchange(0, source, self.got0.at[slot], slot)

    PATHS = ((2, 1, 0),)

    def spot(self, path, stage, other):
        axes = (self.digits[3], self.digits[2], self.digits[1])
        index = [slice(None)] * 3
        for axis in path[: stage - 1]:
            index[axis] = axes[axis]
        axis = path[stage - 1]
        index[axis] = 1 - axes[axis] if other else axes[axis]
        return tuple(index)

    def hop(self, path, stage, slot):
        partner = (3, 2, 1)[path[stage - 1]]
        target = (self.got1, self.got2, self.got3)[stage - 1].at[slot]
        source = self.own.at[(slot,) + self.spot(path, stage, True)]
        return send_to(
            self.partners[partner],
            source,
            target,
            self.send_sem.at[stage, slot],
            self.recv_sem.at[stage, slot],
        )

    def by_path(self, item, work):
        work(self.PATHS[0])

    def add_hop(self, path, stage, slot):
        got = (self.got1, self.got2, self.got3)[stage - 1]
        index = self.spot(path, stage, False)
        free = [k for k in range(3) if isinstance(index[k], slice)]
        for count in range(2 ** len(free)):
            bits = [(count >> k) & 1 for k in range(len(free))]
            full = list(index)
            for k, bit in zip(free, bits):
                full[k] = bit
            at = (slot,) + tuple(full)
            total = self.own[at].astype(f32) + got[(slot,) + tuple(bits)].astype(f32)
            if stage < 3:
                self.own[at] = total.astype(bf16)
            else:
                self.staged[slot] = total

    def store(self, item, slot):
        columns = pl.ds(pl.multiple_of(item * self.step, self.step), self.step)
        return pltpu.make_async_copy(
            self.staged.at[slot], self.out_ref.at[:, columns], self.out_sem.at[slot]
        )

    def wait_sent(self, slot):
        for stage in (1, 2, 3):
            self.hop(self.PATHS[0], stage, slot).wait_send()

    def add_core(self, item, slot, left):
        for i in range(2):
            for j in range(2):
                for k in range(2):
                    total = left(i, j, k).astype(f32) + self.got0[slot, i, j, k].astype(f32)
                    self.own[slot, i, j, k] = total.astype(bf16)
        self.by_path(item, lambda path: self.hop(path, 1, slot).start())

    def later_steps(self, t, count):
        lag = self.lag

        @when((t >= lag) & (t - lag < count))
        def _():
            item = t - lag
            slot = item % SLOTS
            self.hop(self.PATHS[0], 1, slot).wait_recv()

            def work(path):
                self.add_hop(path, 1, slot)
                self.hop(path, 2, slot).start()

            self.by_path(item, work)

        @when((t >= lag + 1) & (t - lag - 1 < count))
        def _():
            item = t - lag - 1
            slot = item % SLOTS
            self.hop(self.PATHS[0], 2, slot).wait_recv()

            def work(path):
                self.add_hop(path, 2, slot)
                self.hop(path, 3, slot).start()

            self.by_path(item, work)

        @when((t >= lag + 2) & (t - lag - 2 < count))
        def _():
            item = t - lag - 2
            slot = item % SLOTS
            self.hop(self.PATHS[0], 3, slot).wait_recv()
            when(item >= SLOTS)(lambda: self.store(0, slot).wait())
            self.by_path(item, lambda path: self.add_hop(path, 3, slot))
            self.store(item, slot).start()

    def run(self, sources, spans, own_sem, beside=(), last=0):
        core = self.digits[0]
        step = self.step
        count = sum(width for _, width in spans) // step

        def over_core(source, column, slot):
            return self.over_core(source.at[:, :, :, 1 - core, :, pl.ds(column, step)], slot)

        def load(source, column, slot):
            return pltpu.make_async_copy(
                source.at[:, :, :, core, :, pl.ds(column, step)],
                self.own.at[slot],
                own_sem.at[slot],
            )

        def tick(t, carry):
            @pl.when(t < count)
            def _():
                slot = t % SLOTS
                pl.when(t >= SLOTS)(lambda: self.wait_sent(slot))
                done = 0
                for source, (column, width) in zip(sources, spans):

                    @pl.when((t >= done) & (t < done + width // step))
                    def _(source=source, done=done, column=column):
                        spot = pl.multiple_of(column + (t - done) * step, step)
                        over_core(source, spot, slot).start()
                        load(source, spot, slot).start()

                    done += width // step

            @pl.when((t >= 1) & (t - 1 < count))
            def _():
                slot = (t - 1) % SLOTS
                load(sources[0], 0, slot).wait()
                over_core(sources[0], 0, slot).wait()
                self.add_core(t - 1, slot, lambda i, j, k: self.own[slot, i, j, k])

            self.later_steps(t, count)
            for begin, end, work in beside:
                pl.when((t >= begin) & (t < end))(functools.partial(work, t))
            return carry

        lax.fori_loop(0, max(count + self.lag + 2, last + 1), tick, 0)
        self.finish(count)

    def finish(self, count):
        for back in range(min(SLOTS, count)):
            slot = (count - 1 - back) % SLOTS
            self.store(0, slot).wait()
            self.wait_sent(slot)


PIECE_REFS = 9


def norm_back_tile(grad, upstream, hidden, shift_rows, factor):
    xhat, scale = spread_rows(hidden)
    inner = grad * (1.0 + factor)
    mean_inner = jnp.mean(inner, axis=-1, keepdims=True)
    mean_cross = jnp.mean(inner * xhat, axis=-1, keepdims=True)
    total = upstream + scale * (inner - mean_inner - xhat * mean_cross)
    scaled = grad * xhat
    sums = [
        [
            jnp.sum(jnp.where(chosen, values, 0.0), axis=0, keepdims=True)
            for values in (grad, scaled)
        ]
        for chosen in shift_rows
    ]
    return total, sums


def finish_kernel(*refs, spans, step, micro, loaded):
    refs = list(refs)
    sources = [refs.pop(0) for _ in spans]
    (
        own_ref, from_low_ref, from_high_ref, normed_t_ref, weight_ref, table_ref,
        up_ref, latent_ref, two_ref, later_ref, sums_ref, lengths_ref, feature_ref, other_ref,
        out_ref, grad_ref, mod_ref, bias_ref, got_other_ref,
        own_sem, back_ref, got_back, qkv_w_ref, weight_sem, g_qkv_ref, first_sums,
        back_send, back_recv, other_sem,
    ) = refs[:29]
    pieces_refs = refs[29 : 29 + PIECE_REFS]
    prep, held, got, small_total, small_send, small_recv = refs[29 + PIECE_REFS :]
    me = lax.axis_index("seq")
    mine = lax.axis_index("tensor")
    digits = seq_digits(me)
    core = digits[0]
    rows, width = latent_ref.shape
    local = own_ref.shape[2]
    block_rows = rows // micro
    near_rows = block_rows + 2 * HALF
    items = lengths_ref.shape[1]
    load = pltpu.make_async_copy(weight_ref.at[:, : 3 * local], qkv_w_ref, weight_sem)
    load.start()
    partners = greet_all(me, mine, digits)
    pieces = Pieces(pieces_refs, out_ref, partners, digits, step)

    def over_tensor(m):
        span = pl.ds(m * block_rows, block_rows)
        return to_tensor(
            mine, back_ref.at[span], got_back.at[span], back_send.at[m], back_recv.at[m]
        )

    def own_table(index):
        return jnp.concatenate(
            [
                table_ref[index, m * near_rows + HALF : (m + 1) * near_rows - HALF]
                for m in range(micro)
            ],
            axis=0,
        )

    def project_back(kind, column):
        lanes = pl.ds(pl.multiple_of(column, step), step)
        total = own_ref[kind, :, lanes]
        if kind:
            blocks = []
            for m in range(micro):
                first = m * block_rows
                blocks.append(
                    total[first : first + HALF] + from_low_ref[m, kind - 1, :, lanes].astype(f32)
                )
                if block_rows > 2 * HALF:
                    blocks.append(total[first + HALF : first + block_rows - HALF])
                blocks.append(
                    total[first + block_rows - HALF : first + block_rows]
                    + from_high_ref[m, kind - 1, :, lanes].astype(f32)
                )
            total = jnp.concatenate(blocks, axis=0)
        if kind < 2:
            tables = own_table(0), -own_table(1), -own_table(2)
            total = jnp.concatenate(
                [turn(total[:, i : i + 128], *tables) for i in range(0, step, 128)], axis=1
            )
        grad = total.astype(bf16)
        lanes = pl.ds(pl.multiple_of(kind * local + column, step), step)
        g_qkv_ref[:, :, :, :, :, lanes] = (
            nn(normed_t_ref[...], grad).astype(bf16).reshape(g_qkv_ref.shape[:5] + (step,))
        )
        grad_ref[...] += nt(grad, qkv_w_ref[:, lanes])

    def send_back():
        back_ref[...] = grad_ref[...].astype(bf16)
        for m in range(micro):
            over_tensor(m).start()

    def norm_one(m):
        over_tensor(m).wait_recv()

        def emit(span, start, total):
            grad_ref[span, :] = total

        norm_back_unit(
            m, 0, block_rows,
            lambda span: back_ref[span, :].astype(f32) + got_back[span, :].astype(f32),
            up_ref, latent_ref, two_ref, later_ref, first_sums, emit,
        )

    def fill(target):
        span = target.shape[2]
        size = 128 * math.gcd(span // 128, width // 128)
        for m in range(micro):
            ends = [lengths_ref[m, 0]]
            for k in range(1, items):
                ends.append(ends[-1] + lengths_ref[m, k])
            first_item = sum((end <= me * block_rows).astype(jnp.int32) for end in ends)
            base = jnp.minimum(first_item, items - 2)
            for k in range(items):
                row = slice(m * items + k, m * items + k + 1)
                for first in range(0, 6 * width, size):
                    ref, at = (
                        (first_sums, first) if first < 2 * width else (sums_ref, first - 2 * width)
                    )
                    target[first // span, row, first % span : first % span + size] = sum(
                        jnp.where(
                            base + item == k, ref[m, item : item + 1, at : at + size], 0.0
                        )
                        for item in range(2)
                    )

    def modulation_grads(total):
        span = total.shape[2]
        for index in range(4):
            lanes = slice(index * span, (index + 1) * span)
            bias_ref[:, lanes] = jnp.sum(total[index], axis=0, keepdims=True)
            mod_ref[:, lanes] = sum(
                feature_ref[:, i : i + 1] * total[index, i : i + 1] for i in range(micro * items)
            )

    small = small_sum(
        partners, mine, core, fill, prep, held, got, small_total, modulation_grads,
        small_send, small_recv,
    )
    work = []
    spot = 0
    columns = local // step
    work.append((0, 1, lambda t: loaded()))
    work.append((0, 1, lambda t: load.wait()))
    spot = 1
    for kind in range(3):
        work.append(
            (spot, spot + columns, lambda t, k=kind, s=spot: project_back(k, (t - s) * step))
        )
        spot += columns
    work.append((spot - 1, spot, lambda t: send_back()))
    spot += 3
    for m in range(micro):
        work.append((spot, spot + 1, lambda t, m=m: norm_one(m)))
        spot += 4 if m < micro - 1 else 1
    for k in range(SMALL_STEPS + 1):
        work.append((spot, spot + 1, lambda t, k=k: small(k)))
        spot += 2 if k < 3 else 1
    grad_ref[...] = jnp.zeros_like(grad_ref)
    over_other = to_tensor(
        mine, other_ref.at[pl.ds(0, block_rows)], got_other_ref, other_sem.at[0], other_sem.at[1]
    )
    over_other.start()
    pieces.run(sources + [g_qkv_ref], spans + ((0, 3 * local),), own_sem, work, spot)
    for m in range(micro):
        over_tensor(m).wait_send()
    over_other.wait()


def finish_stage(
    own, from_low, from_high, normed_t, weights, table, upstream, latent, two, later, sums,
    lengths, features, other, sources, spans, micro, which=0, step=256,
):
    seq_count = lax.axis_size("seq")
    rows, width = latent.shape
    items = lengths.shape[1]
    local = own.shape[2]
    share = width // seq_count
    own_features = features.T
    any_space = pl.BlockSpec(memory_space=pl.ANY)
    vmem = pl.BlockSpec(memory_space=pltpu.VMEM)
    smem = pl.BlockSpec(memory_space=pltpu.SMEM)
    args = [
        own, from_low, from_high, normed_t, weights, table,
        upstream, latent, two, later, sums, lengths, own_features, other,
    ]
    places = (0, 1, 2, 3, 5, 6, 7, 8, 9, 10)
    return pl.pallas_call(
        with_loads(
            functools.partial(finish_kernel, spans=spans, step=step, micro=micro),
            [len(sources) + place for place in places],
        ),
        out_shape=[
            jax.ShapeDtypeStruct((share, sum(span for _, span in spans) + 3 * local), f32),
            jax.ShapeDtypeStruct((rows, width), f32),
            jax.ShapeDtypeStruct((own_features.shape[0], 6 * width), f32),
            jax.ShapeDtypeStruct((1, 6 * width), f32),
            jax.ShapeDtypeStruct((rows // micro, width), bf16),
        ],
        in_specs=[any_space] * (len(sources) + 11) + [smem, vmem, any_space],
        out_specs=[any_space, vmem, vmem, vmem, any_space],
        scratch_shapes=[
            pltpu.SemaphoreType.DMA((SLOTS,)),
            pltpu.VMEM((rows, width), bf16),
            pltpu.VMEM((rows, width), bf16),
            pltpu.VMEM((width, 3 * local), bf16),
            pltpu.SemaphoreType.DMA,
            pltpu.VMEM((2, 2, 2, 2, share, 3 * local), bf16),
            pltpu.VMEM((micro, 2, 2 * width), f32),
            pltpu.SemaphoreType.DMA((micro,)),
            pltpu.SemaphoreType.DMA((micro,)),
            pltpu.SemaphoreType.DMA((2,)),
        ]
        + Pieces.scratch(share, step)
        + small_scratch((micro * items, 6 * width))
        + load_scratch([args[place] for place in places]),
        compiler_params=pltpu.CompilerParams(
            collective_id=which, has_side_effects=True, vmem_limit_bytes=60 * 1024 * 1024
        ),
        cost_estimate=pl.CostEstimate(
            flops=12 * rows * width * local, bytes_accessed=40 * rows * width, transcendentals=0
        ),
        name="finish_stage",
    )(
        *[source.reshape(2, 2, 2, 2, share, source.shape[1]) for source in sources],
        *args,
    )


def finish_apart(grads, back, upstream, latent, two, later, sums, lengths, features, other):
    rows, width = latent.shape
    micro, items = lengths.shape
    totals = [early_sum(grad) for grad in grads]
    latent_grad, first_sums = norm_back(upstream, back, swap(back), latent, two, later, 0, micro)
    pieces = jnp.concatenate([first_sums.reshape(micro, 2, 2 * width), sums], axis=2)
    first_item = jnp.sum(
        (jnp.cumsum(lengths, axis=1) <= lax.axis_index("seq") * (rows // micro)).astype(jnp.int32),
        axis=1,
    )
    base = jnp.minimum(first_item, items - 2)
    spots = (base[:, None] + jnp.arange(2))[:, :, None] == jnp.arange(items)
    item_grad = jnp.sum(jnp.where(spots[..., None], pieces[:, :, None], 0.0), axis=1)
    total = seq_sum(item_grad.reshape(micro * items, 6 * width))
    mod_grad = jnp.dot(features.T, total, precision=highest)
    return totals, latent_grad, mod_grad, jnp.sum(total, axis=0, keepdims=True), swap(other)


def early_sum(grad):
    return lax.psum_scatter(grad, "seq", scatter_dimension=0, tiled=True).astype(f32)


def turn(values, own, below, above):
    quarter = HD // 4
    return (
        values * own
        + pltpu.roll(values, quarter, 1) * below
        + pltpu.roll(values, 2 * HD - quarter, 1) * above
    )


def project_kernel(normed_ref, weight_ref, table_ref, out_ref, *, turned):
    j = pl.program_id(0)
    product = nn(normed_ref[...], weight_ref[...])

    @pl.when(j < turned)
    def _():
        for part in range(product.shape[1] // 128):
            lanes = slice(part * 128, (part + 1) * 128)
            out_ref[:, lanes] = turn(
                product[:, lanes], table_ref[0], table_ref[1], table_ref[2]
            ).astype(bf16)

    @pl.when(j >= turned)
    def _():
        out_ref[...] = product.astype(bf16)


def project(normed, weights, table, local, step=256):
    rows, width = normed.shape
    return pl.pallas_call(
        functools.partial(project_kernel, turned=2 * local // step),
        grid=(3 * local // step,),
        in_specs=[
            pl.BlockSpec((rows, width), lambda j: (0, 0)),
            pl.BlockSpec((width, step), lambda j: (0, j)),
            pl.BlockSpec((3, rows, 128), lambda j: (0, 0, 0)),
        ],
        out_specs=pl.BlockSpec((rows, step), lambda j: (0, j)),
        out_shape=jax.ShapeDtypeStruct((rows, 3 * local), bf16),
        compiler_params=kernel_params(1, 32),
        cost_estimate=pl.CostEstimate(
            flops=2 * rows * width * 3 * local,
            bytes_accessed=2 * (rows * width + 3 * local * (width + rows)),
            transcendentals=0,
        ),
        name="qkv_projection",
    )(normed, weights, table)


def head_lanes(shape):
    return lax.broadcasted_iota(jnp.int32, shape, 1) < HD


def one_head(values, first, which):
    return jnp.where(first if which == 0 else ~first, values, jnp.zeros_like(values))


def soft_rows(scores):
    peak = jnp.max(scores, axis=-1, keepdims=True)
    raised = jnp.exp(scores - peak)
    total = jnp.sum(raised, axis=-1, keepdims=True)
    return raised * (1.0 / total), peak + jnp.log(total)


def attend_rows(query, keys, values, bias):
    first = head_lanes(query.shape)
    out = None
    logs = []
    for which in range(2):
        scores = nt(one_head(query, first, which), keys) * (HD**-0.5) + bias
        weights, log_total = soft_rows(scores)
        mixed = nn(weights.astype(bf16), values)
        out = mixed if which == 0 else jnp.where(first, out, mixed)
        logs.append(log_total)
    return out, logs


def attend_rows_back(query, keys, values, bias, logs, grad):
    first = head_lanes(query.shape)
    query_grad = key_grad = value_grad = None
    for which in range(2):
        own_query = one_head(query, first, which)
        own_grad = one_head(grad, first, which)
        scores = nt(own_query, keys) * (HD**-0.5) + bias
        chances = jnp.exp(scores - logs[which])
        chance_grad = nt(own_grad, values)
        score_grad = (
            chances * (chance_grad - jnp.sum(chances * chance_grad, axis=-1, keepdims=True))
        ).astype(bf16)
        to_query = nn(score_grad, keys) * (HD**-0.5)
        to_key = tn(score_grad, own_query) * (HD**-0.5)
        to_value = tn(chances.astype(bf16), own_grad)
        if which == 0:
            query_grad, key_grad, value_grad = to_query, to_key, to_value
        else:
            query_grad = jnp.where(first, query_grad, to_query)
            key_grad = key_grad + to_key
            value_grad = value_grad + to_value
    return query_grad, key_grad, value_grad


def put_logs(log_ref, rows, logs, pair):
    lane = lax.broadcasted_iota(jnp.int32, (logs[0].shape[0], 128), 1)
    kept = log_ref[rows, :]
    kept = jnp.where(lane == 2 * pair, logs[0], kept)
    log_ref[rows, :] = jnp.where(lane == 2 * pair + 1, logs[1], kept)


def get_logs(log_ref, rows, pair):
    kept = log_ref[rows, :]
    lane = lax.broadcasted_iota(jnp.int32, kept.shape, 1)
    return [
        jnp.sum(jnp.where(lane == 2 * pair + which, kept, 0.0), axis=1, keepdims=True)
        for which in range(2)
    ]


def spread_rows(hidden):
    center = hidden - jnp.mean(hidden, axis=-1, keepdims=True)
    spread = jnp.mean(center * center, axis=-1, keepdims=True)
    scale = lax.rsqrt(spread + norm_eps)
    return center * scale, scale


def item_row(two_ref, later_ref, index):
    width = two_ref.shape[2] // 6
    lanes = slice(index * width, (index + 1) * width)
    return jnp.where(later_ref[...] > 0.5, two_ref[0, 1:2, lanes], two_ref[0, 0:1, lanes])


def norm_kernel(*refs, index, with_weight):
    refs = list(refs)
    base_ref, own_ref, got_ref, two_ref, later_ref = refs[:5]
    weight_ref = refs[5] if with_weight else None
    outs = refs[5 + with_weight :]
    hidden = (
        base_ref[...].astype(f32) + own_ref[...].astype(f32) + got_ref[...].astype(f32)
    )
    xhat, _ = spread_rows(hidden)
    normed = (
        xhat * (1.0 + item_row(two_ref, later_ref, index + 1)) + item_row(two_ref, later_ref, index)
    ).astype(bf16)
    outs[0][...] = hidden
    outs[1][...] = normed
    outs[2][...] = normed.T
    if with_weight:
        outs[3][...] = nn(normed, weight_ref[...]).astype(bf16)


def norm_forward(base, own, got, two, later, index, micro, weights=None, column=0, out_width=0):
    rows, width = base.shape
    tile = rows // micro
    row_tile = pl.BlockSpec((tile, width), lambda i: (i, 0))
    in_specs = [
        row_tile,
        row_tile,
        row_tile,
        pl.BlockSpec((1, 2, 6 * width), lambda i: (i, 0, 0)),
        pl.BlockSpec((tile, 1), lambda i: (i, 0)),
    ]
    out_specs = [row_tile, row_tile, pl.BlockSpec((width, tile), lambda i: (0, i))]
    out_shape = [
        jax.ShapeDtypeStruct((rows, width), f32),
        jax.ShapeDtypeStruct((rows, width), bf16),
        jax.ShapeDtypeStruct((width, rows), bf16),
    ]
    args = [base, own, got, two, later]
    if weights is not None:
        in_specs.append(pl.BlockSpec((width, out_width), lambda i: (0, column)))
        out_specs.append(pl.BlockSpec((tile, out_width), lambda i: (i, 0)))
        out_shape.append(jax.ShapeDtypeStruct((rows, out_width), bf16))
        args.append(weights)
    return pl.pallas_call(
        functools.partial(norm_kernel, index=index, with_weight=weights is not None),
        grid=(micro,),
        in_specs=in_specs,
        out_specs=out_specs,
        out_shape=out_shape,
        compiler_params=kernel_params(1, 40),
        cost_estimate=pl.CostEstimate(
            flops=2 * rows * width * out_width, bytes_accessed=16 * rows * width, transcendentals=0
        ),
        name="norm_forward",
    )(*args)


def norm_back_kernel(*refs, index, with_weight):
    refs = list(refs)
    up_ref, own_ref, got_ref, hidden_ref, two_ref, later_ref = refs[:6]
    weight_ref = refs[6] if with_weight else None
    outs = refs[6 + with_weight :]
    xhat, scale = spread_rows(hidden_ref[...].astype(f32))
    grad = own_ref[...].astype(f32) + got_ref[...].astype(f32)
    inner = grad * (1.0 + item_row(two_ref, later_ref, index + 1))
    mean_inner = jnp.mean(inner, axis=-1, keepdims=True)
    mean_cross = jnp.mean(inner * xhat, axis=-1, keepdims=True)
    total = up_ref[...].astype(f32) + scale * (inner - mean_inner - xhat * mean_cross)
    outs[0][...] = total
    later = later_ref[...] > 0.5
    scaled = grad * xhat
    for item in range(2):
        chosen = later if item else ~later
        outs[1][0, item, 0:1] = jnp.sum(jnp.where(chosen, grad, 0.0), axis=0, keepdims=True)
        outs[1][0, item, 1:2] = jnp.sum(jnp.where(chosen, scaled, 0.0), axis=0, keepdims=True)
    if with_weight:
        rounded = total.astype(bf16)
        outs[2][...] = rounded.T
        outs[3][...] = nn(rounded, weight_ref[...]).astype(bf16)


def norm_back(up, own, got, hidden, two, later, index, micro, weights=None, column=0, out_width=0):
    rows, width = hidden.shape
    tile = rows // micro
    row_tile = pl.BlockSpec((tile, width), lambda i: (i, 0))
    in_specs = [
        row_tile,
        row_tile,
        row_tile,
        row_tile,
        pl.BlockSpec((1, 2, 6 * width), lambda i: (i, 0, 0)),
        pl.BlockSpec((tile, 1), lambda i: (i, 0)),
    ]
    out_specs = [row_tile, pl.BlockSpec((1, 2, 2, width), lambda i: (i, 0, 0, 0))]
    out_shape = [
        jax.ShapeDtypeStruct((rows, width), f32),
        jax.ShapeDtypeStruct((micro, 2, 2, width), f32),
    ]
    args = [up, own, got, hidden, two, later]
    if weights is not None:
        in_specs.append(pl.BlockSpec((width, out_width), lambda i: (0, column)))
        out_specs += [
            pl.BlockSpec((width, tile), lambda i: (0, i)),
            pl.BlockSpec((tile, out_width), lambda i: (i, 0)),
        ]
        out_shape += [
            jax.ShapeDtypeStruct((width, rows), bf16),
            jax.ShapeDtypeStruct((rows, out_width), bf16),
        ]
        args.append(weights)
    return pl.pallas_call(
        functools.partial(norm_back_kernel, index=index, with_weight=weights is not None),
        grid=(micro,),
        in_specs=in_specs,
        out_specs=out_specs,
        out_shape=out_shape,
        compiler_params=kernel_params(1, 48),
        cost_estimate=pl.CostEstimate(
            flops=2 * rows * width * out_width, bytes_accessed=20 * rows * width, transcendentals=0
        ),
        name="norm_back",
    )(*args)


def add_product(acc_ref, out_ref, left, right):
    pair = pl.program_id(1)

    @pl.when(pair == 0)
    def _():
        acc_ref[...] = jnp.zeros_like(acc_ref)

    acc_ref[...] += nt(left, right)

    @pl.when(pair == pl.num_programs(1) - 1)
    def _():
        out_ref[...] = acc_ref[...].astype(bf16)


def self_kernel(q_ref, k_ref, v_ref, bias_ref, weight_ref, out_ref, log_ref, sum_ref, acc_ref):
    pair = pl.program_id(1)
    block_rows = out_ref.shape[0]
    for part in range(block_rows // HALF):
        rows = slice(part * HALF, (part + 1) * HALF)
        span = slice(part * HALF, (part + 3) * HALF)
        out, logs = attend_rows(
            q_ref[(part + 1) * HALF : (part + 2) * HALF, :],
            k_ref[span, :],
            v_ref[span, :],
            bias_ref[rows, :],
        )
        out_ref[rows, :] = out.astype(bf16)
        put_logs(log_ref, rows, logs, pair)
    add_product(acc_ref, sum_ref, out_ref[...], weight_ref[...])


def self_specs(block_rows, pairs):
    near = lambda first: pl.BlockSpec((block_rows + 2 * HALF, 128), lambda m, h: (m, first + h))
    return [
        near(0),
        near(pairs),
        near(2 * pairs),
        pl.BlockSpec((block_rows, 3 * HALF), lambda m, h: (m, 0)),
    ]


def self_attention(qkv, bias, weights, column, micro, block_rows):
    rows = micro * block_rows
    local = qkv.shape[1] // 3
    width = weights.shape[0]
    pairs = local // 128
    return pl.pallas_call(
        self_kernel,
        grid=(micro, pairs),
        in_specs=self_specs(block_rows, pairs)
        + [pl.BlockSpec((width, 128), lambda m, h: (0, column + h))],
        out_specs=[
            pl.BlockSpec((block_rows, 128), lambda m, h: (m, h)),
            pl.BlockSpec((block_rows, 128), lambda m, h: (m, 0)),
            pl.BlockSpec((block_rows, width), lambda m, h: (m, 0)),
        ],
        out_shape=[
            jax.ShapeDtypeStruct((rows, local), bf16),
            jax.ShapeDtypeStruct((rows, 128), f32),
            jax.ShapeDtypeStruct((rows, width), bf16),
        ],
        scratch_shapes=[pltpu.VMEM((block_rows, width), f32)],
        compiler_params=kernel_params(2, 32),
        cost_estimate=pl.CostEstimate(
            flops=rows * 2 * local * (width + 12 * HALF),
            bytes_accessed=20 * rows * local,
            transcendentals=rows * 3 * HALF * 2 * pairs,
        ),
        name="self_attention",
    )(qkv, qkv, qkv, bias, weights)


def self_back_kernel(
    q_ref, k_ref, v_ref, bias_ref, grad_ref, log_ref, own_ref, to_low_ref, to_high_ref
):
    pair = pl.program_id(1)
    parts = grad_ref.shape[0] // HALF
    pieces = [[None] * (parts + 2), [None] * (parts + 2)]
    for part in range(parts):
        rows = slice(part * HALF, (part + 1) * HALF)
        span = slice(part * HALF, (part + 3) * HALF)
        query_grad, key_grad, value_grad = attend_rows_back(
            q_ref[(part + 1) * HALF : (part + 2) * HALF, :],
            k_ref[span, :],
            v_ref[span, :],
            bias_ref[rows, :],
            get_logs(log_ref, rows, pair),
            grad_ref[rows, :],
        )
        own_ref[0, rows, :] = query_grad
        for kind, near_grad in enumerate((key_grad, value_grad)):
            for third in range(3):
                piece = near_grad[third * HALF : (third + 1) * HALF]
                held = pieces[kind][part + third]
                pieces[kind][part + third] = piece if held is None else held + piece
    for kind in range(2):
        to_low_ref[kind] = pieces[kind][0].astype(bf16)
        for part in range(parts):
            own_ref[1 + kind, part * HALF : (part + 1) * HALF, :] = pieces[kind][part + 1]
        to_high_ref[kind] = pieces[kind][parts + 1].astype(bf16)


def self_attention_back(qkv, bias, grad, logs, micro, block_rows):
    rows, local = grad.shape
    pairs = local // 128
    edge = pl.BlockSpec((2, None, HALF, 128), lambda m, h: (0, m, 0, h))
    return pl.pallas_call(
        self_back_kernel,
        grid=(micro, pairs),
        in_specs=self_specs(block_rows, pairs)
        + [
            pl.BlockSpec((block_rows, 128), lambda m, h: (m, h)),
            pl.BlockSpec((block_rows, 128), lambda m, h: (m, 0)),
        ],
        out_specs=[
            pl.BlockSpec((3, block_rows, 128), lambda m, h: (0, m, h)),
            edge,
            edge,
        ],
        out_shape=[
            jax.ShapeDtypeStruct((3, rows, local), f32),
            jax.ShapeDtypeStruct((2, micro, HALF, local), bf16),
            jax.ShapeDtypeStruct((2, micro, HALF, local), bf16),
        ],
        compiler_params=kernel_params(2, 32),
        cost_estimate=pl.CostEstimate(
            flops=20 * rows * 3 * HALF * local,
            bytes_accessed=40 * rows * local,
            transcendentals=rows * 3 * HALF * 2 * pairs,
        ),
        name="self_attention_back",
    )(qkv, qkv, qkv, bias, grad, logs)


def cross_kernel(q_ref, k_ref, v_ref, bias_ref, weight_ref, out_ref, log_ref, sum_ref, acc_ref):
    pair = pl.program_id(1)
    for part in range(q_ref.shape[0] // HALF):
        rows = slice(part * HALF, (part + 1) * HALF)
        out, logs = attend_rows(q_ref[rows, :], k_ref[...], v_ref[...], bias_ref[rows, :])
        out_ref[rows, :] = out.astype(bf16)
        put_logs(log_ref, rows, logs, pair)
    add_product(acc_ref, sum_ref, out_ref[...], weight_ref[...])


def cross_specs(block_rows, pairs):
    return [
        pl.BlockSpec((block_rows, 128), lambda m, h: (m, h)),
        pl.BlockSpec((2 * TXT, 128), lambda m, h: (m, h)),
        pl.BlockSpec((2 * TXT, 128), lambda m, h: (m, h)),
        pl.BlockSpec((block_rows, 2 * TXT), lambda m, h: (m, 0)),
    ]


def cross_attention(query, keys, values, bias, weights, column, micro, block_rows):
    rows, local = query.shape
    width = weights.shape[0]
    pairs = local // 128
    return pl.pallas_call(
        cross_kernel,
        grid=(micro, pairs),
        in_specs=cross_specs(block_rows, pairs)
        + [pl.BlockSpec((width, 128), lambda m, h: (0, column + h))],
        out_specs=[
            pl.BlockSpec((block_rows, 128), lambda m, h: (m, h)),
            pl.BlockSpec((block_rows, 128), lambda m, h: (m, 0)),
            pl.BlockSpec((block_rows, width), lambda m, h: (m, 0)),
        ],
        out_shape=[
            jax.ShapeDtypeStruct((rows, local), bf16),
            jax.ShapeDtypeStruct((rows, 128), f32),
            jax.ShapeDtypeStruct((rows, width), bf16),
        ],
        scratch_shapes=[pltpu.VMEM((block_rows, width), f32)],
        compiler_params=kernel_params(2, 32),
        cost_estimate=pl.CostEstimate(
            flops=rows * 2 * local * (width + 8 * TXT),
            bytes_accessed=16 * rows * local,
            transcendentals=rows * 2 * TXT * 2 * pairs,
        ),
        name="cross_attention",
    )(query, keys, values, bias, weights)


def cross_back_kernel(
    q_ref, k_ref, v_ref, bias_ref, grad_ref, log_ref, weight_ref,
    dq_ref, dk_ref, dv_ref, sum_ref, acc_ref,
):
    pair = pl.program_id(1)
    key_total = value_total = None
    for part in range(q_ref.shape[0] // HALF):
        rows = slice(part * HALF, (part + 1) * HALF)
        query_grad, key_grad, value_grad = attend_rows_back(
            q_ref[rows, :],
            k_ref[...],
            v_ref[...],
            bias_ref[rows, :],
            get_logs(log_ref, rows, pair),
            grad_ref[rows, :],
        )
        dq_ref[rows, :] = query_grad.astype(bf16)
        key_total = key_grad if part == 0 else key_total + key_grad
        value_total = value_grad if part == 0 else value_total + value_grad
    dk_ref[...] = key_total.astype(bf16)
    dv_ref[...] = value_total.astype(bf16)
    add_product(acc_ref, sum_ref, dq_ref[...], weight_ref[...])


def cross_attention_back(
    query, keys, values, bias, grad, logs, weights, column, micro, block_rows
):
    rows, local = query.shape
    width = weights.shape[0]
    pairs = local // 128
    text = pl.BlockSpec((2 * TXT, 128), lambda m, h: (m, h))
    return pl.pallas_call(
        cross_back_kernel,
        grid=(micro, pairs),
        in_specs=cross_specs(block_rows, pairs)
        + [
            pl.BlockSpec((block_rows, 128), lambda m, h: (m, h)),
            pl.BlockSpec((block_rows, 128), lambda m, h: (m, 0)),
            pl.BlockSpec((width, 128), lambda m, h: (0, column + h)),
        ],
        out_specs=[
            pl.BlockSpec((block_rows, 128), lambda m, h: (m, h)),
            text,
            text,
            pl.BlockSpec((block_rows, width), lambda m, h: (m, 0)),
        ],
        out_shape=[
            jax.ShapeDtypeStruct((rows, local), bf16),
            jax.ShapeDtypeStruct(keys.shape, bf16),
            jax.ShapeDtypeStruct(keys.shape, bf16),
            jax.ShapeDtypeStruct((rows, width), bf16),
        ],
        scratch_shapes=[pltpu.VMEM((block_rows, width), f32)],
        compiler_params=kernel_params(2, 32),
        cost_estimate=pl.CostEstimate(
            flops=rows * 2 * local * (width + 20 * TXT),
            bytes_accessed=30 * rows * local,
            transcendentals=rows * 2 * TXT * 2 * pairs,
        ),
        name="cross_attention_back",
    )(query, keys, values, bias, grad, logs, weights)


def ffn_kernel(*refs, summed):
    (
        normed_ref, normed_t_ref, cot_ref, cot_t_ref, outer_ref, gate_ref, up_ref,
        g_outer_ref, g_gate_ref, g_up_ref, out_ref, back_ref, *refs,
    ) = refs
    j = pl.program_id(0)
    step = gate_ref.shape[1]
    if summed:
        sum_ref, out_acc, back_acc, full = refs[:4]
        me = lax.axis_index("seq")
        digits = seq_digits(me)
        core = digits[0]
        partners = [me + stride * (1 - 2 * digit) for stride, digit in zip(STRIDES, digits)]
        pl.when(j == 0)(lambda: [greet(me, digits), None][1])
        pieces = Pieces(refs[4:], sum_ref, partners, digits, step, lag=2)
        count = summed

        def over_core(slot):
            return pieces.over_core(full.at[slot, :, :, :, 1 - core], slot)

        def tick(t):
            @when((t >= 1) & (t - 1 < count))
            def _():
                slot = (t - 1) % SLOTS
                when(t - 1 >= SLOTS)(lambda: pieces.wait_sent(slot))
                over_core(slot).wait()
                pieces.add_core(t - 1, slot, lambda a, b, c: full[slot, a, b, c, core])

            pieces.later_steps(t, count)

    else:
        out_acc, back_acc = refs
    if summed:
        tick(j)
    gate = nn(normed_ref[...], gate_ref[...])
    up = nn(normed_ref[...], up_ref[...])
    grad = nn(cot_ref[...], outer_ref[...])
    chance = 1.0 / (1.0 + jnp.exp(-gate))
    swish = gate * chance
    active = (swish * up).astype(bf16)
    gate_grad = (grad * up * (chance * (1.0 + gate * (1.0 - chance)))).astype(bf16)
    up_grad = (grad * swish).astype(bf16)
    g_up = nn(normed_t_ref[...], up_grad).astype(bf16)
    if summed:

        @pl.when(j < count)
        def _():
            slot = j % SLOTS
            full[slot] = g_up.reshape(full.shape[1:])
            over_core(slot).start()

        @pl.when(j >= count)
        def _():
            g_up_ref[...] = g_up
    else:
        g_up_ref[...] = g_up
    g_gate_ref[...] = nn(normed_t_ref[...], gate_grad).astype(bf16)
    g_outer_ref[...] = nn(cot_t_ref[...], active).astype(bf16)

    @pl.when(j == 0)
    def _():
        out_acc[...] = jnp.zeros_like(out_acc)
        back_acc[...] = jnp.zeros_like(back_acc)

    out_acc[...] += nt(active, outer_ref[...])
    back_acc[...] += nt(gate_grad, gate_ref[...])
    back_acc[...] += nt(up_grad, up_ref[...])

    @pl.when(j == pl.num_programs(0) - 1)
    def _():
        out_ref[...] = out_acc[...].astype(bf16)
        back_ref[...] = back_acc[...].astype(bf16)
        if summed:
            for t in range(pl.num_programs(0), count + 4):
                tick(t)
            pieces.finish(count)


FFN_STEP = 256
SUMMED_STEPS = 9


def feed_forward(normed, normed_t, cotangent, weights, hidden, step=FFN_STEP):
    rows, width = normed.shape
    steps = hidden // step
    seq_count = lax.axis_size("seq")
    share = width // seq_count
    summed = SUMMED_STEPS if seq_count == 16 and share % 16 == 0 else 0
    assert not summed or summed < steps <= 2 * summed
    whole = lambda shape: pl.BlockSpec(shape, lambda j: (0, 0))
    held = lambda shape: pl.BlockSpec(shape, lambda j: (0, 0), pipeline_mode=pl.Buffered(1))
    column = lambda first: pl.BlockSpec((width, step), lambda j: (0, first + j))
    scratch = [pltpu.VMEM((rows, width), f32)] * 2
    out_specs = [
        column(0),
        column(0),
        column(0),
        whole((rows, width)),
        whole((rows, width)),
    ]
    out_shape = [
        jax.ShapeDtypeStruct((width, hidden), bf16),
        jax.ShapeDtypeStruct((width, hidden), bf16),
        jax.ShapeDtypeStruct((width, hidden - summed * step), bf16),
        jax.ShapeDtypeStruct((rows, width), bf16),
        jax.ShapeDtypeStruct((rows, width), bf16),
    ]
    params = kernel_params(1, 56)
    if summed:
        scratch += [pltpu.VMEM((SLOTS, 2, 2, 2, 2, share, step), bf16)]
        scratch += Pieces.scratch(share, step)
        out_specs[2] = pl.BlockSpec((width, step), lambda j: (0, j // summed * (j - summed)))
        out_specs.append(pl.BlockSpec(memory_space=pl.ANY))
        out_shape.append(jax.ShapeDtypeStruct((share, summed * step), f32))
        params = pltpu.CompilerParams(
            dimension_semantics=("arbitrary",),
            collective_id=3,
            has_side_effects=True,
            vmem_limit_bytes=60 * 1024 * 1024,
        )
    outs = pl.pallas_call(
        functools.partial(ffn_kernel, summed=summed),
        grid=(steps,),
        in_specs=[
            held((rows, width)),
            held((width, rows)),
            held((rows, width)),
            held((width, rows)),
            column(0),
            column(steps),
            column(2 * steps),
        ],
        out_specs=out_specs,
        out_shape=out_shape,
        scratch_shapes=scratch,
        compiler_params=params,
        cost_estimate=pl.CostEstimate(
            flops=18 * rows * width * hidden,
            bytes_accessed=12 * width * hidden,
            transcendentals=rows * hidden,
        ),
        name="feed_forward",
    )(normed, normed_t, cotangent, cotangent.T, weights, weights, weights)
    return outs


def qkv_back_kernel(
    own_ref, after_ref, before_ref, normed_t_ref, weight_ref, table_ref,
    grad_ref, back_ref, acc, *, kind_steps, micro, block_rows,
):
    j = pl.program_id(0)
    kind = j // kind_steps
    edges = (kind > 0).astype(f32)
    turned = kind < 2
    near_rows = block_rows + 2 * HALF

    def own_table(index):
        return jnp.concatenate(
            [
                table_ref[index, m * near_rows + HALF : (m + 1) * near_rows - HALF]
                for m in range(micro)
            ],
            axis=0,
        )

    own_factor = jnp.where(turned, own_table(0), 1.0)
    below_factor = jnp.where(turned, -own_table(1), 0.0)
    above_factor = jnp.where(turned, -own_table(2), 0.0)
    total = []
    for m in range(micro):
        first = m * block_rows
        total.append(own_ref[first : first + HALF] + edges * after_ref[m].astype(f32))
        if block_rows > 2 * HALF:
            total.append(own_ref[first + HALF : first + block_rows - HALF])
        total.append(
            own_ref[first + block_rows - HALF : first + block_rows]
            + edges * before_ref[m].astype(f32)
        )
    total = jnp.concatenate(total, axis=0)
    grad = jnp.concatenate(
        [
            turn(total[:, i : i + 128], own_factor, below_factor, above_factor)
            for i in range(0, total.shape[1], 128)
        ],
        axis=1,
    ).astype(bf16)
    grad_ref[...] = nn(normed_t_ref[...], grad).astype(bf16)
    part = nt(grad, weight_ref[...])

    @pl.when(j == 0)
    def _():
        acc[...] = part

    @pl.when(j > 0)
    def _():
        acc[...] += part

    @pl.when(j == pl.num_programs(0) - 1)
    def _():
        back_ref[...] = acc[...].astype(bf16)


def qkv_back(own, after, before, normed_t, weights, table, micro, block_rows, step=256):
    _, rows, local = own.shape
    width = normed_t.shape[0]
    kind_steps = local // step
    edge = pl.BlockSpec(
        (None, micro, HALF, step),
        lambda j: (jnp.maximum(j // kind_steps - 1, 0), 0, 0, j % kind_steps),
    )
    return pl.pallas_call(
        functools.partial(
            qkv_back_kernel, kind_steps=kind_steps, micro=micro, block_rows=block_rows
        ),
        grid=(3 * kind_steps,),
        in_specs=[
            pl.BlockSpec((None, rows, step), lambda j: (j // kind_steps, 0, j % kind_steps)),
            edge,
            edge,
            pl.BlockSpec((width, rows), lambda j: (0, 0)),
            pl.BlockSpec((width, step), lambda j: (0, j)),
            pl.BlockSpec(table.shape, lambda j: (0, 0, 0)),
        ],
        out_specs=[
            pl.BlockSpec((width, step), lambda j: (0, j)),
            pl.BlockSpec((rows, width), lambda j: (0, 0)),
        ],
        out_shape=[
            jax.ShapeDtypeStruct((width, 3 * local), bf16),
            jax.ShapeDtypeStruct((rows, width), bf16),
        ],
        scratch_shapes=[pltpu.VMEM((rows, width), f32)],
        compiler_params=kernel_params(1, 40),
        cost_estimate=pl.CostEstimate(
            flops=12 * rows * width * local,
            bytes_accessed=12 * width * local + 12 * rows * local,
            transcendentals=0,
        ),
        name="qkv_back",
    )(own, after, before, normed_t, weights, table)


def time_features(steps_row):
    half_width = TEMB // 2
    ladder = jnp.exp(-math.log(10000.0) * jnp.arange(half_width, dtype=f32) / half_width)
    angles = steps_row.astype(f32)[:, None] * ladder[None, :]
    return jnp.concatenate([jnp.cos(angles), jnp.sin(angles)], axis=-1)


def with_loads(kernel, places):
    def wrapped(*refs):
        refs = list(refs)
        sems = refs.pop()
        targets = refs[-len(places) :]
        refs = refs[: -len(places)]
        copies = [
            pltpu.make_async_copy(refs[place], target, sems.at[i])
            for i, (place, target) in enumerate(zip(places, targets))
        ]
        for copy in copies:
            copy.start()
        for place, target in zip(places, targets):
            refs[place] = target

        def loaded():
            for copy in copies:
                copy.wait()

        kernel(*refs, loaded=loaded)

    return wrapped


def load_scratch(arrays):
    return [pltpu.VMEM(array.shape, array.dtype) for array in arrays] + [
        pltpu.SemaphoreType.DMA((len(arrays),))
    ]


def norm_back_unit(m, index, block_rows, grad_of, up_ref, hidden_ref, two_ref, later_ref, sums_ref, emit):
    width = hidden_ref.shape[1]
    for start in range(0, block_rows, HALF):
        span = slice(m * block_rows + start, m * block_rows + start + HALF)
        later = later_ref[span, :] > 0.5
        lanes = slice((index + 1) * width, (index + 2) * width)
        factor = jnp.where(later, two_ref[m, 1:2, lanes], two_ref[m, 0:1, lanes])
        total, sums = norm_back_tile(
            grad_of(span),
            up_ref[span, :].astype(f32),
            hidden_ref[span, :].astype(f32),
            (~later, later),
            factor,
        )
        for item in range(2):
            for kind in range(2):
                at = slice(kind * width, (kind + 1) * width)
                before = sums_ref[m, item : item + 1, at] if start else 0.0
                sums_ref[m, item : item + 1, at] = sums[item][kind] + before
        emit(span, start, total)


def cross_stage_kernel(
    back_ref, up_ref, hidden_ref, two_ref, later_ref, weight_ref, q_ref, k_ref, v_ref, bias_ref,
    log_ref, *refs, spans, step, micro, ready, loaded,
):
    sources, refs = refs[: len(spans)], refs[len(spans) :]
    (
        grad_ref, sums_ref, low_t_ref, dq_ref, dk_ref, dv_ref, next_ref, got_next_ref, out_ref,
        own_sem, got_ref, mixed_ref, acc_ref, out_w_ref, query_w_ref, weight_sem,
        swap_send, swap_recv, next_send, next_recv,
    ) = refs[:20]
    refs = refs[20:]
    me = lax.axis_index("seq")
    mine = lax.axis_index("tensor")
    digits = seq_digits(me)
    partners = greet_all(me, mine, digits)
    rows = back_ref.shape[0]
    block_rows = rows // micro
    pairs = q_ref.shape[1] // 128
    text = k_ref.shape[0] // micro

    def over_tensor(m):
        span = pl.ds(m * block_rows, block_rows)
        return to_tensor(
            mine, back_ref.at[span], got_ref.at[span], swap_send.at[m], swap_recv.at[m]
        )

    def over_next(m):
        span = pl.ds(m * block_rows, block_rows)
        return to_tensor(
            mine, next_ref.at[span], got_next_ref.at[span], next_send.at[m], next_recv.at[m]
        )

    def norm_unit(m):
        over_tensor(m).wait_recv()
        if m == 0:
            loaded()
            for load in loads:
                load.wait()

        def emit(span, start, total):
            grad_ref[span, :] = total
            rounded = total.astype(bf16)
            low_t_ref[:, span] = rounded.T
            mixed_ref[start : start + HALF, :] = nn(rounded, out_w_ref[...]).astype(bf16)

        norm_back_unit(
            m, 4, block_rows,
            lambda span: back_ref[span, :].astype(f32) + got_ref[span, :].astype(f32),
            up_ref, hidden_ref, two_ref, later_ref, sums_ref, emit,
        )

    def pair_unit(m, pair):
        lanes = pl.ds(pl.multiple_of(pair * 128, 128), 128)
        keys = slice(m * text, (m + 1) * text)
        key_total = value_total = None
        for start in range(0, block_rows, HALF):
            span = slice(m * block_rows + start, m * block_rows + start + HALF)
            query_grad, key_grad, value_grad = attend_rows_back(
                q_ref[span, lanes],
                k_ref[keys, lanes],
                v_ref[keys, lanes],
                bias_ref[span, :],
                get_logs(log_ref, span, pair),
                mixed_ref[start : start + HALF, lanes],
            )
            dq_ref[span, lanes] = query_grad.astype(bf16)
            key_total = key_grad if start == 0 else key_total + key_grad
            value_total = value_grad if start == 0 else value_total + value_grad
        dk_ref[keys, lanes] = key_total.astype(bf16)
        dv_ref[keys, lanes] = value_total.astype(bf16)
        own = slice(m * block_rows, (m + 1) * block_rows)
        acc_ref[...] += nt(dq_ref[own, lanes], query_w_ref[:, lanes])

    def close(m):
        own = slice(m * block_rows, (m + 1) * block_rows)
        next_ref[own, :] = acc_ref[...].astype(bf16)
        if m < micro - 1:
            acc_ref[...] = jnp.zeros_like(acc_ref)
            over_next(m).start()

    local = q_ref.shape[1]
    loads = [
        pltpu.make_async_copy(
            weight_ref.at[:, k * local : (k + 1) * local], target, weight_sem.at[i]
        )
        for i, (k, target) in enumerate(((5, out_w_ref), (4, query_w_ref)))
    ]
    for load in loads:
        load.start()
    acc_ref[...] = jnp.zeros_like(acc_ref)
    pieces = Pieces(refs, out_ref, partners, digits, step)
    work = []
    spot = 0
    for m in range(micro):
        spot = max(spot, ready * (m + 1))
        work.append((spot, spot + 1, lambda t, m=m: norm_unit(m)))
        spot += 1
        begin = spot

        def pair_units(t, m=m, begin=begin):
            for k in range(2):
                pair_unit(m, 2 * (t - begin) + k)

        work.append((begin, begin + pairs // 2, pair_units))
        spot += pairs // 2
        work.append((spot - 1, spot, lambda t, m=m: close(m)))
    for m in range(micro):
        over_tensor(m).start()
    pieces.run(sources, spans, own_sem, work, spot)
    for m in range(micro):
        over_tensor(m).wait_send()
        if m < micro - 1:
            over_next(m).wait()


def cross_stage(
    back, up, hidden, two, later, query, keys, values, bias, logs, weights, local, sources,
    spans, micro, which=2, step=256,
):
    seq_count = lax.axis_size("seq")
    rows, width = hidden.shape
    share = width // seq_count
    block_rows = rows // micro
    any_space = pl.BlockSpec(memory_space=pl.ANY)
    vmem = pl.BlockSpec(memory_space=pltpu.VMEM)
    args = [back, up, hidden, two, later, weights, query, keys, values, bias, logs]
    places = (1, 2, 3, 4, 6, 7, 8, 9, 10)
    return pl.pallas_call(
        with_loads(
            functools.partial(cross_stage_kernel, spans=spans, step=step, micro=micro, ready=4),
            places,
        ),
        out_shape=[
            jax.ShapeDtypeStruct((rows, width), f32),
            jax.ShapeDtypeStruct((micro, 2, 2 * width), f32),
            jax.ShapeDtypeStruct((width, rows), bf16),
            jax.ShapeDtypeStruct((rows, local), bf16),
            jax.ShapeDtypeStruct(keys.shape, bf16),
            jax.ShapeDtypeStruct(keys.shape, bf16),
            jax.ShapeDtypeStruct((rows, width), bf16),
            jax.ShapeDtypeStruct((rows - block_rows, width), bf16),
            jax.ShapeDtypeStruct((share, sum(span for _, span in spans)), f32),
        ],
        in_specs=[vmem] + [any_space] * (10 + len(spans)),
        out_specs=[vmem] * 7 + [any_space] * 2,
        scratch_shapes=[
            pltpu.SemaphoreType.DMA((SLOTS,)),
            pltpu.VMEM((rows, width), bf16),
            pltpu.VMEM((block_rows, local), bf16),
            pltpu.VMEM((block_rows, width), f32),
            pltpu.VMEM((width, local), bf16),
            pltpu.VMEM((width, local), bf16),
            pltpu.SemaphoreType.DMA((2,)),
        ]
        + [pltpu.SemaphoreType.DMA((micro,))] * 4
        + Pieces.scratch(share, step)
        + load_scratch([args[place] for place in places]),
        compiler_params=pltpu.CompilerParams(
            collective_id=which, has_side_effects=True, vmem_limit_bytes=56 * 1024 * 1024
        ),
        cost_estimate=pl.CostEstimate(
            flops=8 * rows * width * local, bytes_accessed=40 * rows * width, transcendentals=0
        ),
        name="cross_stage",
    )(
        *args,
        *[source.reshape(2, 2, 2, 2, share, source.shape[1]) for source in sources],
    )


def self_stage_kernel(
    back_ref, got_early_ref, up_ref, hidden_ref, two_ref, later_ref, weight_ref, qkv_ref, bias_ref,
    log_ref, other_ref, *refs,
    spans, step, micro, ready, seq_count, loaded,
):
    sources, refs = refs[: len(spans)], refs[len(spans) :]
    (
        grad_ref, sums_ref, low_t_ref, own_ref, from_low_ref, from_high_ref, got_other_ref, out_ref,
        own_sem, got_ref, mixed_ref, to_low_ref, to_high_ref, out_w_ref, weight_sem, swap_sem,
        halo_send, halo_recv,
    ) = refs[:18]
    refs = refs[18:]
    me = lax.axis_index("seq")
    mine = lax.axis_index("tensor")
    digits = seq_digits(me)
    has_low = me > 0
    has_high = me < seq_count - 1
    partners = greet_all(me, mine, digits, ((has_low, me - 1), (has_high, me + 1)))
    rows = back_ref.shape[0]
    block_rows = rows // micro
    near_rows = block_rows + 2 * HALF
    local = qkv_ref.shape[1] // 3
    pairs = local // 128
    last = micro - 1

    def over_tensor():
        return to_tensor(
            mine,
            back_ref.at[pl.ds(last * block_rows, block_rows)],
            got_ref,
            swap_sem.at[0],
            swap_sem.at[1],
        )

    def over_other():
        span = pl.ds(block_rows, rows - block_rows)
        return to_tensor(
            mine, other_ref.at[span], got_other_ref, swap_sem.at[2], swap_sem.at[3]
        )

    def to_low(m):
        return send_to(
            me - 1, to_low_ref.at[m], from_high_ref.at[m], halo_send.at[0, m], halo_recv.at[0, m]
        )

    def to_high(m):
        return send_to(
            me + 1, to_high_ref.at[m], from_low_ref.at[m], halo_send.at[1, m], halo_recv.at[1, m]
        )

    load = pltpu.make_async_copy(
        weight_ref.at[:, 3 * local : 4 * local], out_w_ref, weight_sem
    )
    load.start()

    def norm_unit(m):
        if m == 0:
            loaded()
            load.wait()
        if m == last:
            over_tensor().wait_recv()

        def grad_of(span):
            if m == last:
                other = got_ref[span.start - last * block_rows : span.stop - last * block_rows, :]
            else:
                other = got_early_ref[span, :]
            return back_ref[span, :].astype(f32) + other.astype(f32)

        def emit(span, start, total):
            grad_ref[span, :] = total
            rounded = total.astype(bf16)
            low_t_ref[:, span] = rounded.T
            mixed_ref[start : start + HALF, :] = nn(rounded, out_w_ref[...]).astype(bf16)

        norm_back_unit(
            m, 2, block_rows, grad_of, up_ref, hidden_ref, two_ref, later_ref, sums_ref, emit
        )

    def pair_unit(m, pair):
        def lanes(kind):
            return pl.ds(pl.multiple_of(kind * local + pair * 128, 128), 128)

        parts = block_rows // HALF
        held = [[None] * (parts + 2), [None] * (parts + 2)]
        at = lanes(0)
        for part in range(parts):
            span = slice(m * block_rows + part * HALF, m * block_rows + (part + 1) * HALF)
            own_rows = slice(m * near_rows + (part + 1) * HALF, m * near_rows + (part + 2) * HALF)
            near = slice(m * near_rows + part * HALF, m * near_rows + (part + 3) * HALF)
            query_grad, key_grad, value_grad = attend_rows_back(
                qkv_ref[own_rows, at],
                qkv_ref[near, lanes(1)],
                qkv_ref[near, lanes(2)],
                bias_ref[span, :],
                get_logs(log_ref, span, pair),
                mixed_ref[part * HALF : (part + 1) * HALF, at],
            )
            own_ref[0, span, at] = query_grad
            for kind, near_grad in enumerate((key_grad, value_grad)):
                for third in range(3):
                    piece = near_grad[third * HALF : (third + 1) * HALF]
                    before = held[kind][part + third]
                    held[kind][part + third] = piece if before is None else before + piece
        for kind in range(2):
            to_low_ref[m, kind, :, at] = held[kind][0].astype(bf16)
            for part in range(parts):
                span = slice(m * block_rows + part * HALF, m * block_rows + (part + 1) * HALF)
                own_ref[1 + kind, span, at] = held[kind][part + 1]
            to_high_ref[m, kind, :, at] = held[kind][parts + 1].astype(bf16)

    def close(m):
        pl.when(has_low)(lambda: to_low(m).start())
        pl.when(has_high)(lambda: to_high(m).start())

    pieces = Pieces(refs, out_ref, partners, digits, step)
    work = []
    spot = 1
    for m in range(micro):
        if m == last:
            spot = max(spot, ready)
        work.append((spot, spot + 1, lambda t, m=m: norm_unit(m)))
        spot += 1
        begin = spot

        def pair_units(t, m=m, begin=begin):
            for k in range(2):
                pair_unit(m, 2 * (t - begin) + k)

        work.append((begin, begin + pairs // 2, pair_units))
        spot += pairs // 2
        work.append((spot - 1, spot, lambda t, m=m: close(m)))
    over_tensor().start()
    over_other().start()

    @pl.when(jnp.logical_not(has_low))
    def _():
        from_low_ref[...] = jnp.zeros_like(from_low_ref)

    @pl.when(jnp.logical_not(has_high))
    def _():
        from_high_ref[...] = jnp.zeros_like(from_high_ref)

    pieces.run(sources, spans, own_sem, work, spot)
    over_tensor().wait_send()
    over_other().wait()
    for m in range(micro):

        @pl.when(has_low)
        def _(m=m):
            to_low(m).wait_send()
            to_high(m).wait_recv()

        @pl.when(has_high)
        def _(m=m):
            to_high(m).wait_send()
            to_low(m).wait_recv()


def self_stage(
    back, got_early, up, hidden, two, later, qkv, bias, logs, weights, local, other, sources,
    spans, micro, which=4, step=256,
):
    seq_count = lax.axis_size("seq")
    rows, width = hidden.shape
    share = width // seq_count
    block_rows = rows // micro
    any_space = pl.BlockSpec(memory_space=pl.ANY)
    vmem = pl.BlockSpec(memory_space=pltpu.VMEM)
    args = [back, got_early, up, hidden, two, later, weights, qkv, bias, logs, other]
    places = (1, 2, 3, 4, 5, 7, 8, 9)
    edge = (micro, 2, HALF, local)
    return pl.pallas_call(
        with_loads(
            functools.partial(
                self_stage_kernel,
                spans=spans,
                step=step,
                micro=micro,
                ready=4,
                seq_count=seq_count,
            ),
            places,
        ),
        out_shape=[
            jax.ShapeDtypeStruct((rows, width), f32),
            jax.ShapeDtypeStruct((micro, 2, 2 * width), f32),
            jax.ShapeDtypeStruct((width, rows), bf16),
            jax.ShapeDtypeStruct((3, rows, local), f32),
            jax.ShapeDtypeStruct(edge, bf16),
            jax.ShapeDtypeStruct(edge, bf16),
            jax.ShapeDtypeStruct((rows - block_rows, width), bf16),
            jax.ShapeDtypeStruct((share, sum(span for _, span in spans)), f32),
        ],
        in_specs=[vmem] + [any_space] * (10 + len(spans)),
        out_specs=[vmem] * 6 + [any_space] * 2,
        scratch_shapes=[
            pltpu.SemaphoreType.DMA((SLOTS,)),
            pltpu.VMEM((block_rows, width), bf16),
            pltpu.VMEM((block_rows, local), bf16),
            pltpu.VMEM(edge, bf16),
            pltpu.VMEM(edge, bf16),
            pltpu.VMEM((width, local), bf16),
            pltpu.SemaphoreType.DMA,
            pltpu.SemaphoreType.DMA((4,)),
            pltpu.SemaphoreType.DMA((2, micro)),
            pltpu.SemaphoreType.DMA((2, micro)),
        ]
        + Pieces.scratch(share, step)
        + load_scratch([args[place] for place in places]),
        compiler_params=pltpu.CompilerParams(
            collective_id=which, has_side_effects=True, vmem_limit_bytes=58 * 1024 * 1024
        ),
        cost_estimate=pl.CostEstimate(
            flops=8 * rows * width * local, bytes_accessed=40 * rows * width, transcendentals=0
        ),
        name="self_stage",
    )(
        *args,
        *[source.reshape(2, 2, 2, 2, share, source.shape[1]) for source in sources],
    )


EARLY_COLUMNS = (1024, 1280)


def on_device(
    latents,
    context,
    lengths,
    text_len,
    timesteps,
    self_qkv,
    self_out,
    cross_query,
    cross_kv,
    cross_out,
    ffn_in,
    ffn_out,
    mod_weight,
    mod_bias,
    out_grad,
):
    micro, block_rows, model_width = latents.shape
    seq_count = lax.axis_size("seq")
    me = lax.axis_index("seq")
    frame_count = block_rows * seq_count
    item_count = lengths.shape[1]
    local = self_qkv.shape[2]
    hidden = ffn_in.shape[2]
    rows = micro * block_rows
    text_width = context.shape[2]

    attn_share = jnp.concatenate(
        [
            self_qkv[0],
            self_qkv[1],
            self_qkv[2],
            self_out.T,
            cross_query,
            cross_out.T,
            jnp.concatenate([cross_kv[0], cross_kv[1]], axis=0),
        ],
        axis=1,
    )
    ffn_share = jnp.concatenate([ffn_out.T, ffn_in[0], ffn_in[1]], axis=1)
    features = time_features(timesteps.reshape(-1))
    own_features = lax.dynamic_slice_in_dim(
        features, me * mod_weight.shape[0], mod_weight.shape[0], 1
    )
    bias_share = mod_bias.shape[1]
    bias_wide = lax.dynamic_update_slice_in_dim(
        jnp.zeros((6, model_width), f32), mod_bias.astype(f32), me * bias_share, 1
    )
    mod_part = jnp.dot(
        own_features, mod_weight.astype(f32).reshape(mod_weight.shape[0], -1), precision=highest
    ) + bias_wide.reshape(1, -1)
    (
        attn_all,
        normed_near,
        normed_one_t,
        two,
        later,
        near_table,
        self_bias,
        cross_bias,
    ) = gather_and_prepare(attn_share, mod_part, latents, lengths, text_len)
    ffn_share, attn_all = lax.optimization_barrier((ffn_share, attn_all))
    ffn_all = lax.all_gather(ffn_share, "seq", axis=0, tiled=True)
    pair_w = attn_all[:, 6 * local :].reshape(seq_count, 2, text_width // seq_count, local)
    key_w = pair_w[:, 0].reshape(text_width, local)
    value_w = pair_w[:, 1].reshape(text_width, local)

    first_frame = me * block_rows
    first_item = jnp.sum((jnp.cumsum(lengths, axis=1) <= first_frame).astype(jnp.int32), axis=1)
    base_item = jnp.minimum(first_item, item_count - 2)
    catalog = jnp.arange(item_count, dtype=jnp.int32)

    ahead = [(i, i + 1) for i in range(seq_count - 1)]
    behind = [(i + 1, i) for i in range(seq_count - 1)]
    latent = latents.reshape(rows, model_width)
    cotangent = out_grad.reshape(rows, model_width)
    near_context = jnp.concatenate(
        [
            lax.dynamic_slice_in_dim(context[m], base_item[m] * TXT, 2 * TXT, 0)
            for m in range(micro)
        ]
    )
    column = local // 128

    qkv = project(normed_near, attn_all, near_table, local)
    mixed_one, logs_one, part_one = self_attention(
        qkv, self_bias, attn_all, 3 * column, micro, block_rows
    )
    got_one = swap(part_one)
    text_keys = nn(near_context, key_w).astype(bf16)
    text_values = nn(near_context, value_w).astype(bf16)
    hidden_one, _, normed_two_t, query_two = norm_forward(
        latent, part_one, got_one, two, later, 2, micro, attn_all, 4, local
    )
    mixed_two, logs_two, part_two = cross_attention(
        query_two, text_keys, text_values, cross_bias, attn_all, 5 * column, micro, block_rows
    )
    got_two = swap(part_two)
    hidden_two, normed_three, normed_three_t = norm_forward(
        hidden_one, part_two, got_two, two, later, 4, micro
    )
    g_outer, g_gate, g_up, out_part, back_three, *up_early = feed_forward(
        normed_three, normed_three_t, cotangent, ffn_all, hidden
    )
    outer_total = early_sum(g_outer)

    share = text_width // seq_count
    fused = (
        seq_count == 16 and lax.axis_size("tensor") == 2 and (model_width // seq_count) % 16 == 0
    )

    def cross_grads(two_low_t, query_two_low, text_key_low, text_value_low):
        pair_grad = jnp.concatenate(
            [
                tn(near_context, text_key_low).astype(bf16).reshape(seq_count, share, local),
                tn(near_context, text_value_low).astype(bf16).reshape(seq_count, share, local),
            ],
            axis=1,
        ).reshape(2 * text_width, local)
        return [
            nn(two_low_t, mixed_two).astype(bf16),
            nn(normed_two_t, query_two_low).astype(bf16),
            pair_grad,
        ]

    if fused:
        first, second = EARLY_COLUMNS
        third = hidden - first - second
        (
            hidden_two_grad, sums_three, two_low_t, query_two_low, text_key_low, text_value_low,
            back_two, got_early, totals_a,
        ) = cross_stage(
            back_three, cotangent, hidden_two, two, later, query_two, text_keys, text_values,
            cross_bias, logs_two, attn_all, local, [g_gate], ((0, first),), micro,
        )
        (
            hidden_one_grad, sums_two, one_low_t, own_grads, from_low, from_high, got_last,
            totals_b,
        ) = self_stage(
            back_two, got_early, hidden_two_grad, hidden_one, two, later, qkv, self_bias, logs_one,
            attn_all, local, out_part, [g_gate], ((first, second),), micro,
        )
        crossed = cross_grads(two_low_t, query_two_low, text_key_low, text_value_low)
        g_self_out = nn(one_low_t, mixed_one).astype(bf16)
        sums = jnp.concatenate([sums_two, sums_three], axis=2)
        spans = ((0, g_up.shape[1]),) + ((0, local),) * 4
        sources = [g_up] + crossed + [g_self_out]
        if third:
            spans = ((first + second, third),) + spans
            sources = [g_gate] + sources
        late = third + g_up.shape[1]
        totals_c, latent_grad, mod_grad, bias_sum, got_first = finish_stage(
            own_grads, from_low, from_high, normed_one_t, attn_all, near_table, hidden_one_grad,
            latent, two, later, sums, lengths, own_features, out_part,
            sources, spans, micro,
        )
        totals = [totals_c[:, late + k * local : late + (k + 1) * local] for k in range(4)]
        grad_cross_out, grad_cross_query, grad_cross_kv, grad_self_out = totals
        qkv_total = totals_c[:, late + 4 * local :]
        gate_total = jnp.concatenate([totals_a, totals_b, totals_c[:, :third]], axis=1)
        up_total = jnp.concatenate([up_early[0], totals_c[:, third:late]], axis=1)
        out_got = jnp.concatenate([got_first, got_last], axis=0)
    else:
        got_three = swap(back_three)
        gate_total = early_sum(g_gate)
        up_total = early_sum(g_up)
        hidden_two_grad, sums_three, two_low_t, mixed_two_grad = norm_back(
            cotangent, back_three, got_three, hidden_two, two, later, 4, micro, attn_all, 5, local
        )
        query_two_low, text_key_low, text_value_low, back_two = cross_attention_back(
            query_two, text_keys, text_values, cross_bias, mixed_two_grad, logs_two,
            attn_all, 4 * column, micro, block_rows,
        )
        got_back_two = swap(back_two)
        hidden_one_grad, sums_two, one_low_t, mixed_one_grad = norm_back(
            hidden_two_grad, back_two, got_back_two, hidden_one, two, later, 2, micro,
            attn_all, 3, local,
        )
        own_grads, to_low, to_high = self_attention_back(
            qkv, self_bias, mixed_one_grad, logs_one, micro, block_rows
        )
        from_high = lax.ppermute(to_low, "seq", behind)
        from_low = lax.ppermute(to_high, "seq", ahead)
        g_self_out = nn(one_low_t, mixed_one).astype(bf16)
        g_qkv, back_one = qkv_back(
            own_grads, from_low, from_high, normed_one_t, attn_all, near_table, micro, block_rows
        )
        crossed = cross_grads(two_low_t, query_two_low, text_key_low, text_value_low)
        sums = jnp.concatenate(
            [piece.reshape(micro, 2, 2 * model_width) for piece in (sums_two, sums_three)], axis=2
        )
        totals, latent_grad, mod_grad, bias_sum, out_got = finish_apart(
            crossed + [g_self_out, g_qkv], back_one, hidden_one_grad, latent, two, later, sums,
            lengths, own_features, out_part,
        )
        grad_cross_out, grad_cross_query, grad_cross_kv, grad_self_out, qkv_total = totals
    block_out = (hidden_two + (out_part.astype(f32) + out_got.astype(f32))).astype(bf16)
    mod_grad = mod_grad.reshape(mod_weight.shape)
    bias_grad = lax.dynamic_slice_in_dim(
        bias_sum.reshape(6, model_width), me * bias_share, bias_share, 1
    )

    grad_qkv = jnp.stack([qkv_total[:, i * local : (i + 1) * local] for i in range(3)])
    return (
        block_out.reshape(latents.shape),
        latent_grad.reshape(latents.shape),
        grad_qkv,
        grad_self_out.T,
        grad_cross_query,
        grad_cross_kv.reshape(2, share, local),
        grad_cross_out.T,
        jnp.stack([gate_total, up_total]),
        outer_total.T,
        mod_grad,
        bias_grad,
    )


def solution(mesh):
    return jax.shard_map(
        on_device,
        mesh=mesh,
        in_specs=(
            P(None, "seq", None),
            P(),
            P(),
            P(),
            P(),
            P(None, "seq", "tensor"),
            P("tensor", "seq"),
            P("seq", "tensor"),
            P(None, "seq", "tensor"),
            P("tensor", "seq"),
            P(None, "seq", "tensor"),
            P("tensor", "seq"),
            P("seq", None, None),
            P(None, "seq"),
            P(None, "seq", None),
        ),
        out_specs=(
            P(None, "seq", None),
            P(None, "seq", None),
            P(None, "seq", "tensor"),
            P("tensor", "seq"),
            P("seq", "tensor"),
            P(None, "seq", "tensor"),
            P("tensor", "seq"),
            P(None, "seq", "tensor"),
            P("tensor", "seq"),
            P("seq", None, None),
            P(None, "seq"),
        ),
        check_vma=False,
    )
```

```python
import functools
import math

import jax
import jax.numpy as jnp
import numpy as np
from jax import lax
from jax.experimental import pallas as pl
from jax.experimental.pallas import tpu as pltpu
from jax.sharding import PartitionSpec as P

HD = 64
TXT = 128
TEMB = 256
HALF = 128


norm_eps = 1e-05
highest = lax.Precision.HIGHEST
f32 = jnp.float32
bf16 = jnp.bfloat16


def dot(a, b, dims):
    return lax.dot_general(a, b, ((dims[0], dims[1]), ((), ())), preferred_element_type=f32)


def nn(a, b):
    return dot(a, b, ((1,), (0,)))


def nt(a, b):
    return dot(a, b, ((1,), (1,)))


def tn(a, b):
    return dot(a, b, ((0,), (0,)))


def halves(count):
    stride = 1
    strides = []
    while stride < count:
        strides.append(stride)
        stride *= 2
    return strides


def flip(block, stride):
    count = lax.axis_size("seq")
    return lax.ppermute(block, "seq", [(i, i ^ stride) for i in range(count)])


def swap(part):
    count = lax.axis_size("tensor")
    return lax.ppermute(part, "tensor", [(i, (i + 1) % count) for i in range(count)])


def seq_sum(part):
    for stride in halves(lax.axis_size("seq")):
        part = part + flip(part, stride)
    return part


def kernel_params(grid_rank, mib):
    return pltpu.CompilerParams(
        dimension_semantics=("arbitrary",) * grid_rank, vmem_limit_bytes=mib * 1024 * 1024
    )


STRIDES = (1, 2, 4, 8)


def seq_digits(me):
    return [(me // stride) % 2 for stride in STRIDES]


def greet(me, digits, others=(), mine=None):
    partners = [me + stride * (1 - 2 * digit) for stride, digit in zip(STRIDES, digits)]
    barrier = pltpu.get_barrier_semaphore()

    def tell(**target):
        pl.semaphore_signal(barrier, inc=1, device_id=target, device_id_type=pl.DeviceIdType.MESH)

    expected = len(partners)
    for partner in partners:
        tell(seq=partner)
    if mine is not None:
        tell(tensor=1 - mine)
        expected += 1
    for there, target in others:
        pl.when(there)(functools.partial(tell, seq=target))
        expected = expected + there.astype(jnp.int32)
    pl.semaphore_wait(barrier, expected)
    return partners


def send_to(partner, source, target, send_sem, recv_sem):
    return pltpu.make_async_remote_copy(
        src_ref=source,
        dst_ref=target,
        send_sem=send_sem,
        recv_sem=recv_sem,
        device_id={"seq": partner},
        device_id_type=pl.DeviceIdType.MESH,
    )


def greet_all(me, mine, digits, others=()):
    return greet(me, digits, others, mine)


def to_tensor(mine, source, target, send_sem, recv_sem):
    return pltpu.make_async_remote_copy(
        src_ref=source,
        dst_ref=target,
        send_sem=send_sem,
        recv_sem=recv_sem,
        device_id={"tensor": 1 - mine},
        device_id_type=pl.DeviceIdType.MESH,
    )


SMALL_STEPS = 6


def small_sum(partners, mine, core, fill, prep, held, got, total, finish, send_sem, recv_sem):
    own = 2 * mine + core
    half = pl.ds(2 * mine, 2)

    def exchange(k):
        sems = send_sem.at[k], recv_sem.at[k]
        if k == 0:
            return send_to(partners[0], prep.at[2 * mine + 1 - core], got.at[0], *sems)
        if k < 4:
            return send_to(partners[k], held.at[k], got.at[k], *sems)
        if k == 4:
            return send_to(partners[0], total.at[own], total.at[own], *sems)
        return to_tensor(mine, total.at[half], total.at[half], *sems)

    def step(k):
        if k == 0:
            fill(prep)
        else:
            exchange(k - 1).wait()
        if k == 1:
            held[1] = prep[own] + got[0]
        elif 1 < k < 4:
            held[k] = held[k - 1] + got[k - 1]
        elif k == 4:
            total[own] = held[3] + got[3]
        elif k == SMALL_STEPS:
            finish(total)
        if k < SMALL_STEPS:
            exchange(k).start()

    return step


def small_scratch(shape):
    quarter = (4, shape[0], shape[1] // 4)
    return [pltpu.VMEM(quarter, f32)] * 4 + [pltpu.SemaphoreType.DMA((SMALL_STEPS,))] * 2


def lane_ladder():
    quarter = HD // 4
    return np.exp(-math.log(10000.0) * (np.arange(128) % quarter) / quarter).astype(np.float32)


def prepare(first, frame_count, lengths, text_len, block_rows):
    items = len(lengths)
    ends = [lengths[0]]
    for length in lengths[1:]:
        ends.append(ends[-1] + length)

    def item_of(place):
        return sum((end <= place).astype(jnp.int32) for end in ends)

    def pick(ids, values):
        return sum(jnp.where(ids == k, value, 0) for k, value in enumerate(values))

    near_rows = block_rows + 2 * HALF
    place = first - HALF + lax.broadcasted_iota(jnp.int32, (near_rows, 1), 0)
    ids = item_of(place)
    offset = place - pick(ids, [end - length for end, length in zip(ends, lengths)])
    base = jnp.minimum(item_of(first), items - 2)
    own_ids = ids[HALF : HALF + block_rows]
    self_bias = []
    for part in range(block_rows // HALF):
        row = lax.broadcasted_iota(jnp.int32, (HALF, 1), 0)
        key = lax.broadcasted_iota(jnp.int32, (1, 3 * HALF), 1) - HALF
        key_place = first + part * HALF + key
        inside = (key_place >= 0) & (key_place < frame_count)
        key_ids = jnp.where(inside, item_of(key_place), -1)
        near_enough = jnp.abs(row - key) <= HALF
        same = own_ids[part * HALF : (part + 1) * HALF] == key_ids
        self_bias.append(jnp.where(near_enough & same, 0.0, -1e30))
    slot = lax.broadcasted_iota(jnp.int32, (1, 2 * TXT), 1)
    key_item = jnp.where(slot < TXT, base, base + 1)
    used = jnp.where(slot < TXT, slot, slot - TXT) < pick(key_item, text_len)
    key_item = jnp.where(used, key_item, -1)
    cross_bias = jnp.where(own_ids == key_item, 0.0, -1e30)
    later = (ids != base).astype(f32)
    return base, offset, later, self_bias, cross_bias


def lane_tables(offset, ladder):
    quarter = HD // 4
    angles = offset.astype(f32) * ladder
    lane = lax.broadcasted_iota(jnp.int32, angles.shape, 1) % HD
    cosine = jnp.cos(angles)
    sine = jnp.sin(angles)
    return (
        jnp.where(lane < 2 * quarter, cosine, 1.0),
        jnp.where((lane >= quarter) & (lane < 2 * quarter), sine, 0.0),
        jnp.where(lane < quarter, -sine, 0.0),
    )


def gather_kernel(
    share_ref, part_ref, latent_ref, lengths_ref, text_ref, ladder_ref,
    out_ref, near_normed_ref, normed_t_ref, two_ref, later_ref, table_ref, self_ref, cross_ref,
    near_ref, prep, held, got, total_ref, small_send, small_recv, copy_sem, send_sem, recv_sem,
    near_sem, halo_send, halo_recv, *, pieces, step, y_first, seq_count,
):
    micro, block_rows, width = latent_ref.shape
    items = lengths_ref.shape[1]
    near_rows = block_rows + 2 * HALF
    me = lax.axis_index("seq")
    digits = seq_digits(me)
    core, y, z_lo, z_hi = digits
    first = me * block_rows
    has_low = me > 0
    has_high = me < seq_count - 1
    mine = lax.axis_index("tensor")
    partners = greet_all(me, mine, digits, ((has_low, me - 1), (has_high, me + 1)))

    def fill(target):
        span = target.shape[2]
        for index in range(4):
            target[index] = part_ref[:, index * span : (index + 1) * span]

    small = small_sum(
        partners, mine, core, fill, prep, held, got, total_ref, lambda total: None,
        small_send, small_recv,
    )

    def to_low():
        return send_to(
            me - 1,
            latent_ref.at[:, :HALF],
            near_ref.at[:, near_rows - HALF :],
            halo_send.at[0],
            halo_recv.at[0],
        )

    def to_high():
        return send_to(
            me + 1,
            latent_ref.at[:, block_rows - HALF :],
            near_ref.at[:, :HALF],
            halo_send.at[1],
            halo_recv.at[1],
        )

    def load_own():
        return pltpu.make_async_copy(
            latent_ref, near_ref.at[:, HALF : near_rows - HALF], near_sem
        )

    def piece(p):
        return pl.ds(p * step, step)

    def exchange(p, stage):
        cols = piece(p)
        if p in y_first:
            axis = (1, 3, 2, 0)[stage]
            spots = ((z_hi, z_lo, y, core), (z_hi, z_lo, None, core), (None, z_lo, None, core), None)
        else:
            axis = (3, 2, 1, 0)[stage]
            spots = ((z_hi, z_lo, y, core), (None, z_lo, y, core), (None, None, y, core), None)
        spot = spots[stage] or (None, None, None, core)
        index = tuple(slice(None) if digit is None else digit for digit in spot)
        block = out_ref.at[index + (slice(None), cols)]
        source = share_ref.at[:, cols] if stage == 0 else block
        return send_to(partners[axis], source, block, send_sem.at[stage, p], recv_sem.at[stage, p])

    def own(p):
        return pltpu.make_async_copy(
            share_ref.at[:, piece(p)],
            out_ref.at[z_hi, z_lo, y, core, :, piece(p)],
            copy_sem.at[p],
        )

    def masks(m):
        base, offset, later, self_bias, cross_bias = prepare(
            first,
            seq_count * block_rows,
            [lengths_ref[m, k] for k in range(items)],
            [text_ref[m, k] for k in range(items)],
            block_rows,
        )
        rows = slice(m * block_rows, (m + 1) * block_rows)
        later_ref[rows, :] = later[HALF : HALF + block_rows]
        for part, bias in enumerate(self_bias):
            start = m * block_rows + part * HALF
            self_ref[start : start + HALF, :] = bias
        cross_ref[rows, :] = cross_bias
        state[m] = base, offset, later

    def tables(m, start):
        offset = state[m][1][start : start + HALF]
        target = m * near_rows + start
        for index, values in enumerate(lane_tables(offset, ladder_ref[...])):
            table_ref[index, target : target + HALF, :] = values

    def modulation(m, base):
        span = total_ref.shape[2]
        for which in range(2):
            for index in range(4):
                two_ref[m, which : which + 1, index * span : (index + 1) * span] = sum(
                    jnp.where(
                        base + which == k,
                        total_ref[index, m * items + k : m * items + k + 1],
                        0.0,
                    )
                    for k in range(items)
                )

    def norm(m, start):
        shift = [two_ref[m, which : which + 1, :width] for which in range(2)]
        factor = [two_ref[m, which : which + 1, width : 2 * width] for which in range(2)]
        tile = near_ref[m, start : start + HALF].astype(f32)
        chosen = state[m][2][start : start + HALF] > 0.5
        xhat, _ = spread_rows(tile)
        normed = (
            xhat * (1.0 + jnp.where(chosen, factor[1], factor[0]))
            + jnp.where(chosen, shift[1], shift[0])
        ).astype(bf16)
        target = m * near_rows + start
        near_normed_ref[target : target + HALF, :] = normed
        if HALF <= start < HALF + block_rows:
            target = m * block_rows + start - HALF
            normed_t_ref[:, target : target + HALF] = normed.T

    beside = {}
    state = {}
    gap = 3

    def add(t, work):
        beside.setdefault(t, []).append(work)

    def finish_near():
        load_own().wait()
        pl.when(has_low)(lambda: to_high().wait_recv())
        pl.when(has_high)(lambda: to_low().wait_recv())

    tick = 1
    for m in range(micro):
        add(tick, functools.partial(masks, m))
        for start in range(0, near_rows, HALF):
            tick += 1
            add(tick, functools.partial(tables, m, start))
        tick += 1
    for k in range(1, SMALL_STEPS + 1):
        add(gap * k, functools.partial(small, k))
    tick = gap * SMALL_STEPS
    add(tick, finish_near)
    for m in range(micro):
        tick += 1
        add(tick, lambda m=m: modulation(m, state[m][0]))
        for start in range(0, near_rows, HALF):
            add(tick, functools.partial(norm, m, start))
            tick += 1
    last_tick = tick

    small(0)
    load_own().start()
    pl.when(has_low)(lambda: to_low().start())
    pl.when(has_high)(lambda: to_high().start())

    @pl.when(jnp.logical_not(has_low))
    def _():
        near_ref[:, :HALF] = jnp.zeros((micro, HALF, width), near_ref.dtype)

    @pl.when(jnp.logical_not(has_high))
    def _():
        near_ref[:, near_rows - HALF :] = jnp.zeros((micro, HALF, width), near_ref.dtype)

    lags = (0, 3, 6, 10, 12)
    for t in range(max(pieces + lags[-1], last_tick + 1)):
        if t < pieces:
            exchange(t, 0).start()
            own(t).start()
        for stage in (1, 2, 3):
            p = t - lags[stage]
            if 0 <= p < pieces:
                if stage == 1:
                    own(p).wait()
                exchange(p, stage - 1).wait_recv()
                exchange(p, stage).start()
        if 0 <= t - lags[4] < pieces:
            exchange(t - lags[4], 3).wait_recv()
        for work in beside.get(t, ()):
            work()
    for p in range(pieces):
        for stage in range(4):
            exchange(p, stage).wait_send()
    pl.when(has_low)(lambda: to_low().wait_send())
    pl.when(has_high)(lambda: to_high().wait_send())


def gather_and_prepare(share, part, latents, lengths, text_len, step=256):
    count = lax.axis_size("seq")
    me = lax.axis_index("seq")
    rows, width = share.shape
    micro, block_rows, model_width = latents.shape
    items = lengths.shape[1]
    near_rows = block_rows + 2 * HALF
    own_rows = micro * block_rows
    ladder = jnp.asarray(lane_ladder()).reshape(1, 128)
    if count != 16 or rows % 16 or width % step or lax.axis_size("tensor") != 2:
        ahead = [(i, i + 1) for i in range(count - 1)]
        behind = [(i + 1, i) for i in range(count - 1)]
        low_rows = lax.ppermute(latents[:, block_rows - HALF :], "seq", ahead)
        high_rows = lax.ppermute(latents[:, :HALF], "seq", behind)
        near_latent = jnp.concatenate([low_rows, latents, high_rows], axis=1)
        total = seq_sum(part).reshape(micro, items, 6 * model_width)
        parts = []
        for m in range(micro):
            base, offset, later, self_bias, cross_bias = prepare(
                me * block_rows,
                count * block_rows,
                [lengths[m, k] for k in range(items)],
                [text_len[m, k] for k in range(items)],
                block_rows,
            )
            two = lax.dynamic_slice_in_dim(total[m], base, 2, 0)
            xhat, _ = spread_rows(near_latent[m].astype(f32))
            shift, factor = [
                jnp.where(later > 0.5, two[1], two[0])[:, i * model_width : (i + 1) * model_width]
                for i in range(2)
            ]
            normed = (xhat * (1.0 + factor) + shift).astype(bf16)
            parts.append(
                (
                    normed,
                    normed[HALF : HALF + block_rows].T,
                    two[None],
                    later[HALF : HALF + block_rows],
                    jnp.stack(lane_tables(offset, ladder)),
                    jnp.concatenate(self_bias, axis=0),
                    cross_bias,
                )
            )
        axes = (0, 1, 0, 0, 1, 0, 0)
        joined = [jnp.concatenate(group, axis=axis) for group, axis in zip(zip(*parts), axes)]
        return [lax.all_gather(share, "seq", axis=0, tiled=True)] + joined
    pieces = width // step
    any_space = pl.BlockSpec(memory_space=pl.ANY)
    vmem = pl.BlockSpec(memory_space=pltpu.VMEM)
    smem = pl.BlockSpec(memory_space=pltpu.SMEM)
    outs = pl.pallas_call(
        functools.partial(
            gather_kernel,
            pieces=pieces,
            step=step,
            y_first=tuple(range(pieces // 6, pieces, pieces // 3)),
            seq_count=count,
        ),
        out_shape=[
            jax.ShapeDtypeStruct((2, 2, 2, 2, rows, width), share.dtype),
            jax.ShapeDtypeStruct((micro * near_rows, model_width), bf16),
            jax.ShapeDtypeStruct((model_width, own_rows), bf16),
            jax.ShapeDtypeStruct((micro, 2, 6 * model_width), f32),
            jax.ShapeDtypeStruct((own_rows, 1), f32),
            jax.ShapeDtypeStruct((3, micro * near_rows, 128), f32),
            jax.ShapeDtypeStruct((own_rows, 3 * HALF), f32),
            jax.ShapeDtypeStruct((own_rows, 2 * TXT), f32),
        ],
        in_specs=[any_space, vmem, any_space, smem, smem, vmem],
        out_specs=[any_space] + [vmem] * 7,
        scratch_shapes=[
            pltpu.VMEM((micro, near_rows, model_width), bf16),
        ]
        + small_scratch(part.shape)
        + [
            pltpu.SemaphoreType.DMA((pieces,)),
            pltpu.SemaphoreType.DMA((4, pieces)),
            pltpu.SemaphoreType.DMA((4, pieces)),
            pltpu.SemaphoreType.DMA,
            pltpu.SemaphoreType.DMA((2,)),
            pltpu.SemaphoreType.DMA((2,)),
        ],
        compiler_params=pltpu.CompilerParams(
            collective_id=1, has_side_effects=True, vmem_limit_bytes=60 * 1024 * 1024
        ),
        cost_estimate=pl.CostEstimate(
            flops=0, bytes_accessed=20 * count * rows * width, transcendentals=0
        ),
        name="gather_and_prepare",
    )(share, part, latents, lengths, text_len, ladder)
    return [outs[0].reshape(count * rows, width)] + list(outs[1:])


SLOTS = 6


def when(condition):
    if isinstance(condition, bool):
        return (lambda work: work()) if condition else (lambda work: None)
    return pl.when(condition)


class Pieces:
    def __init__(self, refs, out_ref, partners, digits, step, lag=3):
        (
            self.own, self.got0, self.got1, self.got2, self.got3, self.staged,
            self.out_sem, self.send_sem, self.recv_sem,
        ) = refs
        self.out_ref = out_ref
        self.partners = partners
        self.digits = digits
        self.step = step
        self.lag = lag

    @staticmethod
    def scratch(rows, step):
        return [
            pltpu.VMEM((SLOTS, 2, 2, 2, rows, step), bf16),
            pltpu.VMEM((SLOTS, 2, 2, 2, rows, step), bf16),
            pltpu.VMEM((SLOTS, 2, 2, rows, step), bf16),
            pltpu.VMEM((SLOTS, 2, rows, step), bf16),
            pltpu.VMEM((SLOTS, rows, step), bf16),
            pltpu.VMEM((SLOTS, rows, step), f32),
            pltpu.SemaphoreType.DMA((SLOTS,)),
            pltpu.SemaphoreType.DMA((4, SLOTS)),
            pltpu.SemaphoreType.DMA((4, SLOTS)),
        ]

    def exchange(self, stage, source, target, slot):
        return send_to(
            self.partners[stage],
            source,
            target,
            self.send_sem.at[stage, slot],
            self.recv_sem.at[stage, slot],
        )

    def over_core(self, source, slot):
        return self.exchange(0, source, self.got0.at[slot], slot)

    PATHS = ((2, 1, 0),)

    def spot(self, path, stage, other):
        axes = (self.digits[3], self.digits[2], self.digits[1])
        index = [slice(None)] * 3
        for axis in path[: stage - 1]:
            index[axis] = axes[axis]
        axis = path[stage - 1]
        index[axis] = 1 - axes[axis] if other else axes[axis]
        return tuple(index)

    def hop(self, path, stage, slot):
        partner = (3, 2, 1)[path[stage - 1]]
        target = (self.got1, self.got2, self.got3)[stage - 1].at[slot]
        source = self.own.at[(slot,) + self.spot(path, stage, True)]
        return send_to(
            self.partners[partner],
            source,
            target,
            self.send_sem.at[stage, slot],
            self.recv_sem.at[stage, slot],
        )

    def by_path(self, item, work):
        work(self.PATHS[0])

    def add_hop(self, path, stage, slot):
        got = (self.got1, self.got2, self.got3)[stage - 1]
        index = self.spot(path, stage, False)
        free = [k for k in range(3) if isinstance(index[k], slice)]
        for count in range(2 ** len(free)):
            bits = [(count >> k) & 1 for k in range(len(free))]
            full = list(index)
            for k, bit in zip(free, bits):
                full[k] = bit
            at = (slot,) + tuple(full)
            total = self.own[at].astype(f32) + got[(slot,) + tuple(bits)].astype(f32)
            if stage < 3:
                self.own[at] = total.astype(bf16)
            else:
                self.staged[slot] = total

    def store(self, item, slot):
        columns = pl.ds(pl.multiple_of(item * self.step, self.step), self.step)
        return pltpu.make_async_copy(
            self.staged.at[slot], self.out_ref.at[:, columns], self.out_sem.at[slot]
        )

    def wait_sent(self, slot):
        for stage in (1, 2, 3):
            self.hop(self.PATHS[0], stage, slot).wait_send()

    def add_core(self, item, slot, left):
        for i in range(2):
            for j in range(2):
                for k in range(2):
                    total = left(i, j, k).astype(f32) + self.got0[slot, i, j, k].astype(f32)
                    self.own[slot, i, j, k] = total.astype(bf16)
        self.by_path(item, lambda path: self.hop(path, 1, slot).start())

    def later_steps(self, t, count):
        lag = self.lag

        @when((t >= lag) & (t - lag < count))
        def _():
            item = t - lag
            slot = item % SLOTS
            self.hop(self.PATHS[0], 1, slot).wait_recv()

            def work(path):
                self.add_hop(path, 1, slot)
                self.hop(path, 2, slot).start()

            self.by_path(item, work)

        @when((t >= lag + 1) & (t - lag - 1 < count))
        def _():
            item = t - lag - 1
            slot = item % SLOTS
            self.hop(self.PATHS[0], 2, slot).wait_recv()

            def work(path):
                self.add_hop(path, 2, slot)
                self.hop(path, 3, slot).start()

            self.by_path(item, work)

        @when((t >= lag + 2) & (t - lag - 2 < count))
        def _():
            item = t - lag - 2
            slot = item % SLOTS
            self.hop(self.PATHS[0], 3, slot).wait_recv()
            when(item >= SLOTS)(lambda: self.store(0, slot).wait())
            self.by_path(item, lambda path: self.add_hop(path, 3, slot))
            self.store(item, slot).start()

    def run(self, sources, spans, own_sem, beside=(), last=0):
        core = self.digits[0]
        step = self.step
        count = sum(width for _, width in spans) // step

        def over_core(source, column, slot):
            return self.over_core(source.at[:, :, :, 1 - core, :, pl.ds(column, step)], slot)

        def load(source, column, slot):
            return pltpu.make_async_copy(
                source.at[:, :, :, core, :, pl.ds(column, step)],
                self.own.at[slot],
                own_sem.at[slot],
            )

        def tick(t, carry):
            @pl.when(t < count)
            def _():
                slot = t % SLOTS
                pl.when(t >= SLOTS)(lambda: self.wait_sent(slot))
                done = 0
                for source, (column, width) in zip(sources, spans):

                    @pl.when((t >= done) & (t < done + width // step))
                    def _(source=source, done=done, column=column):
                        spot = pl.multiple_of(column + (t - done) * step, step)
                        over_core(source, spot, slot).start()
                        load(source, spot, slot).start()

                    done += width // step

            @pl.when((t >= 1) & (t - 1 < count))
            def _():
                slot = (t - 1) % SLOTS
                load(sources[0], 0, slot).wait()
                over_core(sources[0], 0, slot).wait()
                self.add_core(t - 1, slot, lambda i, j, k: self.own[slot, i, j, k])

            self.later_steps(t, count)
            for begin, end, work in beside:
                pl.when((t >= begin) & (t < end))(functools.partial(work, t))
            return carry

        lax.fori_loop(0, max(count + self.lag + 2, last + 1), tick, 0)
        self.finish(count)

    def finish(self, count):
        for back in range(min(SLOTS, count)):
            slot = (count - 1 - back) % SLOTS
            self.store(0, slot).wait()
            self.wait_sent(slot)


PIECE_REFS = 9


def norm_back_tile(grad, upstream, hidden, shift_rows, factor):
    xhat, scale = spread_rows(hidden)
    inner = grad * (1.0 + factor)
    mean_inner = jnp.mean(inner, axis=-1, keepdims=True)
    mean_cross = jnp.mean(inner * xhat, axis=-1, keepdims=True)
    total = upstream + scale * (inner - mean_inner - xhat * mean_cross)
    scaled = grad * xhat
    sums = [
        [
            jnp.sum(jnp.where(chosen, values, 0.0), axis=0, keepdims=True)
            for values in (grad, scaled)
        ]
        for chosen in shift_rows
    ]
    return total, sums


def finish_kernel(*refs, spans, step, micro, loaded):
    refs = list(refs)
    sources = [refs.pop(0) for _ in spans]
    (
        own_ref, from_low_ref, from_high_ref, normed_t_ref, weight_ref, table_ref,
        up_ref, latent_ref, two_ref, later_ref, sums_ref, lengths_ref, feature_ref, other_ref,
        out_ref, grad_ref, mod_ref, bias_ref, got_other_ref,
        own_sem, back_ref, got_back, qkv_w_ref, weight_sem, g_qkv_ref, first_sums,
        back_send, back_recv, other_sem,
    ) = refs[:29]
    pieces_refs = refs[29 : 29 + PIECE_REFS]
    prep, held, got, small_total, small_send, small_recv = refs[29 + PIECE_REFS :]
    me = lax.axis_index("seq")
    mine = lax.axis_index("tensor")
    digits = seq_digits(me)
    core = digits[0]
    rows, width = latent_ref.shape
    local = own_ref.shape[2]
    block_rows = rows // micro
    near_rows = block_rows + 2 * HALF
    items = lengths_ref.shape[1]
    load = pltpu.make_async_copy(weight_ref.at[:, : 3 * local], qkv_w_ref, weight_sem)
    load.start()
    partners = greet_all(me, mine, digits)
    pieces = Pieces(pieces_refs, out_ref, partners, digits, step)

    def over_tensor(m):
        span = pl.ds(m * block_rows, block_rows)
        return to_tensor(
            mine, back_ref.at[span], got_back.at[span], back_send.at[m], back_recv.at[m]
        )

    def own_table(index):
        return jnp.concatenate(
            [
                table_ref[index, m * near_rows + HALF : (m + 1) * near_rows - HALF]
                for m in range(micro)
            ],
            axis=0,
        )

    def project_back(kind, column):
        lanes = pl.ds(pl.multiple_of(column, step), step)
        total = own_ref[kind, :, lanes]
        if kind:
            blocks = []
            for m in range(micro):
                first = m * block_rows
                blocks.append(
                    total[first : first + HALF] + from_low_ref[m, kind - 1, :, lanes].astype(f32)
                )
                if block_rows > 2 * HALF:
                    blocks.append(total[first + HALF : first + block_rows - HALF])
                blocks.append(
                    total[first + block_rows - HALF : first + block_rows]
                    + from_high_ref[m, kind - 1, :, lanes].astype(f32)
                )
            total = jnp.concatenate(blocks, axis=0)
        if kind < 2:
            tables = own_table(0), -own_table(1), -own_table(2)
            total = jnp.concatenate(
                [turn(total[:, i : i + 128], *tables) for i in range(0, step, 128)], axis=1
            )
        grad = total.astype(bf16)
        lanes = pl.ds(pl.multiple_of(kind * local + column, step), step)
        g_qkv_ref[:, :, :, :, :, lanes] = (
            nn(normed_t_ref[...], grad).astype(bf16).reshape(g_qkv_ref.shape[:5] + (step,))
        )
        grad_ref[...] += nt(grad, qkv_w_ref[:, lanes])

    def send_back():
        back_ref[...] = grad_ref[...].astype(bf16)
        for m in range(micro):
            over_tensor(m).start()

    def norm_one(m):
        over_tensor(m).wait_recv()

        def emit(span, start, total):
            grad_ref[span, :] = total

        norm_back_unit(
            m, 0, block_rows,
            lambda span: back_ref[span, :].astype(f32) + got_back[span, :].astype(f32),
            up_ref, latent_ref, two_ref, later_ref, first_sums, emit,
        )

    def fill(target):
        span = target.shape[2]
        size = 128 * math.gcd(span // 128, width // 128)
        for m in range(micro):
            ends = [lengths_ref[m, 0]]
            for k in range(1, items):
                ends.append(ends[-1] + lengths_ref[m, k])
            first_item = sum((end <= me * block_rows).astype(jnp.int32) for end in ends)
            base = jnp.minimum(first_item, items - 2)
            for k in range(items):
                row = slice(m * items + k, m * items + k + 1)
                for first in range(0, 6 * width, size):
                    ref, at = (
                        (first_sums, first) if first < 2 * width else (sums_ref, first - 2 * width)
                    )
                    target[first // span, row, first % span : first % span + size] = sum(
                        jnp.where(
                            base + item == k, ref[m, item : item + 1, at : at + size], 0.0
                        )
                        for item in range(2)
                    )

    def modulation_grads(total):
        span = total.shape[2]
        for index in range(4):
            lanes = slice(index * span, (index + 1) * span)
            bias_ref[:, lanes] = jnp.sum(total[index], axis=0, keepdims=True)
            mod_ref[:, lanes] = sum(
                feature_ref[:, i : i + 1] * total[index, i : i + 1] for i in range(micro * items)
            )

    small = small_sum(
        partners, mine, core, fill, prep, held, got, small_total, modulation_grads,
        small_send, small_recv,
    )
    work = []
    spot = 0
    columns = local // step
    work.append((0, 1, lambda t: loaded()))
    work.append((0, 1, lambda t: load.wait()))
    spot = 1
    for kind in range(3):
        work.append(
            (spot, spot + columns, lambda t, k=kind, s=spot: project_back(k, (t - s) * step))
        )
        spot += columns
    work.append((spot - 1, spot, lambda t: send_back()))
    spot += 3
    for m in range(micro):
        work.append((spot, spot + 1, lambda t, m=m: norm_one(m)))
        spot += 4 if m < micro - 1 else 1
    for k in range(SMALL_STEPS + 1):
        work.append((spot, spot + 1, lambda t, k=k: small(k)))
        spot += 2 if k < 3 else 1
    grad_ref[...] = jnp.zeros_like(grad_ref)
    over_other = to_tensor(
        mine, other_ref.at[pl.ds(0, block_rows)], got_other_ref, other_sem.at[0], other_sem.at[1]
    )
    over_other.start()
    pieces.run(sources + [g_qkv_ref], spans + ((0, 3 * local),), own_sem, work, spot)
    for m in range(micro):
        over_tensor(m).wait_send()
    over_other.wait()


def finish_stage(
    own, from_low, from_high, normed_t, weights, table, upstream, latent, two, later, sums,
    lengths, features, other, sources, spans, micro, which=0, step=256,
):
    seq_count = lax.axis_size("seq")
    rows, width = latent.shape
    items = lengths.shape[1]
    local = own.shape[2]
    share = width // seq_count
    own_features = features.T
    any_space = pl.BlockSpec(memory_space=pl.ANY)
    vmem = pl.BlockSpec(memory_space=pltpu.VMEM)
    smem = pl.BlockSpec(memory_space=pltpu.SMEM)
    args = [
        own, from_low, from_high, normed_t, weights, table,
        upstream, latent, two, later, sums, lengths, own_features, other,
    ]
    places = (0, 1, 2, 3, 5, 6, 7, 8, 9, 10)
    return pl.pallas_call(
        with_loads(
            functools.partial(finish_kernel, spans=spans, step=step, micro=micro),
            [len(sources) + place for place in places],
        ),
        out_shape=[
            jax.ShapeDtypeStruct((share, sum(span for _, span in spans) + 3 * local), f32),
            jax.ShapeDtypeStruct((rows, width), f32),
            jax.ShapeDtypeStruct((own_features.shape[0], 6 * width), f32),
            jax.ShapeDtypeStruct((1, 6 * width), f32),
            jax.ShapeDtypeStruct((rows // micro, width), bf16),
        ],
        in_specs=[any_space] * (len(sources) + 11) + [smem, vmem, any_space],
        out_specs=[any_space, vmem, vmem, vmem, any_space],
        scratch_shapes=[
            pltpu.SemaphoreType.DMA((SLOTS,)),
            pltpu.VMEM((rows, width), bf16),
            pltpu.VMEM((rows, width), bf16),
            pltpu.VMEM((width, 3 * local), bf16),
            pltpu.SemaphoreType.DMA,
            pltpu.VMEM((2, 2, 2, 2, share, 3 * local), bf16),
            pltpu.VMEM((micro, 2, 2 * width), f32),
            pltpu.SemaphoreType.DMA((micro,)),
            pltpu.SemaphoreType.DMA((micro,)),
            pltpu.SemaphoreType.DMA((2,)),
        ]
        + Pieces.scratch(share, step)
        + small_scratch((micro * items, 6 * width))
        + load_scratch([args[place] for place in places]),
        compiler_params=pltpu.CompilerParams(
            collective_id=which, has_side_effects=True, vmem_limit_bytes=60 * 1024 * 1024
        ),
        cost_estimate=pl.CostEstimate(
            flops=12 * rows * width * local, bytes_accessed=40 * rows * width, transcendentals=0
        ),
        name="finish_stage",
    )(
        *[source.reshape(2, 2, 2, 2, share, source.shape[1]) for source in sources],
        *args,
    )


def finish_apart(grads, back, upstream, latent, two, later, sums, lengths, features, other):
    rows, width = latent.shape
    micro, items = lengths.shape
    totals = [early_sum(grad) for grad in grads]
    latent_grad, first_sums = norm_back(upstream, back, swap(back), latent, two, later, 0, micro)
    pieces = jnp.concatenate([first_sums.reshape(micro, 2, 2 * width), sums], axis=2)
    first_item = jnp.sum(
        (jnp.cumsum(lengths, axis=1) <= lax.axis_index("seq") * (rows // micro)).astype(jnp.int32),
        axis=1,
    )
    base = jnp.minimum(first_item, items - 2)
    spots = (base[:, None] + jnp.arange(2))[:, :, None] == jnp.arange(items)
    item_grad = jnp.sum(jnp.where(spots[..., None], pieces[:, :, None], 0.0), axis=1)
    total = seq_sum(item_grad.reshape(micro * items, 6 * width))
    mod_grad = jnp.dot(features.T, total, precision=highest)
    return totals, latent_grad, mod_grad, jnp.sum(total, axis=0, keepdims=True), swap(other)


def early_sum(grad):
    return lax.psum_scatter(grad, "seq", scatter_dimension=0, tiled=True).astype(f32)


def turn(values, own, below, above):
    quarter = HD // 4
    return (
        values * own
        + pltpu.roll(values, quarter, 1) * below
        + pltpu.roll(values, 2 * HD - quarter, 1) * above
    )


def project_kernel(normed_ref, weight_ref, table_ref, out_ref, *, turned):
    j = pl.program_id(0)
    product = nn(normed_ref[...], weight_ref[...])

    @pl.when(j < turned)
    def _():
        for part in range(product.shape[1] // 128):
            lanes = slice(part * 128, (part + 1) * 128)
            out_ref[:, lanes] = turn(
                product[:, lanes], table_ref[0], table_ref[1], table_ref[2]
            ).astype(bf16)

    @pl.when(j >= turned)
    def _():
        out_ref[...] = product.astype(bf16)


def project(normed, weights, table, local, step=256):
    rows, width = normed.shape
    return pl.pallas_call(
        functools.partial(project_kernel, turned=2 * local // step),
        grid=(3 * local // step,),
        in_specs=[
            pl.BlockSpec((rows, width), lambda j: (0, 0)),
            pl.BlockSpec((width, step), lambda j: (0, j)),
            pl.BlockSpec((3, rows, 128), lambda j: (0, 0, 0)),
        ],
        out_specs=pl.BlockSpec((rows, step), lambda j: (0, j)),
        out_shape=jax.ShapeDtypeStruct((rows, 3 * local), bf16),
        compiler_params=kernel_params(1, 60),
        cost_estimate=pl.CostEstimate(
            flops=2 * rows * width * 3 * local,
            bytes_accessed=2 * (rows * width + 3 * local * (width + rows)),
            transcendentals=0,
        ),
        name="qkv_projection",
    )(normed, weights, table)


def head_lanes(shape):
    return lax.broadcasted_iota(jnp.int32, shape, 1) < HD


def one_head(values, first, which):
    return jnp.where(first if which == 0 else ~first, values, jnp.zeros_like(values))


def soft_rows(scores):
    peak = jnp.max(scores, axis=-1, keepdims=True)
    raised = jnp.exp(scores - peak)
    total = jnp.sum(raised, axis=-1, keepdims=True)
    return raised * (1.0 / total), peak + jnp.log(total)


def attend_rows(query, keys, values, bias):
    first = head_lanes(query.shape)
    out = None
    logs = []
    for which in range(2):
        scores = nt(one_head(query, first, which), keys) * (HD**-0.5) + bias
        weights, log_total = soft_rows(scores)
        mixed = nn(weights.astype(bf16), values)
        out = mixed if which == 0 else jnp.where(first, out, mixed)
        logs.append(log_total)
    return out, logs


def attend_rows_back(query, keys, values, bias, logs, grad):
    first = head_lanes(query.shape)
    query_grad = key_grad = value_grad = None
    for which in range(2):
        own_query = one_head(query, first, which)
        own_grad = one_head(grad, first, which)
        scores = nt(own_query, keys) * (HD**-0.5) + bias
        chances = jnp.exp(scores - logs[which])
        chance_grad = nt(own_grad, values)
        score_grad = (
            chances * (chance_grad - jnp.sum(chances * chance_grad, axis=-1, keepdims=True))
        ).astype(bf16)
        to_query = nn(score_grad, keys) * (HD**-0.5)
        to_key = tn(score_grad, own_query) * (HD**-0.5)
        to_value = tn(chances.astype(bf16), own_grad)
        if which == 0:
            query_grad, key_grad, value_grad = to_query, to_key, to_value
        else:
            query_grad = jnp.where(first, query_grad, to_query)
            key_grad = key_grad + to_key
            value_grad = value_grad + to_value
    return query_grad, key_grad, value_grad


def put_logs(log_ref, rows, logs, pair):
    lane = lax.broadcasted_iota(jnp.int32, (logs[0].shape[0], 128), 1)
    kept = log_ref[rows, :]
    kept = jnp.where(lane == 2 * pair, logs[0], kept)
    log_ref[rows, :] = jnp.where(lane == 2 * pair + 1, logs[1], kept)


def get_logs(log_ref, rows, pair):
    kept = log_ref[rows, :]
    lane = lax.broadcasted_iota(jnp.int32, kept.shape, 1)
    return [
        jnp.sum(jnp.where(lane == 2 * pair + which, kept, 0.0), axis=1, keepdims=True)
        for which in range(2)
    ]


def spread_rows(hidden):
    center = hidden - jnp.mean(hidden, axis=-1, keepdims=True)
    spread = jnp.mean(center * center, axis=-1, keepdims=True)
    scale = lax.rsqrt(spread + norm_eps)
    return center * scale, scale


def item_row(two_ref, later_ref, index):
    width = two_ref.shape[2] // 6
    lanes = slice(index * width, (index + 1) * width)
    return jnp.where(later_ref[...] > 0.5, two_ref[0, 1:2, lanes], two_ref[0, 0:1, lanes])


def norm_kernel(*refs, index, with_weight):
    refs = list(refs)
    base_ref, own_ref, got_ref, two_ref, later_ref = refs[:5]
    weight_ref = refs[5] if with_weight else None
    outs = refs[5 + with_weight :]
    hidden = (
        base_ref[...].astype(f32) + own_ref[...].astype(f32) + got_ref[...].astype(f32)
    )
    xhat, _ = spread_rows(hidden)
    normed = (
        xhat * (1.0 + item_row(two_ref, later_ref, index + 1)) + item_row(two_ref, later_ref, index)
    ).astype(bf16)
    outs[0][...] = hidden
    outs[1][...] = normed
    outs[2][...] = normed.T
    if with_weight:
        outs[3][...] = nn(normed, weight_ref[...]).astype(bf16)


def norm_forward(base, own, got, two, later, index, micro, weights=None, column=0, out_width=0):
    rows, width = base.shape
    tile = rows // micro
    row_tile = pl.BlockSpec((tile, width), lambda i: (i, 0))
    in_specs = [
        row_tile,
        row_tile,
        row_tile,
        pl.BlockSpec((1, 2, 6 * width), lambda i: (i, 0, 0)),
        pl.BlockSpec((tile, 1), lambda i: (i, 0)),
    ]
    out_specs = [row_tile, row_tile, pl.BlockSpec((width, tile), lambda i: (0, i))]
    out_shape = [
        jax.ShapeDtypeStruct((rows, width), f32),
        jax.ShapeDtypeStruct((rows, width), bf16),
        jax.ShapeDtypeStruct((width, rows), bf16),
    ]
    args = [base, own, got, two, later]
    if weights is not None:
        in_specs.append(pl.BlockSpec((width, out_width), lambda i: (0, column)))
        out_specs.append(pl.BlockSpec((tile, out_width), lambda i: (i, 0)))
        out_shape.append(jax.ShapeDtypeStruct((rows, out_width), bf16))
        args.append(weights)
    return pl.pallas_call(
        functools.partial(norm_kernel, index=index, with_weight=weights is not None),
        grid=(micro,),
        in_specs=in_specs,
        out_specs=out_specs,
        out_shape=out_shape,
        compiler_params=kernel_params(1, 60),
        cost_estimate=pl.CostEstimate(
            flops=2 * rows * width * out_width, bytes_accessed=16 * rows * width, transcendentals=0
        ),
        name="norm_forward",
    )(*args)


def norm_back_kernel(*refs, index, with_weight):
    refs = list(refs)
    up_ref, own_ref, got_ref, hidden_ref, two_ref, later_ref = refs[:6]
    weight_ref = refs[6] if with_weight else None
    outs = refs[6 + with_weight :]
    xhat, scale = spread_rows(hidden_ref[...].astype(f32))
    grad = own_ref[...].astype(f32) + got_ref[...].astype(f32)
    inner = grad * (1.0 + item_row(two_ref, later_ref, index + 1))
    mean_inner = jnp.mean(inner, axis=-1, keepdims=True)
    mean_cross = jnp.mean(inner * xhat, axis=-1, keepdims=True)
    total = up_ref[...].astype(f32) + scale * (inner - mean_inner - xhat * mean_cross)
    outs[0][...] = total
    later = later_ref[...] > 0.5
    scaled = grad * xhat
    for item in range(2):
        chosen = later if item else ~later
        outs[1][0, item, 0:1] = jnp.sum(jnp.where(chosen, grad, 0.0), axis=0, keepdims=True)
        outs[1][0, item, 1:2] = jnp.sum(jnp.where(chosen, scaled, 0.0), axis=0, keepdims=True)
    if with_weight:
        rounded = total.astype(bf16)
        outs[2][...] = rounded.T
        outs[3][...] = nn(rounded, weight_ref[...]).astype(bf16)


def norm_back(up, own, got, hidden, two, later, index, micro, weights=None, column=0, out_width=0):
    rows, width = hidden.shape
    tile = rows // micro
    row_tile = pl.BlockSpec((tile, width), lambda i: (i, 0))
    in_specs = [
        row_tile,
        row_tile,
        row_tile,
        row_tile,
        pl.BlockSpec((1, 2, 6 * width), lambda i: (i, 0, 0)),
        pl.BlockSpec((tile, 1), lambda i: (i, 0)),
    ]
    out_specs = [row_tile, pl.BlockSpec((1, 2, 2, width), lambda i: (i, 0, 0, 0))]
    out_shape = [
        jax.ShapeDtypeStruct((rows, width), f32),
        jax.ShapeDtypeStruct((micro, 2, 2, width), f32),
    ]
    args = [up, own, got, hidden, two, later]
    if weights is not None:
        in_specs.append(pl.BlockSpec((width, out_width), lambda i: (0, column)))
        out_specs += [
            pl.BlockSpec((width, tile), lambda i: (0, i)),
            pl.BlockSpec((tile, out_width), lambda i: (i, 0)),
        ]
        out_shape += [
            jax.ShapeDtypeStruct((width, rows), bf16),
            jax.ShapeDtypeStruct((rows, out_width), bf16),
        ]
        args.append(weights)
    return pl.pallas_call(
        functools.partial(norm_back_kernel, index=index, with_weight=weights is not None),
        grid=(micro,),
        in_specs=in_specs,
        out_specs=out_specs,
        out_shape=out_shape,
        compiler_params=kernel_params(1, 60),
        cost_estimate=pl.CostEstimate(
            flops=2 * rows * width * out_width, bytes_accessed=20 * rows * width, transcendentals=0
        ),
        name="norm_back",
    )(*args)


def add_product(acc_ref, out_ref, left, right):
    pair = pl.program_id(1)

    @pl.when(pair == 0)
    def _():
        acc_ref[...] = jnp.zeros_like(acc_ref)

    acc_ref[...] += nt(left, right)

    @pl.when(pair == pl.num_programs(1) - 1)
    def _():
        out_ref[...] = acc_ref[...].astype(bf16)


def self_kernel(q_ref, k_ref, v_ref, bias_ref, weight_ref, out_ref, log_ref, sum_ref, acc_ref):
    pair = pl.program_id(1)
    block_rows = out_ref.shape[0]
    for part in range(block_rows // HALF):
        rows = slice(part * HALF, (part + 1) * HALF)
        span = slice(part * HALF, (part + 3) * HALF)
        out, logs = attend_rows(
            q_ref[(part + 1) * HALF : (part + 2) * HALF, :],
            k_ref[span, :],
            v_ref[span, :],
            bias_ref[rows, :],
        )
        out_ref[rows, :] = out.astype(bf16)
        put_logs(log_ref, rows, logs, pair)
    add_product(acc_ref, sum_ref, out_ref[...], weight_ref[...])


def self_specs(block_rows, pairs):
    near = lambda first: pl.BlockSpec((block_rows + 2 * HALF, 128), lambda m, h: (m, first + h))
    return [
        near(0),
        near(pairs),
        near(2 * pairs),
        pl.BlockSpec((block_rows, 3 * HALF), lambda m, h: (m, 0)),
    ]


def self_attention(qkv, bias, weights, column, micro, block_rows):
    rows = micro * block_rows
    local = qkv.shape[1] // 3
    width = weights.shape[0]
    pairs = local // 128
    return pl.pallas_call(
        self_kernel,
        grid=(micro, pairs),
        in_specs=self_specs(block_rows, pairs)
        + [pl.BlockSpec((width, 128), lambda m, h: (0, column + h))],
        out_specs=[
            pl.BlockSpec((block_rows, 128), lambda m, h: (m, h)),
            pl.BlockSpec((block_rows, 128), lambda m, h: (m, 0)),
            pl.BlockSpec((block_rows, width), lambda m, h: (m, 0)),
        ],
        out_shape=[
            jax.ShapeDtypeStruct((rows, local), bf16),
            jax.ShapeDtypeStruct((rows, 128), f32),
            jax.ShapeDtypeStruct((rows, width), bf16),
        ],
        scratch_shapes=[pltpu.VMEM((block_rows, width), f32)],
        compiler_params=kernel_params(2, 60),
        cost_estimate=pl.CostEstimate(
            flops=rows * 2 * local * (width + 12 * HALF),
            bytes_accessed=20 * rows * local,
            transcendentals=rows * 3 * HALF * 2 * pairs,
        ),
        name="self_attention",
    )(qkv, qkv, qkv, bias, weights)


def self_back_kernel(
    q_ref, k_ref, v_ref, bias_ref, grad_ref, log_ref, own_ref, to_low_ref, to_high_ref
):
    pair = pl.program_id(1)
    parts = grad_ref.shape[0] // HALF
    pieces = [[None] * (parts + 2), [None] * (parts + 2)]
    for part in range(parts):
        rows = slice(part * HALF, (part + 1) * HALF)
        span = slice(part * HALF, (part + 3) * HALF)
        query_grad, key_grad, value_grad = attend_rows_back(
            q_ref[(part + 1) * HALF : (part + 2) * HALF, :],
            k_ref[span, :],
            v_ref[span, :],
            bias_ref[rows, :],
            get_logs(log_ref, rows, pair),
            grad_ref[rows, :],
        )
        own_ref[0, rows, :] = query_grad
        for kind, near_grad in enumerate((key_grad, value_grad)):
            for third in range(3):
                piece = near_grad[third * HALF : (third + 1) * HALF]
                held = pieces[kind][part + third]
                pieces[kind][part + third] = piece if held is None else held + piece
    for kind in range(2):
        to_low_ref[kind] = pieces[kind][0].astype(bf16)
        for part in range(parts):
            own_ref[1 + kind, part * HALF : (part + 1) * HALF, :] = pieces[kind][part + 1]
        to_high_ref[kind] = pieces[kind][parts + 1].astype(bf16)


def self_attention_back(qkv, bias, grad, logs, micro, block_rows):
    rows, local = grad.shape
    pairs = local // 128
    edge = pl.BlockSpec((2, None, HALF, 128), lambda m, h: (0, m, 0, h))
    return pl.pallas_call(
        self_back_kernel,
        grid=(micro, pairs),
        in_specs=self_specs(block_rows, pairs)
        + [
            pl.BlockSpec((block_rows, 128), lambda m, h: (m, h)),
            pl.BlockSpec((block_rows, 128), lambda m, h: (m, 0)),
        ],
        out_specs=[
            pl.BlockSpec((3, block_rows, 128), lambda m, h: (0, m, h)),
            edge,
            edge,
        ],
        out_shape=[
            jax.ShapeDtypeStruct((3, rows, local), f32),
            jax.ShapeDtypeStruct((2, micro, HALF, local), bf16),
            jax.ShapeDtypeStruct((2, micro, HALF, local), bf16),
        ],
        compiler_params=kernel_params(2, 60),
        cost_estimate=pl.CostEstimate(
            flops=20 * rows * 3 * HALF * local,
            bytes_accessed=40 * rows * local,
            transcendentals=rows * 3 * HALF * 2 * pairs,
        ),
        name="self_attention_back",
    )(qkv, qkv, qkv, bias, grad, logs)


def cross_kernel(q_ref, k_ref, v_ref, bias_ref, weight_ref, out_ref, log_ref, sum_ref, acc_ref):
    pair = pl.program_id(1)
    for part in range(q_ref.shape[0] // HALF):
        rows = slice(part * HALF, (part + 1) * HALF)
        out, logs = attend_rows(q_ref[rows, :], k_ref[...], v_ref[...], bias_ref[rows, :])
        out_ref[rows, :] = out.astype(bf16)
        put_logs(log_ref, rows, logs, pair)
    add_product(acc_ref, sum_ref, out_ref[...], weight_ref[...])


def cross_specs(block_rows, pairs):
    return [
        pl.BlockSpec((block_rows, 128), lambda m, h: (m, h)),
        pl.BlockSpec((2 * TXT, 128), lambda m, h: (m, h)),
        pl.BlockSpec((2 * TXT, 128), lambda m, h: (m, h)),
        pl.BlockSpec((block_rows, 2 * TXT), lambda m, h: (m, 0)),
    ]


def cross_attention(query, keys, values, bias, weights, column, micro, block_rows):
    rows, local = query.shape
    width = weights.shape[0]
    pairs = local // 128
    return pl.pallas_call(
        cross_kernel,
        grid=(micro, pairs),
        in_specs=cross_specs(block_rows, pairs)
        + [pl.BlockSpec((width, 128), lambda m, h: (0, column + h))],
        out_specs=[
            pl.BlockSpec((block_rows, 128), lambda m, h: (m, h)),
            pl.BlockSpec((block_rows, 128), lambda m, h: (m, 0)),
            pl.BlockSpec((block_rows, width), lambda m, h: (m, 0)),
        ],
        out_shape=[
            jax.ShapeDtypeStruct((rows, local), bf16),
            jax.ShapeDtypeStruct((rows, 128), f32),
            jax.ShapeDtypeStruct((rows, width), bf16),
        ],
        scratch_shapes=[pltpu.VMEM((block_rows, width), f32)],
        compiler_params=kernel_params(2, 60),
        cost_estimate=pl.CostEstimate(
            flops=rows * 2 * local * (width + 8 * TXT),
            bytes_accessed=16 * rows * local,
            transcendentals=rows * 2 * TXT * 2 * pairs,
        ),
        name="cross_attention",
    )(query, keys, values, bias, weights)


def cross_back_kernel(
    q_ref, k_ref, v_ref, bias_ref, grad_ref, log_ref, weight_ref,
    dq_ref, dk_ref, dv_ref, sum_ref, acc_ref,
):
    pair = pl.program_id(1)
    key_total = value_total = None
    for part in range(q_ref.shape[0] // HALF):
        rows = slice(part * HALF, (part + 1) * HALF)
        query_grad, key_grad, value_grad = attend_rows_back(
            q_ref[rows, :],
            k_ref[...],
            v_ref[...],
            bias_ref[rows, :],
            get_logs(log_ref, rows, pair),
            grad_ref[rows, :],
        )
        dq_ref[rows, :] = query_grad.astype(bf16)
        key_total = key_grad if part == 0 else key_total + key_grad
        value_total = value_grad if part == 0 else value_total + value_grad
    dk_ref[...] = key_total.astype(bf16)
    dv_ref[...] = value_total.astype(bf16)
    add_product(acc_ref, sum_ref, dq_ref[...], weight_ref[...])


def cross_attention_back(
    query, keys, values, bias, grad, logs, weights, column, micro, block_rows
):
    rows, local = query.shape
    width = weights.shape[0]
    pairs = local // 128
    text = pl.BlockSpec((2 * TXT, 128), lambda m, h: (m, h))
    return pl.pallas_call(
        cross_back_kernel,
        grid=(micro, pairs),
        in_specs=cross_specs(block_rows, pairs)
        + [
            pl.BlockSpec((block_rows, 128), lambda m, h: (m, h)),
            pl.BlockSpec((block_rows, 128), lambda m, h: (m, 0)),
            pl.BlockSpec((width, 128), lambda m, h: (0, column + h)),
        ],
        out_specs=[
            pl.BlockSpec((block_rows, 128), lambda m, h: (m, h)),
            text,
            text,
            pl.BlockSpec((block_rows, width), lambda m, h: (m, 0)),
        ],
        out_shape=[
            jax.ShapeDtypeStruct((rows, local), bf16),
            jax.ShapeDtypeStruct(keys.shape, bf16),
            jax.ShapeDtypeStruct(keys.shape, bf16),
            jax.ShapeDtypeStruct((rows, width), bf16),
        ],
        scratch_shapes=[pltpu.VMEM((block_rows, width), f32)],
        compiler_params=kernel_params(2, 60),
        cost_estimate=pl.CostEstimate(
            flops=rows * 2 * local * (width + 20 * TXT),
            bytes_accessed=30 * rows * local,
            transcendentals=rows * 2 * TXT * 2 * pairs,
        ),
        name="cross_attention_back",
    )(query, keys, values, bias, grad, logs, weights)


def ffn_kernel(*refs, summed):
    (
        normed_ref, normed_t_ref, cot_ref, cot_t_ref, outer_ref, gate_ref, up_ref,
        g_outer_ref, g_gate_ref, g_up_ref, out_ref, back_ref, *refs,
    ) = refs
    j = pl.program_id(0)
    step = gate_ref.shape[1]
    if summed:
        sum_ref, out_acc, back_acc, full = refs[:4]
        me = lax.axis_index("seq")
        digits = seq_digits(me)
        core = digits[0]
        partners = [me + stride * (1 - 2 * digit) for stride, digit in zip(STRIDES, digits)]
        pl.when(j == 0)(lambda: [greet(me, digits), None][1])
        pieces = Pieces(refs[4:], sum_ref, partners, digits, step, lag=2)
        count = summed

        def over_core(slot):
            return pieces.over_core(full.at[slot, :, :, :, 1 - core], slot)

        def tick(t):
            @when((t >= 1) & (t - 1 < count))
            def _():
                slot = (t - 1) % SLOTS
                when(t - 1 >= SLOTS)(lambda: pieces.wait_sent(slot))
                over_core(slot).wait()
                pieces.add_core(t - 1, slot, lambda a, b, c: full[slot, a, b, c, core])

            pieces.later_steps(t, count)

    else:
        out_acc, back_acc = refs
    if summed:
        tick(j)
    gate = nn(normed_ref[...], gate_ref[...])
    up = nn(normed_ref[...], up_ref[...])
    grad = nn(cot_ref[...], outer_ref[...])
    chance = 1.0 / (1.0 + jnp.exp(-gate))
    swish = gate * chance
    active = (swish * up).astype(bf16)
    gate_grad = (grad * up * (chance * (1.0 + gate * (1.0 - chance)))).astype(bf16)
    up_grad = (grad * swish).astype(bf16)
    g_up = nn(normed_t_ref[...], up_grad).astype(bf16)
    if summed:

        @pl.when(j < count)
        def _():
            slot = j % SLOTS
            full[slot] = g_up.reshape(full.shape[1:])
            over_core(slot).start()

        @pl.when(j >= count)
        def _():
            g_up_ref[...] = g_up
    else:
        g_up_ref[...] = g_up
    g_gate_ref[...] = nn(normed_t_ref[...], gate_grad).astype(bf16)
    g_outer_ref[...] = nn(cot_t_ref[...], active).astype(bf16)

    @pl.when(j == 0)
    def _():
        out_acc[...] = jnp.zeros_like(out_acc)
        back_acc[...] = jnp.zeros_like(back_acc)

    out_acc[...] += nt(active, outer_ref[...])
    back_acc[...] += nt(gate_grad, gate_ref[...])
    back_acc[...] += nt(up_grad, up_ref[...])

    @pl.when(j == pl.num_programs(0) - 1)
    def _():
        out_ref[...] = out_acc[...].astype(bf16)
        back_ref[...] = back_acc[...].astype(bf16)
        if summed:
            for t in range(pl.num_programs(0), count + 4):
                tick(t)
            pieces.finish(count)


FFN_STEP = 256
SUMMED_STEPS = 9


def feed_forward(normed, normed_t, cotangent, weights, hidden, step=FFN_STEP):
    rows, width = normed.shape
    steps = hidden // step
    seq_count = lax.axis_size("seq")
    share = width // seq_count
    summed = SUMMED_STEPS if seq_count == 16 and share % 16 == 0 else 0
    assert not summed or summed < steps <= 2 * summed
    whole = lambda shape: pl.BlockSpec(shape, lambda j: (0, 0))
    held = lambda shape: pl.BlockSpec(shape, lambda j: (0, 0), pipeline_mode=pl.Buffered(1))
    column = lambda first: pl.BlockSpec((width, step), lambda j: (0, first + j))
    scratch = [pltpu.VMEM((rows, width), f32)] * 2
    out_specs = [
        column(0),
        column(0),
        column(0),
        whole((rows, width)),
        whole((rows, width)),
    ]
    out_shape = [
        jax.ShapeDtypeStruct((width, hidden), bf16),
        jax.ShapeDtypeStruct((width, hidden), bf16),
        jax.ShapeDtypeStruct((width, hidden - summed * step), bf16),
        jax.ShapeDtypeStruct((rows, width), bf16),
        jax.ShapeDtypeStruct((rows, width), bf16),
    ]
    params = kernel_params(1, 60)
    if summed:
        scratch += [pltpu.VMEM((SLOTS, 2, 2, 2, 2, share, step), bf16)]
        scratch += Pieces.scratch(share, step)
        out_specs[2] = pl.BlockSpec((width, step), lambda j: (0, j // summed * (j - summed)))
        out_specs.append(pl.BlockSpec(memory_space=pl.ANY))
        out_shape.append(jax.ShapeDtypeStruct((share, summed * step), f32))
        params = pltpu.CompilerParams(
            dimension_semantics=("arbitrary",),
            collective_id=3,
            has_side_effects=True,
            vmem_limit_bytes=60 * 1024 * 1024,
        )
    outs = pl.pallas_call(
        functools.partial(ffn_kernel, summed=summed),
        grid=(steps,),
        in_specs=[
            held((rows, width)),
            held((width, rows)),
            held((rows, width)),
            held((width, rows)),
            column(0),
            column(steps),
            column(2 * steps),
        ],
        out_specs=out_specs,
        out_shape=out_shape,
        scratch_shapes=scratch,
        compiler_params=params,
        cost_estimate=pl.CostEstimate(
            flops=18 * rows * width * hidden,
            bytes_accessed=12 * width * hidden,
            transcendentals=rows * hidden,
        ),
        name="feed_forward",
    )(normed, normed_t, cotangent, cotangent.T, weights, weights, weights)
    return outs


def qkv_back_kernel(
    own_ref, after_ref, before_ref, normed_t_ref, weight_ref, table_ref,
    grad_ref, back_ref, acc, *, kind_steps, micro, block_rows,
):
    j = pl.program_id(0)
    kind = j // kind_steps
    edges = (kind > 0).astype(f32)
    turned = kind < 2
    near_rows = block_rows + 2 * HALF

    def own_table(index):
        return jnp.concatenate(
            [
                table_ref[index, m * near_rows + HALF : (m + 1) * near_rows - HALF]
                for m in range(micro)
            ],
            axis=0,
        )

    own_factor = jnp.where(turned, own_table(0), 1.0)
    below_factor = jnp.where(turned, -own_table(1), 0.0)
    above_factor = jnp.where(turned, -own_table(2), 0.0)
    total = []
    for m in range(micro):
        first = m * block_rows
        total.append(own_ref[first : first + HALF] + edges * after_ref[m].astype(f32))
        if block_rows > 2 * HALF:
            total.append(own_ref[first + HALF : first + block_rows - HALF])
        total.append(
            own_ref[first + block_rows - HALF : first + block_rows]
            + edges * before_ref[m].astype(f32)
        )
    total = jnp.concatenate(total, axis=0)
    grad = jnp.concatenate(
        [
            turn(total[:, i : i + 128], own_factor, below_factor, above_factor)
            for i in range(0, total.shape[1], 128)
        ],
        axis=1,
    ).astype(bf16)
    grad_ref[...] = nn(normed_t_ref[...], grad).astype(bf16)
    part = nt(grad, weight_ref[...])

    @pl.when(j == 0)
    def _():
        acc[...] = part

    @pl.when(j > 0)
    def _():
        acc[...] += part

    @pl.when(j == pl.num_programs(0) - 1)
    def _():
        back_ref[...] = acc[...].astype(bf16)


def qkv_back(own, after, before, normed_t, weights, table, micro, block_rows, step=256):
    _, rows, local = own.shape
    width = normed_t.shape[0]
    kind_steps = local // step
    edge = pl.BlockSpec(
        (None, micro, HALF, step),
        lambda j: (jnp.maximum(j // kind_steps - 1, 0), 0, 0, j % kind_steps),
    )
    return pl.pallas_call(
        functools.partial(
            qkv_back_kernel, kind_steps=kind_steps, micro=micro, block_rows=block_rows
        ),
        grid=(3 * kind_steps,),
        in_specs=[
            pl.BlockSpec((None, rows, step), lambda j: (j // kind_steps, 0, j % kind_steps)),
            edge,
            edge,
            pl.BlockSpec((width, rows), lambda j: (0, 0)),
            pl.BlockSpec((width, step), lambda j: (0, j)),
            pl.BlockSpec(table.shape, lambda j: (0, 0, 0)),
        ],
        out_specs=[
            pl.BlockSpec((width, step), lambda j: (0, j)),
            pl.BlockSpec((rows, width), lambda j: (0, 0)),
        ],
        out_shape=[
            jax.ShapeDtypeStruct((width, 3 * local), bf16),
            jax.ShapeDtypeStruct((rows, width), bf16),
        ],
        scratch_shapes=[pltpu.VMEM((rows, width), f32)],
        compiler_params=kernel_params(1, 60),
        cost_estimate=pl.CostEstimate(
            flops=12 * rows * width * local,
            bytes_accessed=12 * width * local + 12 * rows * local,
            transcendentals=0,
        ),
        name="qkv_back",
    )(own, after, before, normed_t, weights, table)


def time_features(steps_row):
    half_width = TEMB // 2
    ladder = jnp.exp(-math.log(10000.0) * jnp.arange(half_width, dtype=f32) / half_width)
    angles = steps_row.astype(f32)[:, None] * ladder[None, :]
    return jnp.concatenate([jnp.cos(angles), jnp.sin(angles)], axis=-1)


def with_loads(kernel, places):
    def wrapped(*refs):
        refs = list(refs)
        sems = refs.pop()
        targets = refs[-len(places) :]
        refs = refs[: -len(places)]
        copies = [
            pltpu.make_async_copy(refs[place], target, sems.at[i])
            for i, (place, target) in enumerate(zip(places, targets))
        ]
        for copy in copies:
            copy.start()
        for place, target in zip(places, targets):
            refs[place] = target

        def loaded():
            for copy in copies:
                copy.wait()

        kernel(*refs, loaded=loaded)

    return wrapped


def load_scratch(arrays):
    return [pltpu.VMEM(array.shape, array.dtype) for array in arrays] + [
        pltpu.SemaphoreType.DMA((len(arrays),))
    ]


def norm_back_unit(m, index, block_rows, grad_of, up_ref, hidden_ref, two_ref, later_ref, sums_ref, emit):
    width = hidden_ref.shape[1]
    for start in range(0, block_rows, HALF):
        span = slice(m * block_rows + start, m * block_rows + start + HALF)
        later = later_ref[span, :] > 0.5
        lanes = slice((index + 1) * width, (index + 2) * width)
        factor = jnp.where(later, two_ref[m, 1:2, lanes], two_ref[m, 0:1, lanes])
        total, sums = norm_back_tile(
            grad_of(span),
            up_ref[span, :].astype(f32),
            hidden_ref[span, :].astype(f32),
            (~later, later),
            factor,
        )
        for item in range(2):
            for kind in range(2):
                at = slice(kind * width, (kind + 1) * width)
                before = sums_ref[m, item : item + 1, at] if start else 0.0
                sums_ref[m, item : item + 1, at] = sums[item][kind] + before
        emit(span, start, total)


def cross_stage_kernel(
    back_ref, up_ref, hidden_ref, two_ref, later_ref, weight_ref, q_ref, k_ref, v_ref, bias_ref,
    log_ref, *refs, spans, step, micro, ready, loaded,
):
    sources, refs = refs[: len(spans)], refs[len(spans) :]
    (
        grad_ref, sums_ref, low_t_ref, dq_ref, dk_ref, dv_ref, next_ref, got_next_ref, out_ref,
        own_sem, got_ref, mixed_ref, acc_ref, out_w_ref, query_w_ref, weight_sem,
        swap_send, swap_recv, next_send, next_recv,
    ) = refs[:20]
    refs = refs[20:]
    me = lax.axis_index("seq")
    mine = lax.axis_index("tensor")
    digits = seq_digits(me)
    partners = greet_all(me, mine, digits)
    rows = back_ref.shape[0]
    block_rows = rows // micro
    pairs = q_ref.shape[1] // 128
    text = k_ref.shape[0] // micro

    def over_tensor(m):
        span = pl.ds(m * block_rows, block_rows)
        return to_tensor(
            mine, back_ref.at[span], got_ref.at[span], swap_send.at[m], swap_recv.at[m]
        )

    def over_next(m):
        span = pl.ds(m * block_rows, block_rows)
        return to_tensor(
            mine, next_ref.at[span], got_next_ref.at[span], next_send.at[m], next_recv.at[m]
        )

    def norm_unit(m):
        over_tensor(m).wait_recv()
        if m == 0:
            loaded()
            for load in loads:
                load.wait()

        def emit(span, start, total):
            grad_ref[span, :] = total
            rounded = total.astype(bf16)
            low_t_ref[:, span] = rounded.T
            mixed_ref[start : start + HALF, :] = nn(rounded, out_w_ref[...]).astype(bf16)

        norm_back_unit(
            m, 4, block_rows,
            lambda span: back_ref[span, :].astype(f32) + got_ref[span, :].astype(f32),
            up_ref, hidden_ref, two_ref, later_ref, sums_ref, emit,
        )

    def pair_unit(m, pair):
        lanes = pl.ds(pl.multiple_of(pair * 128, 128), 128)
        keys = slice(m * text, (m + 1) * text)
        key_total = value_total = None
        for start in range(0, block_rows, HALF):
            span = slice(m * block_rows + start, m * block_rows + start + HALF)
            query_grad, key_grad, value_grad = attend_rows_back(
                q_ref[span, lanes],
                k_ref[keys, lanes],
                v_ref[keys, lanes],
                bias_ref[span, :],
                get_logs(log_ref, span, pair),
                mixed_ref[start : start + HALF, lanes],
            )
            dq_ref[span, lanes] = query_grad.astype(bf16)
            key_total = key_grad if start == 0 else key_total + key_grad
            value_total = value_grad if start == 0 else value_total + value_grad
        dk_ref[keys, lanes] = key_total.astype(bf16)
        dv_ref[keys, lanes] = value_total.astype(bf16)
        own = slice(m * block_rows, (m + 1) * block_rows)
        acc_ref[...] += nt(dq_ref[own, lanes], query_w_ref[:, lanes])

    def close(m):
        own = slice(m * block_rows, (m + 1) * block_rows)
        next_ref[own, :] = acc_ref[...].astype(bf16)
        if m < micro - 1:
            acc_ref[...] = jnp.zeros_like(acc_ref)
            over_next(m).start()

    local = q_ref.shape[1]
    loads = [
        pltpu.make_async_copy(
            weight_ref.at[:, k * local : (k + 1) * local], target, weight_sem.at[i]
        )
        for i, (k, target) in enumerate(((5, out_w_ref), (4, query_w_ref)))
    ]
    for load in loads:
        load.start()
    acc_ref[...] = jnp.zeros_like(acc_ref)
    pieces = Pieces(refs, out_ref, partners, digits, step)
    work = []
    spot = 0
    for m in range(micro):
        spot = max(spot, ready * (m + 1))
        work.append((spot, spot + 1, lambda t, m=m: norm_unit(m)))
        spot += 1
        begin = spot

        def pair_units(t, m=m, begin=begin):
            for k in range(2):
                pair_unit(m, 2 * (t - begin) + k)

        work.append((begin, begin + pairs // 2, pair_units))
        spot += pairs // 2
        work.append((spot - 1, spot, lambda t, m=m: close(m)))
    for m in range(micro):
        over_tensor(m).start()
    pieces.run(sources, spans, own_sem, work, spot)
    for m in range(micro):
        over_tensor(m).wait_send()
        if m < micro - 1:
            over_next(m).wait()


def cross_stage(
    back, up, hidden, two, later, query, keys, values, bias, logs, weights, local, sources,
    spans, micro, which=2, step=256,
):
    seq_count = lax.axis_size("seq")
    rows, width = hidden.shape
    share = width // seq_count
    block_rows = rows // micro
    any_space = pl.BlockSpec(memory_space=pl.ANY)
    vmem = pl.BlockSpec(memory_space=pltpu.VMEM)
    args = [back, up, hidden, two, later, weights, query, keys, values, bias, logs]
    places = (1, 2, 3, 4, 6, 7, 8, 9, 10)
    return pl.pallas_call(
        with_loads(
            functools.partial(cross_stage_kernel, spans=spans, step=step, micro=micro, ready=4),
            places,
        ),
        out_shape=[
            jax.ShapeDtypeStruct((rows, width), f32),
            jax.ShapeDtypeStruct((micro, 2, 2 * width), f32),
            jax.ShapeDtypeStruct((width, rows), bf16),
            jax.ShapeDtypeStruct((rows, local), bf16),
            jax.ShapeDtypeStruct(keys.shape, bf16),
            jax.ShapeDtypeStruct(keys.shape, bf16),
            jax.ShapeDtypeStruct((rows, width), bf16),
            jax.ShapeDtypeStruct((rows - block_rows, width), bf16),
            jax.ShapeDtypeStruct((share, sum(span for _, span in spans)), f32),
        ],
        in_specs=[vmem] + [any_space] * (10 + len(spans)),
        out_specs=[vmem] * 7 + [any_space] * 2,
        scratch_shapes=[
            pltpu.SemaphoreType.DMA((SLOTS,)),
            pltpu.VMEM((rows, width), bf16),
            pltpu.VMEM((block_rows, local), bf16),
            pltpu.VMEM((block_rows, width), f32),
            pltpu.VMEM((width, local), bf16),
            pltpu.VMEM((width, local), bf16),
            pltpu.SemaphoreType.DMA((2,)),
        ]
        + [pltpu.SemaphoreType.DMA((micro,))] * 4
        + Pieces.scratch(share, step)
        + load_scratch([args[place] for place in places]),
        compiler_params=pltpu.CompilerParams(
            collective_id=which, has_side_effects=True, vmem_limit_bytes=60 * 1024 * 1024
        ),
        cost_estimate=pl.CostEstimate(
            flops=8 * rows * width * local, bytes_accessed=40 * rows * width, transcendentals=0
        ),
        name="cross_stage",
    )(
        *args,
        *[source.reshape(2, 2, 2, 2, share, source.shape[1]) for source in sources],
    )


def self_stage_kernel(
    back_ref, got_early_ref, up_ref, hidden_ref, two_ref, later_ref, weight_ref, qkv_ref, bias_ref,
    log_ref, other_ref, *refs,
    spans, step, micro, ready, seq_count, loaded,
):
    sources, refs = refs[: len(spans)], refs[len(spans) :]
    (
        grad_ref, sums_ref, low_t_ref, own_ref, from_low_ref, from_high_ref, got_other_ref, out_ref,
        own_sem, got_ref, mixed_ref, to_low_ref, to_high_ref, out_w_ref, weight_sem, swap_sem,
        halo_send, halo_recv,
    ) = refs[:18]
    refs = refs[18:]
    me = lax.axis_index("seq")
    mine = lax.axis_index("tensor")
    digits = seq_digits(me)
    has_low = me > 0
    has_high = me < seq_count - 1
    partners = greet_all(me, mine, digits, ((has_low, me - 1), (has_high, me + 1)))
    rows = back_ref.shape[0]
    block_rows = rows // micro
    near_rows = block_rows + 2 * HALF
    local = qkv_ref.shape[1] // 3
    pairs = local // 128
    last = micro - 1

    def over_tensor():
        return to_tensor(
            mine,
            back_ref.at[pl.ds(last * block_rows, block_rows)],
            got_ref,
            swap_sem.at[0],
            swap_sem.at[1],
        )

    def over_other():
        span = pl.ds(block_rows, rows - block_rows)
        return to_tensor(
            mine, other_ref.at[span], got_other_ref, swap_sem.at[2], swap_sem.at[3]
        )

    def to_low(m):
        return send_to(
            me - 1, to_low_ref.at[m], from_high_ref.at[m], halo_send.at[0, m], halo_recv.at[0, m]
        )

    def to_high(m):
        return send_to(
            me + 1, to_high_ref.at[m], from_low_ref.at[m], halo_send.at[1, m], halo_recv.at[1, m]
        )

    load = pltpu.make_async_copy(
        weight_ref.at[:, 3 * local : 4 * local], out_w_ref, weight_sem
    )
    load.start()

    def norm_unit(m):
        if m == 0:
            loaded()
            load.wait()
        if m == last:
            over_tensor().wait_recv()

        def grad_of(span):
            if m == last:
                other = got_ref[span.start - last * block_rows : span.stop - last * block_rows, :]
            else:
                other = got_early_ref[span, :]
            return back_ref[span, :].astype(f32) + other.astype(f32)

        def emit(span, start, total):
            grad_ref[span, :] = total
            rounded = total.astype(bf16)
            low_t_ref[:, span] = rounded.T
            mixed_ref[start : start + HALF, :] = nn(rounded, out_w_ref[...]).astype(bf16)

        norm_back_unit(
            m, 2, block_rows, grad_of, up_ref, hidden_ref, two_ref, later_ref, sums_ref, emit
        )

    def pair_unit(m, pair):
        def lanes(kind):
            return pl.ds(pl.multiple_of(kind * local + pair * 128, 128), 128)

        parts = block_rows // HALF
        held = [[None] * (parts + 2), [None] * (parts + 2)]
        at = lanes(0)
        for part in range(parts):
            span = slice(m * block_rows + part * HALF, m * block_rows + (part + 1) * HALF)
            own_rows = slice(m * near_rows + (part + 1) * HALF, m * near_rows + (part + 2) * HALF)
            near = slice(m * near_rows + part * HALF, m * near_rows + (part + 3) * HALF)
            query_grad, key_grad, value_grad = attend_rows_back(
                qkv_ref[own_rows, at],
                qkv_ref[near, lanes(1)],
                qkv_ref[near, lanes(2)],
                bias_ref[span, :],
                get_logs(log_ref, span, pair),
                mixed_ref[part * HALF : (part + 1) * HALF, at],
            )
            own_ref[0, span, at] = query_grad
            for kind, near_grad in enumerate((key_grad, value_grad)):
                for third in range(3):
                    piece = near_grad[third * HALF : (third + 1) * HALF]
                    before = held[kind][part + third]
                    held[kind][part + third] = piece if before is None else before + piece
        for kind in range(2):
            to_low_ref[m, kind, :, at] = held[kind][0].astype(bf16)
            for part in range(parts):
                span = slice(m * block_rows + part * HALF, m * block_rows + (part + 1) * HALF)
                own_ref[1 + kind, span, at] = held[kind][part + 1]
            to_high_ref[m, kind, :, at] = held[kind][parts + 1].astype(bf16)

    def close(m):
        pl.when(has_low)(lambda: to_low(m).start())
        pl.when(has_high)(lambda: to_high(m).start())

    pieces = Pieces(refs, out_ref, partners, digits, step)
    work = []
    spot = 1
    for m in range(micro):
        if m == last:
            spot = max(spot, ready)
        work.append((spot, spot + 1, lambda t, m=m: norm_unit(m)))
        spot += 1
        begin = spot

        def pair_units(t, m=m, begin=begin):
            for k in range(2):
                pair_unit(m, 2 * (t - begin) + k)

        work.append((begin, begin + pairs // 2, pair_units))
        spot += pairs // 2
        work.append((spot - 1, spot, lambda t, m=m: close(m)))
    over_tensor().start()
    over_other().start()

    @pl.when(jnp.logical_not(has_low))
    def _():
        from_low_ref[...] = jnp.zeros_like(from_low_ref)

    @pl.when(jnp.logical_not(has_high))
    def _():
        from_high_ref[...] = jnp.zeros_like(from_high_ref)

    pieces.run(sources, spans, own_sem, work, spot)
    over_tensor().wait_send()
    over_other().wait()
    for m in range(micro):

        @pl.when(has_low)
        def _(m=m):
            to_low(m).wait_send()
            to_high(m).wait_recv()

        @pl.when(has_high)
        def _(m=m):
            to_high(m).wait_send()
            to_low(m).wait_recv()


def self_stage(
    back, got_early, up, hidden, two, later, qkv, bias, logs, weights, local, other, sources,
    spans, micro, which=4, step=256,
):
    seq_count = lax.axis_size("seq")
    rows, width = hidden.shape
    share = width // seq_count
    block_rows = rows // micro
    any_space = pl.BlockSpec(memory_space=pl.ANY)
    vmem = pl.BlockSpec(memory_space=pltpu.VMEM)
    args = [back, got_early, up, hidden, two, later, weights, qkv, bias, logs, other]
    places = (1, 2, 3, 4, 5, 7, 8, 9)
    edge = (micro, 2, HALF, local)
    return pl.pallas_call(
        with_loads(
            functools.partial(
                self_stage_kernel,
                spans=spans,
                step=step,
                micro=micro,
                ready=4,
                seq_count=seq_count,
            ),
            places,
        ),
        out_shape=[
            jax.ShapeDtypeStruct((rows, width), f32),
            jax.ShapeDtypeStruct((micro, 2, 2 * width), f32),
            jax.ShapeDtypeStruct((width, rows), bf16),
            jax.ShapeDtypeStruct((3, rows, local), f32),
            jax.ShapeDtypeStruct(edge, bf16),
            jax.ShapeDtypeStruct(edge, bf16),
            jax.ShapeDtypeStruct((rows - block_rows, width), bf16),
            jax.ShapeDtypeStruct((share, sum(span for _, span in spans)), f32),
        ],
        in_specs=[vmem] + [any_space] * (10 + len(spans)),
        out_specs=[vmem] * 6 + [any_space] * 2,
        scratch_shapes=[
            pltpu.SemaphoreType.DMA((SLOTS,)),
            pltpu.VMEM((block_rows, width), bf16),
            pltpu.VMEM((block_rows, local), bf16),
            pltpu.VMEM(edge, bf16),
            pltpu.VMEM(edge, bf16),
            pltpu.VMEM((width, local), bf16),
            pltpu.SemaphoreType.DMA,
            pltpu.SemaphoreType.DMA((4,)),
            pltpu.SemaphoreType.DMA((2, micro)),
            pltpu.SemaphoreType.DMA((2, micro)),
        ]
        + Pieces.scratch(share, step)
        + load_scratch([args[place] for place in places]),
        compiler_params=pltpu.CompilerParams(
            collective_id=which, has_side_effects=True, vmem_limit_bytes=60 * 1024 * 1024
        ),
        cost_estimate=pl.CostEstimate(
            flops=8 * rows * width * local, bytes_accessed=40 * rows * width, transcendentals=0
        ),
        name="self_stage",
    )(
        *args,
        *[source.reshape(2, 2, 2, 2, share, source.shape[1]) for source in sources],
    )


EARLY_COLUMNS = (1024, 1280)


def on_device(
    latents,
    context,
    lengths,
    text_len,
    timesteps,
    self_qkv,
    self_out,
    cross_query,
    cross_kv,
    cross_out,
    ffn_in,
    ffn_out,
    mod_weight,
    mod_bias,
    out_grad,
):
    micro, block_rows, model_width = latents.shape
    seq_count = lax.axis_size("seq")
    me = lax.axis_index("seq")
    frame_count = block_rows * seq_count
    item_count = lengths.shape[1]
    local = self_qkv.shape[2]
    hidden = ffn_in.shape[2]
    rows = micro * block_rows
    text_width = context.shape[2]

    attn_share = jnp.concatenate(
        [
            self_qkv[0],
            self_qkv[1],
            self_qkv[2],
            self_out.T,
            cross_query,
            cross_out.T,
            jnp.concatenate([cross_kv[0], cross_kv[1]], axis=0),
        ],
        axis=1,
    )
    ffn_share = jnp.concatenate([ffn_out.T, ffn_in[0], ffn_in[1]], axis=1)
    features = time_features(timesteps.reshape(-1))
    own_features = lax.dynamic_slice_in_dim(
        features, me * mod_weight.shape[0], mod_weight.shape[0], 1
    )
    bias_share = mod_bias.shape[1]
    bias_wide = lax.dynamic_update_slice_in_dim(
        jnp.zeros((6, model_width), f32), mod_bias.astype(f32), me * bias_share, 1
    )
    mod_part = jnp.dot(
        own_features, mod_weight.astype(f32).reshape(mod_weight.shape[0], -1), precision=highest
    ) + bias_wide.reshape(1, -1)
    (
        attn_all,
        normed_near,
        normed_one_t,
        two,
        later,
        near_table,
        self_bias,
        cross_bias,
    ) = gather_and_prepare(attn_share, mod_part, latents, lengths, text_len)
    ffn_share, attn_all = lax.optimization_barrier((ffn_share, attn_all))
    ffn_all = lax.all_gather(ffn_share, "seq", axis=0, tiled=True)
    pair_w = attn_all[:, 6 * local :].reshape(seq_count, 2, text_width // seq_count, local)
    key_w = pair_w[:, 0].reshape(text_width, local)
    value_w = pair_w[:, 1].reshape(text_width, local)

    first_frame = me * block_rows
    first_item = jnp.sum((jnp.cumsum(lengths, axis=1) <= first_frame).astype(jnp.int32), axis=1)
    base_item = jnp.minimum(first_item, item_count - 2)
    catalog = jnp.arange(item_count, dtype=jnp.int32)

    ahead = [(i, i + 1) for i in range(seq_count - 1)]
    behind = [(i + 1, i) for i in range(seq_count - 1)]
    latent = latents.reshape(rows, model_width)
    cotangent = out_grad.reshape(rows, model_width)
    near_context = jnp.concatenate(
        [
            lax.dynamic_slice_in_dim(context[m], base_item[m] * TXT, 2 * TXT, 0)
            for m in range(micro)
        ]
    )
    column = local // 128

    qkv = project(normed_near, attn_all, near_table, local)
    mixed_one, logs_one, part_one = self_attention(
        qkv, self_bias, attn_all, 3 * column, micro, block_rows
    )
    got_one = swap(part_one)
    text_keys = nn(near_context, key_w).astype(bf16)
    text_values = nn(near_context, value_w).astype(bf16)
    hidden_one, _, normed_two_t, query_two = norm_forward(
        latent, part_one, got_one, two, later, 2, micro, attn_all, 4, local
    )
    mixed_two, logs_two, part_two = cross_attention(
        query_two, text_keys, text_values, cross_bias, attn_all, 5 * column, micro, block_rows
    )
    got_two = swap(part_two)
    hidden_two, normed_three, normed_three_t = norm_forward(
        hidden_one, part_two, got_two, two, later, 4, micro
    )
    g_outer, g_gate, g_up, out_part, back_three, *up_early = feed_forward(
        normed_three, normed_three_t, cotangent, ffn_all, hidden
    )
    outer_total = early_sum(g_outer)

    share = text_width // seq_count
    fused = (
        seq_count == 16 and lax.axis_size("tensor") == 2 and (model_width // seq_count) % 16 == 0
    )

    def cross_grads(two_low_t, query_two_low, text_key_low, text_value_low):
        pair_grad = jnp.concatenate(
            [
                tn(near_context, text_key_low).astype(bf16).reshape(seq_count, share, local),
                tn(near_context, text_value_low).astype(bf16).reshape(seq_count, share, local),
            ],
            axis=1,
        ).reshape(2 * text_width, local)
        return [
            nn(two_low_t, mixed_two).astype(bf16),
            nn(normed_two_t, query_two_low).astype(bf16),
            pair_grad,
        ]

    if fused:
        first, second = EARLY_COLUMNS
        third = hidden - first - second
        (
            hidden_two_grad, sums_three, two_low_t, query_two_low, text_key_low, text_value_low,
            back_two, got_early, totals_a,
        ) = cross_stage(
            back_three, cotangent, hidden_two, two, later, query_two, text_keys, text_values,
            cross_bias, logs_two, attn_all, local, [g_gate], ((0, first),), micro,
        )
        (
            hidden_one_grad, sums_two, one_low_t, own_grads, from_low, from_high, got_last,
            totals_b,
        ) = self_stage(
            back_two, got_early, hidden_two_grad, hidden_one, two, later, qkv, self_bias, logs_one,
            attn_all, local, out_part, [g_gate], ((first, second),), micro,
        )
        crossed = cross_grads(two_low_t, query_two_low, text_key_low, text_value_low)
        g_self_out = nn(one_low_t, mixed_one).astype(bf16)
        sums = jnp.concatenate([sums_two, sums_three], axis=2)
        spans = ((0, g_up.shape[1]),) + ((0, local),) * 4
        sources = [g_up] + crossed + [g_self_out]
        if third:
            spans = ((first + second, third),) + spans
            sources = [g_gate] + sources
        late = third + g_up.shape[1]
        totals_c, latent_grad, mod_grad, bias_sum, got_first = finish_stage(
            own_grads, from_low, from_high, normed_one_t, attn_all, near_table, hidden_one_grad,
            latent, two, later, sums, lengths, own_features, out_part,
            sources, spans, micro,
        )
        totals = [totals_c[:, late + k * local : late + (k + 1) * local] for k in range(4)]
        grad_cross_out, grad_cross_query, grad_cross_kv, grad_self_out = totals
        qkv_total = totals_c[:, late + 4 * local :]
        gate_total = jnp.concatenate([totals_a, totals_b, totals_c[:, :third]], axis=1)
        up_total = jnp.concatenate([up_early[0], totals_c[:, third:late]], axis=1)
        out_got = jnp.concatenate([got_first, got_last], axis=0)
    else:
        got_three = swap(back_three)
        gate_total = early_sum(g_gate)
        up_total = early_sum(g_up)
        hidden_two_grad, sums_three, two_low_t, mixed_two_grad = norm_back(
            cotangent, back_three, got_three, hidden_two, two, later, 4, micro, attn_all, 5, local
        )
        query_two_low, text_key_low, text_value_low, back_two = cross_attention_back(
            query_two, text_keys, text_values, cross_bias, mixed_two_grad, logs_two,
            attn_all, 4 * column, micro, block_rows,
        )
        got_back_two = swap(back_two)
        hidden_one_grad, sums_two, one_low_t, mixed_one_grad = norm_back(
            hidden_two_grad, back_two, got_back_two, hidden_one, two, later, 2, micro,
            attn_all, 3, local,
        )
        own_grads, to_low, to_high = self_attention_back(
            qkv, self_bias, mixed_one_grad, logs_one, micro, block_rows
        )
        from_high = lax.ppermute(to_low, "seq", behind)
        from_low = lax.ppermute(to_high, "seq", ahead)
        g_self_out = nn(one_low_t, mixed_one).astype(bf16)
        g_qkv, back_one = qkv_back(
            own_grads, from_low, from_high, normed_one_t, attn_all, near_table, micro, block_rows
        )
        crossed = cross_grads(two_low_t, query_two_low, text_key_low, text_value_low)
        sums = jnp.concatenate(
            [piece.reshape(micro, 2, 2 * model_width) for piece in (sums_two, sums_three)], axis=2
        )
        totals, latent_grad, mod_grad, bias_sum, out_got = finish_apart(
            crossed + [g_self_out, g_qkv], back_one, hidden_one_grad, latent, two, later, sums,
            lengths, own_features, out_part,
        )
        grad_cross_out, grad_cross_query, grad_cross_kv, grad_self_out, qkv_total = totals
    block_out = (hidden_two + (out_part.astype(f32) + out_got.astype(f32))).astype(bf16)
    mod_grad = mod_grad.reshape(mod_weight.shape)
    bias_grad = lax.dynamic_slice_in_dim(
        bias_sum.reshape(6, model_width), me * bias_share, bias_share, 1
    )

    grad_qkv = jnp.stack([qkv_total[:, i * local : (i + 1) * local] for i in range(3)])
    return (
        block_out.reshape(latents.shape),
        latent_grad.reshape(latents.shape),
        grad_qkv,
        grad_self_out.T,
        grad_cross_query,
        grad_cross_kv.reshape(2, share, local),
        grad_cross_out.T,
        jnp.stack([gate_total, up_total]),
        outer_total.T,
        mod_grad,
        bias_grad,
    )


def solution(mesh):
    return jax.shard_map(
        on_device,
        mesh=mesh,
        in_specs=(
            P(None, "seq", None),
            P(),
            P(),
            P(),
            P(),
            P(None, "seq", "tensor"),
            P("tensor", "seq"),
            P("seq", "tensor"),
            P(None, "seq", "tensor"),
            P("tensor", "seq"),
            P(None, "seq", "tensor"),
            P("tensor", "seq"),
            P("seq", None, None),
            P(None, "seq"),
            P(None, "seq", None),
        ),
        out_specs=(
            P(None, "seq", None),
            P(None, "seq", None),
            P(None, "seq", "tensor"),
            P("tensor", "seq"),
            P("seq", "tensor"),
            P(None, "seq", "tensor"),
            P("tensor", "seq"),
            P(None, "seq", "tensor"),
            P("tensor", "seq"),
            P("seq", None, None),
            P(None, "seq"),
        ),
        check_vma=False,
    )
```

```python
import functools
import math

import jax
import jax.numpy as jnp
import numpy as np
from jax import lax
from jax.experimental import pallas as pl
from jax.experimental.pallas import tpu as pltpu
from jax.sharding import PartitionSpec as P

HD = 64
TXT = 128
TEMB = 256
HALF = 128


norm_eps = 1e-05
highest = lax.Precision.HIGHEST
f32 = jnp.float32
bf16 = jnp.bfloat16


def dot(a, b, dims):
    return lax.dot_general(a, b, ((dims[0], dims[1]), ((), ())), preferred_element_type=f32)


def nn(a, b):
    return dot(a, b, ((1,), (0,)))


def nt(a, b):
    return dot(a, b, ((1,), (1,)))


def tn(a, b):
    return dot(a, b, ((0,), (0,)))


def halves(count):
    stride = 1
    strides = []
    while stride < count:
        strides.append(stride)
        stride *= 2
    return strides


def flip(block, stride):
    count = lax.axis_size("seq")
    return lax.ppermute(block, "seq", [(i, i ^ stride) for i in range(count)])


def swap(part):
    count = lax.axis_size("tensor")
    return lax.ppermute(part, "tensor", [(i, (i + 1) % count) for i in range(count)])


def seq_sum(part):
    for stride in halves(lax.axis_size("seq")):
        part = part + flip(part, stride)
    return part


def kernel_params(grid_rank, mib):
    return pltpu.CompilerParams(
        dimension_semantics=("arbitrary",) * grid_rank, vmem_limit_bytes=mib * 1024 * 1024
    )


STRIDES = (1, 2, 4, 8)


def seq_digits(me):
    return [(me // stride) % 2 for stride in STRIDES]


def greet(me, digits, others=(), mine=None):
    partners = [me + stride * (1 - 2 * digit) for stride, digit in zip(STRIDES, digits)]
    barrier = pltpu.get_barrier_semaphore()

    def tell(**target):
        pl.semaphore_signal(barrier, inc=1, device_id=target, device_id_type=pl.DeviceIdType.MESH)

    expected = len(partners)
    for partner in partners:
        tell(seq=partner)
    if mine is not None:
        tell(tensor=1 - mine)
        expected += 1
    for there, target in others:
        pl.when(there)(functools.partial(tell, seq=target))
        expected = expected + there.astype(jnp.int32)
    pl.semaphore_wait(barrier, expected)
    return partners


def send_to(partner, source, target, send_sem, recv_sem):
    return pltpu.make_async_remote_copy(
        src_ref=source,
        dst_ref=target,
        send_sem=send_sem,
        recv_sem=recv_sem,
        device_id={"seq": partner},
        device_id_type=pl.DeviceIdType.MESH,
    )


def greet_all(me, mine, digits, others=()):
    return greet(me, digits, others, mine)


def to_tensor(mine, source, target, send_sem, recv_sem):
    return pltpu.make_async_remote_copy(
        src_ref=source,
        dst_ref=target,
        send_sem=send_sem,
        recv_sem=recv_sem,
        device_id={"tensor": 1 - mine},
        device_id_type=pl.DeviceIdType.MESH,
    )


SMALL_STEPS = 6


def small_sum(partners, mine, core, fill, prep, held, got, total, finish, send_sem, recv_sem):
    own = 2 * mine + core
    half = pl.ds(2 * mine, 2)

    def exchange(k):
        sems = send_sem.at[k], recv_sem.at[k]
        if k == 0:
            return send_to(partners[0], prep.at[2 * mine + 1 - core], got.at[0], *sems)
        if k < 4:
            return send_to(partners[k], held.at[k], got.at[k], *sems)
        if k == 4:
            return send_to(partners[0], total.at[own], total.at[own], *sems)
        return to_tensor(mine, total.at[half], total.at[half], *sems)

    def step(k):
        if k == 0:
            fill(prep)
        else:
            exchange(k - 1).wait()
        if k == 1:
            held[1] = prep[own] + got[0]
        elif 1 < k < 4:
            held[k] = held[k - 1] + got[k - 1]
        elif k == 4:
            total[own] = held[3] + got[3]
        elif k == SMALL_STEPS:
            finish(total)
        if k < SMALL_STEPS:
            exchange(k).start()

    return step


def small_scratch(shape):
    quarter = (4, shape[0], shape[1] // 4)
    return [pltpu.VMEM(quarter, f32)] * 4 + [pltpu.SemaphoreType.DMA((SMALL_STEPS,))] * 2


def lane_ladder():
    quarter = HD // 4
    return np.exp(-math.log(10000.0) * (np.arange(128) % quarter) / quarter).astype(np.float32)


def prepare(first, frame_count, lengths, text_len, block_rows):
    items = len(lengths)
    ends = [lengths[0]]
    for length in lengths[1:]:
        ends.append(ends[-1] + length)

    def item_of(place):
        return sum((end <= place).astype(jnp.int32) for end in ends)

    def pick(ids, values):
        return sum(jnp.where(ids == k, value, 0) for k, value in enumerate(values))

    near_rows = block_rows + 2 * HALF
    place = first - HALF + lax.broadcasted_iota(jnp.int32, (near_rows, 1), 0)
    ids = item_of(place)
    offset = place - pick(ids, [end - length for end, length in zip(ends, lengths)])
    base = jnp.minimum(item_of(first), items - 2)
    own_ids = ids[HALF : HALF + block_rows]
    self_bias = []
    for part in range(block_rows // HALF):
        row = lax.broadcasted_iota(jnp.int32, (HALF, 1), 0)
        key = lax.broadcasted_iota(jnp.int32, (1, 3 * HALF), 1) - HALF
        key_place = first + part * HALF + key
        inside = (key_place >= 0) & (key_place < frame_count)
        key_ids = jnp.where(inside, item_of(key_place), -1)
        near_enough = jnp.abs(row - key) <= HALF
        same = own_ids[part * HALF : (part + 1) * HALF] == key_ids
        self_bias.append(jnp.where(near_enough & same, 0.0, -1e30))
    slot = lax.broadcasted_iota(jnp.int32, (1, 2 * TXT), 1)
    key_item = jnp.where(slot < TXT, base, base + 1)
    used = jnp.where(slot < TXT, slot, slot - TXT) < pick(key_item, text_len)
    key_item = jnp.where(used, key_item, -1)
    cross_bias = jnp.where(own_ids == key_item, 0.0, -1e30)
    later = (ids != base).astype(f32)
    return base, offset, later, self_bias, cross_bias


def lane_tables(offset, ladder):
    quarter = HD // 4
    angles = offset.astype(f32) * ladder
    lane = lax.broadcasted_iota(jnp.int32, angles.shape, 1) % HD
    cosine = jnp.cos(angles)
    sine = jnp.sin(angles)
    return (
        jnp.where(lane < 2 * quarter, cosine, 1.0),
        jnp.where((lane >= quarter) & (lane < 2 * quarter), sine, 0.0),
        jnp.where(lane < quarter, -sine, 0.0),
    )


def gather_kernel(
    share_ref, part_ref, latent_ref, lengths_ref, text_ref, ladder_ref,
    out_ref, near_normed_ref, normed_t_ref, two_ref, later_ref, table_ref, self_ref, cross_ref,
    near_ref, prep, held, got, total_ref, small_send, small_recv, copy_sem, send_sem, recv_sem,
    near_sem, halo_send, halo_recv, *, pieces, step, y_first, seq_count,
):
    micro, block_rows, width = latent_ref.shape
    items = lengths_ref.shape[1]
    near_rows = block_rows + 2 * HALF
    me = lax.axis_index("seq")
    digits = seq_digits(me)
    core, y, z_lo, z_hi = digits
    first = me * block_rows
    has_low = me > 0
    has_high = me < seq_count - 1
    mine = lax.axis_index("tensor")
    partners = greet_all(me, mine, digits, ((has_low, me - 1), (has_high, me + 1)))

    def fill(target):
        span = target.shape[2]
        for index in range(4):
            target[index] = part_ref[:, index * span : (index + 1) * span]

    small = small_sum(
        partners, mine, core, fill, prep, held, got, total_ref, lambda total: None,
        small_send, small_recv,
    )

    def to_low():
        return send_to(
            me - 1,
            latent_ref.at[:, :HALF],
            near_ref.at[:, near_rows - HALF :],
            halo_send.at[0],
            halo_recv.at[0],
        )

    def to_high():
        return send_to(
            me + 1,
            latent_ref.at[:, block_rows - HALF :],
            near_ref.at[:, :HALF],
            halo_send.at[1],
            halo_recv.at[1],
        )

    def load_own():
        return pltpu.make_async_copy(
            latent_ref, near_ref.at[:, HALF : near_rows - HALF], near_sem
        )

    def piece(p):
        return pl.ds(p * step, step)

    def exchange(p, stage):
        cols = piece(p)
        if p in y_first:
            axis = (1, 3, 2, 0)[stage]
            spots = ((z_hi, z_lo, y, core), (z_hi, z_lo, None, core), (None, z_lo, None, core), None)
        else:
            axis = (3, 2, 1, 0)[stage]
            spots = ((z_hi, z_lo, y, core), (None, z_lo, y, core), (None, None, y, core), None)
        spot = spots[stage] or (None, None, None, core)
        index = tuple(slice(None) if digit is None else digit for digit in spot)
        block = out_ref.at[index + (slice(None), cols)]
        source = share_ref.at[:, cols] if stage == 0 else block
        return send_to(partners[axis], source, block, send_sem.at[stage, p], recv_sem.at[stage, p])

    def own(p):
        return pltpu.make_async_copy(
            share_ref.at[:, piece(p)],
            out_ref.at[z_hi, z_lo, y, core, :, piece(p)],
            copy_sem.at[p],
        )

    def masks(m):
        base, offset, later, self_bias, cross_bias = prepare(
            first,
            seq_count * block_rows,
            [lengths_ref[m, k] for k in range(items)],
            [text_ref[m, k] for k in range(items)],
            block_rows,
        )
        rows = slice(m * block_rows, (m + 1) * block_rows)
        later_ref[rows, :] = later[HALF : HALF + block_rows]
        for part, bias in enumerate(self_bias):
            start = m * block_rows + part * HALF
            self_ref[start : start + HALF, :] = bias
        cross_ref[rows, :] = cross_bias
        state[m] = base, offset, later

    def tables(m, start):
        offset = state[m][1][start : start + HALF]
        target = m * near_rows + start
        for index, values in enumerate(lane_tables(offset, ladder_ref[...])):
            table_ref[index, target : target + HALF, :] = values

    def modulation(m, base):
        span = total_ref.shape[2]
        for which in range(2):
            for index in range(4):
                two_ref[m, which : which + 1, index * span : (index + 1) * span] = sum(
                    jnp.where(
                        base + which == k,
                        total_ref[index, m * items + k : m * items + k + 1],
                        0.0,
                    )
                    for k in range(items)
                )

    def norm(m, start):
        shift = [two_ref[m, which : which + 1, :width] for which in range(2)]
        factor = [two_ref[m, which : which + 1, width : 2 * width] for which in range(2)]
        tile = near_ref[m, start : start + HALF].astype(f32)
        chosen = state[m][2][start : start + HALF] > 0.5
        xhat, _ = spread_rows(tile)
        normed = (
            xhat * (1.0 + jnp.where(chosen, factor[1], factor[0]))
            + jnp.where(chosen, shift[1], shift[0])
        ).astype(bf16)
        target = m * near_rows + start
        near_normed_ref[target : target + HALF, :] = normed
        if HALF <= start < HALF + block_rows:
            target = m * block_rows + start - HALF
            normed_t_ref[:, target : target + HALF] = normed.T

    beside = {}
    state = {}
    gap = 3

    def add(t, work):
        beside.setdefault(t, []).append(work)

    def finish_near():
        load_own().wait()
        pl.when(has_low)(lambda: to_high().wait_recv())
        pl.when(has_high)(lambda: to_low().wait_recv())

    tick = 1
    for m in range(micro):
        add(tick, functools.partial(masks, m))
        for start in range(0, near_rows, HALF):
            tick += 1
            add(tick, functools.partial(tables, m, start))
        tick += 1
    for k in range(1, SMALL_STEPS + 1):
        add(gap * k, functools.partial(small, k))
    tick = gap * SMALL_STEPS
    add(tick, finish_near)
    for m in range(micro):
        tick += 1
        add(tick, lambda m=m: modulation(m, state[m][0]))
        for start in range(0, near_rows, HALF):
            add(tick, functools.partial(norm, m, start))
            tick += 1
    last_tick = tick

    small(0)
    load_own().start()
    pl.when(has_low)(lambda: to_low().start())
    pl.when(has_high)(lambda: to_high().start())

    @pl.when(jnp.logical_not(has_low))
    def _():
        near_ref[:, :HALF] = jnp.zeros((micro, HALF, width), near_ref.dtype)

    @pl.when(jnp.logical_not(has_high))
    def _():
        near_ref[:, near_rows - HALF :] = jnp.zeros((micro, HALF, width), near_ref.dtype)

    lags = (0, 3, 6, 10, 12)
    for t in range(max(pieces + lags[-1], last_tick + 1)):
        if t < pieces:
            exchange(t, 0).start()
            own(t).start()
        for stage in (1, 2, 3):
            p = t - lags[stage]
            if 0 <= p < pieces:
                if stage == 1:
                    own(p).wait()
                exchange(p, stage - 1).wait_recv()
                exchange(p, stage).start()
        if 0 <= t - lags[4] < pieces:
            exchange(t - lags[4], 3).wait_recv()
        for work in beside.get(t, ()):
            work()
    for p in range(pieces):
        for stage in range(4):
            exchange(p, stage).wait_send()
    pl.when(has_low)(lambda: to_low().wait_send())
    pl.when(has_high)(lambda: to_high().wait_send())


def gather_and_prepare(share, part, latents, lengths, text_len, step=256):
    count = lax.axis_size("seq")
    me = lax.axis_index("seq")
    rows, width = share.shape
    micro, block_rows, model_width = latents.shape
    items = lengths.shape[1]
    near_rows = block_rows + 2 * HALF
    own_rows = micro * block_rows
    ladder = jnp.asarray(lane_ladder()).reshape(1, 128)
    if count != 16 or rows % 16 or width % step or lax.axis_size("tensor") != 2:
        ahead = [(i, i + 1) for i in range(count - 1)]
        behind = [(i + 1, i) for i in range(count - 1)]
        low_rows = lax.ppermute(latents[:, block_rows - HALF :], "seq", ahead)
        high_rows = lax.ppermute(latents[:, :HALF], "seq", behind)
        near_latent = jnp.concatenate([low_rows, latents, high_rows], axis=1)
        total = seq_sum(part).reshape(micro, items, 6 * model_width)
        parts = []
        for m in range(micro):
            base, offset, later, self_bias, cross_bias = prepare(
                me * block_rows,
                count * block_rows,
                [lengths[m, k] for k in range(items)],
                [text_len[m, k] for k in range(items)],
                block_rows,
            )
            two = lax.dynamic_slice_in_dim(total[m], base, 2, 0)
            xhat, _ = spread_rows(near_latent[m].astype(f32))
            shift, factor = [
                jnp.where(later > 0.5, two[1], two[0])[:, i * model_width : (i + 1) * model_width]
                for i in range(2)
            ]
            normed = (xhat * (1.0 + factor) + shift).astype(bf16)
            parts.append(
                (
                    normed,
                    normed[HALF : HALF + block_rows].T,
                    two[None],
                    later[HALF : HALF + block_rows],
                    jnp.stack(lane_tables(offset, ladder)),
                    jnp.concatenate(self_bias, axis=0),
                    cross_bias,
                )
            )
        axes = (0, 1, 0, 0, 1, 0, 0)
        joined = [jnp.concatenate(group, axis=axis) for group, axis in zip(zip(*parts), axes)]
        return [lax.all_gather(share, "seq", axis=0, tiled=True)] + joined
    pieces = width // step
    any_space = pl.BlockSpec(memory_space=pl.ANY)
    vmem = pl.BlockSpec(memory_space=pltpu.VMEM)
    smem = pl.BlockSpec(memory_space=pltpu.SMEM)
    outs = pl.pallas_call(
        functools.partial(
            gather_kernel,
            pieces=pieces,
            step=step,
            y_first=tuple(range(pieces // 6, pieces, pieces // 3)),
            seq_count=count,
        ),
        out_shape=[
            jax.ShapeDtypeStruct((2, 2, 2, 2, rows, width), share.dtype),
            jax.ShapeDtypeStruct((micro * near_rows, model_width), bf16),
            jax.ShapeDtypeStruct((model_width, own_rows), bf16),
            jax.ShapeDtypeStruct((micro, 2, 6 * model_width), f32),
            jax.ShapeDtypeStruct((own_rows, 1), f32),
            jax.ShapeDtypeStruct((3, micro * near_rows, 128), f32),
            jax.ShapeDtypeStruct((own_rows, 3 * HALF), f32),
            jax.ShapeDtypeStruct((own_rows, 2 * TXT), f32),
        ],
        in_specs=[any_space, vmem, any_space, smem, smem, vmem],
        out_specs=[any_space] + [vmem] * 7,
        scratch_shapes=[
            pltpu.VMEM((micro, near_rows, model_width), bf16),
        ]
        + small_scratch(part.shape)
        + [
            pltpu.SemaphoreType.DMA((pieces,)),
            pltpu.SemaphoreType.DMA((4, pieces)),
            pltpu.SemaphoreType.DMA((4, pieces)),
            pltpu.SemaphoreType.DMA,
            pltpu.SemaphoreType.DMA((2,)),
            pltpu.SemaphoreType.DMA((2,)),
        ],
        compiler_params=pltpu.CompilerParams(
            collective_id=1, has_side_effects=True, vmem_limit_bytes=60 * 1024 * 1024
        ),
        cost_estimate=pl.CostEstimate(
            flops=0, bytes_accessed=20 * count * rows * width, transcendentals=0
        ),
        name="gather_and_prepare",
    )(share, part, latents, lengths, text_len, ladder)
    return [outs[0].reshape(count * rows, width)] + list(outs[1:])


SLOTS = 6


def when(condition):
    if isinstance(condition, bool):
        return (lambda work: work()) if condition else (lambda work: None)
    return pl.when(condition)


class Pieces:
    def __init__(self, refs, out_ref, partners, digits, step, lag=3):
        (
            self.own, self.got0, self.got1, self.got2, self.got3, self.staged,
            self.out_sem, self.send_sem, self.recv_sem,
        ) = refs
        self.out_ref = out_ref
        self.partners = partners
        self.digits = digits
        self.step = step
        self.lag = lag

    @staticmethod
    def scratch(rows, step):
        return [
            pltpu.VMEM((SLOTS, 2, 2, 2, rows, step), bf16),
            pltpu.VMEM((SLOTS, 2, 2, 2, rows, step), bf16),
            pltpu.VMEM((SLOTS, 2, 2, rows, step), bf16),
            pltpu.VMEM((SLOTS, 2, rows, step), bf16),
            pltpu.VMEM((SLOTS, rows, step), bf16),
            pltpu.VMEM((SLOTS, rows, step), f32),
            pltpu.SemaphoreType.DMA((SLOTS,)),
            pltpu.SemaphoreType.DMA((4, SLOTS)),
            pltpu.SemaphoreType.DMA((4, SLOTS)),
        ]

    def exchange(self, stage, source, target, slot):
        return send_to(
            self.partners[stage],
            source,
            target,
            self.send_sem.at[stage, slot],
            self.recv_sem.at[stage, slot],
        )

    def over_core(self, source, slot):
        return self.exchange(0, source, self.got0.at[slot], slot)

    PATHS = ((2, 1, 0),)

    def spot(self, path, stage, other):
        axes = (self.digits[3], self.digits[2], self.digits[1])
        index = [slice(None)] * 3
        for axis in path[: stage - 1]:
            index[axis] = axes[axis]
        axis = path[stage - 1]
        index[axis] = 1 - axes[axis] if other else axes[axis]
        return tuple(index)

    def hop(self, path, stage, slot):
        partner = (3, 2, 1)[path[stage - 1]]
        target = (self.got1, self.got2, self.got3)[stage - 1].at[slot]
        source = self.own.at[(slot,) + self.spot(path, stage, True)]
        return send_to(
            self.partners[partner],
            source,
            target,
            self.send_sem.at[stage, slot],
            self.recv_sem.at[stage, slot],
        )

    def by_path(self, item, work):
        work(self.PATHS[0])

    def add_hop(self, path, stage, slot):
        got = (self.got1, self.got2, self.got3)[stage - 1]
        index = self.spot(path, stage, False)
        free = [k for k in range(3) if isinstance(index[k], slice)]
        for count in range(2 ** len(free)):
            bits = [(count >> k) & 1 for k in range(len(free))]
            full = list(index)
            for k, bit in zip(free, bits):
                full[k] = bit
            at = (slot,) + tuple(full)
            total = self.own[at].astype(f32) + got[(slot,) + tuple(bits)].astype(f32)
            if stage < 3:
                self.own[at] = total.astype(bf16)
            else:
                self.staged[slot] = total

    def store(self, item, slot):
        columns = pl.ds(pl.multiple_of(item * self.step, self.step), self.step)
        return pltpu.make_async_copy(
            self.staged.at[slot], self.out_ref.at[:, columns], self.out_sem.at[slot]
        )

    def wait_sent(self, slot):
        for stage in (1, 2, 3):
            self.hop(self.PATHS[0], stage, slot).wait_send()

    def add_core(self, item, slot, left):
        for i in range(2):
            for j in range(2):
                for k in range(2):
                    total = left(i, j, k).astype(f32) + self.got0[slot, i, j, k].astype(f32)
                    self.own[slot, i, j, k] = total.astype(bf16)
        self.by_path(item, lambda path: self.hop(path, 1, slot).start())

    def later_steps(self, t, count):
        lag = self.lag

        @when((t >= lag) & (t - lag < count))
        def _():
            item = t - lag
            slot = item % SLOTS
            self.hop(self.PATHS[0], 1, slot).wait_recv()

            def work(path):
                self.add_hop(path, 1, slot)
                self.hop(path, 2, slot).start()

            self.by_path(item, work)

        @when((t >= lag + 1) & (t - lag - 1 < count))
        def _():
            item = t - lag - 1
            slot = item % SLOTS
            self.hop(self.PATHS[0], 2, slot).wait_recv()

            def work(path):
                self.add_hop(path, 2, slot)
                self.hop(path, 3, slot).start()

            self.by_path(item, work)

        @when((t >= lag + 2) & (t - lag - 2 < count))
        def _():
            item = t - lag - 2
            slot = item % SLOTS
            self.hop(self.PATHS[0], 3, slot).wait_recv()
            when(item >= SLOTS)(lambda: self.store(0, slot).wait())
            self.by_path(item, lambda path: self.add_hop(path, 3, slot))
            self.store(item, slot).start()

    def run(self, sources, spans, own_sem, beside=(), last=0):
        core = self.digits[0]
        step = self.step
        count = sum(width for _, width in spans) // step

        def over_core(source, column, slot):
            return self.over_core(source.at[:, :, :, 1 - core, :, pl.ds(column, step)], slot)

        def load(source, column, slot):
            return pltpu.make_async_copy(
                source.at[:, :, :, core, :, pl.ds(column, step)],
                self.own.at[slot],
                own_sem.at[slot],
            )

        def tick(t, carry):
            @pl.when(t < count)
            def _():
                slot = t % SLOTS
                pl.when(t >= SLOTS)(lambda: self.wait_sent(slot))
                done = 0
                for source, (column, width) in zip(sources, spans):

                    @pl.when((t >= done) & (t < done + width // step))
                    def _(source=source, done=done, column=column):
                        spot = pl.multiple_of(column + (t - done) * step, step)
                        over_core(source, spot, slot).start()
                        load(source, spot, slot).start()

                    done += width // step

            @pl.when((t >= 1) & (t - 1 < count))
            def _():
                slot = (t - 1) % SLOTS
                load(sources[0], 0, slot).wait()
                over_core(sources[0], 0, slot).wait()
                self.add_core(t - 1, slot, lambda i, j, k: self.own[slot, i, j, k])

            self.later_steps(t, count)
            for begin, end, work in beside:
                pl.when((t >= begin) & (t < end))(functools.partial(work, t))
            return carry

        lax.fori_loop(0, max(count + self.lag + 2, last + 1), tick, 0)
        self.finish(count)

    def finish(self, count):
        for back in range(min(SLOTS, count)):
            slot = (count - 1 - back) % SLOTS
            self.store(0, slot).wait()
            self.wait_sent(slot)


PIECE_REFS = 9


def norm_back_tile(grad, upstream, hidden, shift_rows, factor):
    xhat, scale = spread_rows(hidden)
    inner = grad * (1.0 + factor)
    mean_inner = jnp.mean(inner, axis=-1, keepdims=True)
    mean_cross = jnp.mean(inner * xhat, axis=-1, keepdims=True)
    total = upstream + scale * (inner - mean_inner - xhat * mean_cross)
    scaled = grad * xhat
    sums = [
        [
            jnp.sum(jnp.where(chosen, values, 0.0), axis=0, keepdims=True)
            for values in (grad, scaled)
        ]
        for chosen in shift_rows
    ]
    return total, sums


def finish_kernel(*refs, spans, step, micro, loaded):
    refs = list(refs)
    sources = [refs.pop(0) for _ in spans]
    (
        own_ref, from_low_ref, from_high_ref, normed_t_ref, weight_ref, table_ref,
        up_ref, latent_ref, two_ref, later_ref, sums_ref, lengths_ref, feature_ref, other_ref,
        out_ref, grad_ref, mod_ref, bias_ref, got_other_ref,
        own_sem, back_ref, got_back, qkv_w_ref, weight_sem, g_qkv_ref, first_sums,
        back_send, back_recv, other_sem,
    ) = refs[:29]
    pieces_refs = refs[29 : 29 + PIECE_REFS]
    prep, held, got, small_total, small_send, small_recv = refs[29 + PIECE_REFS :]
    me = lax.axis_index("seq")
    mine = lax.axis_index("tensor")
    digits = seq_digits(me)
    core = digits[0]
    rows, width = latent_ref.shape
    local = own_ref.shape[2]
    block_rows = rows // micro
    near_rows = block_rows + 2 * HALF
    items = lengths_ref.shape[1]
    load = pltpu.make_async_copy(weight_ref.at[:, : 3 * local], qkv_w_ref, weight_sem)
    load.start()
    partners = greet_all(me, mine, digits)
    pieces = Pieces(pieces_refs, out_ref, partners, digits, step)

    def over_tensor(m):
        span = pl.ds(m * block_rows, block_rows)
        return to_tensor(
            mine, back_ref.at[span], got_back.at[span], back_send.at[m], back_recv.at[m]
        )

    def own_table(index):
        return jnp.concatenate(
            [
                table_ref[index, m * near_rows + HALF : (m + 1) * near_rows - HALF]
                for m in range(micro)
            ],
            axis=0,
        )

    def project_back(kind, column):
        lanes = pl.ds(pl.multiple_of(column, step), step)
        total = own_ref[kind, :, lanes]
        if kind:
            blocks = []
            for m in range(micro):
                first = m * block_rows
                blocks.append(
                    total[first : first + HALF] + from_low_ref[m, kind - 1, :, lanes].astype(f32)
                )
                if block_rows > 2 * HALF:
                    blocks.append(total[first + HALF : first + block_rows - HALF])
                blocks.append(
                    total[first + block_rows - HALF : first + block_rows]
                    + from_high_ref[m, kind - 1, :, lanes].astype(f32)
                )
            total = jnp.concatenate(blocks, axis=0)
        if kind < 2:
            tables = own_table(0), -own_table(1), -own_table(2)
            total = jnp.concatenate(
                [turn(total[:, i : i + 128], *tables) for i in range(0, step, 128)], axis=1
            )
        grad = total.astype(bf16)
        lanes = pl.ds(pl.multiple_of(kind * local + column, step), step)
        g_qkv_ref[:, :, :, :, :, lanes] = (
            nn(normed_t_ref[...], grad).astype(bf16).reshape(g_qkv_ref.shape[:5] + (step,))
        )
        grad_ref[...] += nt(grad, qkv_w_ref[:, lanes])

    def send_back():
        back_ref[...] = grad_ref[...].astype(bf16)
        for m in range(micro):
            over_tensor(m).start()

    def norm_one(m):
        over_tensor(m).wait_recv()

        def emit(span, start, total):
            grad_ref[span, :] = total

        norm_back_unit(
            m, 0, block_rows,
            lambda span: back_ref[span, :].astype(f32) + got_back[span, :].astype(f32),
            up_ref, latent_ref, two_ref, later_ref, first_sums, emit,
        )

    def fill(target):
        span = target.shape[2]
        size = 128 * math.gcd(span // 128, width // 128)
        for m in range(micro):
            ends = [lengths_ref[m, 0]]
            for k in range(1, items):
                ends.append(ends[-1] + lengths_ref[m, k])
            first_item = sum((end <= me * block_rows).astype(jnp.int32) for end in ends)
            base = jnp.minimum(first_item, items - 2)
            for k in range(items):
                row = slice(m * items + k, m * items + k + 1)
                for first in range(0, 6 * width, size):
                    ref, at = (
                        (first_sums, first) if first < 2 * width else (sums_ref, first - 2 * width)
                    )
                    target[first // span, row, first % span : first % span + size] = sum(
                        jnp.where(
                            base + item == k, ref[m, item : item + 1, at : at + size], 0.0
                        )
                        for item in range(2)
                    )

    def modulation_grads(total):
        span = total.shape[2]
        for index in range(4):
            lanes = slice(index * span, (index + 1) * span)
            bias_ref[:, lanes] = jnp.sum(total[index], axis=0, keepdims=True)
            mod_ref[:, lanes] = sum(
                feature_ref[:, i : i + 1] * total[index, i : i + 1] for i in range(micro * items)
            )

    small = small_sum(
        partners, mine, core, fill, prep, held, got, small_total, modulation_grads,
        small_send, small_recv,
    )
    work = []
    spot = 0
    columns = local // step
    work.append((0, 1, lambda t: loaded()))
    work.append((0, 1, lambda t: load.wait()))
    spot = 1
    for kind in range(3):
        work.append(
            (spot, spot + columns, lambda t, k=kind, s=spot: project_back(k, (t - s) * step))
        )
        spot += columns
    work.append((spot - 1, spot, lambda t: send_back()))
    spot += 3
    for m in range(micro):
        work.append((spot, spot + 1, lambda t, m=m: norm_one(m)))
        spot += 4 if m < micro - 1 else 1
    for k in range(SMALL_STEPS + 1):
        work.append((spot, spot + 1, lambda t, k=k: small(k)))
        spot += 2 if k < 3 else 1
    grad_ref[...] = jnp.zeros_like(grad_ref)
    over_other = to_tensor(
        mine, other_ref.at[pl.ds(0, block_rows)], got_other_ref, other_sem.at[0], other_sem.at[1]
    )
    over_other.start()
    pieces.run(sources + [g_qkv_ref], spans + ((0, 3 * local),), own_sem, work, spot)
    for m in range(micro):
        over_tensor(m).wait_send()
    over_other.wait()


def finish_stage(
    own, from_low, from_high, normed_t, weights, table, upstream, latent, two, later, sums,
    lengths, features, other, sources, spans, micro, which=0, step=256,
):
    seq_count = lax.axis_size("seq")
    rows, width = latent.shape
    items = lengths.shape[1]
    local = own.shape[2]
    share = width // seq_count
    own_features = features.T
    any_space = pl.BlockSpec(memory_space=pl.ANY)
    vmem = pl.BlockSpec(memory_space=pltpu.VMEM)
    smem = pl.BlockSpec(memory_space=pltpu.SMEM)
    args = [
        own, from_low, from_high, normed_t, weights, table,
        upstream, latent, two, later, sums, lengths, own_features, other,
    ]
    places = (0, 1, 2, 3, 5, 6, 7, 8, 9, 10)
    return pl.pallas_call(
        with_loads(
            functools.partial(finish_kernel, spans=spans, step=step, micro=micro),
            [len(sources) + place for place in places],
        ),
        out_shape=[
            jax.ShapeDtypeStruct((share, sum(span for _, span in spans) + 3 * local), f32),
            jax.ShapeDtypeStruct((rows, width), f32),
            jax.ShapeDtypeStruct((own_features.shape[0], 6 * width), f32),
            jax.ShapeDtypeStruct((1, 6 * width), f32),
            jax.ShapeDtypeStruct((rows // micro, width), bf16),
        ],
        in_specs=[any_space] * (len(sources) + 11) + [smem, vmem, any_space],
        out_specs=[any_space, vmem, vmem, vmem, any_space],
        scratch_shapes=[
            pltpu.SemaphoreType.DMA((SLOTS,)),
            pltpu.VMEM((rows, width), bf16),
            pltpu.VMEM((rows, width), bf16),
            pltpu.VMEM((width, 3 * local), bf16),
            pltpu.SemaphoreType.DMA,
            pltpu.VMEM((2, 2, 2, 2, share, 3 * local), bf16),
            pltpu.VMEM((micro, 2, 2 * width), f32),
            pltpu.SemaphoreType.DMA((micro,)),
            pltpu.SemaphoreType.DMA((micro,)),
            pltpu.SemaphoreType.DMA((2,)),
        ]
        + Pieces.scratch(share, step)
        + small_scratch((micro * items, 6 * width))
        + load_scratch([args[place] for place in places]),
        compiler_params=pltpu.CompilerParams(
            collective_id=which, has_side_effects=True, vmem_limit_bytes=60 * 1024 * 1024
        ),
        cost_estimate=pl.CostEstimate(
            flops=12 * rows * width * local, bytes_accessed=40 * rows * width, transcendentals=0
        ),
        name="finish_stage",
    )(
        *[source.reshape(2, 2, 2, 2, share, source.shape[1]) for source in sources],
        *args,
    )


def finish_apart(grads, back, upstream, latent, two, later, sums, lengths, features, other):
    rows, width = latent.shape
    micro, items = lengths.shape
    totals = [early_sum(grad) for grad in grads]
    latent_grad, first_sums = norm_back(upstream, back, swap(back), latent, two, later, 0, micro)
    pieces = jnp.concatenate([first_sums.reshape(micro, 2, 2 * width), sums], axis=2)
    first_item = jnp.sum(
        (jnp.cumsum(lengths, axis=1) <= lax.axis_index("seq") * (rows // micro)).astype(jnp.int32),
        axis=1,
    )
    base = jnp.minimum(first_item, items - 2)
    spots = (base[:, None] + jnp.arange(2))[:, :, None] == jnp.arange(items)
    item_grad = jnp.sum(jnp.where(spots[..., None], pieces[:, :, None], 0.0), axis=1)
    total = seq_sum(item_grad.reshape(micro * items, 6 * width))
    mod_grad = jnp.dot(features.T, total, precision=highest)
    return totals, latent_grad, mod_grad, jnp.sum(total, axis=0, keepdims=True), swap(other)


def early_sum(grad):
    return lax.psum_scatter(grad, "seq", scatter_dimension=0, tiled=True).astype(f32)


def turn(values, own, below, above):
    quarter = HD // 4
    return (
        values * own
        + pltpu.roll(values, quarter, 1) * below
        + pltpu.roll(values, 2 * HD - quarter, 1) * above
    )


def project_kernel(normed_ref, weight_ref, table_ref, out_ref, *, turned):
    j = pl.program_id(0)
    product = nn(normed_ref[...], weight_ref[...])

    @pl.when(j < turned)
    def _():
        for part in range(product.shape[1] // 128):
            lanes = slice(part * 128, (part + 1) * 128)
            out_ref[:, lanes] = turn(
                product[:, lanes], table_ref[0], table_ref[1], table_ref[2]
            ).astype(bf16)

    @pl.when(j >= turned)
    def _():
        out_ref[...] = product.astype(bf16)


def project(normed, weights, table, local, step=256):
    rows, width = normed.shape
    return pl.pallas_call(
        functools.partial(project_kernel, turned=2 * local // step),
        grid=(3 * local // step,),
        in_specs=[
            pl.BlockSpec((rows, width), lambda j: (0, 0)),
            pl.BlockSpec((width, step), lambda j: (0, j)),
            pl.BlockSpec((3, rows, 128), lambda j: (0, 0, 0)),
        ],
        out_specs=pl.BlockSpec((rows, step), lambda j: (0, j)),
        out_shape=jax.ShapeDtypeStruct((rows, 3 * local), bf16),
        compiler_params=kernel_params(1, 60),
        cost_estimate=pl.CostEstimate(
            flops=2 * rows * width * 3 * local,
            bytes_accessed=2 * (rows * width + 3 * local * (width + rows)),
            transcendentals=0,
        ),
        name="qkv_projection",
    )(normed, weights, table)


def head_lanes(shape):
    return lax.broadcasted_iota(jnp.int32, shape, 1) < HD


def one_head(values, first, which):
    return jnp.where(first if which == 0 else ~first, values, jnp.zeros_like(values))


def soft_rows(scores):
    peak = jnp.max(scores, axis=-1, keepdims=True)
    raised = jnp.exp(scores - peak)
    total = jnp.sum(raised, axis=-1, keepdims=True)
    return raised * (1.0 / total), peak + jnp.log(total)


def attend_rows(query, keys, values, bias):
    first = head_lanes(query.shape)
    out = None
    logs = []
    for which in range(2):
        scores = nt(one_head(query, first, which), keys) * (HD**-0.5) + bias
        weights, log_total = soft_rows(scores)
        mixed = nn(weights.astype(bf16), values)
        out = mixed if which == 0 else jnp.where(first, out, mixed)
        logs.append(log_total)
    return out, logs


def attend_rows_back(query, keys, values, bias, logs, grad):
    first = head_lanes(query.shape)
    query_grad = key_grad = value_grad = None
    for which in range(2):
        own_query = one_head(query, first, which)
        own_grad = one_head(grad, first, which)
        scores = nt(own_query, keys) * (HD**-0.5) + bias
        chances = jnp.exp(scores - logs[which])
        chance_grad = nt(own_grad, values)
        score_grad = (
            chances * (chance_grad - jnp.sum(chances * chance_grad, axis=-1, keepdims=True))
        ).astype(bf16)
        to_query = nn(score_grad, keys) * (HD**-0.5)
        to_key = tn(score_grad, own_query) * (HD**-0.5)
        to_value = tn(chances.astype(bf16), own_grad)
        if which == 0:
            query_grad, key_grad, value_grad = to_query, to_key, to_value
        else:
            query_grad = jnp.where(first, query_grad, to_query)
            key_grad = key_grad + to_key
            value_grad = value_grad + to_value
    return query_grad, key_grad, value_grad


def put_logs(log_ref, rows, logs, pair):
    lane = lax.broadcasted_iota(jnp.int32, (logs[0].shape[0], 128), 1)
    kept = log_ref[rows, :]
    kept = jnp.where(lane == 2 * pair, logs[0], kept)
    log_ref[rows, :] = jnp.where(lane == 2 * pair + 1, logs[1], kept)


def get_logs(log_ref, rows, pair):
    kept = log_ref[rows, :]
    lane = lax.broadcasted_iota(jnp.int32, kept.shape, 1)
    return [
        jnp.sum(jnp.where(lane == 2 * pair + which, kept, 0.0), axis=1, keepdims=True)
        for which in range(2)
    ]


def spread_rows(hidden):
    center = hidden - jnp.mean(hidden, axis=-1, keepdims=True)
    spread = jnp.mean(center * center, axis=-1, keepdims=True)
    scale = lax.rsqrt(spread + norm_eps)
    return center * scale, scale


def item_row(two_ref, later_ref, index):
    width = two_ref.shape[2] // 6
    lanes = slice(index * width, (index + 1) * width)
    return jnp.where(later_ref[...] > 0.5, two_ref[0, 1:2, lanes], two_ref[0, 0:1, lanes])


def norm_kernel(*refs, index, with_weight):
    refs = list(refs)
    base_ref, own_ref, got_ref, two_ref, later_ref = refs[:5]
    weight_ref = refs[5] if with_weight else None
    outs = refs[5 + with_weight :]
    hidden = (
        base_ref[...].astype(f32) + own_ref[...].astype(f32) + got_ref[...].astype(f32)
    )
    xhat, _ = spread_rows(hidden)
    normed = (
        xhat * (1.0 + item_row(two_ref, later_ref, index + 1)) + item_row(two_ref, later_ref, index)
    ).astype(bf16)
    outs[0][...] = hidden
    outs[1][...] = normed
    outs[2][...] = normed.T
    if with_weight:
        outs[3][...] = nn(normed, weight_ref[...]).astype(bf16)


def norm_forward(base, own, got, two, later, index, micro, weights=None, column=0, out_width=0):
    rows, width = base.shape
    tile = rows // micro
    row_tile = pl.BlockSpec((tile, width), lambda i: (i, 0))
    in_specs = [
        row_tile,
        row_tile,
        row_tile,
        pl.BlockSpec((1, 2, 6 * width), lambda i: (i, 0, 0)),
        pl.BlockSpec((tile, 1), lambda i: (i, 0)),
    ]
    out_specs = [row_tile, row_tile, pl.BlockSpec((width, tile), lambda i: (0, i))]
    out_shape = [
        jax.ShapeDtypeStruct((rows, width), f32),
        jax.ShapeDtypeStruct((rows, width), bf16),
        jax.ShapeDtypeStruct((width, rows), bf16),
    ]
    args = [base, own, got, two, later]
    if weights is not None:
        in_specs.append(pl.BlockSpec((width, out_width), lambda i: (0, column)))
        out_specs.append(pl.BlockSpec((tile, out_width), lambda i: (i, 0)))
        out_shape.append(jax.ShapeDtypeStruct((rows, out_width), bf16))
        args.append(weights)
    return pl.pallas_call(
        functools.partial(norm_kernel, index=index, with_weight=weights is not None),
        grid=(micro,),
        in_specs=in_specs,
        out_specs=out_specs,
        out_shape=out_shape,
        compiler_params=kernel_params(1, 60),
        cost_estimate=pl.CostEstimate(
            flops=2 * rows * width * out_width, bytes_accessed=16 * rows * width, transcendentals=0
        ),
        name="norm_forward",
    )(*args)


def norm_back_kernel(*refs, index, with_weight):
    refs = list(refs)
    up_ref, own_ref, got_ref, hidden_ref, two_ref, later_ref = refs[:6]
    weight_ref = refs[6] if with_weight else None
    outs = refs[6 + with_weight :]
    xhat, scale = spread_rows(hidden_ref[...].astype(f32))
    grad = own_ref[...].astype(f32) + got_ref[...].astype(f32)
    inner = grad * (1.0 + item_row(two_ref, later_ref, index + 1))
    mean_inner = jnp.mean(inner, axis=-1, keepdims=True)
    mean_cross = jnp.mean(inner * xhat, axis=-1, keepdims=True)
    total = up_ref[...].astype(f32) + scale * (inner - mean_inner - xhat * mean_cross)
    outs[0][...] = total
    later = later_ref[...] > 0.5
    scaled = grad * xhat
    for item in range(2):
        chosen = later if item else ~later
        outs[1][0, item, 0:1] = jnp.sum(jnp.where(chosen, grad, 0.0), axis=0, keepdims=True)
        outs[1][0, item, 1:2] = jnp.sum(jnp.where(chosen, scaled, 0.0), axis=0, keepdims=True)
    if with_weight:
        rounded = total.astype(bf16)
        outs[2][...] = rounded.T
        outs[3][...] = nn(rounded, weight_ref[...]).astype(bf16)


def norm_back(up, own, got, hidden, two, later, index, micro, weights=None, column=0, out_width=0):
    rows, width = hidden.shape
    tile = rows // micro
    row_tile = pl.BlockSpec((tile, width), lambda i: (i, 0))
    in_specs = [
        row_tile,
        row_tile,
        row_tile,
        row_tile,
        pl.BlockSpec((1, 2, 6 * width), lambda i: (i, 0, 0)),
        pl.BlockSpec((tile, 1), lambda i: (i, 0)),
    ]
    out_specs = [row_tile, pl.BlockSpec((1, 2, 2, width), lambda i: (i, 0, 0, 0))]
    out_shape = [
        jax.ShapeDtypeStruct((rows, width), f32),
        jax.ShapeDtypeStruct((micro, 2, 2, width), f32),
    ]
    args = [up, own, got, hidden, two, later]
    if weights is not None:
        in_specs.append(pl.BlockSpec((width, out_width), lambda i: (0, column)))
        out_specs += [
            pl.BlockSpec((width, tile), lambda i: (0, i)),
            pl.BlockSpec((tile, out_width), lambda i: (i, 0)),
        ]
        out_shape += [
            jax.ShapeDtypeStruct((width, rows), bf16),
            jax.ShapeDtypeStruct((rows, out_width), bf16),
        ]
        args.append(weights)
    return pl.pallas_call(
        functools.partial(norm_back_kernel, index=index, with_weight=weights is not None),
        grid=(micro,),
        in_specs=in_specs,
        out_specs=out_specs,
        out_shape=out_shape,
        compiler_params=kernel_params(1, 60),
        cost_estimate=pl.CostEstimate(
            flops=2 * rows * width * out_width, bytes_accessed=20 * rows * width, transcendentals=0
        ),
        name="norm_back",
    )(*args)


def add_product(acc_ref, out_ref, left, right):
    pair = pl.program_id(1)

    @pl.when(pair == 0)
    def _():
        acc_ref[...] = jnp.zeros_like(acc_ref)

    acc_ref[...] += nt(left, right)

    @pl.when(pair == pl.num_programs(1) - 1)
    def _():
        out_ref[...] = acc_ref[...].astype(bf16)


def self_kernel(q_ref, k_ref, v_ref, bias_ref, weight_ref, out_ref, log_ref, sum_ref, acc_ref):
    pair = pl.program_id(1)
    block_rows = out_ref.shape[0]
    for part in range(block_rows // HALF):
        rows = slice(part * HALF, (part + 1) * HALF)
        span = slice(part * HALF, (part + 3) * HALF)
        out, logs = attend_rows(
            q_ref[(part + 1) * HALF : (part + 2) * HALF, :],
            k_ref[span, :],
            v_ref[span, :],
            bias_ref[rows, :],
        )
        out_ref[rows, :] = out.astype(bf16)
        put_logs(log_ref, rows, logs, pair)
    add_product(acc_ref, sum_ref, out_ref[...], weight_ref[...])


def self_specs(block_rows, pairs):
    near = lambda first: pl.BlockSpec((block_rows + 2 * HALF, 128), lambda m, h: (m, first + h))
    return [
        near(0),
        near(pairs),
        near(2 * pairs),
        pl.BlockSpec((block_rows, 3 * HALF), lambda m, h: (m, 0)),
    ]


def self_attention(qkv, bias, weights, column, micro, block_rows):
    rows = micro * block_rows
    local = qkv.shape[1] // 3
    width = weights.shape[0]
    pairs = local // 128
    return pl.pallas_call(
        self_kernel,
        grid=(micro, pairs),
        in_specs=self_specs(block_rows, pairs)
        + [pl.BlockSpec((width, 128), lambda m, h: (0, column + h))],
        out_specs=[
            pl.BlockSpec((block_rows, 128), lambda m, h: (m, h)),
            pl.BlockSpec((block_rows, 128), lambda m, h: (m, 0)),
            pl.BlockSpec((block_rows, width), lambda m, h: (m, 0)),
        ],
        out_shape=[
            jax.ShapeDtypeStruct((rows, local), bf16),
            jax.ShapeDtypeStruct((rows, 128), f32),
            jax.ShapeDtypeStruct((rows, width), bf16),
        ],
        scratch_shapes=[pltpu.VMEM((block_rows, width), f32)],
        compiler_params=kernel_params(2, 60),
        cost_estimate=pl.CostEstimate(
            flops=rows * 2 * local * (width + 12 * HALF),
            bytes_accessed=20 * rows * local,
            transcendentals=rows * 3 * HALF * 2 * pairs,
        ),
        name="self_attention",
    )(qkv, qkv, qkv, bias, weights)


def self_back_kernel(
    q_ref, k_ref, v_ref, bias_ref, grad_ref, log_ref, own_ref, to_low_ref, to_high_ref
):
    pair = pl.program_id(1)
    parts = grad_ref.shape[0] // HALF
    pieces = [[None] * (parts + 2), [None] * (parts + 2)]
    for part in range(parts):
        rows = slice(part * HALF, (part + 1) * HALF)
        span = slice(part * HALF, (part + 3) * HALF)
        query_grad, key_grad, value_grad = attend_rows_back(
            q_ref[(part + 1) * HALF : (part + 2) * HALF, :],
            k_ref[span, :],
            v_ref[span, :],
            bias_ref[rows, :],
            get_logs(log_ref, rows, pair),
            grad_ref[rows, :],
        )
        own_ref[0, rows, :] = query_grad
        for kind, near_grad in enumerate((key_grad, value_grad)):
            for third in range(3):
                piece = near_grad[third * HALF : (third + 1) * HALF]
                held = pieces[kind][part + third]
                pieces[kind][part + third] = piece if held is None else held + piece
    for kind in range(2):
        to_low_ref[kind] = pieces[kind][0].astype(bf16)
        for part in range(parts):
            own_ref[1 + kind, part * HALF : (part + 1) * HALF, :] = pieces[kind][part + 1]
        to_high_ref[kind] = pieces[kind][parts + 1].astype(bf16)


def self_attention_back(qkv, bias, grad, logs, micro, block_rows):
    rows, local = grad.shape
    pairs = local // 128
    edge = pl.BlockSpec((2, None, HALF, 128), lambda m, h: (0, m, 0, h))
    return pl.pallas_call(
        self_back_kernel,
        grid=(micro, pairs),
        in_specs=self_specs(block_rows, pairs)
        + [
            pl.BlockSpec((block_rows, 128), lambda m, h: (m, h)),
            pl.BlockSpec((block_rows, 128), lambda m, h: (m, 0)),
        ],
        out_specs=[
            pl.BlockSpec((3, block_rows, 128), lambda m, h: (0, m, h)),
            edge,
            edge,
        ],
        out_shape=[
            jax.ShapeDtypeStruct((3, rows, local), f32),
            jax.ShapeDtypeStruct((2, micro, HALF, local), bf16),
            jax.ShapeDtypeStruct((2, micro, HALF, local), bf16),
        ],
        compiler_params=kernel_params(2, 60),
        cost_estimate=pl.CostEstimate(
            flops=20 * rows * 3 * HALF * local,
            bytes_accessed=40 * rows * local,
            transcendentals=rows * 3 * HALF * 2 * pairs,
        ),
        name="self_attention_back",
    )(qkv, qkv, qkv, bias, grad, logs)


def cross_kernel(q_ref, k_ref, v_ref, bias_ref, weight_ref, out_ref, log_ref, sum_ref, acc_ref):
    pair = pl.program_id(1)
    for part in range(q_ref.shape[0] // HALF):
        rows = slice(part * HALF, (part + 1) * HALF)
        out, logs = attend_rows(q_ref[rows, :], k_ref[...], v_ref[...], bias_ref[rows, :])
        out_ref[rows, :] = out.astype(bf16)
        put_logs(log_ref, rows, logs, pair)
    add_product(acc_ref, sum_ref, out_ref[...], weight_ref[...])


def cross_specs(block_rows, pairs):
    return [
        pl.BlockSpec((block_rows, 128), lambda m, h: (m, h)),
        pl.BlockSpec((2 * TXT, 128), lambda m, h: (m, h)),
        pl.BlockSpec((2 * TXT, 128), lambda m, h: (m, h)),
        pl.BlockSpec((block_rows, 2 * TXT), lambda m, h: (m, 0)),
    ]


def cross_attention(query, keys, values, bias, weights, column, micro, block_rows):
    rows, local = query.shape
    width = weights.shape[0]
    pairs = local // 128
    return pl.pallas_call(
        cross_kernel,
        grid=(micro, pairs),
        in_specs=cross_specs(block_rows, pairs)
        + [pl.BlockSpec((width, 128), lambda m, h: (0, column + h))],
        out_specs=[
            pl.BlockSpec((block_rows, 128), lambda m, h: (m, h)),
            pl.BlockSpec((block_rows, 128), lambda m, h: (m, 0)),
            pl.BlockSpec((block_rows, width), lambda m, h: (m, 0)),
        ],
        out_shape=[
            jax.ShapeDtypeStruct((rows, local), bf16),
            jax.ShapeDtypeStruct((rows, 128), f32),
            jax.ShapeDtypeStruct((rows, width), bf16),
        ],
        scratch_shapes=[pltpu.VMEM((block_rows, width), f32)],
        compiler_params=kernel_params(2, 60),
        cost_estimate=pl.CostEstimate(
            flops=rows * 2 * local * (width + 8 * TXT),
            bytes_accessed=16 * rows * local,
            transcendentals=rows * 2 * TXT * 2 * pairs,
        ),
        name="cross_attention",
    )(query, keys, values, bias, weights)


def cross_back_kernel(
    q_ref, k_ref, v_ref, bias_ref, grad_ref, log_ref, weight_ref,
    dq_ref, dk_ref, dv_ref, sum_ref, acc_ref,
):
    pair = pl.program_id(1)
    key_total = value_total = None
    for part in range(q_ref.shape[0] // HALF):
        rows = slice(part * HALF, (part + 1) * HALF)
        query_grad, key_grad, value_grad = attend_rows_back(
            q_ref[rows, :],
            k_ref[...],
            v_ref[...],
            bias_ref[rows, :],
            get_logs(log_ref, rows, pair),
            grad_ref[rows, :],
        )
        dq_ref[rows, :] = query_grad.astype(bf16)
        key_total = key_grad if part == 0 else key_total + key_grad
        value_total = value_grad if part == 0 else value_total + value_grad
    dk_ref[...] = key_total.astype(bf16)
    dv_ref[...] = value_total.astype(bf16)
    add_product(acc_ref, sum_ref, dq_ref[...], weight_ref[...])


def cross_attention_back(
    query, keys, values, bias, grad, logs, weights, column, micro, block_rows
):
    rows, local = query.shape
    width = weights.shape[0]
    pairs = local // 128
    text = pl.BlockSpec((2 * TXT, 128), lambda m, h: (m, h))
    return pl.pallas_call(
        cross_back_kernel,
        grid=(micro, pairs),
        in_specs=cross_specs(block_rows, pairs)
        + [
            pl.BlockSpec((block_rows, 128), lambda m, h: (m, h)),
            pl.BlockSpec((block_rows, 128), lambda m, h: (m, 0)),
            pl.BlockSpec((width, 128), lambda m, h: (0, column + h)),
        ],
        out_specs=[
            pl.BlockSpec((block_rows, 128), lambda m, h: (m, h)),
            text,
            text,
            pl.BlockSpec((block_rows, width), lambda m, h: (m, 0)),
        ],
        out_shape=[
            jax.ShapeDtypeStruct((rows, local), bf16),
            jax.ShapeDtypeStruct(keys.shape, bf16),
            jax.ShapeDtypeStruct(keys.shape, bf16),
            jax.ShapeDtypeStruct((rows, width), bf16),
        ],
        scratch_shapes=[pltpu.VMEM((block_rows, width), f32)],
        compiler_params=kernel_params(2, 60),
        cost_estimate=pl.CostEstimate(
            flops=rows * 2 * local * (width + 20 * TXT),
            bytes_accessed=30 * rows * local,
            transcendentals=rows * 2 * TXT * 2 * pairs,
        ),
        name="cross_attention_back",
    )(query, keys, values, bias, grad, logs, weights)


def ffn_kernel(*refs, summed):
    (
        normed_ref, normed_t_ref, cot_ref, cot_t_ref, outer_ref, gate_ref, up_ref,
        g_outer_ref, g_gate_ref, g_up_ref, out_ref, back_ref, *refs,
    ) = refs
    j = pl.program_id(0)
    step = gate_ref.shape[1]
    if summed:
        sum_ref, out_acc, back_acc, full = refs[:4]
        me = lax.axis_index("seq")
        digits = seq_digits(me)
        core = digits[0]
        partners = [me + stride * (1 - 2 * digit) for stride, digit in zip(STRIDES, digits)]
        pl.when(j == 0)(lambda: [greet(me, digits), None][1])
        pieces = Pieces(refs[4:], sum_ref, partners, digits, step, lag=2)
        count = summed

        def over_core(slot):
            return pieces.over_core(full.at[slot, :, :, :, 1 - core], slot)

        def tick(t):
            @when((t >= 1) & (t - 1 < count))
            def _():
                slot = (t - 1) % SLOTS
                when(t - 1 >= SLOTS)(lambda: pieces.wait_sent(slot))
                over_core(slot).wait()
                pieces.add_core(t - 1, slot, lambda a, b, c: full[slot, a, b, c, core])

            pieces.later_steps(t, count)

    else:
        out_acc, back_acc = refs
    if summed:
        tick(j)
    gate = nn(normed_ref[...], gate_ref[...])
    up = nn(normed_ref[...], up_ref[...])
    grad = nn(cot_ref[...], outer_ref[...])
    chance = 1.0 / (1.0 + jnp.exp(-gate))
    swish = gate * chance
    active = (swish * up).astype(bf16)
    gate_grad = (grad * up * (chance * (1.0 + gate * (1.0 - chance)))).astype(bf16)
    up_grad = (grad * swish).astype(bf16)
    g_up = nn(normed_t_ref[...], up_grad).astype(bf16)
    if summed:

        @pl.when(j < count)
        def _():
            slot = j % SLOTS
            full[slot] = g_up.reshape(full.shape[1:])
            over_core(slot).start()

        @pl.when(j >= count)
        def _():
            g_up_ref[...] = g_up
    else:
        g_up_ref[...] = g_up
    g_gate_ref[...] = nn(normed_t_ref[...], gate_grad).astype(bf16)
    g_outer_ref[...] = nn(cot_t_ref[...], active).astype(bf16)

    @pl.when(j == 0)
    def _():
        out_acc[...] = jnp.zeros_like(out_acc)
        back_acc[...] = jnp.zeros_like(back_acc)

    out_acc[...] += nt(active, outer_ref[...])
    back_acc[...] += nt(gate_grad, gate_ref[...])
    back_acc[...] += nt(up_grad, up_ref[...])

    @pl.when(j == pl.num_programs(0) - 1)
    def _():
        out_ref[...] = out_acc[...].astype(bf16)
        back_ref[...] = back_acc[...].astype(bf16)
        if summed:
            for t in range(pl.num_programs(0), count + 4):
                tick(t)
            pieces.finish(count)


FFN_STEP = 256
SUMMED_STEPS = 9


def feed_forward(normed, normed_t, cotangent, weights, hidden, step=FFN_STEP):
    rows, width = normed.shape
    steps = hidden // step
    seq_count = lax.axis_size("seq")
    share = width // seq_count
    summed = SUMMED_STEPS if seq_count == 16 and share % 16 == 0 else 0
    assert not summed or summed < steps <= 2 * summed
    whole = lambda shape: pl.BlockSpec(shape, lambda j: (0, 0))
    held = lambda shape: pl.BlockSpec(shape, lambda j: (0, 0), pipeline_mode=pl.Buffered(1))
    column = lambda first: pl.BlockSpec((width, step), lambda j: (0, first + j))
    scratch = [pltpu.VMEM((rows, width), f32)] * 2
    out_specs = [
        column(0),
        column(0),
        column(0),
        whole((rows, width)),
        whole((rows, width)),
    ]
    out_shape = [
        jax.ShapeDtypeStruct((width, hidden), bf16),
        jax.ShapeDtypeStruct((width, hidden), bf16),
        jax.ShapeDtypeStruct((width, hidden - summed * step), bf16),
        jax.ShapeDtypeStruct((rows, width), bf16),
        jax.ShapeDtypeStruct((rows, width), bf16),
    ]
    params = kernel_params(1, 60)
    if summed:
        scratch += [pltpu.VMEM((SLOTS, 2, 2, 2, 2, share, step), bf16)]
        scratch += Pieces.scratch(share, step)
        out_specs[2] = pl.BlockSpec((width, step), lambda j: (0, j // summed * (j - summed)))
        out_specs.append(pl.BlockSpec(memory_space=pl.ANY))
        out_shape.append(jax.ShapeDtypeStruct((share, summed * step), f32))
        params = pltpu.CompilerParams(
            dimension_semantics=("arbitrary",),
            collective_id=3,
            has_side_effects=True,
            vmem_limit_bytes=60 * 1024 * 1024,
        )
    outs = pl.pallas_call(
        functools.partial(ffn_kernel, summed=summed),
        grid=(steps,),
        in_specs=[
            held((rows, width)),
            held((width, rows)),
            held((rows, width)),
            held((width, rows)),
            column(0),
            column(steps),
            column(2 * steps),
        ],
        out_specs=out_specs,
        out_shape=out_shape,
        scratch_shapes=scratch,
        compiler_params=params,
        cost_estimate=pl.CostEstimate(
            flops=18 * rows * width * hidden,
            bytes_accessed=12 * width * hidden,
            transcendentals=rows * hidden,
        ),
        name="feed_forward",
    )(normed, normed_t, cotangent, cotangent.T, weights, weights, weights)
    return outs


def qkv_back_kernel(
    own_ref, after_ref, before_ref, normed_t_ref, weight_ref, table_ref,
    grad_ref, back_ref, acc, *, kind_steps, micro, block_rows,
):
    j = pl.program_id(0)
    kind = j // kind_steps
    edges = (kind > 0).astype(f32)
    turned = kind < 2
    near_rows = block_rows + 2 * HALF

    def own_table(index):
        return jnp.concatenate(
            [
                table_ref[index, m * near_rows + HALF : (m + 1) * near_rows - HALF]
                for m in range(micro)
            ],
            axis=0,
        )

    own_factor = jnp.where(turned, own_table(0), 1.0)
    below_factor = jnp.where(turned, -own_table(1), 0.0)
    above_factor = jnp.where(turned, -own_table(2), 0.0)
    total = []
    for m in range(micro):
        first = m * block_rows
        total.append(own_ref[first : first + HALF] + edges * after_ref[m].astype(f32))
        if block_rows > 2 * HALF:
            total.append(own_ref[first + HALF : first + block_rows - HALF])
        total.append(
            own_ref[first + block_rows - HALF : first + block_rows]
            + edges * before_ref[m].astype(f32)
        )
    total = jnp.concatenate(total, axis=0)
    grad = jnp.concatenate(
        [
            turn(total[:, i : i + 128], own_factor, below_factor, above_factor)
            for i in range(0, total.shape[1], 128)
        ],
        axis=1,
    ).astype(bf16)
    grad_ref[...] = nn(normed_t_ref[...], grad).astype(bf16)
    part = nt(grad, weight_ref[...])

    @pl.when(j == 0)
    def _():
        acc[...] = part

    @pl.when(j > 0)
    def _():
        acc[...] += part

    @pl.when(j == pl.num_programs(0) - 1)
    def _():
        back_ref[...] = acc[...].astype(bf16)


def qkv_back(own, after, before, normed_t, weights, table, micro, block_rows, step=256):
    _, rows, local = own.shape
    width = normed_t.shape[0]
    kind_steps = local // step
    edge = pl.BlockSpec(
        (None, micro, HALF, step),
        lambda j: (jnp.maximum(j // kind_steps - 1, 0), 0, 0, j % kind_steps),
    )
    return pl.pallas_call(
        functools.partial(
            qkv_back_kernel, kind_steps=kind_steps, micro=micro, block_rows=block_rows
        ),
        grid=(3 * kind_steps,),
        in_specs=[
            pl.BlockSpec((None, rows, step), lambda j: (j // kind_steps, 0, j % kind_steps)),
            edge,
            edge,
            pl.BlockSpec((width, rows), lambda j: (0, 0)),
            pl.BlockSpec((width, step), lambda j: (0, j)),
            pl.BlockSpec(table.shape, lambda j: (0, 0, 0)),
        ],
        out_specs=[
            pl.BlockSpec((width, step), lambda j: (0, j)),
            pl.BlockSpec((rows, width), lambda j: (0, 0)),
        ],
        out_shape=[
            jax.ShapeDtypeStruct((width, 3 * local), bf16),
            jax.ShapeDtypeStruct((rows, width), bf16),
        ],
        scratch_shapes=[pltpu.VMEM((rows, width), f32)],
        compiler_params=kernel_params(1, 60),
        cost_estimate=pl.CostEstimate(
            flops=12 * rows * width * local,
            bytes_accessed=12 * width * local + 12 * rows * local,
            transcendentals=0,
        ),
        name="qkv_back",
    )(own, after, before, normed_t, weights, table)


def time_features(steps_row):
    half_width = TEMB // 2
    ladder = jnp.exp(-math.log(10000.0) * jnp.arange(half_width, dtype=f32) / half_width)
    angles = steps_row.astype(f32)[:, None] * ladder[None, :]
    return jnp.concatenate([jnp.cos(angles), jnp.sin(angles)], axis=-1)


def with_loads(kernel, places):
    def wrapped(*refs):
        refs = list(refs)
        sems = refs.pop()
        targets = refs[-len(places) :]
        refs = refs[: -len(places)]
        copies = [
            pltpu.make_async_copy(refs[place], target, sems.at[i])
            for i, (place, target) in enumerate(zip(places, targets))
        ]
        for copy in copies:
            copy.start()
        for place, target in zip(places, targets):
            refs[place] = target

        def loaded():
            for copy in copies:
                copy.wait()

        kernel(*refs, loaded=loaded)

    return wrapped


def load_scratch(arrays):
    return [pltpu.VMEM(array.shape, array.dtype) for array in arrays] + [
        pltpu.SemaphoreType.DMA((len(arrays),))
    ]


def norm_back_unit(m, index, block_rows, grad_of, up_ref, hidden_ref, two_ref, later_ref, sums_ref, emit):
    width = hidden_ref.shape[1]
    for start in range(0, block_rows, HALF):
        span = slice(m * block_rows + start, m * block_rows + start + HALF)
        later = later_ref[span, :] > 0.5
        lanes = slice((index + 1) * width, (index + 2) * width)
        factor = jnp.where(later, two_ref[m, 1:2, lanes], two_ref[m, 0:1, lanes])
        total, sums = norm_back_tile(
            grad_of(span),
            up_ref[span, :].astype(f32),
            hidden_ref[span, :].astype(f32),
            (~later, later),
            factor,
        )
        for item in range(2):
            for kind in range(2):
                at = slice(kind * width, (kind + 1) * width)
                before = sums_ref[m, item : item + 1, at] if start else 0.0
                sums_ref[m, item : item + 1, at] = sums[item][kind] + before
        emit(span, start, total)


def cross_stage_kernel(
    back_ref, up_ref, hidden_ref, two_ref, later_ref, weight_ref, q_ref, k_ref, v_ref, bias_ref,
    log_ref, *refs, spans, step, micro, ready, loaded,
):
    sources, refs = refs[: len(spans)], refs[len(spans) :]
    (
        grad_ref, sums_ref, low_t_ref, dq_ref, dk_ref, dv_ref, next_ref, got_next_ref, out_ref,
        own_sem, got_ref, mixed_ref, acc_ref, out_w_ref, query_w_ref, weight_sem,
        swap_send, swap_recv, next_send, next_recv,
    ) = refs[:20]
    refs = refs[20:]
    me = lax.axis_index("seq")
    mine = lax.axis_index("tensor")
    digits = seq_digits(me)
    partners = greet_all(me, mine, digits)
    rows = back_ref.shape[0]
    block_rows = rows // micro
    pairs = q_ref.shape[1] // 128
    text = k_ref.shape[0] // micro

    def over_tensor(m):
        span = pl.ds(m * block_rows, block_rows)
        return to_tensor(
            mine, back_ref.at[span], got_ref.at[span], swap_send.at[m], swap_recv.at[m]
        )

    def over_next(m):
        span = pl.ds(m * block_rows, block_rows)
        return to_tensor(
            mine, next_ref.at[span], got_next_ref.at[span], next_send.at[m], next_recv.at[m]
        )

    def norm_unit(m):
        over_tensor(m).wait_recv()
        if m == 0:
            loaded()
            for load in loads:
                load.wait()

        def emit(span, start, total):
            grad_ref[span, :] = total
            rounded = total.astype(bf16)
            low_t_ref[:, span] = rounded.T
            mixed_ref[start : start + HALF, :] = nn(rounded, out_w_ref[...]).astype(bf16)

        norm_back_unit(
            m, 4, block_rows,
            lambda span: back_ref[span, :].astype(f32) + got_ref[span, :].astype(f32),
            up_ref, hidden_ref, two_ref, later_ref, sums_ref, emit,
        )

    def pair_unit(m, pair):
        lanes = pl.ds(pl.multiple_of(pair * 128, 128), 128)
        keys = slice(m * text, (m + 1) * text)
        key_total = value_total = None
        for start in range(0, block_rows, HALF):
            span = slice(m * block_rows + start, m * block_rows + start + HALF)
            query_grad, key_grad, value_grad = attend_rows_back(
                q_ref[span, lanes],
                k_ref[keys, lanes],
                v_ref[keys, lanes],
                bias_ref[span, :],
                get_logs(log_ref, span, pair),
                mixed_ref[start : start + HALF, lanes],
            )
            dq_ref[span, lanes] = query_grad.astype(bf16)
            key_total = key_grad if start == 0 else key_total + key_grad
            value_total = value_grad if start == 0 else value_total + value_grad
        dk_ref[keys, lanes] = key_total.astype(bf16)
        dv_ref[keys, lanes] = value_total.astype(bf16)
        own = slice(m * block_rows, (m + 1) * block_rows)
        acc_ref[...] += nt(dq_ref[own, lanes], query_w_ref[:, lanes])

    def close(m):
        own = slice(m * block_rows, (m + 1) * block_rows)
        next_ref[own, :] = acc_ref[...].astype(bf16)
        if m < micro - 1:
            acc_ref[...] = jnp.zeros_like(acc_ref)
            over_next(m).start()

    local = q_ref.shape[1]
    loads = [
        pltpu.make_async_copy(
            weight_ref.at[:, k * local : (k + 1) * local], target, weight_sem.at[i]
        )
        for i, (k, target) in enumerate(((5, out_w_ref), (4, query_w_ref)))
    ]
    for load in loads:
        load.start()
    acc_ref[...] = jnp.zeros_like(acc_ref)
    pieces = Pieces(refs, out_ref, partners, digits, step)
    work = []
    spot = 0
    for m in range(micro):
        spot = max(spot, ready * (m + 1))
        work.append((spot, spot + 1, lambda t, m=m: norm_unit(m)))
        spot += 1
        begin = spot

        def pair_units(t, m=m, begin=begin):
            for k in range(2):
                pair_unit(m, 2 * (t - begin) + k)

        work.append((begin, begin + pairs // 2, pair_units))
        spot += pairs // 2
        work.append((spot - 1, spot, lambda t, m=m: close(m)))
    for m in range(micro):
        over_tensor(m).start()
    pieces.run(sources, spans, own_sem, work, spot)
    for m in range(micro):
        over_tensor(m).wait_send()
        if m < micro - 1:
            over_next(m).wait()


def cross_stage(
    back, up, hidden, two, later, query, keys, values, bias, logs, weights, local, sources,
    spans, micro, which=2, step=256,
):
    seq_count = lax.axis_size("seq")
    rows, width = hidden.shape
    share = width // seq_count
    block_rows = rows // micro
    any_space = pl.BlockSpec(memory_space=pl.ANY)
    vmem = pl.BlockSpec(memory_space=pltpu.VMEM)
    args = [back, up, hidden, two, later, weights, query, keys, values, bias, logs]
    places = (1, 2, 3, 4, 6, 7, 8, 9, 10)
    return pl.pallas_call(
        with_loads(
            functools.partial(cross_stage_kernel, spans=spans, step=step, micro=micro, ready=4),
            places,
        ),
        out_shape=[
            jax.ShapeDtypeStruct((rows, width), f32),
            jax.ShapeDtypeStruct((micro, 2, 2 * width), f32),
            jax.ShapeDtypeStruct((width, rows), bf16),
            jax.ShapeDtypeStruct((rows, local), bf16),
            jax.ShapeDtypeStruct(keys.shape, bf16),
            jax.ShapeDtypeStruct(keys.shape, bf16),
            jax.ShapeDtypeStruct((rows, width), bf16),
            jax.ShapeDtypeStruct((rows - block_rows, width), bf16),
            jax.ShapeDtypeStruct((share, sum(span for _, span in spans)), f32),
        ],
        in_specs=[vmem] + [any_space] * (10 + len(spans)),
        out_specs=[vmem] * 7 + [any_space] * 2,
        scratch_shapes=[
            pltpu.SemaphoreType.DMA((SLOTS,)),
            pltpu.VMEM((rows, width), bf16),
            pltpu.VMEM((block_rows, local), bf16),
            pltpu.VMEM((block_rows, width), f32),
            pltpu.VMEM((width, local), bf16),
            pltpu.VMEM((width, local), bf16),
            pltpu.SemaphoreType.DMA((2,)),
        ]
        + [pltpu.SemaphoreType.DMA((micro,))] * 4
        + Pieces.scratch(share, step)
        + load_scratch([args[place] for place in places]),
        compiler_params=pltpu.CompilerParams(
            collective_id=which, has_side_effects=True, vmem_limit_bytes=60 * 1024 * 1024
        ),
        cost_estimate=pl.CostEstimate(
            flops=8 * rows * width * local, bytes_accessed=40 * rows * width, transcendentals=0
        ),
        name="cross_stage",
    )(
        *args,
        *[source.reshape(2, 2, 2, 2, share, source.shape[1]) for source in sources],
    )


def self_stage_kernel(
    back_ref, got_early_ref, up_ref, hidden_ref, two_ref, later_ref, weight_ref, qkv_ref, bias_ref,
    log_ref, other_ref, mixed_one_ref, two_low_t_ref, mixed_two_ref, two_t_ref, dq_ref, *refs,
    spans, step, micro, ready, seq_count, loaded,
):
    sources, refs = refs[: len(spans)], refs[len(spans) :]
    (
        grad_ref, sums_ref, own_ref, from_low_ref, from_high_ref, got_other_ref, out_ref,
        g_cross_out_ref, g_cross_query_ref, g_self_out_ref,
        own_sem, got_ref, mixed_ref, to_low_ref, to_high_ref, out_w_ref, weight_sem, swap_sem,
        halo_send, halo_recv, low_t_ref, product_ref, product_sem,
    ) = refs[:23]
    refs = refs[23:]
    me = lax.axis_index("seq")
    mine = lax.axis_index("tensor")
    digits = seq_digits(me)
    has_low = me > 0
    has_high = me < seq_count - 1
    partners = greet_all(me, mine, digits, ((has_low, me - 1), (has_high, me + 1)))
    rows = back_ref.shape[0]
    block_rows = rows // micro
    near_rows = block_rows + 2 * HALF
    local = qkv_ref.shape[1] // 3
    pairs = local // 128
    last = micro - 1

    def over_tensor():
        return to_tensor(
            mine,
            back_ref.at[pl.ds(last * block_rows, block_rows)],
            got_ref,
            swap_sem.at[0],
            swap_sem.at[1],
        )

    def over_other():
        span = pl.ds(block_rows, rows - block_rows)
        return to_tensor(
            mine, other_ref.at[span], got_other_ref, swap_sem.at[2], swap_sem.at[3]
        )

    def to_low(m):
        return send_to(
            me - 1, to_low_ref.at[m], from_high_ref.at[m], halo_send.at[0, m], halo_recv.at[0, m]
        )

    def to_high(m):
        return send_to(
            me + 1, to_high_ref.at[m], from_low_ref.at[m], halo_send.at[1, m], halo_recv.at[1, m]
        )

    load = pltpu.make_async_copy(
        weight_ref.at[:, 3 * local : 4 * local], out_w_ref, weight_sem
    )
    load.start()

    def norm_unit(m):
        if m == 0:
            loaded()
            load.wait()
        if m == last:
            over_tensor().wait_recv()

        def grad_of(span):
            if m == last:
                other = got_ref[span.start - last * block_rows : span.stop - last * block_rows, :]
            else:
                other = got_early_ref[span, :]
            return back_ref[span, :].astype(f32) + other.astype(f32)

        def emit(span, start, total):
            grad_ref[span, :] = total
            rounded = total.astype(bf16)
            low_t_ref[:, span] = rounded.T
            mixed_ref[start : start + HALF, :] = nn(rounded, out_w_ref[...]).astype(bf16)

        norm_back_unit(
            m, 2, block_rows, grad_of, up_ref, hidden_ref, two_ref, later_ref, sums_ref, emit
        )

    def pair_unit(m, pair):
        def lanes(kind):
            return pl.ds(pl.multiple_of(kind * local + pair * 128, 128), 128)

        parts = block_rows // HALF
        held = [[None] * (parts + 2), [None] * (parts + 2)]
        at = lanes(0)
        for part in range(parts):
            span = slice(m * block_rows + part * HALF, m * block_rows + (part + 1) * HALF)
            own_rows = slice(m * near_rows + (part + 1) * HALF, m * near_rows + (part + 2) * HALF)
            near = slice(m * near_rows + part * HALF, m * near_rows + (part + 3) * HALF)
            query_grad, key_grad, value_grad = attend_rows_back(
                qkv_ref[own_rows, at],
                qkv_ref[near, lanes(1)],
                qkv_ref[near, lanes(2)],
                bias_ref[span, :],
                get_logs(log_ref, span, pair),
                mixed_ref[part * HALF : (part + 1) * HALF, at],
            )
            own_ref[0, span, at] = query_grad
            for kind, near_grad in enumerate((key_grad, value_grad)):
                for third in range(3):
                    piece = near_grad[third * HALF : (third + 1) * HALF]
                    before = held[kind][part + third]
                    held[kind][part + third] = piece if before is None else before + piece
        for kind in range(2):
            to_low_ref[m, kind, :, at] = held[kind][0].astype(bf16)
            for part in range(parts):
                span = slice(m * block_rows + part * HALF, m * block_rows + (part + 1) * HALF)
                own_ref[1 + kind, span, at] = held[kind][part + 1]
            to_high_ref[m, kind, :, at] = held[kind][parts + 1].astype(bf16)

    products = (
        (two_low_t_ref, mixed_two_ref, g_cross_out_ref),
        (two_t_ref, dq_ref, g_cross_query_ref),
        (low_t_ref, mixed_one_ref, g_self_out_ref),
    )

    def put(k):
        return pltpu.make_async_copy(product_ref.at[k], products[k][2], product_sem.at[k])

    def product_unit(k):
        left, right, _ = products[k]
        product_ref[k] = nn(left[...], right[...]).astype(bf16)
        put(k).start()

    def close(m):
        pl.when(has_low)(lambda: to_low(m).start())
        pl.when(has_high)(lambda: to_high(m).start())

    pieces = Pieces(refs, out_ref, partners, digits, step)
    work = []
    spot = 1
    for m in range(micro):
        if m == last:
            spot = max(spot, ready)
        work.append((spot, spot + 1, lambda t, m=m: norm_unit(m)))
        spot += 1
        begin = spot

        def pair_units(t, m=m, begin=begin):
            for k in range(2):
                pair_unit(m, 2 * (t - begin) + k)

        work.append((begin, begin + pairs // 2, pair_units))
        spot += pairs // 2
        work.append((spot - 1, spot, lambda t, m=m: close(m)))
    for k in range(len(products)):
        work.append((spot, spot + 1, lambda t, k=k: product_unit(k)))
        spot += 1
    over_tensor().start()
    over_other().start()

    @pl.when(jnp.logical_not(has_low))
    def _():
        from_low_ref[...] = jnp.zeros_like(from_low_ref)

    @pl.when(jnp.logical_not(has_high))
    def _():
        from_high_ref[...] = jnp.zeros_like(from_high_ref)

    pieces.run(sources, spans, own_sem, work, spot)
    over_tensor().wait_send()
    over_other().wait()
    for k in range(len(products)):
        put(k).wait()
    for m in range(micro):

        @pl.when(has_low)
        def _(m=m):
            to_low(m).wait_send()
            to_high(m).wait_recv()

        @pl.when(has_high)
        def _(m=m):
            to_high(m).wait_send()
            to_low(m).wait_recv()


def self_stage(
    back, got_early, up, hidden, two, later, qkv, bias, logs, weights, local, other, products, sources,
    spans, micro, which=4, step=256,
):
    seq_count = lax.axis_size("seq")
    rows, width = hidden.shape
    share = width // seq_count
    block_rows = rows // micro
    any_space = pl.BlockSpec(memory_space=pl.ANY)
    vmem = pl.BlockSpec(memory_space=pltpu.VMEM)
    args = [back, got_early, up, hidden, two, later, weights, qkv, bias, logs, other, *products]
    places = (1, 2, 3, 4, 5, 7, 8, 9, 11, 12, 13, 14, 15)
    edge = (micro, 2, HALF, local)
    return pl.pallas_call(
        with_loads(
            functools.partial(
                self_stage_kernel,
                spans=spans,
                step=step,
                micro=micro,
                ready=4,
                seq_count=seq_count,
            ),
            places,
        ),
        out_shape=[
            jax.ShapeDtypeStruct((rows, width), f32),
            jax.ShapeDtypeStruct((micro, 2, 2 * width), f32),
            jax.ShapeDtypeStruct((3, rows, local), f32),
            jax.ShapeDtypeStruct(edge, bf16),
            jax.ShapeDtypeStruct(edge, bf16),
            jax.ShapeDtypeStruct((rows - block_rows, width), bf16),
            jax.ShapeDtypeStruct((share, sum(span for _, span in spans)), f32),
        ]
        + [jax.ShapeDtypeStruct((width, local), bf16)] * 3,
        in_specs=[vmem] + [any_space] * (15 + len(spans)),
        out_specs=[vmem] * 5 + [any_space] * 5,
        scratch_shapes=[
            pltpu.SemaphoreType.DMA((SLOTS,)),
            pltpu.VMEM((block_rows, width), bf16),
            pltpu.VMEM((block_rows, local), bf16),
            pltpu.VMEM(edge, bf16),
            pltpu.VMEM(edge, bf16),
            pltpu.VMEM((width, local), bf16),
            pltpu.SemaphoreType.DMA,
            pltpu.SemaphoreType.DMA((4,)),
            pltpu.SemaphoreType.DMA((2, micro)),
            pltpu.SemaphoreType.DMA((2, micro)),
            pltpu.VMEM((width, rows), bf16),
            pltpu.VMEM((3, width, local), bf16),
            pltpu.SemaphoreType.DMA((3,)),
        ]
        + Pieces.scratch(share, step)
        + load_scratch([args[place] for place in places]),
        compiler_params=pltpu.CompilerParams(
            collective_id=which, has_side_effects=True, vmem_limit_bytes=60 * 1024 * 1024
        ),
        cost_estimate=pl.CostEstimate(
            flops=8 * rows * width * local, bytes_accessed=40 * rows * width, transcendentals=0
        ),
        name="self_stage",
    )(
        *args,
        *[source.reshape(2, 2, 2, 2, share, source.shape[1]) for source in sources],
    )


EARLY_COLUMNS = (1024, 1280)


def on_device(
    latents,
    context,
    lengths,
    text_len,
    timesteps,
    self_qkv,
    self_out,
    cross_query,
    cross_kv,
    cross_out,
    ffn_in,
    ffn_out,
    mod_weight,
    mod_bias,
    out_grad,
):
    micro, block_rows, model_width = latents.shape
    seq_count = lax.axis_size("seq")
    me = lax.axis_index("seq")
    frame_count = block_rows * seq_count
    item_count = lengths.shape[1]
    local = self_qkv.shape[2]
    hidden = ffn_in.shape[2]
    rows = micro * block_rows
    text_width = context.shape[2]

    attn_share = jnp.concatenate(
        [
            self_qkv[0],
            self_qkv[1],
            self_qkv[2],
            self_out.T,
            cross_query,
            cross_out.T,
            jnp.concatenate([cross_kv[0], cross_kv[1]], axis=0),
        ],
        axis=1,
    )
    ffn_share = jnp.concatenate([ffn_out.T, ffn_in[0], ffn_in[1]], axis=1)
    features = time_features(timesteps.reshape(-1))
    own_features = lax.dynamic_slice_in_dim(
        features, me * mod_weight.shape[0], mod_weight.shape[0], 1
    )
    bias_share = mod_bias.shape[1]
    bias_wide = lax.dynamic_update_slice_in_dim(
        jnp.zeros((6, model_width), f32), mod_bias.astype(f32), me * bias_share, 1
    )
    mod_part = jnp.dot(
        own_features, mod_weight.astype(f32).reshape(mod_weight.shape[0], -1), precision=highest
    ) + bias_wide.reshape(1, -1)
    (
        attn_all,
        normed_near,
        normed_one_t,
        two,
        later,
        near_table,
        self_bias,
        cross_bias,
    ) = gather_and_prepare(attn_share, mod_part, latents, lengths, text_len)
    ffn_share, attn_all = lax.optimization_barrier((ffn_share, attn_all))
    ffn_all = lax.all_gather(ffn_share, "seq", axis=0, tiled=True)
    pair_w = attn_all[:, 6 * local :].reshape(seq_count, 2, text_width // seq_count, local)
    key_w = pair_w[:, 0].reshape(text_width, local)
    value_w = pair_w[:, 1].reshape(text_width, local)

    first_frame = me * block_rows
    first_item = jnp.sum((jnp.cumsum(lengths, axis=1) <= first_frame).astype(jnp.int32), axis=1)
    base_item = jnp.minimum(first_item, item_count - 2)
    catalog = jnp.arange(item_count, dtype=jnp.int32)

    ahead = [(i, i + 1) for i in range(seq_count - 1)]
    behind = [(i + 1, i) for i in range(seq_count - 1)]
    latent = latents.reshape(rows, model_width)
    cotangent = out_grad.reshape(rows, model_width)
    near_context = jnp.concatenate(
        [
            lax.dynamic_slice_in_dim(context[m], base_item[m] * TXT, 2 * TXT, 0)
            for m in range(micro)
        ]
    )
    column = local // 128

    qkv = project(normed_near, attn_all, near_table, local)
    mixed_one, logs_one, part_one = self_attention(
        qkv, self_bias, attn_all, 3 * column, micro, block_rows
    )
    got_one = swap(part_one)
    text_keys = nn(near_context, key_w).astype(bf16)
    text_values = nn(near_context, value_w).astype(bf16)
    hidden_one, _, normed_two_t, query_two = norm_forward(
        latent, part_one, got_one, two, later, 2, micro, attn_all, 4, local
    )
    mixed_two, logs_two, part_two = cross_attention(
        query_two, text_keys, text_values, cross_bias, attn_all, 5 * column, micro, block_rows
    )
    got_two = swap(part_two)
    hidden_two, normed_three, normed_three_t = norm_forward(
        hidden_one, part_two, got_two, two, later, 4, micro
    )
    g_outer, g_gate, g_up, out_part, back_three, *up_early = feed_forward(
        normed_three, normed_three_t, cotangent, ffn_all, hidden
    )
    outer_total = early_sum(g_outer)

    share = text_width // seq_count
    fused = (
        seq_count == 16 and lax.axis_size("tensor") == 2 and (model_width // seq_count) % 16 == 0
    )

    def pair_grads(text_key_low, text_value_low):
        return jnp.concatenate(
            [
                tn(near_context, text_key_low).astype(bf16).reshape(seq_count, share, local),
                tn(near_context, text_value_low).astype(bf16).reshape(seq_count, share, local),
            ],
            axis=1,
        ).reshape(2 * text_width, local)

    if fused:
        first, second = EARLY_COLUMNS
        third = hidden - first - second
        (
            hidden_two_grad, sums_three, two_low_t, query_two_low, text_key_low, text_value_low,
            back_two, got_early, totals_a,
        ) = cross_stage(
            back_three, cotangent, hidden_two, two, later, query_two, text_keys, text_values,
            cross_bias, logs_two, attn_all, local, [g_gate], ((0, first),), micro,
        )
        (
            hidden_one_grad, sums_two, own_grads, from_low, from_high, got_last, totals_b,
            g_cross_out, g_cross_query, g_self_out,
        ) = self_stage(
            back_two, got_early, hidden_two_grad, hidden_one, two, later, qkv, self_bias, logs_one,
            attn_all, local, out_part,
            (mixed_one, two_low_t, mixed_two, normed_two_t, query_two_low),
            [g_gate], ((first, second),), micro,
        )
        crossed = [g_cross_out, g_cross_query, pair_grads(text_key_low, text_value_low)]
        sums = jnp.concatenate([sums_two, sums_three], axis=2)
        spans = ((0, g_up.shape[1]),) + ((0, local),) * 4
        sources = [g_up] + crossed + [g_self_out]
        if third:
            spans = ((first + second, third),) + spans
            sources = [g_gate] + sources
        late = third + g_up.shape[1]
        totals_c, latent_grad, mod_grad, bias_sum, got_first = finish_stage(
            own_grads, from_low, from_high, normed_one_t, attn_all, near_table, hidden_one_grad,
            latent, two, later, sums, lengths, own_features, out_part,
            sources, spans, micro,
        )
        totals = [totals_c[:, late + k * local : late + (k + 1) * local] for k in range(4)]
        grad_cross_out, grad_cross_query, grad_cross_kv, grad_self_out = totals
        qkv_total = totals_c[:, late + 4 * local :]
        gate_total = jnp.concatenate([totals_a, totals_b, totals_c[:, :third]], axis=1)
        up_total = jnp.concatenate([up_early[0], totals_c[:, third:late]], axis=1)
        out_got = jnp.concatenate([got_first, got_last], axis=0)
    else:
        got_three = swap(back_three)
        gate_total = early_sum(g_gate)
        up_total = early_sum(g_up)
        hidden_two_grad, sums_three, two_low_t, mixed_two_grad = norm_back(
            cotangent, back_three, got_three, hidden_two, two, later, 4, micro, attn_all, 5, local
        )
        query_two_low, text_key_low, text_value_low, back_two = cross_attention_back(
            query_two, text_keys, text_values, cross_bias, mixed_two_grad, logs_two,
            attn_all, 4 * column, micro, block_rows,
        )
        got_back_two = swap(back_two)
        hidden_one_grad, sums_two, one_low_t, mixed_one_grad = norm_back(
            hidden_two_grad, back_two, got_back_two, hidden_one, two, later, 2, micro,
            attn_all, 3, local,
        )
        own_grads, to_low, to_high = self_attention_back(
            qkv, self_bias, mixed_one_grad, logs_one, micro, block_rows
        )
        from_high = lax.ppermute(to_low, "seq", behind)
        from_low = lax.ppermute(to_high, "seq", ahead)
        g_self_out = nn(one_low_t, mixed_one).astype(bf16)
        g_qkv, back_one = qkv_back(
            own_grads, from_low, from_high, normed_one_t, attn_all, near_table, micro, block_rows
        )
        crossed = [
            nn(two_low_t, mixed_two).astype(bf16),
            nn(normed_two_t, query_two_low).astype(bf16),
            pair_grads(text_key_low, text_value_low),
        ]
        sums = jnp.concatenate(
            [piece.reshape(micro, 2, 2 * model_width) for piece in (sums_two, sums_three)], axis=2
        )
        totals, latent_grad, mod_grad, bias_sum, out_got = finish_apart(
            crossed + [g_self_out, g_qkv], back_one, hidden_one_grad, latent, two, later, sums,
            lengths, own_features, out_part,
        )
        grad_cross_out, grad_cross_query, grad_cross_kv, grad_self_out, qkv_total = totals
    block_out = (hidden_two + (out_part.astype(f32) + out_got.astype(f32))).astype(bf16)
    mod_grad = mod_grad.reshape(mod_weight.shape)
    bias_grad = lax.dynamic_slice_in_dim(
        bias_sum.reshape(6, model_width), me * bias_share, bias_share, 1
    )

    grad_qkv = jnp.stack([qkv_total[:, i * local : (i + 1) * local] for i in range(3)])
    return (
        block_out.reshape(latents.shape),
        latent_grad.reshape(latents.shape),
        grad_qkv,
        grad_self_out.T,
        grad_cross_query,
        grad_cross_kv.reshape(2, share, local),
        grad_cross_out.T,
        jnp.stack([gate_total, up_total]),
        outer_total.T,
        mod_grad,
        bias_grad,
    )


def solution(mesh):
    return jax.shard_map(
        on_device,
        mesh=mesh,
        in_specs=(
            P(None, "seq", None),
            P(),
            P(),
            P(),
            P(),
            P(None, "seq", "tensor"),
            P("tensor", "seq"),
            P("seq", "tensor"),
            P(None, "seq", "tensor"),
            P("tensor", "seq"),
            P(None, "seq", "tensor"),
            P("tensor", "seq"),
            P("seq", None, None),
            P(None, "seq"),
            P(None, "seq", None),
        ),
        out_specs=(
            P(None, "seq", None),
            P(None, "seq", None),
            P(None, "seq", "tensor"),
            P("tensor", "seq"),
            P("seq", "tensor"),
            P(None, "seq", "tensor"),
            P("tensor", "seq"),
            P(None, "seq", "tensor"),
            P("tensor", "seq"),
            P("seq", None, None),
            P(None, "seq"),
        ),
        check_vma=False,
    )
```
